32 devices in a mesh: row: 4 (over x, core), seq: 8 (over z, y).
Axes of the slice: x: 2, y: 2, z: 4, core: 2. Of those that a mesh axis runs over, the one named last changes fastest.
Arguments:
- frames: float32 [4, 1024, 768], P('row', 'seq'), may hold values from -6 to 6
- clip_lengths: int32 [4, 6], P('row'), may hold values from 0 to 1024, as said below
- query_weight: bfloat16 [768, 768], replicated, may hold values from -0.21875 to 0.21875
- query_bias: float32 [768], replicated, may hold values from -3 to 3
- key_weight: bfloat16 [768, 768], replicated, may hold values from -0.21875 to 0.21875
- value_weight: bfloat16 [768, 768], replicated, may hold values from -0.21875 to 0.21875
- value_bias: float32 [768], replicated, may hold values from -0.3 to 0.3
- out_weight: bfloat16 [768, 768], replicated, may hold values from -3.5 to 3.5
- out_bias: float32 [768], replicated, may hold values from -0.6 to 0.6
- norm1_gain: float32 [768], replicated, may hold values from 0.5 to 1.5
- norm1_bias: float32 [768], replicated, may hold values from -0.6 to 0.6
- up_weight: bfloat16 [768, 3072], replicated, may hold values from -0.21875 to 0.21875
- up_bias: float32 [3072], replicated, may hold values from -1.2 to 1.2
- down_weight: bfloat16 [3072, 768], replicated, may hold values from -0.109375 to 0.109375
- down_bias: float32 [768], replicated, may hold values from -0.6 to 0.6
- norm2_gain: float32 [768], replicated, may hold values from 0.5 to 1.5
- norm2_bias: float32 [768], replicated, may hold values from -0.6 to 0.6
- cotangent: float32 [4, 1024, 768], P('row', 'seq'), may hold values from -6 to 6
Outputs:
- encoded: float32 [4, 1024, 768], P('row', 'seq')
- frames_grad: float32 [4, 1024, 768], P('row', 'seq')
- query_weight_grad: float32 [768, 768], replicated
- query_bias_grad: float32 [768], replicated
- key_weight_grad: float32 [768, 768], replicated
- value_weight_grad: float32 [768, 768], replicated
- value_bias_grad: float32 [768], replicated
- out_weight_grad: float32 [768, 768], replicated
- out_bias_grad: float32 [768], replicated
- norm1_gain_grad: float32 [768], replicated
- norm1_bias_grad: float32 [768], replicated
- up_weight_grad: float32 [768, 3072], replicated
- up_bias_grad: float32 [3072], replicated
- down_weight_grad: float32 [3072, 768], replicated
- down_bias_grad: float32 [768], replicated
- norm2_gain_grad: float32 [768], replicated
- norm2_bias_grad: float32 [768], replicated
The draws below stay inside these ranges and needn't reach their ends.
Inputs may be any that keep to these rules, and one draw needn't show every extreme that they name: `clip_lengths`: each row's entries sum to 1024, nonzero entries first. The rows fall into aligned groups of 1 row, or of 2 rows where 1 is 1; in each group exactly one row, chosen by the seed, is a single recording: first entry 1024, the rest 0. In the other rows every nonzero entry is 250 or 1500, except the last nonzero one, which is cut at the row's end.
All inputs are finite; a program needn't handle non-finite values.
Results may differ from the reference program's by a relative error of at most 0.02.
Values may be sent and summed in bfloat16 or wider, within the bound.
A program may use at most 192 MiB of HBM per device.

```python
import math
from functools import partial
import jax
import jax.numpy as jnp
from jax import lax

D = 768
H = 12
HD = 64
FF = 3072
ROWS_DEV = 1
CLIP = 250
LONG_CLIP = 1500
ROWS = 4
ROW_LEN = 1024
MAXC = 6


def draw_clip_lengths(key, part):
    key = jax.random.fold_in(key, 11)
    choose_key, kind_key = jax.random.split(key)
    group_rows = max(ROWS_DEV, 2)
    groups = ROWS // group_rows
    chosen = jax.random.randint(choose_key, (groups,), 0, group_rows)
    row_index = jnp.arange(ROWS, dtype=jnp.int32)
    single_row = row_index % group_rows == jnp.repeat(chosen, group_rows)
    clip_kinds = jax.random.randint(kind_key, (ROWS, MAXC), 0, 6)
    clip_sizes = jnp.where(clip_kinds == 0, LONG_CLIP, CLIP).astype(jnp.int32)
    clip_ends = jnp.minimum(jnp.cumsum(clip_sizes, axis=1), ROW_LEN).astype(jnp.int32)
    clip_starts = jnp.concatenate([jnp.zeros((ROWS, 1), jnp.int32), clip_ends[:, :-1]], axis=1)
    column = jnp.arange(MAXC, dtype=jnp.int32)
    whole_row = jnp.where(column == 0, ROW_LEN, 0).astype(jnp.int32)
    return jnp.where(single_row[:, None], whole_row[None, :], clip_ends - clip_starts).astype(jnp.int32)


def level_of(own_key, extent, pieces, least, high):
    gain, own = 1.0, jax.random.fold_in(own_key, 6)
    for dim, shards_of in pieces:
        draws = jnp.exp(jax.random.uniform(jax.random.fold_in(own, dim), (shards_of,), jnp.float32, least / len(pieces), high / len(pieces)))
        gain = gain * jnp.repeat(draws, extent[dim] // shards_of).reshape([-1 if axis == dim else 1 for axis in range(len(extent))])
    return gain


def noise(rng, shape, spread, most, cuts=(), held_as=jnp.bfloat16):
    loudness = level_of(rng, shape, cuts, -0.22, 0.18) if cuts else 1.0
    entries = jax.random.normal(rng, shape, jnp.float32) * spread * loudness
    return jnp.minimum(jnp.maximum(entries, -most), most).astype(held_as)


def setup_inputs(seed: int = 0) -> dict:
    key_list = jax.random.split(jax.random.key(seed), 19)
    frames = noise(key_list[0], (ROWS, ROW_LEN, D), 1.0, 6.0, ((0, 4), (1, 8)), jnp.float32)
    clip_lengths = draw_clip_lengths(jax.random.fold_in(key_list[18], 71), 0)
    query_weight = noise(key_list[2], (D, D), D ** -0.5, 0.21875)
    query_bias = noise(key_list[3], (D,), 0.5, 3.0, (), jnp.float32)
    key_weight = noise(key_list[4], (D, D), D ** -0.5, 0.21875)
    value_weight = noise(key_list[5], (D, D), D ** -0.5, 0.21875)
    value_bias = noise(key_list[6], (D,), 0.05, 0.3, (), jnp.float32)
    out_weight = noise(key_list[7], (D, D), (max(D // CLIP, 1)) ** -0.5, 3.5)
    out_bias = noise(key_list[8], (D,), 0.1, 0.6, (), jnp.float32)
    norm1_gain = jnp.clip(1.0 + 0.1 * jax.random.normal(key_list[9], (D,), jnp.float32), 0.5, 1.5)
    norm1_bias = noise(key_list[10], (D,), 0.1, 0.6, (), jnp.float32)
    up_weight = noise(key_list[11], (D, FF), D ** -0.5, 0.21875)
    up_bias = noise(key_list[12], (FF,), 0.2, 1.2, (), jnp.float32)
    down_weight = noise(key_list[13], (FF, D), FF ** -0.5, 0.109375)
    down_bias = noise(key_list[14], (D,), 0.1, 0.6, (), jnp.float32)
    norm2_gain = jnp.clip(1.0 + 0.1 * jax.random.normal(key_list[15], (D,), jnp.float32), 0.5, 1.5)
    norm2_bias = noise(key_list[16], (D,), 0.1, 0.6, (), jnp.float32)
    cotangent = noise(key_list[17], (ROWS, ROW_LEN, D), 1.0, 6.0, ((0, 4), (1, 8)), jnp.float32)
    return {"frames": frames, "clip_lengths": clip_lengths, "query_weight": query_weight, "query_bias": query_bias, "key_weight": key_weight, "value_weight": value_weight, "value_bias": value_bias, "out_weight": out_weight, "out_bias": out_bias, "norm1_gain": norm1_gain, "norm1_bias": norm1_bias, "up_weight": up_weight, "up_bias": up_bias, "down_weight": down_weight, "down_bias": down_bias, "norm2_gain": norm2_gain, "norm2_bias": norm2_bias, "cotangent": cotangent}


@jax.custom_vjp
def low(v):
    return lax.optimization_barrier(v.astype(jnp.bfloat16)).astype(jnp.float32)

@jax.custom_vjp
def low_back(v):
    return v

def low_keep(v):
    return (low(v), None)

def low_pass(kept, grad):
    return (grad,)

def back_keep(v):
    return (v, None)

def back_low(kept, grad):
    return (low(grad),)
low.defvjp(low_keep, low_pass)
low_back.defvjp(back_keep, back_low)
MASK_SCORE = -1e+30
NORM_EPSILON = 1e-05
FULL_PRECISION = lax.Precision.HIGHEST

def layer_norm(summed, norm_gain, norm_shift):
    centre = lax.optimization_barrier(jnp.mean(summed, axis=-1, keepdims=True))
    centered = summed - centre
    inverse = lax.rsqrt(lax.optimization_barrier(jnp.mean(centered * centered, axis=-1, keepdims=True)) + NORM_EPSILON)
    return centered * inverse * norm_gain + norm_shift

def project(inputs, matrix):
    return jnp.einsum('rsk,kn->rsn', inputs, matrix, precision=FULL_PRECISION)

def clip_numbers(clip_lengths):
    clip_ends = jnp.cumsum(clip_lengths, axis=1).astype(jnp.int32)
    position = jnp.arange(ROW_LEN, dtype=jnp.int32)
    return lax.optimization_barrier(jnp.sum((clip_ends[:, None, :] <= position[None, :, None]).astype(jnp.int32), axis=-1))

def row_attention(operands):
    queries, keys_row, values_row, numbers = operands
    length = queries.shape[0]
    block_rows = math.gcd(length, 512)
    factor = HD ** (-0.5)

    @jax.checkpoint
    def query_block(begin):
        query_rows = lax.dynamic_slice_in_dim(queries, begin, block_rows, 0)
        query_numbers = lax.dynamic_slice_in_dim(numbers, begin, block_rows, 0)
        scores = low_back(jnp.einsum('qhd,khd->hqk', query_rows, keys_row, precision=FULL_PRECISION) * factor)
        allowed = (query_numbers[:, None] == numbers[None, :])[None]
        masked = jnp.where(allowed, scores, MASK_SCORE)
        row_peak = lax.optimization_barrier(jnp.max(masked, axis=-1, keepdims=True))
        powers = jnp.exp(masked - row_peak)
        weights = low(powers / lax.optimization_barrier(jnp.sum(powers, axis=-1, keepdims=True)))
        return jnp.einsum('hqk,khd->qhd', weights, values_row, precision=FULL_PRECISION)
    begins = jnp.arange(length // block_rows, dtype=jnp.int32) * block_rows
    return lax.map(query_block, begins).reshape(length, H * HD)

def encoder_layer(numbers, frames, query_weight, query_bias, key_weight, value_weight, value_bias, out_weight, out_bias, norm1_gain, norm1_bias, up_weight, up_bias, down_weight, down_bias, norm2_gain, norm2_bias):
    frames_low = low(frames)
    queries = low(low_back(project(frames_low, query_weight) + query_bias))
    keys_all = low(low_back(project(frames_low, key_weight)))
    values_all = low(low_back(project(frames_low, value_weight) + value_bias))
    heads_shape = (frames.shape[0], frames.shape[1], H, HD)
    attended = lax.map(jax.checkpoint(row_attention), (queries.reshape(heads_shape), keys_all.reshape(heads_shape), values_all.reshape(heads_shape), numbers))
    attended = low(low_back(attended))
    branch = low_back(project(attended, out_weight) + out_bias)
    hidden = layer_norm(frames + branch, norm1_gain, norm1_bias)
    hidden_low = low(hidden)
    before = low_back(project(hidden_low, up_weight) + up_bias)
    active = low(jax.nn.gelu(before, approximate=False))
    feed_forward = low_back(project(active, down_weight) + down_bias)
    return layer_norm(hidden + feed_forward, norm2_gain, norm2_bias)

def reference(frames, clip_lengths, query_weight, query_bias, key_weight, value_weight, value_bias, out_weight, out_bias, norm1_gain, norm1_bias, up_weight, up_bias, down_weight, down_bias, norm2_gain, norm2_bias, cotangent):
    numbers = clip_numbers(clip_lengths)
    tensors = (query_weight, query_bias, key_weight, value_weight, value_bias, out_weight, out_bias, norm1_gain, norm1_bias, up_weight, up_bias, down_weight, down_bias, norm2_gain, norm2_bias)
    widened = [tensor.astype(jnp.float32) for tensor in tensors]
    encoded, backward = jax.vjp(partial(encoder_layer, numbers), frames.astype(jnp.float32), *widened)
    gradients = backward(cotangent.astype(jnp.float32))
    return (encoded, gradients[0], gradients[1], gradients[2], gradients[3], gradients[4], gradients[5], gradients[6], gradients[7], gradients[8], gradients[9], gradients[10], gradients[11], gradients[12], gradients[13], gradients[14], gradients[15])
```

```python
from functools import partial
import math

import jax
import jax.numpy as jnp
from jax import lax
from jax.experimental import pallas as pl
from jax.experimental.pallas import tpu as pltpu
from jax.sharding import PartitionSpec as P

H = 12
HD = 64


MASK_SCORE = -1e30
NORM_EPSILON = 1e-05


def from_behind(value, axis, by):
    count = lax.axis_size(axis)
    return lax.ppermute(value, axis, [(i, (i + by) % count) for i in range(count)])


def layer_norm(summed, norm_gain, norm_shift):
    centre = jnp.mean(summed, axis=-1, keepdims=True)
    centered = summed - centre
    inverse = lax.rsqrt(jnp.mean(centered * centered, axis=-1, keepdims=True) + NORM_EPSILON)
    normed = centered * inverse
    return (normed * norm_gain + norm_shift, normed, inverse)


def layer_norm_back(upstream, normed, inverse, norm_gain):
    scaled = upstream * norm_gain
    first_mean = jnp.mean(scaled, axis=-1, keepdims=True)
    second_mean = jnp.mean(scaled * normed, axis=-1, keepdims=True)
    summed_grad = inverse * (scaled - first_mean - normed * second_mean)
    return (summed_grad, jnp.sum(upstream * normed, axis=(0, 1)), jnp.sum(upstream, axis=(0, 1)))


def project(inputs, matrix):
    return jnp.einsum("rsk,kn->rsn", inputs, matrix, preferred_element_type=jnp.float32)


def project_back(upstream, matrix):
    return jnp.einsum("rsn,kn->rsk", upstream, matrix, preferred_element_type=jnp.float32)


def matrix_grad(inputs, upstream):
    return jnp.einsum("rsk,rsn->kn", inputs, upstream, preferred_element_type=jnp.float32)


def column_sum(upstream):
    return jnp.sum(upstream.astype(jnp.float32), axis=(0, 1))


def clip_numbers(clip_ends, position):
    return jnp.sum((clip_ends[:, None, :] <= position[None, :, None]).astype(jnp.int32), axis=-1)


def split_heads(tensor):
    return tensor.reshape(tensor.shape[0], tensor.shape[1], H, HD)


def join_heads(tensor):
    return tensor.reshape(tensor.shape[0], tensor.shape[1], H * HD)


def head_scores(queries, keys_block):
    return jnp.einsum(
        "rqhd,rkhd->rhqk", queries, keys_block, preferred_element_type=jnp.float32
    ) * HD ** (-0.5)


def allowed_pairs(query_numbers, key_numbers):
    return (query_numbers[:, :, None] == key_numbers[:, None, :])[:, None]


def online_update(running, queries, query_numbers, keys_block, values_block, key_numbers):
    run_peak, run_total, run_values = running
    allowed = allowed_pairs(query_numbers, key_numbers)
    masked = jnp.where(allowed, head_scores(queries, keys_block), MASK_SCORE)
    new_peak = jnp.maximum(run_peak, jnp.max(masked, axis=-1))
    weights = jnp.where(allowed, jnp.exp(masked - new_peak[..., None]), 0.0)
    rescale = jnp.exp(run_peak - new_peak)
    new_total = run_total * rescale + jnp.sum(weights, axis=-1)
    contrib = jnp.einsum(
        "rhqk,rkhd->rqhd",
        weights.astype(jnp.bfloat16),
        values_block,
        preferred_element_type=jnp.float32,
    )
    new_values = run_values * jnp.swapaxes(rescale, 1, 2)[..., None] + contrib
    return (new_peak, new_total, new_values)


def block_back(
    queries, grad_heads, log_total, delta_rows, query_numbers, keys_flat, values_flat, key_numbers
):
    keys_block = split_heads(keys_flat)
    values_block = split_heads(values_flat)
    allowed = allowed_pairs(query_numbers, key_numbers)
    shifted = jnp.where(
        allowed, head_scores(queries, keys_block) - log_total[..., None], MASK_SCORE
    )
    weights = jnp.exp(shifted)
    grad_weights = jnp.einsum(
        "rqhd,rkhd->rhqk", grad_heads, values_block, preferred_element_type=jnp.float32
    )
    grad_scores = (weights * (grad_weights - delta_rows[..., None])).astype(jnp.bfloat16)
    factor = HD ** (-0.5)
    query_part = (
        jnp.einsum("rhqk,rkhd->rqhd", grad_scores, keys_block, preferred_element_type=jnp.float32)
        * factor
    )
    key_part = (
        jnp.einsum("rhqk,rqhd->rkhd", grad_scores, queries, preferred_element_type=jnp.float32)
        * factor
    )
    value_part = jnp.einsum(
        "rhqk,rqhd->rkhd",
        weights.astype(jnp.bfloat16),
        grad_heads,
        preferred_element_type=jnp.float32,
    )
    return (join_heads(query_part), join_heads(key_part), join_heads(value_part))


def per_device(
    frames,
    clip_lengths,
    query_weight,
    query_bias,
    key_weight,
    value_weight,
    value_bias,
    out_weight,
    out_bias,
    norm1_gain,
    norm1_bias,
    up_weight,
    up_bias,
    down_weight,
    down_bias,
    norm2_gain,
    norm2_bias,
    cotangent,
):
    row_count = frames.shape[0]
    shard_len = frames.shape[1]
    cycle_size = lax.axis_size("seq")
    seq_place = lax.axis_index("seq")
    clip_ends = jnp.cumsum(clip_lengths, axis=1)
    offsets = jnp.arange(shard_len, dtype=jnp.int32)
    own_numbers = clip_numbers(clip_ends, seq_place * shard_len + offsets)
    frames_low = frames.astype(jnp.bfloat16)
    queries = split_heads((project(frames_low, query_weight) + query_bias).astype(jnp.bfloat16))
    keys_own = project(frames_low, key_weight).astype(jnp.bfloat16)
    values_own = (project(frames_low, value_weight) + value_bias).astype(jnp.bfloat16)
    initial = (
        jnp.full((row_count, H, shard_len), MASK_SCORE, jnp.float32),
        jnp.zeros((row_count, H, shard_len), jnp.float32),
        jnp.zeros((row_count, shard_len, H, HD), jnp.float32),
    )
    key_piece = lax.all_gather(keys_own, "seq", axis=1, tiled=True)
    value_piece = lax.all_gather(values_own, "seq", axis=1, tiled=True)
    piece_len = key_piece.shape[1]
    block_len = math.gcd(piece_len, 512)

    def attend_block(block_index, carried):
        offset = block_index * block_len
        key_block = lax.dynamic_slice_in_dim(key_piece, offset, block_len, 1)
        value_block = lax.dynamic_slice_in_dim(value_piece, offset, block_len, 1)
        position = offset + jnp.arange(block_len, dtype=jnp.int32)
        return online_update(
            carried,
            queries,
            own_numbers,
            split_heads(key_block),
            split_heads(value_block),
            clip_numbers(clip_ends, position),
        )

    run_peak, run_total, run_values = lax.fori_loop(
        0, piece_len // block_len, attend_block, initial
    )
    log_total = run_peak + jnp.log(run_total)
    attended_heads = run_values / jnp.swapaxes(run_total, 1, 2)[..., None]
    attended = join_heads(attended_heads)
    attended_low = attended.astype(jnp.bfloat16)
    branch = project(attended_low, out_weight) + out_bias
    hidden, unit_first, inverse_first = layer_norm(frames + branch, norm1_gain, norm1_bias)
    hidden_low = hidden.astype(jnp.bfloat16)
    before = project(hidden_low, up_weight) + up_bias
    active, gelu_back = jax.vjp(partial(jax.nn.gelu, approximate=False), before)
    active_low = active.astype(jnp.bfloat16)
    encoded, unit_second, inverse_second = layer_norm(
        hidden + project(active_low, down_weight) + down_bias, norm2_gain, norm2_bias
    )
    grad_mid, norm2_gain_grad, norm2_bias_grad = layer_norm_back(
        cotangent, unit_second, inverse_second, norm2_gain
    )
    grad_ffn = grad_mid.astype(jnp.bfloat16)
    down_weight_grad = matrix_grad(active_low, grad_ffn)
    down_bias_grad = column_sum(grad_ffn)
    grad_before = gelu_back(project_back(grad_ffn, down_weight))[0].astype(jnp.bfloat16)
    up_weight_grad = matrix_grad(hidden_low, grad_before)
    up_bias_grad = column_sum(grad_before)
    grad_hidden = grad_mid + project_back(grad_before, up_weight)
    grad_first, norm1_gain_grad, norm1_bias_grad = layer_norm_back(
        grad_hidden, unit_first, inverse_first, norm1_gain
    )
    grad_branch = grad_first.astype(jnp.bfloat16)
    out_weight_grad = matrix_grad(attended_low, grad_branch)
    out_bias_grad = column_sum(grad_branch)
    grad_attended = project_back(grad_branch, out_weight).astype(jnp.bfloat16)
    grad_heads = split_heads(grad_attended)
    delta_rows = jnp.swapaxes(
        jnp.sum(grad_heads.astype(jnp.float32) * attended_heads, axis=-1), 1, 2
    )
    query_start, key_start, value_start = block_back(
        queries, grad_heads, log_total, delta_rows, own_numbers, keys_own, values_own, own_numbers
    )

    def key_step(distance, carried):
        key_now, value_now, query_sum, key_sum, value_sum = carried
        key_now, value_now = from_behind((key_now, value_now), "seq", 1)
        key_sum, value_sum = (
            from_behind(key_sum.astype(jnp.bfloat16), "seq", 1).astype(key_sum.dtype),
            from_behind(value_sum.astype(jnp.bfloat16), "seq", 1).astype(value_sum.dtype),
        )
        source = (seq_place - distance) % cycle_size
        source_numbers = clip_numbers(clip_ends, source * shard_len + offsets)
        query_part, key_part, value_part = block_back(
            queries,
            grad_heads,
            log_total,
            delta_rows,
            own_numbers,
            key_now,
            value_now,
            source_numbers,
        )
        return (
            key_now,
            value_now,
            query_sum + query_part,
            key_sum + key_part,
            value_sum + value_part,
        )

    carried = lax.fori_loop(
        1, cycle_size, key_step, (keys_own, values_own, query_start, key_start, value_start)
    )
    query_total = carried[2]
    key_total, value_total = (
        from_behind(carried[3].astype(jnp.bfloat16), "seq", 1).astype(jnp.float32),
        from_behind(carried[4].astype(jnp.bfloat16), "seq", 1).astype(jnp.float32),
    )
    query_low = query_total.astype(jnp.bfloat16)
    key_low = key_total.astype(jnp.bfloat16)
    value_low = value_total.astype(jnp.bfloat16)
    query_weight_grad = matrix_grad(frames_low, query_low)
    query_bias_grad = column_sum(query_low)
    key_weight_grad = matrix_grad(frames_low, key_low)
    value_weight_grad = matrix_grad(frames_low, value_low)
    value_bias_grad = column_sum(value_low)
    frames_grad = (
        grad_first
        + project_back(query_low, query_weight)
        + project_back(key_low, key_weight)
        + project_back(value_low, value_weight)
    )
    shares = (
        lax.psum_scatter(query_weight_grad, "seq", scatter_dimension=0, tiled=True),
        lax.psum_scatter(query_bias_grad, "seq", scatter_dimension=0, tiled=True),
        lax.psum_scatter(key_weight_grad, "seq", scatter_dimension=0, tiled=True),
        lax.psum_scatter(value_weight_grad, "seq", scatter_dimension=0, tiled=True),
        lax.psum_scatter(value_bias_grad, "seq", scatter_dimension=0, tiled=True),
        lax.psum_scatter(out_weight_grad, "seq", scatter_dimension=0, tiled=True),
        lax.psum_scatter(out_bias_grad, "seq", scatter_dimension=0, tiled=True),
        lax.psum_scatter(norm1_gain_grad, "seq", scatter_dimension=0, tiled=True),
        lax.psum_scatter(norm1_bias_grad, "seq", scatter_dimension=0, tiled=True),
        lax.psum_scatter(up_weight_grad, "seq", scatter_dimension=0, tiled=True),
        lax.psum_scatter(up_bias_grad, "seq", scatter_dimension=0, tiled=True),
        lax.psum_scatter(down_weight_grad, "seq", scatter_dimension=0, tiled=True),
        lax.psum_scatter(down_bias_grad, "seq", scatter_dimension=0, tiled=True),
        lax.psum_scatter(norm2_gain_grad, "seq", scatter_dimension=0, tiled=True),
        lax.psum_scatter(norm2_bias_grad, "seq", scatter_dimension=0, tiled=True),
    )
    shares = (
        lax.psum(shares[0].astype(jnp.bfloat16), "row").astype(jnp.float32),
        lax.psum(shares[1].astype(jnp.bfloat16), "row").astype(jnp.float32),
        lax.psum(shares[2].astype(jnp.bfloat16), "row").astype(jnp.float32),
        lax.psum(shares[3].astype(jnp.bfloat16), "row").astype(jnp.float32),
        lax.psum(shares[4].astype(jnp.bfloat16), "row").astype(jnp.float32),
        lax.psum(shares[5].astype(jnp.bfloat16), "row").astype(jnp.float32),
        lax.psum(shares[6].astype(jnp.bfloat16), "row").astype(jnp.float32),
        lax.psum(shares[7].astype(jnp.bfloat16), "row").astype(jnp.float32),
        lax.psum(shares[8].astype(jnp.bfloat16), "row").astype(jnp.float32),
        lax.psum(shares[9].astype(jnp.bfloat16), "row").astype(jnp.float32),
        lax.psum(shares[10].astype(jnp.bfloat16), "row").astype(jnp.float32),
        lax.psum(shares[11].astype(jnp.bfloat16), "row").astype(jnp.float32),
        lax.psum(shares[12].astype(jnp.bfloat16), "row").astype(jnp.float32),
        lax.psum(shares[13].astype(jnp.bfloat16), "row").astype(jnp.float32),
        lax.psum(shares[14].astype(jnp.bfloat16), "row").astype(jnp.float32),
    )
    totals = (
        lax.all_gather(shares[0].astype(jnp.bfloat16), "seq", axis=0, tiled=True).astype(
            jnp.float32
        ),
        lax.all_gather(shares[1].astype(jnp.bfloat16), "seq", axis=0, tiled=True).astype(
            jnp.float32
        ),
        lax.all_gather(shares[2].astype(jnp.bfloat16), "seq", axis=0, tiled=True).astype(
            jnp.float32
        ),
        lax.all_gather(shares[3].astype(jnp.bfloat16), "seq", axis=0, tiled=True).astype(
            jnp.float32
        ),
        lax.all_gather(shares[4].astype(jnp.bfloat16), "seq", axis=0, tiled=True).astype(
            jnp.float32
        ),
        lax.all_gather(shares[5].astype(jnp.bfloat16), "seq", axis=0, tiled=True).astype(
            jnp.float32
        ),
        lax.all_gather(shares[6].astype(jnp.bfloat16), "seq", axis=0, tiled=True).astype(
            jnp.float32
        ),
        lax.all_gather(shares[7].astype(jnp.bfloat16), "seq", axis=0, tiled=True).astype(
            jnp.float32
        ),
        lax.all_gather(shares[8].astype(jnp.bfloat16), "seq", axis=0, tiled=True).astype(
            jnp.float32
        ),
        lax.all_gather(shares[9].astype(jnp.bfloat16), "seq", axis=0, tiled=True).astype(
            jnp.float32
        ),
        lax.all_gather(shares[10].astype(jnp.bfloat16), "seq", axis=0, tiled=True).astype(
            jnp.float32
        ),
        lax.all_gather(shares[11].astype(jnp.bfloat16), "seq", axis=0, tiled=True).astype(
            jnp.float32
        ),
        lax.all_gather(shares[12].astype(jnp.bfloat16), "seq", axis=0, tiled=True).astype(
            jnp.float32
        ),
        lax.all_gather(shares[13].astype(jnp.bfloat16), "seq", axis=0, tiled=True).astype(
            jnp.float32
        ),
        lax.all_gather(shares[14].astype(jnp.bfloat16), "seq", axis=0, tiled=True).astype(
            jnp.float32
        ),
    )
    return (
        encoded,
        frames_grad,
        totals[0],
        totals[1],
        totals[2],
        totals[3],
        totals[4],
        totals[5],
        totals[6],
        totals[7],
        totals[8],
        totals[9],
        totals[10],
        totals[11],
        totals[12],
        totals[13],
        totals[14],
    )


MESH = pl.DeviceIdType.MESH
LANES = 128
F32, BF16 = jnp.float32, jnp.bfloat16
WAYS = 4
DOWN, UP, ATTN = 0, 1, 2


def dot(a, b):
    return jnp.dot(a, b, preferred_element_type=F32)


def dot_nt(a, b):
    return lax.dot_general(a, b, (((1,), (1,)), ((), ())), preferred_element_type=F32)


def dot_tn(a, b):
    return lax.dot_general(a, b, (((0,), (0,)), ((), ())), preferred_element_type=F32)


def rows_norm(value):
    centre = jnp.mean(value, axis=-1, keepdims=True)
    centered = value - centre
    inverse = lax.rsqrt(jnp.mean(centered * centered, axis=-1, keepdims=True) + NORM_EPSILON)
    return centered * inverse, inverse


def rows_norm_back(scaled, unit, inverse):
    first = jnp.mean(scaled, axis=-1, keepdims=True)
    second = jnp.mean(scaled * unit, axis=-1, keepdims=True)
    return inverse * (scaled - first - unit * second)


def layer_kernel(
    T,
    D,
    S,
    entries,
    frames,
    cotangent,
    lengths,
    query_w,
    key_w,
    value_w,
    out_w,
    up_w,
    down_w,
    query_b,
    value_b,
    out_b,
    gain1,
    bias1,
    up_b,
    down_b,
    gain2,
    bias2,
    encoded,
    frames_grad,
    vectors,
    sum_down,
    sum_up,
    sum_attn,
    fall,
    wq,
    wkv,
    wo,
    wup,
    wdn,
    kv,
    qs,
    qsT,
    mask,
    probs,
    att32,
    att16,
    attf,
    hq,
    fq,
    ar,
    br,
    asend,
    bsend,
    dgelu,
    hid32,
    unit1,
    rstd1,
    gmid,
    gfirst,
    gbr,
    da16,
    daT,
    dq16,
    dkvT,
    ys,
    yr,
    own,
    zl,
    zr,
    gm,
    dr,
    xs,
    xr,
    vl,
    vr,
    dxs,
    dxr,
    dxo,
    stage,
    vsend,
    vrecv,
    wsem,
    frs,
    fss,
    fys,
    msr,
    mss,
    zlr,
    zls,
    zrr,
    zrs,
    agzr,
    agzs,
    ag2r,
    ag2s,
    ag3r,
    ag3s,
    agdr,
    agds,
    lsem,
):
    HW, T2 = D // 2, 2 * T
    blocks = HW // LANES
    EIGHTH, SIXTEENTH = D // 8, D // 16
    row, seq = lax.axis_index("row"), lax.axis_index("seq")
    x, c = lax.div(row, 2), lax.rem(row, 2)
    z, y = lax.div(seq, 2), lax.rem(seq, 2)
    sib, xn, yn = (2 * x + 1 - c, seq), (2 * (1 - x) + c, seq), (row, 2 * z + 1 - y)
    cross = (2 * (1 - x) + 1 - c, seq)
    zp = (row, 2 * jnp.minimum(z + 1, 3) + y)
    zm = (row, 2 * jnp.maximum(z - 1, 0) + y)
    zz = (row, 2 * jnp.where(z < 2, z + 2, z - 2) + y)
    z1 = (row, 2 * (z + 1 - 2 * lax.rem(z, 2)) + y)
    not_first, not_last = z > 0, z < 3

    def many(value, of):
        return pl.multiple_of(value, of)

    def at(start, size, of=None):
        return pl.ds(many(start, size if of is None else of), size)

    waits = []

    def send(src, dst, ssem, rsem, device):
        return pltpu.make_async_remote_copy(
            src_ref=src, dst_ref=dst, send_sem=ssem, recv_sem=rsem, device_id=device, device_id_type=MESH
        )

    def start(src, dst, ssem, rsem, device, when=None):
        copy = send(src, dst, ssem, rsem, device)
        if when is None:
            copy.start()
            waits.append(copy.wait_send)
        else:
            pl.when(when)(copy.start)
            waits.append(lambda: pl.when(when)(copy.wait_send))

    def arrived(ref, rsem):
        send(ref, ref, mss.at[0], rsem, sib).wait_recv()

    names = {}

    def one(name):
        index = names.setdefault(name, len(names))
        return mss.at[index], msr.at[index]

    loads = [
        pltpu.make_async_copy(query_w.at[:, at(HW * y, HW)], wq, wsem.at[0]),
        pltpu.make_async_copy(key_w.at[:, at(HW * y, HW)], wkv.at[:, pl.ds(0, HW)], wsem.at[1]),
        pltpu.make_async_copy(value_w.at[:, at(HW * y, HW)], wkv.at[:, pl.ds(HW, HW)], wsem.at[2]),
        pltpu.make_async_copy(out_w, wo, wsem.at[3]),
        pltpu.make_async_copy(up_w, wup, wsem.at[4]),
        pltpu.make_async_copy(down_w, wdn, wsem.at[5]),
    ]
    for load in loads:
        load.start()
    barrier = pltpu.get_barrier_semaphore()
    for device, when in ((sib, None), (xn, None), (yn, None), (zz, None), (cross, None), (zp, not_last), (zm, not_first)):

        def greet(device=device):
            pl.semaphore_signal(barrier, inc=1, device_id=device, device_id_type=MESH)

        greet() if when is None else pl.when(when)(greet)
    fall[at(T * seq, T), :] = frames[...].astype(BF16)
    vectors[...] = jnp.zeros_like(vectors)

    @pl.when(z == 0)
    def _():
        zl[...] = jnp.zeros_like(zl)
        vl[...] = jnp.zeros_like(vl)

    @pl.when(z == 3)
    def _():
        zr[...] = jnp.zeros_like(zr)
        vr[...] = jnp.zeros_like(vr)

    pl.semaphore_wait(barrier, jnp.where(not_first & not_last, 7, 6))

    def slab(z_, y_):
        return fall.at[at(T * (2 * z_ + y_), T), :]

    def push(z_, direction):
        device = (zp, zm, yn)[direction]
        sem = fss.at[direction, z_]
        return send(slab(z_, y), slab(z_, y), sem, frs.at[2 * z_ + y], device)

    bias_kv = jnp.concatenate([jnp.zeros((1, HW), F32), value_b[:, at(HW * y, HW)]], axis=1)

    def keys_values(z_, y_):
        rows = at(T * (2 * z_ + y_), T)
        kv[rows, :] = (dot(fall[rows, :], wkv[...]) + bias_kv).astype(BF16)

    pl.when(not_last)(lambda: push(z, 0).start())
    pl.when(not_first)(lambda: push(z, 1).start())
    push(z, 2).start()
    loads[1].wait()
    loads[2].wait()
    keys_values(z, y)

    @pl.loop(0, 4)
    def _(k):
        left, right = z - k - 1, z + k + 1

        @pl.when(left >= 0)
        def _():
            arrived(slab(left, y), frs.at[2 * left + y])
            pl.when(not_last)(lambda: push(left, 0).start())
            push(left, 2).start()

        @pl.when(right <= 3)
        def _():
            arrived(slab(right, y), frs.at[2 * right + y])
            pl.when(not_first)(lambda: push(right, 1).start())
            push(right, 2).start()

        pl.when(left >= 0)(lambda: keys_values(left, y))
        pl.when(right <= 3)(lambda: keys_values(right, y))

        @pl.when(z - k >= 0)
        def _():
            arrived(slab(z - k, 1 - y), frs.at[2 * (z - k) + 1 - y])
            keys_values(z - k, 1 - y)

        @pl.when((k > 0) & (z + k <= 3))
        def _():
            arrived(slab(z + k, 1 - y), frs.at[2 * (z + k) + 1 - y])
            keys_values(z + k, 1 - y)

    def frames_sent():
        @pl.loop(0, 4)
        def _(j):
            push(j, 2).wait_send()
            pl.when(not_last & (j <= z))(lambda: push(j, 0).wait_send())
            pl.when(not_first & (j >= z))(lambda: push(j, 1).wait_send())

    waits.append(frames_sent)
    pair_rows = at(T2 * z, T2)
    loads[0].wait()
    query = (dot(fall[pair_rows, :], wq[...]) + query_b[:, at(HW * y, HW)]).astype(BF16).astype(F32)
    query = query * HD ** (-0.5)
    qs[...] = query.astype(BF16)
    qsT[...] = query.T.astype(BF16)
    key_at = lax.broadcasted_iota(jnp.int32, (1, S), 1)
    query_at = lax.broadcasted_iota(jnp.int32, (T2, 1), 0) + T2 * z
    key_number, query_number = jnp.zeros((1, S), jnp.int32), jnp.zeros((T2, 1), jnp.int32)
    clip_end = jnp.int32(0)
    for entry in range(entries):
        clip_end = clip_end + lengths[0, entry]
        key_number = key_number + jnp.where(clip_end <= key_at, 1, 0)
        query_number = query_number + jnp.where(clip_end <= query_at, 1, 0)
    mask[...] = jnp.where(query_number == key_number, 0.0, MASK_SCORE)

    low_half = lax.broadcasted_iota(jnp.int32, (T2, LANES), 1) < HD

    def half(value, which):
        return jnp.where(low_half == (which == 0), value, 0.0)

    @pl.loop(0, blocks)
    def _(b):
        lanes, value_lanes = at(LANES * b, LANES), at(HW + LANES * b, LANES, LANES)
        queries = qs[:, lanes].astype(F32)
        outs = []
        for which in range(2):
            scores = dot_nt(half(queries, which).astype(BF16), kv[:, lanes]) + mask[...]
            powers = jnp.exp(scores - jnp.max(scores, axis=-1, keepdims=True))
            low = (powers * (1.0 / jnp.sum(powers, axis=-1, keepdims=True))).astype(BF16)
            probs[2 * b + which] = low
            outs.append(dot(low, kv[:, value_lanes]))
        out = jnp.where(low_half, outs[0], outs[1])
        att32[:, lanes] = out
        att16[:, lanes] = out.astype(BF16)

    mine, other = at(T * y, T), at(T * (1 - y), T)
    heads_here = at(HW * y, HW)
    start(att16.at[other, :], attf.at[:, heads_here], *one("att"), yn)
    attf[:, heads_here] = att16[mine, :]
    loads[3].wait()
    arrived(attf.at[:, at(HW * (1 - y), HW)], one("att")[1])
    branch = dot(attf[...], wo[...]) + out_b[...]
    unit, inverse = rows_norm(frames[...] + branch)
    hidden = unit * gain1[...] + bias1[...]
    unit1[...] = unit
    rstd1[...] = jnp.broadcast_to(inverse, (T, LANES))
    hid32[...] = hidden
    hq[at(T * row, T), :] = hidden.astype(BF16)
    hidden_here = hq.at[at(T * row, T), :]
    start(hidden_here, hidden_here, *one("hid_x"), xn)
    start(hidden_here, hidden_here, *one("hid_d"), sib)

    def quad(order):
        x_ = jnp.where(order < 2, 1 - x, x)
        c_ = jnp.where(lax.rem(order, 2) == 0, c, 1 - c)
        return 2 * x_ + c_

    def spread(sent, got, ssem, rsem, to):
        @pl.when(to != row)
        def _():
            send(sent.at[to], got.at[at(T * row, T), :], ssem.at[to], rsem.at[row], (to, seq)).start()

    def spread_sent(sent, ssem):
        @pl.loop(0, 4)
        def _(to):
            @pl.when(to != row)
            def _():
                send(sent.at[to], sent.at[to], ssem.at[to], ssem.at[to], sib).wait_send()

    def spread_arrived(got, rsem):
        @pl.loop(0, 4)
        def _(source):
            pl.when(source != row)(lambda: arrived(got.at[at(T * source, T), :], rsem.at[source]))

    loads[4].wait()
    scale = 2.0 ** -0.5

    @pl.loop(0, 4)
    def _(order):
        to = quad(order)
        columns = at(D * to, D)
        before = dot(hidden_here[...], wup[:, columns]) + up_b[:, columns]
        rise = 0.5 * (1.0 + lax.erf(before * scale))
        dgelu[to] = rise + before * jnp.exp(-0.5 * before * before) * (2.0 * math.pi) ** -0.5
        asend[to] = (before * rise).astype(BF16)
        spread(asend, ar, fys.at[0], fys.at[1], to)

    waits.append(lambda: spread_sent(asend, fys.at[0]))
    ar[at(T * row, T), :] = asend[row]
    loads[5].wait()
    fed = hid32[...] + down_b[...]
    for quarter in range(4):
        fed = fed + dot(asend[quarter], wdn[pl.ds(D * quarter, D), :])
    unit2, inverse2 = rows_norm(fed)
    encoded[...] = unit2 * gain2[...] + bias2[...]
    cot = cotangent[...]
    grad_mid = rows_norm_back(cot * gain2[...], unit2, inverse2)
    vectors[10:11, :] = jnp.sum(cot * unit2, axis=0, keepdims=True)
    vectors[11:12, :] = jnp.sum(cot, axis=0, keepdims=True)
    gmid[...] = grad_mid
    fq[at(T * row, T), :] = grad_mid.astype(BF16)
    ffn_here = fq.at[at(T * row, T), :]
    start(ffn_here, ffn_here, *one("ffn_x"), xn)
    start(ffn_here, ffn_here, *one("ffn_d"), sib)
    vectors[9:10, :] = jnp.sum(ffn_here[...].astype(F32), axis=0, keepdims=True)

    @pl.loop(0, 4)
    def _(order):
        to = quad(order)
        quarter = at(D * to, D)
        back = dot_nt(ffn_here[...], wdn[quarter, :]) * dgelu[to]
        low = back.astype(BF16)
        bsend[to] = low
        spread(bsend, br, fys.at[2], fys.at[3], to)
        vectors[pl.ds(5 + to, 1), :] = jnp.sum(low.astype(F32), axis=0, keepdims=True)
        gmid[...] += dot_nt(low, wup[:, quarter])

    waits.append(lambda: spread_sent(bsend, fys.at[2]))
    br[at(T * row, T), :] = bsend[row]
    grad_hidden = gmid[...]
    unit = unit1[...]
    grad_first = rows_norm_back(grad_hidden * gain1[...], unit, rstd1[:, 0:1])
    vectors[3:4, :] = jnp.sum(grad_hidden * unit, axis=0, keepdims=True)
    vectors[4:5, :] = jnp.sum(grad_hidden, axis=0, keepdims=True)
    gfirst[...] = grad_first
    gbr[mine, :] = grad_first.astype(BF16)
    vectors[2:3, :] = jnp.sum(gbr[mine, :].astype(F32), axis=0, keepdims=True)
    start(gbr.at[mine, :], gbr.at[mine, :], *one("gbr"), yn)

    from_x, from_d, from_xd = 2 * (1 - x) + c, 2 * x + 1 - c, 2 * (1 - x) + 1 - c

    def pass_on(buffer, name):
        part = buffer.at[at(T * from_x, T), :]
        arrived(part, one(name + "_x")[1])
        start(part, part, *one(name + "_xd"), sib)

    def quad_ready(buffer, name):
        arrived(buffer.at[at(T * from_d, T), :], one(name + "_d")[1])
        arrived(buffer.at[at(T * from_xd, T), :], one(name + "_xd")[1])

    pass_on(hq, "hid")
    pass_on(fq, "ffn")

    def y_send(t, left, right):
        ys[t] = dot_tn(left[:, at(HW * (1 - y), HW)], right[...]).astype(BF16)
        start(ys.at[t], yr.at[t], *one(("y", t)), yn)
        own[t] = dot_tn(left[:, at(HW * y, HW)], right[...])

    def y_add(t):
        arrived(yr.at[t], one(("y", t))[1])
        own[t] += yr[t].astype(F32)

    def z_step(t, i):
        j = 3 - i
        pl.when(not_first & (z < j))(lambda: arrived(zl.at[t, j], zlr.at[t, j]))

        @pl.when(z < j)
        def _():
            zl[t, j] = (own[t, pl.ds(EIGHTH * j, EIGHTH), :] + zl[t, j].astype(F32)).astype(BF16)

        start(zl.at[t, j], zl.at[t, j], zls.at[t, j], zlr.at[t, j], zp, z < j)
        j_ = i
        pl.when(not_last & (z > j_))(lambda: arrived(zr.at[t, j_], zrr.at[t, j_]))

        @pl.when(z > j_)
        def _():
            zr[t, j_] = (own[t, pl.ds(EIGHTH * j_, EIGHTH), :] + zr[t, j_].astype(F32)).astype(BF16)

        start(zr.at[t, j_], zr.at[t, j_], zrs.at[t, j_], zrr.at[t, j_], zm, z > j_)

    def z_end(t):
        pl.when(not_first)(lambda: arrived(zl.at[t, z], zlr.at[t, z]))
        pl.when(not_last)(lambda: arrived(zr.at[t, z], zrr.at[t, z]))
        total = own[t, at(EIGHTH * z, EIGHTH), :] + zl[t, z].astype(F32) + zr[t, z].astype(F32)
        stage[t] = total.astype(BF16)

    def tile(t, h, q_, z_, y_):
        first = HW * y_ + EIGHTH * z_ + SIXTEENTH * h
        if t == UP:
            return sum_up.at[at(first, SIXTEENTH), at(D * q_, D)]
        whole = sum_down if t == DOWN else sum_attn
        return whole.at[at(D * q_ + first, SIXTEENTH), :]

    def gather_state(t, h):
        u = 2 * t + h
        over_y, over_x = (row, 1 - y), (from_x, y)
        second, third = ((over_y, yn), (over_x, xn)) if h == 0 else ((over_x, xn), (over_y, yn))
        both = (from_x, 1 - y)
        return u, second, third, both

    def gather_send(t, h, place, z_, ssem, rsem, device, src=None):
        there = tile(t, h, place[0], z_, place[1])
        return send(there if src is None else src, there, ssem, rsem, device)

    def to_next(t, h, z_, src=None):
        u, second, third, _ = gather_state(t, h)
        here = (row, y)
        gather_send(t, h, here, z_, ag2s.at[u, z_], ag2r.at[u, z_], second[1], src).start()
        gather_send(t, h, here, z_, ag3s.at[u, z_], ag3r.at[u, z_], third[1], src).start()
        gather_send(t, h, here, z_, agds.at[u], agdr.at[u], sib, src).start()

    def along_z(t, h, z_, direction, src=None):
        u = 2 * t + h
        return gather_send(
            t, h, (row, y), z_, agzs.at[u, direction, z_], agzr.at[u, z_], (zp, zm)[direction], src
        )

    def gather_own(t):
        for h in range(2):
            src = stage.at[t, pl.ds(SIXTEENTH * h, SIXTEENTH), :]
            pltpu.make_async_copy(src, tile(t, h, row, z, y), lsem.at[2 * t + h]).start()
            pl.when(not_last)(lambda: along_z(t, h, z, 0, src).start())
            pl.when(not_first)(lambda: along_z(t, h, z, 1, src).start())
            to_next(t, h, z, src)

    def gather_z(t, k):
        for h in range(2):
            u = 2 * t + h
            left, right = z - k, z + k

            @pl.when(left >= 0)
            def _():
                arrived(tile(t, h, row, left, y), agzr.at[u, left])
                pl.when(not_last)(lambda: along_z(t, h, left, 0).start())
                to_next(t, h, left)

            @pl.when(right <= 3)
            def _():
                arrived(tile(t, h, row, right, y), agzr.at[u, right])
                pl.when(not_first)(lambda: along_z(t, h, right, 1).start())
                to_next(t, h, right)

    def gather_second(t, k):
        for h in range(2):
            u, second, third, _ = gather_state(t, h)

            def take(z_):
                place = second[0]
                arrived(tile(t, h, place[0], z_, place[1]), ag2r.at[u, z_])
                gather_send(t, h, place, z_, ag3s.at[u, 4 + z_], ag3r.at[u, 4 + z_], third[1]).start()
                gather_send(t, h, place, z_, agds.at[u], agdr.at[u], sib).start()

            pl.when(z - k >= 0)(lambda: take(z - k))
            pl.when((k > 0) & (z + k <= 3))(lambda: take(z + k))

    def gather_third(t, k):
        for h in range(2):
            u, second, third, both = gather_state(t, h)

            def take(z_):
                for offset, place in ((0, third[0]), (4, both)):
                    arrived(tile(t, h, place[0], z_, place[1]), ag3r.at[u, offset + z_])
                    gather_send(t, h, place, z_, agds.at[u], agdr.at[u], sib).start()

            pl.when(z - k >= 0)(lambda: take(z - k))
            pl.when((k > 0) & (z + k <= 3))(lambda: take(z + k))

    def gather_end(t):
        for h in range(2):
            u = 2 * t + h
            part = tile(t, h, row, z, y)
            pltpu.make_async_copy(stage.at[t, pl.ds(SIXTEENTH * h, SIXTEENTH), :], part, lsem.at[u]).wait()

            @pl.loop(0, 4)
            def _(j):
                pl.when(not_last & (j <= z))(lambda: along_z(t, h, j, 0).wait_send())
                pl.when(not_first & (j >= z))(lambda: along_z(t, h, j, 1).wait_send())
                send(part, part, ag2s.at[u, j], ag2r.at[u, j], sib).wait_send()
                send(part, part, ag3s.at[u, j], ag3r.at[u, j], sib).wait_send()
                send(part, part, ag3s.at[u, 4 + j], ag3r.at[u, 4 + j], sib).wait_send()

            whole = sum_down.at[pl.ds(0, D), :]
            send(whole, whole, agds.at[u], agdr.at[u], sib).wait()

    arrived(gbr.at[other, :], one("gbr")[1])
    da = dot_nt(gbr[...], wo[heads_here, :]).astype(BF16)
    da16[...] = da
    daT[...] = da.astype(F32).T.astype(BF16)
    gm[3] = dot_tn(att16[...], gbr[...]).astype(BF16)

    quad_ready(fq, "ffn")
    spread_arrived(ar, fys.at[1])
    y_send(DOWN, ar, fq)

    def attention_back(b):
        lanes, value_lanes = at(LANES * b, LANES), at(HW + LANES * b, LANES, LANES)
        heads = da16[:, lanes].astype(F32)
        product = heads * att32[:, lanes]
        parts = []
        for which in range(2):
            delta = jnp.sum(half(product, which), axis=-1, keepdims=True)
            grad_probs = dot_nt(half(heads, which).astype(BF16), kv[:, value_lanes])
            low = probs[2 * b + which]
            grad_scores = (low.astype(F32) * (grad_probs - delta)).astype(BF16)
            parts.append(dot(grad_scores, kv[:, lanes]))
            head = at(LANES * b + HD * which, HD)
            dkvT[head, :] = dot(qsT[head, :], grad_scores).astype(BF16)
            dkvT[at(HW + LANES * b + HD * which, HD), :] = dot(daT[head, :], low).astype(BF16)
        dq16[:, lanes] = (jnp.where(low_half, parts[0], parts[1]) * HD ** (-0.5)).astype(BF16)

    @pl.loop(0, blocks)
    def _(b):
        attention_back(b)

    quad_ready(hq, "hid")
    spread_arrived(br, fys.at[3])
    y_send(UP, hq, br)
    y_add(DOWN)
    for i in range(3):
        z_step(DOWN, i)

    gm[0] = dot_tn(dq16[...], fall[pair_rows, :]).astype(BF16)
    for matrix in range(2):
        gm[1 + matrix] = dot(dkvT[pl.ds(HW * matrix, HW), :], fall[...]).astype(BF16)
    vectors[0:1, heads_here] = jnp.sum(dq16[...].astype(F32), axis=0, keepdims=True)
    ones = jnp.ones((8, S), BF16)
    vectors[1:2, heads_here] = dot_nt(ones, dkvT[pl.ds(HW, HW), :])[0:1, :]
    for slot in range(2):
        start(gm.at[1 - c + 2 * slot], dr.at[slot], *one(("d", slot)), sib)
    z_end(DOWN)
    gather_own(DOWN)
    for slot in range(2):
        arrived(dr.at[slot], one(("d", slot))[1])
    xs[...] = (gm[c + 2 * (1 - x)].astype(F32) + dr[1 - x].astype(F32)).astype(BF16)
    start(xs, xr, *one("xs"), xn)
    own[ATTN] = gm[c + 2 * x].astype(F32) + dr[x].astype(F32)
    y_add(UP)
    for i in range(3):
        z_step(UP, i)
    gather_z(DOWN, 1)
    gather_second(DOWN, 0)
    z_end(UP)
    gather_own(UP)
    arrived(xr, one("xs")[1])
    own[ATTN] += xr[...].astype(F32)
    for i in range(3):
        z_step(ATTN, i)
    gather_z(DOWN, 2)
    gather_second(DOWN, 1)
    gather_third(DOWN, 0)
    gather_z(UP, 1)
    gather_second(UP, 0)
    z_end(ATTN)
    gather_own(ATTN)

    def kv_step(i):
        j = 3 - i
        pl.when(not_first & (z < j))(lambda: arrived(vl.at[j], zlr.at[3, j]))

        @pl.when(z < j)
        def _():
            vl[j] = (dkvT[:, pl.ds(T2 * j, T2)].astype(F32) + vl[j].astype(F32)).astype(BF16)

        start(vl.at[j], vl.at[j], zls.at[3, j], zlr.at[3, j], zp, z < j)
        j_ = i
        pl.when(not_last & (z > j_))(lambda: arrived(vr.at[j_], zrr.at[3, j_]))

        @pl.when(z > j_)
        def _():
            vr[j_] = (dkvT[:, pl.ds(T2 * j_, T2)].astype(F32) + vr[j_].astype(F32)).astype(BF16)

        start(vr.at[j_], vr.at[j_], zrs.at[3, j_], zrr.at[3, j_], zm, z > j_)

    for i in range(3):
        kv_step(i)

    def vector_step(i, device):
        vsend[i] = vectors[...]
        start(vsend.at[i], vrecv.at[i], *one(("v", i)), device)
        arrived(vrecv.at[i], one(("v", i))[1])
        vectors[...] += vrecv[i]

    gather_z(DOWN, 3)
    gather_second(DOWN, 2)
    gather_third(DOWN, 1)
    vector_step(0, sib)
    gather_z(UP, 2)
    gather_second(UP, 1)
    gather_third(UP, 0)
    vector_step(1, xn)
    gather_z(ATTN, 1)
    gather_second(ATTN, 0)
    gather_second(DOWN, 3)
    gather_third(DOWN, 2)
    vector_step(2, yn)
    gather_z(UP, 3)
    gather_second(UP, 2)
    gather_third(UP, 1)
    vector_step(3, z1)
    gather_z(ATTN, 2)
    gather_second(ATTN, 1)
    gather_third(ATTN, 0)
    gather_third(DOWN, 3)
    vector_step(4, zz)

    pl.when(not_first)(lambda: arrived(vl.at[z], zlr.at[3, z]))
    pl.when(not_last)(lambda: arrived(vr.at[z], zrr.at[3, z]))
    total = dkvT[:, pair_rows].astype(F32) + vl[z].astype(F32) + vr[z].astype(F32)
    into = dot_nt(total.T.astype(BF16), wkv[...]) + dot_nt(dq16[...], wq[...])
    dxo[...] = into
    dxs[...] = dxo[other, :].astype(BF16)
    start(dxs, dxr, *one("dx"), yn)

    gather_z(ATTN, 3)
    gather_second(UP, 3)
    gather_third(UP, 2)
    gather_second(ATTN, 2)
    gather_third(ATTN, 1)
    arrived(dxr, one("dx")[1])
    frames_grad[...] = gfirst[...] + dxo[mine, :] + dxr[...].astype(F32)
    gather_third(UP, 3)
    gather_second(ATTN, 3)
    gather_third(ATTN, 2)
    gather_third(ATTN, 3)
    for t in (DOWN, UP, ATTN):
        gather_end(t)
    for wait in waits:
        wait()


def fused_layer(
    frames,
    clip_lengths,
    query_weight,
    query_bias,
    key_weight,
    value_weight,
    value_bias,
    out_weight,
    out_bias,
    norm1_gain,
    norm1_bias,
    up_weight,
    up_bias,
    down_weight,
    down_bias,
    norm2_gain,
    norm2_bias,
    cotangent,
):
    T, D = frames.shape[1], frames.shape[2]
    F = up_weight.shape[1]
    S = T * lax.axis_size("seq")
    HW, T2, EIGHTH = D // 2, 2 * T, D // 8
    blocks = HW // LANES
    entries = clip_lengths.shape[1]
    vmem, smem, hbm = (
        pl.BlockSpec(memory_space=pltpu.VMEM),
        pl.BlockSpec(memory_space=pltpu.SMEM),
        pl.BlockSpec(memory_space=pl.ANY),
    )
    dma = pltpu.SemaphoreType.DMA
    low, wide = (lambda *shape: pltpu.VMEM(shape, BF16)), (lambda *shape: pltpu.VMEM(shape, F32))
    scratch = dict(
        fall=low(S, D),
        wq=low(D, HW),
        wkv=low(D, D),
        wo=low(D, D),
        wup=low(D, F),
        wdn=low(F, D),
        kv=low(S, D),
        qs=low(T2, HW),
        qsT=low(HW, T2),
        mask=wide(T2, S),
        probs=low(2 * blocks, T2, S),
        att32=wide(T2, HW),
        att16=low(T2, HW),
        attf=low(T, D),
        hq=low(4 * T, D),
        fq=low(4 * T, D),
        ar=low(4 * T, D),
        br=low(4 * T, D),
        asend=low(4, T, D),
        bsend=low(4, T, D),
        dgelu=wide(4, T, D),
        hid32=wide(T, D),
        unit1=wide(T, D),
        rstd1=wide(T, LANES),
        gmid=wide(T, D),
        gfirst=wide(T, D),
        gbr=low(T2, D),
        da16=low(T2, HW),
        daT=low(HW, T2),
        dq16=low(T2, HW),
        dkvT=low(D, S),
        ys=low(2, HW, D),
        yr=low(2, HW, D),
        own=wide(3, HW, D),
        zl=low(3, 4, EIGHTH, D),
        zr=low(3, 4, EIGHTH, D),
        gm=low(4, HW, D),
        dr=low(2, HW, D),
        xs=low(HW, D),
        xr=low(HW, D),
        vl=low(4, D, T2),
        vr=low(4, D, T2),
        dxs=low(T, D),
        dxr=low(T, D),
        dxo=wide(T2, D),
        stage=low(3, EIGHTH, D),
        vsend=wide(5, 16, D),
        vrecv=wide(5, 16, D),
        wsem=dma((6,)),
        frs=dma((8,)),
        fss=dma((3, 4)),
        fys=dma((4, 4)),
        msr=dma((24,)),
        mss=dma((24,)),
        zlr=dma((4, 4)),
        zls=dma((4, 4)),
        zrr=dma((4, 4)),
        zrs=dma((4, 4)),
        agzr=dma((6, 4)),
        agzs=dma((6, 2, 4)),
        ag2r=dma((6, 4)),
        ag2s=dma((6, 4)),
        ag3r=dma((6, 8)),
        ag3s=dma((6, 8)),
        agdr=dma((6,)),
        agds=dma((6,)),
        lsem=dma((6,)),
    )
    encoded, frames_grad, vectors, sum_down, sum_up, sum_attn = pl.pallas_call(
        partial(layer_kernel, T, D, S, entries),
        out_shape=(
            jax.ShapeDtypeStruct((T, D), F32),
            jax.ShapeDtypeStruct((T, D), F32),
            jax.ShapeDtypeStruct((16, D), F32),
            jax.ShapeDtypeStruct((F, D), BF16),
            jax.ShapeDtypeStruct((D, F), BF16),
            jax.ShapeDtypeStruct((4 * D, D), BF16),
        ),
        in_specs=[vmem, vmem, smem] + [hbm] * 6 + [vmem] * 9,
        out_specs=(vmem, vmem, vmem, hbm, hbm, hbm),
        scratch_shapes=list(scratch.values()),
        compiler_params=pltpu.CompilerParams(
            collective_id=0, has_side_effects=True, vmem_limit_bytes=63 << 20
        ),
        name="layer",
    )(
        frames[0],
        cotangent[0],
        clip_lengths,
        query_weight,
        key_weight,
        value_weight,
        out_weight,
        up_weight,
        down_weight,
        query_bias[None],
        value_bias[None],
        out_bias[None],
        norm1_gain[None],
        norm1_bias[None],
        up_bias[None],
        down_bias[None],
        norm2_gain[None],
        norm2_bias[None],
    )
    attn = [sum_attn[D * m : D * (m + 1)].astype(F32) for m in range(4)]
    return (
        encoded[None],
        frames_grad[None],
        attn[0].T,
        vectors[0],
        attn[1].T,
        attn[2].T,
        vectors[1],
        attn[3],
        vectors[2],
        vectors[3],
        vectors[4],
        sum_up.astype(F32),
        vectors[5:9].reshape(F),
        sum_down.astype(F32),
        vectors[9],
        vectors[10],
        vectors[11],
    )


def solution(mesh):
    in_specs = (
        P("row", "seq", None),
        P("row", None),
        P(),
        P(),
        P(),
        P(),
        P(),
        P(),
        P(),
        P(),
        P(),
        P(),
        P(),
        P(),
        P(),
        P(),
        P(),
        P("row", "seq", None),
    )
    out_specs = (
        P("row", "seq", None),
        P("row", "seq", None),
        P(),
        P(),
        P(),
        P(),
        P(),
        P(),
        P(),
        P(),
        P(),
        P(),
        P(),
        P(),
        P(),
        P(),
        P(),
    )
    shape = dict(mesh.shape)
    fused = shape["row"] == 4 and shape["seq"] == 8
    return jax.shard_map(
        fused_layer if fused else per_device, mesh=mesh, in_specs=in_specs, out_specs=out_specs, check_vma=False
    )
```

```python
import contextlib
from functools import partial
import math

import jax
import jax.numpy as jnp
from jax import lax
from jax.experimental import pallas as pl
from jax.experimental.pallas import tpu as pltpu
from jax.sharding import PartitionSpec as P

H = 12
HD = 64


MASK_SCORE = -1e30
NORM_EPSILON = 1e-05


def from_behind(value, axis, by):
    count = lax.axis_size(axis)
    return lax.ppermute(value, axis, [(i, (i + by) % count) for i in range(count)])


def layer_norm(summed, norm_gain, norm_shift):
    centre = jnp.mean(summed, axis=-1, keepdims=True)
    centered = summed - centre
    inverse = lax.rsqrt(jnp.mean(centered * centered, axis=-1, keepdims=True) + NORM_EPSILON)
    normed = centered * inverse
    return (normed * norm_gain + norm_shift, normed, inverse)


def layer_norm_back(upstream, normed, inverse, norm_gain):
    scaled = upstream * norm_gain
    first_mean = jnp.mean(scaled, axis=-1, keepdims=True)
    second_mean = jnp.mean(scaled * normed, axis=-1, keepdims=True)
    summed_grad = inverse * (scaled - first_mean - normed * second_mean)
    return (summed_grad, jnp.sum(upstream * normed, axis=(0, 1)), jnp.sum(upstream, axis=(0, 1)))


def project(inputs, matrix):
    return jnp.einsum("rsk,kn->rsn", inputs, matrix, preferred_element_type=jnp.float32)


def project_back(upstream, matrix):
    return jnp.einsum("rsn,kn->rsk", upstream, matrix, preferred_element_type=jnp.float32)


def matrix_grad(inputs, upstream):
    return jnp.einsum("rsk,rsn->kn", inputs, upstream, preferred_element_type=jnp.float32)


def column_sum(upstream):
    return jnp.sum(upstream.astype(jnp.float32), axis=(0, 1))


def clip_numbers(clip_ends, position):
    return jnp.sum((clip_ends[:, None, :] <= position[None, :, None]).astype(jnp.int32), axis=-1)


def split_heads(tensor):
    return tensor.reshape(tensor.shape[0], tensor.shape[1], H, HD)


def join_heads(tensor):
    return tensor.reshape(tensor.shape[0], tensor.shape[1], H * HD)


def head_scores(queries, keys_block):
    return jnp.einsum(
        "rqhd,rkhd->rhqk", queries, keys_block, preferred_element_type=jnp.float32
    ) * HD ** (-0.5)


def allowed_pairs(query_numbers, key_numbers):
    return (query_numbers[:, :, None] == key_numbers[:, None, :])[:, None]


def online_update(running, queries, query_numbers, keys_block, values_block, key_numbers):
    run_peak, run_total, run_values = running
    allowed = allowed_pairs(query_numbers, key_numbers)
    masked = jnp.where(allowed, head_scores(queries, keys_block), MASK_SCORE)
    new_peak = jnp.maximum(run_peak, jnp.max(masked, axis=-1))
    weights = jnp.where(allowed, jnp.exp(masked - new_peak[..., None]), 0.0)
    rescale = jnp.exp(run_peak - new_peak)
    new_total = run_total * rescale + jnp.sum(weights, axis=-1)
    contrib = jnp.einsum(
        "rhqk,rkhd->rqhd",
        weights.astype(jnp.bfloat16),
        values_block,
        preferred_element_type=jnp.float32,
    )
    new_values = run_values * jnp.swapaxes(rescale, 1, 2)[..., None] + contrib
    return (new_peak, new_total, new_values)


def block_back(
    queries, grad_heads, log_total, delta_rows, query_numbers, keys_flat, values_flat, key_numbers
):
    keys_block = split_heads(keys_flat)
    values_block = split_heads(values_flat)
    allowed = allowed_pairs(query_numbers, key_numbers)
    shifted = jnp.where(
        allowed, head_scores(queries, keys_block) - log_total[..., None], MASK_SCORE
    )
    weights = jnp.exp(shifted)
    grad_weights = jnp.einsum(
        "rqhd,rkhd->rhqk", grad_heads, values_block, preferred_element_type=jnp.float32
    )
    grad_scores = (weights * (grad_weights - delta_rows[..., None])).astype(jnp.bfloat16)
    factor = HD ** (-0.5)
    query_part = (
        jnp.einsum("rhqk,rkhd->rqhd", grad_scores, keys_block, preferred_element_type=jnp.float32)
        * factor
    )
    key_part = (
        jnp.einsum("rhqk,rqhd->rkhd", grad_scores, queries, preferred_element_type=jnp.float32)
        * factor
    )
    value_part = jnp.einsum(
        "rhqk,rqhd->rkhd",
        weights.astype(jnp.bfloat16),
        grad_heads,
        preferred_element_type=jnp.float32,
    )
    return (join_heads(query_part), join_heads(key_part), join_heads(value_part))


def per_device(
    frames,
    clip_lengths,
    query_weight,
    query_bias,
    key_weight,
    value_weight,
    value_bias,
    out_weight,
    out_bias,
    norm1_gain,
    norm1_bias,
    up_weight,
    up_bias,
    down_weight,
    down_bias,
    norm2_gain,
    norm2_bias,
    cotangent,
):
    row_count = frames.shape[0]
    shard_len = frames.shape[1]
    cycle_size = lax.axis_size("seq")
    seq_place = lax.axis_index("seq")
    clip_ends = jnp.cumsum(clip_lengths, axis=1)
    offsets = jnp.arange(shard_len, dtype=jnp.int32)
    own_numbers = clip_numbers(clip_ends, seq_place * shard_len + offsets)
    frames_low = frames.astype(jnp.bfloat16)
    queries = split_heads((project(frames_low, query_weight) + query_bias).astype(jnp.bfloat16))
    keys_own = project(frames_low, key_weight).astype(jnp.bfloat16)
    values_own = (project(frames_low, value_weight) + value_bias).astype(jnp.bfloat16)
    initial = (
        jnp.full((row_count, H, shard_len), MASK_SCORE, jnp.float32),
        jnp.zeros((row_count, H, shard_len), jnp.float32),
        jnp.zeros((row_count, shard_len, H, HD), jnp.float32),
    )
    key_piece = lax.all_gather(keys_own, "seq", axis=1, tiled=True)
    value_piece = lax.all_gather(values_own, "seq", axis=1, tiled=True)
    piece_len = key_piece.shape[1]
    block_len = math.gcd(piece_len, 512)

    def attend_block(block_index, carried):
        offset = block_index * block_len
        key_block = lax.dynamic_slice_in_dim(key_piece, offset, block_len, 1)
        value_block = lax.dynamic_slice_in_dim(value_piece, offset, block_len, 1)
        position = offset + jnp.arange(block_len, dtype=jnp.int32)
        return online_update(
            carried,
            queries,
            own_numbers,
            split_heads(key_block),
            split_heads(value_block),
            clip_numbers(clip_ends, position),
        )

    run_peak, run_total, run_values = lax.fori_loop(
        0, piece_len // block_len, attend_block, initial
    )
    log_total = run_peak + jnp.log(run_total)
    attended_heads = run_values / jnp.swapaxes(run_total, 1, 2)[..., None]
    attended = join_heads(attended_heads)
    attended_low = attended.astype(jnp.bfloat16)
    branch = project(attended_low, out_weight) + out_bias
    hidden, unit_first, inverse_first = layer_norm(frames + branch, norm1_gain, norm1_bias)
    hidden_low = hidden.astype(jnp.bfloat16)
    before = project(hidden_low, up_weight) + up_bias
    active, gelu_back = jax.vjp(partial(jax.nn.gelu, approximate=False), before)
    active_low = active.astype(jnp.bfloat16)
    encoded, unit_second, inverse_second = layer_norm(
        hidden + project(active_low, down_weight) + down_bias, norm2_gain, norm2_bias
    )
    grad_mid, norm2_gain_grad, norm2_bias_grad = layer_norm_back(
        cotangent, unit_second, inverse_second, norm2_gain
    )
    grad_ffn = grad_mid.astype(jnp.bfloat16)
    down_weight_grad = matrix_grad(active_low, grad_ffn)
    down_bias_grad = column_sum(grad_ffn)
    grad_before = gelu_back(project_back(grad_ffn, down_weight))[0].astype(jnp.bfloat16)
    up_weight_grad = matrix_grad(hidden_low, grad_before)
    up_bias_grad = column_sum(grad_before)
    grad_hidden = grad_mid + project_back(grad_before, up_weight)
    grad_first, norm1_gain_grad, norm1_bias_grad = layer_norm_back(
        grad_hidden, unit_first, inverse_first, norm1_gain
    )
    grad_branch = grad_first.astype(jnp.bfloat16)
    out_weight_grad = matrix_grad(attended_low, grad_branch)
    out_bias_grad = column_sum(grad_branch)
    grad_attended = project_back(grad_branch, out_weight).astype(jnp.bfloat16)
    grad_heads = split_heads(grad_attended)
    delta_rows = jnp.swapaxes(
        jnp.sum(grad_heads.astype(jnp.float32) * attended_heads, axis=-1), 1, 2
    )
    query_start, key_start, value_start = block_back(
        queries, grad_heads, log_total, delta_rows, own_numbers, keys_own, values_own, own_numbers
    )

    def key_step(distance, carried):
        key_now, value_now, query_sum, key_sum, value_sum = carried
        key_now, value_now = from_behind((key_now, value_now), "seq", 1)
        key_sum, value_sum = (
            from_behind(key_sum.astype(jnp.bfloat16), "seq", 1).astype(key_sum.dtype),
            from_behind(value_sum.astype(jnp.bfloat16), "seq", 1).astype(value_sum.dtype),
        )
        source = (seq_place - distance) % cycle_size
        source_numbers = clip_numbers(clip_ends, source * shard_len + offsets)
        query_part, key_part, value_part = block_back(
            queries,
            grad_heads,
            log_total,
            delta_rows,
            own_numbers,
            key_now,
            value_now,
            source_numbers,
        )
        return (
            key_now,
            value_now,
            query_sum + query_part,
            key_sum + key_part,
            value_sum + value_part,
        )

    carried = lax.fori_loop(
        1, cycle_size, key_step, (keys_own, values_own, query_start, key_start, value_start)
    )
    query_total = carried[2]
    key_total, value_total = (
        from_behind(carried[3].astype(jnp.bfloat16), "seq", 1).astype(jnp.float32),
        from_behind(carried[4].astype(jnp.bfloat16), "seq", 1).astype(jnp.float32),
    )
    query_low = query_total.astype(jnp.bfloat16)
    key_low = key_total.astype(jnp.bfloat16)
    value_low = value_total.astype(jnp.bfloat16)
    query_weight_grad = matrix_grad(frames_low, query_low)
    query_bias_grad = column_sum(query_low)
    key_weight_grad = matrix_grad(frames_low, key_low)
    value_weight_grad = matrix_grad(frames_low, value_low)
    value_bias_grad = column_sum(value_low)
    frames_grad = (
        grad_first
        + project_back(query_low, query_weight)
        + project_back(key_low, key_weight)
        + project_back(value_low, value_weight)
    )
    shares = (
        lax.psum_scatter(query_weight_grad, "seq", scatter_dimension=0, tiled=True),
        lax.psum_scatter(query_bias_grad, "seq", scatter_dimension=0, tiled=True),
        lax.psum_scatter(key_weight_grad, "seq", scatter_dimension=0, tiled=True),
        lax.psum_scatter(value_weight_grad, "seq", scatter_dimension=0, tiled=True),
        lax.psum_scatter(value_bias_grad, "seq", scatter_dimension=0, tiled=True),
        lax.psum_scatter(out_weight_grad, "seq", scatter_dimension=0, tiled=True),
        lax.psum_scatter(out_bias_grad, "seq", scatter_dimension=0, tiled=True),
        lax.psum_scatter(norm1_gain_grad, "seq", scatter_dimension=0, tiled=True),
        lax.psum_scatter(norm1_bias_grad, "seq", scatter_dimension=0, tiled=True),
        lax.psum_scatter(up_weight_grad, "seq", scatter_dimension=0, tiled=True),
        lax.psum_scatter(up_bias_grad, "seq", scatter_dimension=0, tiled=True),
        lax.psum_scatter(down_weight_grad, "seq", scatter_dimension=0, tiled=True),
        lax.psum_scatter(down_bias_grad, "seq", scatter_dimension=0, tiled=True),
        lax.psum_scatter(norm2_gain_grad, "seq", scatter_dimension=0, tiled=True),
        lax.psum_scatter(norm2_bias_grad, "seq", scatter_dimension=0, tiled=True),
    )
    shares = (
        lax.psum(shares[0].astype(jnp.bfloat16), "row").astype(jnp.float32),
        lax.psum(shares[1].astype(jnp.bfloat16), "row").astype(jnp.float32),
        lax.psum(shares[2].astype(jnp.bfloat16), "row").astype(jnp.float32),
        lax.psum(shares[3].astype(jnp.bfloat16), "row").astype(jnp.float32),
        lax.psum(shares[4].astype(jnp.bfloat16), "row").astype(jnp.float32),
        lax.psum(shares[5].astype(jnp.bfloat16), "row").astype(jnp.float32),
        lax.psum(shares[6].astype(jnp.bfloat16), "row").astype(jnp.float32),
        lax.psum(shares[7].astype(jnp.bfloat16), "row").astype(jnp.float32),
        lax.psum(shares[8].astype(jnp.bfloat16), "row").astype(jnp.float32),
        lax.psum(shares[9].astype(jnp.bfloat16), "row").astype(jnp.float32),
        lax.psum(shares[10].astype(jnp.bfloat16), "row").astype(jnp.float32),
        lax.psum(shares[11].astype(jnp.bfloat16), "row").astype(jnp.float32),
        lax.psum(shares[12].astype(jnp.bfloat16), "row").astype(jnp.float32),
        lax.psum(shares[13].astype(jnp.bfloat16), "row").astype(jnp.float32),
        lax.psum(shares[14].astype(jnp.bfloat16), "row").astype(jnp.float32),
    )
    totals = (
        lax.all_gather(shares[0].astype(jnp.bfloat16), "seq", axis=0, tiled=True).astype(
            jnp.float32
        ),
        lax.all_gather(shares[1].astype(jnp.bfloat16), "seq", axis=0, tiled=True).astype(
            jnp.float32
        ),
        lax.all_gather(shares[2].astype(jnp.bfloat16), "seq", axis=0, tiled=True).astype(
            jnp.float32
        ),
        lax.all_gather(shares[3].astype(jnp.bfloat16), "seq", axis=0, tiled=True).astype(
            jnp.float32
        ),
        lax.all_gather(shares[4].astype(jnp.bfloat16), "seq", axis=0, tiled=True).astype(
            jnp.float32
        ),
        lax.all_gather(shares[5].astype(jnp.bfloat16), "seq", axis=0, tiled=True).astype(
            jnp.float32
        ),
        lax.all_gather(shares[6].astype(jnp.bfloat16), "seq", axis=0, tiled=True).astype(
            jnp.float32
        ),
        lax.all_gather(shares[7].astype(jnp.bfloat16), "seq", axis=0, tiled=True).astype(
            jnp.float32
        ),
        lax.all_gather(shares[8].astype(jnp.bfloat16), "seq", axis=0, tiled=True).astype(
            jnp.float32
        ),
        lax.all_gather(shares[9].astype(jnp.bfloat16), "seq", axis=0, tiled=True).astype(
            jnp.float32
        ),
        lax.all_gather(shares[10].astype(jnp.bfloat16), "seq", axis=0, tiled=True).astype(
            jnp.float32
        ),
        lax.all_gather(shares[11].astype(jnp.bfloat16), "seq", axis=0, tiled=True).astype(
            jnp.float32
        ),
        lax.all_gather(shares[12].astype(jnp.bfloat16), "seq", axis=0, tiled=True).astype(
            jnp.float32
        ),
        lax.all_gather(shares[13].astype(jnp.bfloat16), "seq", axis=0, tiled=True).astype(
            jnp.float32
        ),
        lax.all_gather(shares[14].astype(jnp.bfloat16), "seq", axis=0, tiled=True).astype(
            jnp.float32
        ),
    )
    return (
        encoded,
        frames_grad,
        totals[0],
        totals[1],
        totals[2],
        totals[3],
        totals[4],
        totals[5],
        totals[6],
        totals[7],
        totals[8],
        totals[9],
        totals[10],
        totals[11],
        totals[12],
        totals[13],
        totals[14],
    )


MESH = pl.DeviceIdType.MESH
LANES = 128
F32, BF16 = jnp.float32, jnp.bfloat16
VMEM_GRANT = 49 << 20
DOWN, UP, ATTN = 0, 1, 2

PIECES = (
    (DOWN, "zyx", 0, 3),
    (DOWN, "zxy", 3, 3),
    (UP, "zyx", 0, 3),
    (UP, "zxy", 3, 3),
    (ATTN, "zyx", 0, 2),
    (ATTN, "zxy", 2, 2),
    (ATTN, "yxz", 4, 2),
)


def dot(a, b):
    return jnp.dot(a, b, preferred_element_type=F32)


def dot_nt(a, b):
    return lax.dot_general(a, b, (((1,), (1,)), ((), ())), preferred_element_type=F32)


def dot_tn(a, b):
    return lax.dot_general(a, b, (((0,), (0,)), ((), ())), preferred_element_type=F32)


def rows_norm(value):
    centre = jnp.mean(value, axis=-1, keepdims=True)
    centered = value - centre
    inverse = lax.rsqrt(jnp.mean(centered * centered, axis=-1, keepdims=True) + NORM_EPSILON)
    return centered * inverse, inverse


def rows_norm_back(scaled, unit, inverse):
    first = jnp.mean(scaled, axis=-1, keepdims=True)
    second = jnp.mean(scaled * unit, axis=-1, keepdims=True)
    return inverse * (scaled - first - unit * second)


def layer_kernel(
    T,
    D,
    S,
    entries,
    frames,
    cotangent,
    lengths,
    query_w,
    key_w,
    value_w,
    out_w,
    up_w,
    down_w,
    query_b,
    value_b,
    out_b,
    gain1,
    bias1,
    up_b,
    down_b,
    gain2,
    bias2,
    encoded,
    frames_grad,
    vectors,
    sum_down,
    sum_up,
    sum_attn,
    bias_rows,
    up_rows,
    fall,
    wqkv,
    wo,
    wup,
    wdn,
    qall,
    kv,
    mask,
    probs,
    stat,
    lsed,
    att32,
    att16,
    attf,
    hq,
    fq,
    ar,
    br,
    asend,
    bsend,
    dgelu,
    hid32,
    unit1,
    rstd1,
    gmid,
    gfirst,
    gbr,
    doall,
    dkv32,
    dall,
    part_down,
    part_up,
    part_attn,
    got_down,
    got_up,
    got_attn,
    gm,
    dr,
    xs,
    xr,
    dxs,
    dxr,
    dxo,
    vsend,
    vrecv,
    vz,
    wsem,
    hes,
    her,
    frs,
    fss,
    abr,
    abs_,
    msr,
    mss,
    dor,
    dos,
    zsr,
    zss,
    agr,
    ags,
    agdr,
    vzr,
    vzs,
):
    HW, T2, FO = D // 2, 2 * T, wup.shape[1] // 8
    blocks = HW // LANES
    EIGHTH, SIXTEENTH = D // 8, D // 16
    out_b, gain1, bias1, down_b, gain2, bias2 = (
        ref[...].reshape(1, D) for ref in (out_b, gain1, bias1, down_b, gain2, bias2)
    )
    row, seq = lax.axis_index("row"), lax.axis_index("seq")
    x, c = lax.div(row, 2), lax.rem(row, 2)
    z, y = lax.div(seq, 2), lax.rem(seq, 2)
    not_first, not_last = z > 0, z < 3

    def device(x_, c_, y_, z_=z):
        return (2 * x_ + c_, 2 * z_ + y_)

    def octant(x_, c_, y_):
        return 4 * y_ + 2 * x_ + c_

    sib, xn, yn = device(x, 1 - c, y), device(1 - x, c, y), device(x, c, 1 - y)
    zp, zm = device(x, c, y, jnp.minimum(z + 1, 3)), device(x, c, y, jnp.maximum(z - 1, 0))

    def many(value, of):
        return pl.multiple_of(value, of)

    def at(start, size, of=None):
        return pl.ds(many(start, size if of is None else of), size)

    waits = []
    scope = contextlib.ExitStack()

    def phase(name):
        scope.close()
        if name:
            scope.enter_context(jax.named_scope(name))

    def send(src, dst, ssem, rsem, to):
        return pltpu.make_async_remote_copy(
            src_ref=src, dst_ref=dst, send_sem=ssem, recv_sem=rsem, device_id=to, device_id_type=MESH
        )

    def start(src, dst, ssem, rsem, to):
        send(src, dst, ssem, rsem, to).start()

    def arrived(ref, rsem):
        send(ref, ref, mss.at[0], rsem, sib).wait_recv()

    def sent(ref, ssem):
        waits.append(send(ref, ref, ssem, msr.at[0], sib).wait_send)

    def sent_along_z(ref_of, ssem, rest=0, lines=1):
        for blocks_sent, when in ((1, (z == 0) | (z == 3)), (5, (z > 0) & (z < 3))):
            ref = ref_of(rest + lines * blocks_sent)
            copy = send(ref, ref, ssem, msr.at[0], sib)
            waits.append(partial(pl.when(when), copy.wait_send))

    send_names, names = {}, {}

    def group(name):
        return mss.at[send_names.setdefault(name, len(send_names))]

    def one(name, family=None):
        return group(family or name), got_of(name)

    def got_of(name):
        return msr.at[names.setdefault(name, len(names))]

    phase("enter")
    heads_here = at(HW * y, HW)
    loads = [
        pltpu.make_async_copy(query_w.at[:, heads_here], wqkv.at[:, pl.ds(0, HW)], wsem.at[0]),
        pltpu.make_async_copy(key_w.at[:, heads_here], wqkv.at[:, pl.ds(HW, HW)], wsem.at[1]),
        pltpu.make_async_copy(value_w.at[:, heads_here], wqkv.at[:, pl.ds(2 * HW, HW)], wsem.at[2]),
        pltpu.make_async_copy(out_w, wo, wsem.at[3]),
        pltpu.make_async_copy(up_w, wup, wsem.at[4]),
        pltpu.make_async_copy(down_w, wdn, wsem.at[5]),
    ]
    barrier = pltpu.get_barrier_semaphore()
    peers = [device(x_, c_, y_) for x_ in (x, 1 - x) for c_ in (c, 1 - c) for y_ in (y, 1 - y)][1:]
    peers += [device(x, c, y, lax.rem(z + k, 4)) for k in (1, 2, 3)]
    for peer in peers:
        pl.semaphore_signal(barrier, inc=1, device_id=peer, device_id_type=MESH)
    for load in loads:
        load.start()
    fall[at(T * seq, T), :] = frames[...].astype(BF16)
    vectors[...] = jnp.zeros_like(vectors)
    bias_rows[0:1, :] = query_b[...].reshape(1, D)
    bias_rows[1:2, :] = value_b[...].reshape(1, D)
    for quarter in range(4):
        up_rows[quarter] = jnp.broadcast_to(up_b[pl.ds(D * quarter, D)].reshape(1, D), (8, D))
    pl.semaphore_wait(barrier, len(peers))

    phase("frames_gather")

    def slab(z_, y_):
        return fall.at[at(T * (2 * z_ + y_), T), :]

    def push(z_, direction):
        to = (zp, zm, yn)[direction]
        return send(slab(z_, y), slab(z_, y), fss.at[direction // 2], frs.at[2 * z_ + y], to)

    pl.when(not_last)(lambda: push(z, 0).start())
    pl.when(not_first)(lambda: push(z, 1).start())
    push(z, 2).start()
    query_bias, value_bias = bias_rows[0:1, heads_here], bias_rows[1:2, heads_here]
    for load in loads[:3]:
        load.wait()

    def project_slab(z_, y_):
        rows = at(T * (2 * z_ + y_), T)
        flat = dot(fall[rows, :], wqkv[...])
        query = (flat[:, :HW] + query_bias).astype(BF16).astype(F32) * HD ** (-0.5)
        qall[rows, :] = query.astype(BF16)
        kv[rows, pl.ds(0, HW)] = flat[:, HW : 2 * HW].astype(BF16)
        kv[rows, pl.ds(HW, HW)] = (flat[:, 2 * HW :] + value_bias).astype(BF16)

    project_slab(z, y)
    key_at = lax.broadcasted_iota(jnp.int32, (1, S), 1)
    query_at = lax.broadcasted_iota(jnp.int32, (T2, 1), 0) + T2 * z
    key_number, query_number = jnp.zeros((1, S), jnp.int32), jnp.zeros((T2, 1), jnp.int32)
    clip_end = jnp.int32(0)
    for entry in range(entries):
        clip_end = clip_end + lengths[0, entry]
        key_number = key_number + jnp.where(clip_end <= key_at, 1, 0)
        query_number = query_number + jnp.where(clip_end <= query_at, 1, 0)
    mask[...] = jnp.where(query_number == key_number, 0.0, MASK_SCORE)

    @pl.loop(0, 4)
    def _(k):
        left, right = z - k - 1, z + k + 1

        @pl.when(left >= 0)
        def _():
            arrived(slab(left, y), frs.at[2 * left + y])
            pl.when(not_last)(lambda: push(left, 0).start())
            push(left, 2).start()

        @pl.when(right <= 3)
        def _():
            arrived(slab(right, y), frs.at[2 * right + y])
            pl.when(not_first)(lambda: push(right, 1).start())
            push(right, 2).start()

        pl.when(left >= 0)(lambda: project_slab(left, y))
        pl.when(right <= 3)(lambda: project_slab(right, y))

        @pl.when(z - k >= 0)
        def _():
            arrived(slab(z - k, 1 - y), frs.at[2 * (z - k) + 1 - y])
            project_slab(z - k, 1 - y)

        @pl.when((k > 0) & (z + k <= 3))
        def _():
            arrived(slab(z + k, 1 - y), frs.at[2 * (z + k) + 1 - y])
            project_slab(z + k, 1 - y)

    sent(fall.at[pl.ds(0, 4 * T), :], fss.at[1])
    sent_along_z(lambda count: fall.at[pl.ds(0, T * count), :], fss.at[0])

    phase("attention")
    pair_rows = at(T2 * z, T2)
    lane = lax.broadcasted_iota(jnp.int32, (T2, LANES), 1)
    low_half = lane < HD

    def half(value, which):
        return jnp.where(low_half == (which == 0), value, 0.0)

    stat[...] = jnp.zeros_like(stat)
    mine, other = at(T * y, T), at(T * (1 - y), T)

    def heads_push(b):
        part, there = at(LANES * b, LANES), at(HW * y + LANES * b, LANES, LANES)
        return send(att16.at[other, part], attf.at[:, there], hes.at[0], her.at[b], yn)

    @pl.loop(0, blocks)
    def _(b):
        lanes, value_lanes = at(LANES * b, LANES), at(HW + LANES * b, LANES, LANES)
        queries = qall[pair_rows, lanes].astype(F32)
        outs = []
        for which in range(2):
            scores = dot_nt(half(queries, which).astype(BF16), kv[:, lanes]) + mask[...]
            peak = jnp.max(scores, axis=-1, keepdims=True)
            powers = jnp.exp(scores - peak)
            total = jnp.sum(powers, axis=-1, keepdims=True)
            low = (powers * (1.0 / total)).astype(BF16)
            probs[2 * b + which] = low
            outs.append(dot(low, kv[:, value_lanes]))
            stat[0] = jnp.where(lane == 2 * b + which, peak + jnp.log(total), stat[0])
        out = jnp.where(low_half, outs[0], outs[1])
        att32[:, lanes] = out
        att16[:, lanes] = out.astype(BF16)
        heads_push(b).start()

    phase("heads_exchange")
    attf[:, heads_here] = att16[mine, :]
    lsed[z, 0:8, :] = stat[0].T[0:8, :]
    loads[3].wait()
    for b in range(blocks):
        arrived(attf.at[:, at(HW * (1 - y) + LANES * b, LANES, LANES)], her.at[b])
    sent(att16.at[pl.ds(0, T), :], hes.at[0])
    phase("out_norm1")
    branch = dot(attf[...], wo[...]) + out_b
    unit, inverse = rows_norm(frames[...] + branch)
    hidden = unit * gain1 + bias1
    unit1[...] = unit
    rstd1[...] = jnp.broadcast_to(inverse, (T, LANES))
    hid32[...] = hidden
    here = at(T * octant(x, c, y), T)

    def rows_of(buffer, x_, c_, y_):
        return buffer.at[at(T * octant(x_, c_, y_), T), :]

    def halves_of(buffer, x_, c_, y_):
        first = T * octant(x_, c_, y_)
        return buffer.at[at(first, T // 2), :], buffer.at[at(first + T // 2, T // 2), :]

    def share(buffer, name, to, tag):
        own = rows_of(buffer, x, c, y)
        start(own, own, *one(name + tag, name), to)

    def from_x(buffer, name):
        part, top = rows_of(buffer, 1 - x, c, y), halves_of(buffer, 1 - x, c, y)[0]
        arrived(part, got_of(name + "_x"))
        start(top, top, *one(name + "_top", name), yn)
        start(part, part, *one(name + "_dx", name), sib)

    def from_y(buffer, name):
        part, bottom = rows_of(buffer, x, c, 1 - y), halves_of(buffer, x, c, 1 - y)[1]
        arrived(part, got_of(name + "_y"))
        start(bottom, bottom, *one(name + "_bottom", name), xn)
        start(part, part, *one(name + "_dy", name), sib)

    def from_diagonal(buffer, name):
        part = rows_of(buffer, 1 - x, c, 1 - y)
        top, bottom = halves_of(buffer, 1 - x, c, 1 - y)
        arrived(top, got_of(name + "_top"))
        arrived(bottom, got_of(name + "_bottom"))
        start(part, part, *one(name + "_dd", name), sib)

    def from_sibling(buffer, name):
        arrived(rows_of(buffer, x, 1 - c, y), got_of(name + "_d"))
        arrived(rows_of(buffer, 1 - x, 1 - c, y), got_of(name + "_dx"))
        arrived(rows_of(buffer, x, 1 - c, 1 - y), got_of(name + "_dy"))
        arrived(rows_of(buffer, 1 - x, 1 - c, 1 - y), got_of(name + "_dd"))

    def spread(sent, got, index, x_, c_, y_):
        to = octant(x_, c_, y_)
        copy = send(
            sent.at[to],
            got.at[here, :],
            abs_.at[index],
            abr.at[index, octant(x, c, y)],
            device(x_, c_, y_),
        )
        copy.start()

    def spread_chip(sent, got, index, x_, y_):
        for c_ in (c, 1 - c):
            spread(sent, got, index, x_, c_, y_)

    def spread_diagonal(sent, got, index):
        spread_chip(sent, got, index, 1 - x, 1 - y)

    def spread_y(sent, got, index):
        spread_chip(sent, got, index, x, 1 - y)

    def spread_arrived(got, index):
        for x_, c_, y_ in [(x_, c_, y_) for x_ in (x, 1 - x) for c_ in (c, 1 - c) for y_ in (y, 1 - y)][1:]:
            arrived(rows_of(got, x_, c_, y_), abr.at[index, octant(x_, c_, y_)])

    chips = ((1 - x, y), (x, 1 - y), (1 - x, 1 - y), (x, y))

    sent(hq.at[pl.ds(0, 7 * T), :], group("hid"))
    sent(fq.at[pl.ds(0, 7 * T), :], group("ffn"))
    for index, got in enumerate((ar, br)):
        sent(got.at[pl.ds(0, 7 * T), :], abs_.at[index])
    hq[here, :] = hidden.astype(BF16)
    share(hq, "hid", xn, "_x")
    share(hq, "hid", yn, "_y")
    share(hq, "hid", sib, "_d")

    phase("up_gelu")
    loads[4].wait()
    scale = 2.0 ** -0.5
    for order, (x_, y_) in enumerate(chips):
        chip = 2 * y_ + x_
        before = dot(hq[here, :], wup[:, at(D * chip, D)]) + up_rows[chip][0:1, :]
        rise = 0.5 * (1.0 + lax.erf(before * scale))
        dgelu[chip] = rise + before * jnp.exp(-0.5 * before * before) * (2.0 * math.pi) ** -0.5
        active = (before * rise).astype(BF16)
        asend[2 * chip] = active[:, :FO]
        asend[2 * chip + 1] = active[:, FO:]
        if order < 2:
            spread_chip(asend, ar, 0, x_, y_)
    spread(asend, ar, 0, x, 1 - c, y)
    ar[here, :] = asend[octant(x, c, y)]
    phase("down_norm2")
    loads[5].wait()
    fed = hid32[...] + down_b
    for eighth in range(8):
        fed = fed + dot(asend[eighth], wdn[pl.ds(FO * eighth, FO), :])
    unit2, inverse2 = rows_norm(fed)
    encoded[...] = unit2 * gain2 + bias2
    cot = cotangent[...]
    grad_mid = rows_norm_back(cot * gain2, unit2, inverse2)
    vectors[10:11, :] = jnp.sum(cot * unit2, axis=0, keepdims=True)
    vectors[11:12, :] = jnp.sum(cot, axis=0, keepdims=True)
    gmid[...] = grad_mid
    fq[here, :] = grad_mid.astype(BF16)
    share(fq, "ffn", xn, "_x")
    share(fq, "ffn", sib, "_d")
    vectors[9:10, :] = jnp.sum(fq[here, :].astype(F32), axis=0, keepdims=True)
    phase("ffn_back")
    for order, (x_, y_) in enumerate(chips):
        chip = 2 * y_ + x_
        quarter = at(D * chip, D)
        low = (dot_nt(fq[here, :], wdn[quarter, :]) * dgelu[chip]).astype(BF16)
        bsend[2 * chip] = low[:, :FO]
        bsend[2 * chip + 1] = low[:, FO:]
        if order == 0:
            spread_chip(bsend, br, 1, x_, y_)
        vectors[pl.ds(5 + chip, 1), :] = jnp.sum(low.astype(F32), axis=0, keepdims=True)
        gmid[...] += dot_nt(low, wup[:, quarter])
    spread(bsend, br, 1, x, 1 - c, y)
    br[here, :] = bsend[octant(x, c, y)]
    phase("norm1_back")
    grad_hidden = gmid[...]
    unit = unit1[...]
    grad_first = rows_norm_back(grad_hidden * gain1, unit, rstd1[:, 0:1])
    vectors[3:4, :] = jnp.sum(grad_hidden * unit, axis=0, keepdims=True)
    vectors[4:5, :] = jnp.sum(grad_hidden, axis=0, keepdims=True)
    gfirst[...] = grad_first
    gbr[mine, :] = grad_first.astype(BF16)
    start(gbr.at[mine, :], gbr.at[mine, :], *one("gbr"), yn)
    sent(gbr.at[mine, :], group("gbr"))
    vectors[2:3, :] = jnp.sum(gbr[mine, :].astype(F32), axis=0, keepdims=True)

    parts, gots = (part_down, part_up, part_attn), (got_down, got_up, got_attn)
    slab_rows = (FO // 4, D // 4, EIGHTH)

    def part_slab(t, j):
        return parts[t].at[at(slab_rows[t] * j, slab_rows[t]), :]

    outer = (z == 0) | (z == 3)
    near = jnp.where(z < 2, 1 - z, 5 - z)
    inner_there, outer_there = jnp.where(z < 2, 2, 1), jnp.where(z < 2, 3, 0)

    def part_send(t, src, j, to, slot):
        start(src, gots[t].at[slot], zss.at[t], zsr.at[t, slot], device(x, c, y, to))

    def sum_send(t):
        sent(parts[t].at[pl.ds(0, 3 * slab_rows[t]), :], zss.at[t])

        @pl.when(outer)
        def _():
            for j in (outer_there, inner_there, near):
                part_send(t, part_slab(t, j), j, near, j)

        @pl.when(jnp.logical_not(outer))
        def _():
            part_send(t, part_slab(t, near), near, near, z)

    def sum_pass(t):
        @pl.when(jnp.logical_not(outer))
        def _():
            for j, slot in ((outer_there, z), (inner_there, outer_there)):
                got = gots[t].at[j]
                arrived(got, zsr.at[t, j])
                got[...] = (got[...].astype(F32) + part_slab(t, j)[...].astype(F32)).astype(BF16)
                part_send(t, got, j, j, slot)

    def own_tile(t):
        if t == DOWN:
            return sum_down.at[at(FO * octant(x, c, y) + EIGHTH // 2 * 2 * z, EIGHTH, EIGHTH), :]
        if t == UP:
            return sum_up.at[at(D // 4 * z, D // 4), at(FO * octant(x, c, y), FO)]
        return sum_attn.at[at(D * row + HW * y + EIGHTH * z, EIGHTH), :]

    def sum_end(t):
        total = part_slab(t, z)[...].astype(F32)
        for slot in (jnp.where(outer, near, z), jnp.where(outer, inner_there, near)):
            arrived(gots[t].at[slot], zsr.at[t, slot])
            total = total + gots[t][slot].astype(F32)
        own_tile(t)[...] = total.astype(BF16)

    unit_rows = (SIXTEENTH // 3, EIGHTH // 3, SIXTEENTH // 3)

    def tile(u, x_, y_, z_):
        t, _, first, count = PIECES[u]
        rows = unit_rows[t]
        if t == DOWN:
            start_row = FO * octant(x_, c, y_) + EIGHTH * z_ + rows * first
            return sum_down.at[at(start_row, rows * count, rows), :]
        if t == UP:
            start_row = D // 4 * z_ + rows * first
            return sum_up.at[at(start_row, rows * count, rows), at(FO * octant(x_, c, y_), FO)]
        start_row = D * (2 * x_ + c) + HW * y_ + EIGHTH * z_ + rows * first
        return sum_attn.at[at(start_row, rows * count, rows), :]

    def gather_send(u, place, z_, ssem, rsem, to):
        part = tile(u, *place, z_)
        return send(part, part, ssem, rsem, to)

    def to_sibling(u, place, z_):
        gather_send(u, place, z_, ags.at[u], agdr.at[u], sib).start()

    places = ((x, y), (1 - x, y), (x, 1 - y), (1 - x, 1 - y))

    def order_of(u):
        over_y, over_x = (2, yn), (1, xn)
        return (over_y, over_x) if PIECES[u][1] in ("zyx", "yxz") else (over_x, over_y)

    def z_last(u):
        return PIECES[u][1][2] == "z"

    def along_z(u, p, z_, direction):
        to = (zp, zm)[direction]
        return gather_send(u, places[p], z_, ags.at[u], agr.at[u, 4 * p + z_], to)

    def z_out(u, p):
        pl.when(not_last)(lambda: along_z(u, p, z, 0).start())
        pl.when(not_first)(lambda: along_z(u, p, z, 1).start())

    def second_sem(u, z_):
        return agr.at[u, 16] if z_last(u) else agr.at[u, 4 + z_]

    def third_sem(u, slot):
        return agr.at[u, (17 if z_last(u) else 8) + slot]

    def to_second(u, place, z_):
        gather_send(u, place, z_, ags.at[u], second_sem(u, z_), order_of(u)[0][1]).start()

    def to_third(u, place, slot):
        z_ = z if z_last(u) else lax.rem(slot, 4)
        gather_send(u, place, z_, ags.at[u], third_sem(u, slot), order_of(u)[1][1]).start()

    def gather_own(t):
        for u in pieces_of(t):
            z_out(u, 0)
        for u in pieces_of(t):
            to_second(u, places[0], z)
            to_third(u, places[0], 0 if z_last(u) else z)
            to_sibling(u, places[0], z)

    def pieces_of(t, last=None):
        return [u for u in range(len(PIECES)) if PIECES[u][0] == t and last in (None, z_last(u))]

    def sides(k, take):
        pl.when(z - k >= 0)(lambda: take(z - k, not_last, 0))
        if k > 0:
            pl.when(z + k <= 3)(lambda: take(z + k, not_first, 1))

    def gather_z(t, k):
        for u in pieces_of(t, False):

            def take(z_, more, direction):
                arrived(tile(u, *places[0], z_), agr.at[u, z_])
                pl.when(more)(lambda: along_z(u, 0, z_, direction).start())
                to_second(u, places[0], z_)
                to_third(u, places[0], z_)
                to_sibling(u, places[0], z_)

            sides(k, take)

    def gather_second(t, k):
        for u in pieces_of(t, False):

            def take(z_, more, direction):
                place = places[order_of(u)[0][0]]
                arrived(tile(u, *place, z_), second_sem(u, z_))
                to_third(u, place, 4 + z_)
                to_sibling(u, place, z_)

            sides(k, take)

    def gather_third(t, k):
        for u in pieces_of(t, False):

            def take(z_, more, direction):
                for offset, p in ((0, order_of(u)[1][0]), (4, 3)):
                    arrived(tile(u, *places[p], z_), third_sem(u, offset + z_))
                    to_sibling(u, places[p], z_)

            sides(k, take)

    def plane_first(t):
        for u in pieces_of(t, True):
            p = order_of(u)[0][0]
            arrived(tile(u, *places[p], z), second_sem(u, z))
            to_third(u, places[p], 1)
            z_out(u, p)
            to_sibling(u, places[p], z)

    def plane_second(t):
        for u in pieces_of(t, True):
            for slot, p in ((0, order_of(u)[1][0]), (1, 3)):
                arrived(tile(u, *places[p], z), third_sem(u, slot))
                z_out(u, p)
                to_sibling(u, places[p], z)

    def plane_z(t, k):
        for u in pieces_of(t, True):
            for p in (0, order_of(u)[0][0], order_of(u)[1][0], 3):

                def take(z_, more, direction):
                    arrived(tile(u, *places[p], z_), agr.at[u, 4 * p + z_])
                    pl.when(more)(lambda: along_z(u, p, z_, direction).start())
                    to_sibling(u, places[p], z_)

                sides(k, take)

    def gather_end():
        for u, (_, _, _, count) in enumerate(PIECES):

            def as_many(blocks_sent):
                return sum_down.at[pl.ds(0, unit_rows[DOWN] * count * blocks_sent), :]

            arrived(as_many(16), agdr.at[u])
            if z_last(u):
                sent_along_z(as_many, ags.at[u], 19, 4)
            else:
                sent_along_z(as_many, ags.at[u], 28)

    def out_back():
        arrived(gbr.at[other, :], got_of("gbr"))
        da = dot_nt(gbr[...], wo[heads_here, :]).astype(BF16)
        doall[pair_rows, :] = da
        product = da.astype(F32) * att32[...]
        stat[1] = jnp.zeros((T2, LANES), F32)
        for head in range(2 * blocks):
            lanes = slice(LANES * (head // 2), LANES * (head // 2 + 1))
            delta = jnp.sum(half(product[:, lanes], head % 2), axis=-1, keepdims=True)
            stat[1] = jnp.where(lane == head, delta, stat[1])
        lsed[z, 8:16, :] = stat[1].T[0:8, :]
        pl.when(not_last)(lambda: grads_push(z, 0))
        pl.when(not_first)(lambda: grads_push(z, 1))
        gm[3] = dot_tn(att16[...], gbr[...]).astype(BF16)

    def grads_rows(z_):
        return doall.at[at(T2 * z_, T2), :], lsed.at[z_]

    def grads_copies(z_, direction):
        to = (zp, zm)[direction]
        return [
            send(ref, ref, dos.at[index], dor.at[index, z_], to)
            for index, ref in enumerate(grads_rows(z_))
        ]

    def grads_push(z_, direction):
        for copy in grads_copies(z_, direction):
            copy.start()

    sent_along_z(lambda count: fall.at[pl.ds(0, T * count), :], dos.at[0])
    sent_along_z(lambda count: lsed.at[pl.ds(0, count)], dos.at[1])

    def grads_arrive(k):
        def take(z_, more, direction):
            for index, ref in enumerate(grads_rows(z_)):
                arrived(ref, dor.at[index, z_])
            pl.when(more)(lambda: grads_push(z_, direction))

        pl.when(z - k >= 0)(lambda: take(z - k, not_last, 0))
        pl.when(z + k <= 3)(lambda: take(z + k, not_first, 1))

    def queries_back():
        @pl.loop(0, blocks)
        def _(b):
            lanes, value_lanes = at(LANES * b, LANES), at(HW + LANES * b, LANES, LANES)
            heads = doall[pair_rows, lanes].astype(F32)
            product = heads * att32[:, lanes]
            pieces = []
            for which in range(2):
                delta = jnp.sum(half(product, which), axis=-1, keepdims=True)
                grad_probs = dot_nt(half(heads, which).astype(BF16), kv[:, value_lanes])
                grad_scores = probs[2 * b + which].astype(F32) * (grad_probs - delta)
                pieces.append(dot(grad_scores.astype(BF16), kv[:, lanes]))
            total = jnp.where(low_half, pieces[0], pieces[1]) * HD ** (-0.5)
            dall[:, lanes] = total.astype(BF16)

    def keys_back(z_):
        rows = at(T2 * z_, T2)

        @pl.loop(0, blocks)
        def _(b):
            lanes, value_lanes = at(LANES * b, LANES), at(HW + LANES * b, LANES, LANES)
            keys, values = kv[pair_rows, lanes].astype(F32), kv[pair_rows, value_lanes].astype(F32)
            queries, grads = qall[rows, lanes], doall[rows, lanes]
            key_pieces, value_pieces = [], []
            for which in range(2):
                head = 2 * b + which
                scores = dot_nt(half(keys, which).astype(BF16), queries) + mask[:, rows]
                powers = jnp.exp(scores - lsed[z_, pl.ds(head, 1), :])
                grad_probs = dot_nt(half(values, which).astype(BF16), grads)
                grad_scores = powers * (grad_probs - lsed[z_, pl.ds(8 + head, 1), :])
                key_pieces.append(dot(grad_scores.astype(BF16), queries))
                value_pieces.append(dot(powers.astype(BF16), grads))
            dkv32[:, lanes] += jnp.where(low_half, key_pieces[0], key_pieces[1])
            dkv32[:, value_lanes] += jnp.where(low_half, value_pieces[0], value_pieces[1])

    def keys_back_at(k):
        pl.when(z - k >= 0)(lambda: keys_back(z - k))
        if k > 0:
            pl.when(z + k <= 3)(lambda: keys_back(z + k))

    def attention_weights():
        dall[:, pl.ds(HW, D)] = dkv32[...].astype(BF16)
        grads = dot_tn(dall[...], fall[pair_rows, :])
        for matrix in range(3):
            gm[matrix] = grads[HW * matrix : HW * (matrix + 1), :].astype(BF16)
        sent(dr, group("d"))
        for slot in range(2):
            start(gm.at[1 - c + 2 * slot], dr.at[slot], *one(("d", slot), "d"), sib)

    def input_grad():
        into = dot_nt(dall[...], wqkv[...])
        dxo[...] = into
        dxs[...] = dxo[other, :].astype(BF16)
        start(dxs, dxr, *one("dx"), yn)
        sent(dxs, group("dx"))
        sums = jnp.sum(dall[...].astype(F32), axis=0, keepdims=True)
        vectors[0:1, heads_here] = sums[:, :HW]
        vectors[1:2, heads_here] = sums[:, 2 * HW :]

    def input_grad_end():
        arrived(dxr, got_of("dx"))
        frames_grad[...] = gfirst[...] + dxo[mine, :] + dxr[...].astype(F32)

    def attention_x():
        for slot in range(2):
            arrived(dr.at[slot], got_of(("d", slot)))
        xs[...] = (gm[c + 2 * (1 - x)].astype(F32) + dr[1 - x].astype(F32)).astype(BF16)
        start(xs, xr, *one("xs"), xn)
        sent(xs, group("xs"))

    def attention_z():
        arrived(xr, got_of("xs"))
        part_attn[...] = (gm[c + 2 * x].astype(F32) + dr[x].astype(F32) + xr[...].astype(F32)).astype(BF16)
        sum_send(ATTN)

    def down_grad():
        part_down[...] = dot_tn(ar[...], fq[...]).astype(BF16)
        sum_send(DOWN)

    def up_grad():
        part_up[...] = dot_tn(hq[...], br[...]).astype(BF16)
        sum_send(UP)

    def vector_step(i, to):
        vsend[i] = vectors[...]
        start(vsend.at[i], vrecv.at[i], *one(("v", i)), to)
        sent(vsend.at[i], group(("v", i)))

    def vector_add(i):
        arrived(vrecv.at[i], got_of(("v", i)))
        vectors[...] += vrecv[i]

    def vector_z():
        vsend[3] = vectors[...]
        vz[z] = vectors[...]
        sent(vz.at[pl.ds(0, 3)], vzs.at[0])
        for k in (1, 2, 3):
            j = lax.rem(z + k, 4)
            start(vsend.at[3], vz.at[z], vzs.at[0], vzr.at[z], device(x, c, y, j))

    def vector_end():
        for k in (1, 2, 3):
            j = lax.rem(z + k, 4)
            arrived(vz.at[j], vzr.at[j])
        vectors[...] = (vz[0] + vz[1]) + (vz[2] + vz[3])

    dkv32[...] = jnp.zeros_like(dkv32)
    phase("hid_forward")
    from_x(hq, "hid")
    from_y(hq, "hid")
    phase("out_back")
    out_back()
    share(fq, "ffn", yn, "_y")
    spread_diagonal(asend, ar, 0)
    phase("queries_back")
    queries_back()
    phase("ffn_x")
    from_x(fq, "ffn")
    phase("keys_back0")
    keys_back_at(0)
    phase("ffn_y")
    from_y(fq, "ffn")
    spread_y(bsend, br, 1)
    phase("grads1")
    grads_arrive(1)
    spread_diagonal(bsend, br, 1)
    phase("keys_back1")
    keys_back_at(1)
    phase("hid_diag")
    from_diagonal(hq, "hid")
    phase("grads2")
    grads_arrive(2)
    phase("keys_back2")
    keys_back_at(2)
    phase("ffn_diag")
    from_diagonal(fq, "ffn")
    phase("grads3")
    grads_arrive(3)
    phase("keys_back3")
    keys_back_at(3)
    phase("attn_weights")
    attention_weights()
    phase("wait_down")
    from_sibling(fq, "ffn")
    spread_arrived(ar, 0)
    phase("down_grad")
    down_grad()
    phase("attention_x")
    attention_x()
    phase("input_grad")
    input_grad()
    phase("wait_up")
    from_sibling(hq, "hid")
    spread_arrived(br, 1)
    phase("up_grad")
    up_grad()
    phase("vec0")
    vector_step(0, sib)
    vector_add(0)
    vector_step(1, xn)
    phase("down_pass")
    sum_pass(DOWN)
    phase("up_pass")
    sum_pass(UP)
    phase("down_end")
    sum_end(DOWN)
    gather_own(DOWN)
    vector_add(1)
    vector_step(2, yn)
    phase("attention_z")
    attention_z()
    phase("g_d1")
    gather_z(DOWN, 1)
    gather_second(DOWN, 0)
    phase("up_end")
    sum_end(UP)
    gather_own(UP)
    phase("attn_pass")
    sum_pass(ATTN)
    vector_add(2)
    vector_z()
    input_grad_end()
    phase("g_d2")
    gather_z(DOWN, 2)
    gather_second(DOWN, 1)
    gather_third(DOWN, 0)
    phase("attn_end")
    sum_end(ATTN)
    gather_own(ATTN)
    phase("g1")
    gather_z(UP, 1)
    gather_second(UP, 0)
    vector_end()
    phase("g2")
    gather_z(DOWN, 3)
    gather_second(DOWN, 2)
    gather_third(DOWN, 1)
    gather_z(UP, 2)
    gather_second(UP, 1)
    gather_third(UP, 0)
    plane_first(ATTN)
    gather_z(ATTN, 1)
    gather_second(ATTN, 0)
    plane_second(ATTN)
    phase("g3")
    gather_second(DOWN, 3)
    gather_third(DOWN, 2)
    gather_z(UP, 3)
    gather_second(UP, 2)
    gather_third(UP, 1)
    gather_z(ATTN, 2)
    gather_second(ATTN, 1)
    gather_third(ATTN, 0)
    plane_z(ATTN, 1)
    phase("g4")
    gather_third(DOWN, 3)
    gather_second(UP, 3)
    gather_third(UP, 2)
    gather_z(ATTN, 3)
    gather_second(ATTN, 2)
    gather_third(ATTN, 1)
    plane_z(ATTN, 2)
    phase("g5")
    gather_third(UP, 3)
    gather_second(ATTN, 3)
    gather_third(ATTN, 2)
    plane_z(ATTN, 3)
    gather_third(ATTN, 3)
    phase("gather_end")
    gather_end()
    phase("sends_end")
    assert (len(send_names), len(names)) == (mss.shape[0], msr.shape[0])
    for wait in waits:
        wait()
    phase(None)


def fused_layer(
    frames,
    clip_lengths,
    query_weight,
    query_bias,
    key_weight,
    value_weight,
    value_bias,
    out_weight,
    out_bias,
    norm1_gain,
    norm1_bias,
    up_weight,
    up_bias,
    down_weight,
    down_bias,
    norm2_gain,
    norm2_bias,
    cotangent,
):
    T, D = frames.shape[1], frames.shape[2]
    F = up_weight.shape[1]
    S = T * lax.axis_size("seq")
    HW, T2, EIGHTH, FO = D // 2, 2 * T, D // 8, F // 8
    blocks = HW // LANES
    entries = clip_lengths.shape[1]
    vmem, smem, hbm = (
        pl.BlockSpec(memory_space=pltpu.VMEM),
        pl.BlockSpec(memory_space=pltpu.SMEM),
        pl.BlockSpec(memory_space=pl.ANY),
    )
    dma, n = pltpu.SemaphoreType.DMA, len(PIECES)
    low, wide = (lambda *shape: pltpu.VMEM(shape, BF16)), (lambda *shape: pltpu.VMEM(shape, F32))
    scratch = dict(
        bias_rows=wide(8, D),
        up_rows=wide(4, 8, D),
        fall=low(S, D),
        wqkv=low(D, 3 * HW),
        wo=low(D, D),
        wup=low(D, F),
        wdn=low(F, D),
        qall=low(S, HW),
        kv=low(S, D),
        mask=wide(T2, S),
        probs=low(2 * blocks, T2, S),
        stat=wide(2, T2, LANES),
        lsed=wide(5, 16, T2),
        att32=wide(T2, HW),
        att16=low(T2, HW),
        attf=low(T, D),
        hq=low(8 * T, D),
        fq=low(8 * T, D),
        ar=low(8 * T, FO),
        br=low(8 * T, FO),
        asend=low(8, T, FO),
        bsend=low(8, T, FO),
        dgelu=wide(4, T, D),
        hid32=wide(T, D),
        unit1=wide(T, D),
        rstd1=wide(T, LANES),
        gmid=wide(T, D),
        gfirst=wide(T, D),
        gbr=low(T2, D),
        doall=low(S, HW),
        dkv32=wide(T2, D),
        dall=low(T2, 3 * HW),
        part_down=low(FO, D),
        part_up=low(D, FO),
        part_attn=low(HW, D),
        got_down=low(4, FO // 4, D),
        got_up=low(4, D // 4, FO),
        got_attn=low(4, EIGHTH, D),
        gm=low(4, HW, D),
        dr=low(2, HW, D),
        xs=low(HW, D),
        xr=low(HW, D),
        dxs=low(T, D),
        dxr=low(T, D),
        dxo=wide(T2, D),
        vsend=wide(4, 16, D),
        vrecv=wide(3, 16, D),
        vz=wide(4, 16, D),
        wsem=dma((6,)),
        hes=dma((1,)),
        her=dma((blocks,)),
        frs=dma((8,)),
        fss=dma((2,)),
        abr=dma((2, 8)),
        abs_=dma((2,)),
        msr=dma((24,)),
        mss=dma((9,)),
        dor=dma((2, 4)),
        dos=dma((2,)),
        zsr=dma((3, 4)),
        zss=dma((3,)),
        agr=dma((n, 19)),
        ags=dma((n,)),
        agdr=dma((n,)),
        vzr=dma((4,)),
        vzs=dma((1,)),
    )
    results = pl.pallas_call(
        partial(layer_kernel, T, D, S, entries),
        out_shape=(
            pltpu.VMEM((T, D), F32),
            pltpu.VMEM((T, D), F32),
            pltpu.VMEM((16, D), F32),
            pltpu.VMEM((F, D), BF16),
            pltpu.VMEM((D, F), BF16),
            pltpu.VMEM((4 * D, D), BF16),
        ),
        in_specs=[vmem, vmem, smem] + [hbm] * 6 + [vmem] * 9,
        out_specs=(vmem,) * 6,
        scratch_shapes=list(scratch.values()),
        compiler_params=pltpu.CompilerParams(
            collective_id=0, has_side_effects=True, vmem_limit_bytes=VMEM_GRANT
        ),
        name="layer",
    )(
        frames[0],
        cotangent[0],
        clip_lengths,
        query_weight,
        key_weight,
        value_weight,
        out_weight,
        up_weight,
        down_weight,
        query_bias,
        value_bias,
        out_bias,
        norm1_gain,
        norm1_bias,
        up_bias,
        down_bias,
        norm2_gain,
        norm2_bias,
    )
    return widen(*results)


def widen_kernel(
    last,
    T,
    D,
    encoded,
    frames_grad,
    vectors,
    down,
    up,
    attn,
    encoded_out,
    frames_grad_out,
    query_out,
    query_b,
    key_out,
    value_out,
    value_b,
    out_out,
    out_b,
    gain1,
    bias1,
    up_out,
    up_b,
    down_out,
    down_b,
    gain2,
    bias2,
    sems,
):
    step = pl.program_id(0)
    copies = [
        pltpu.make_async_copy(encoded, encoded_out, sems.at[0]),
        pltpu.make_async_copy(frames_grad, frames_grad_out, sems.at[1]),
    ]

    @pl.when(step == 0)
    def _():
        for copy in copies:
            copy.start()
        for ref, index in (
            (query_b, 0),
            (value_b, 1),
            (out_b, 2),
            (gain1, 3),
            (bias1, 4),
            (down_b, 9),
            (gain2, 10),
            (bias2, 11),
        ):
            ref[...] = vectors[index : index + 1, :].reshape(D)
        for quarter in range(4):
            up_b[pl.ds(D * quarter, D)] = vectors[5 + quarter : 6 + quarter, :].reshape(D)

    def rows(size, first=0):
        return pl.ds(pl.multiple_of(first + size * step, size), size)

    down_out[...] = down[rows(down_out.shape[0]), :].astype(F32)
    up_out[...] = up[rows(up_out.shape[0]), :].astype(F32)
    out_out[...] = attn[rows(LANES, 3 * D), :].astype(F32)
    for m, target in enumerate((query_out, key_out, value_out)):
        target[...] = attn[rows(LANES, m * D), :].astype(F32).T

    @pl.when(step == last)
    def _():
        for copy in copies:
            copy.wait()


def widen(encoded, frames_grad, vectors, sum_down, sum_up, sum_attn):
    T, D = encoded.shape
    F = sum_up.shape[1]
    steps = D // LANES
    hbm, vmem = pl.BlockSpec(memory_space=pl.ANY), pl.BlockSpec(memory_space=pltpu.VMEM)
    parts = (encoded, frames_grad, vectors, sum_down, sum_up, sum_attn)
    parts = [pltpu.with_memory_space_constraint(part, pltpu.VMEM) for part in parts]

    def down(width):
        return pl.BlockSpec((width, D), lambda i: (i, 0))

    up = pl.BlockSpec((D // steps, F), lambda i: (i, 0))
    turned = pl.BlockSpec((D, LANES), lambda i: (0, i))
    flat = pl.BlockSpec((D,), lambda i: (0,))
    wide_flat = pl.BlockSpec((F,), lambda i: (0,))
    square, vector = jax.ShapeDtypeStruct((D, D), F32), jax.ShapeDtypeStruct((D,), F32)
    tokens = jax.ShapeDtypeStruct((T, D), F32)
    outs = (
        (tokens, hbm),
        (tokens, hbm),
        (square, turned),
        (vector, flat),
        (square, turned),
        (square, turned),
        (vector, flat),
        (square, down(LANES)),
        (vector, flat),
        (vector, flat),
        (vector, flat),
        (jax.ShapeDtypeStruct((D, F), F32), up),
        (jax.ShapeDtypeStruct((F,), F32), wide_flat),
        (jax.ShapeDtypeStruct((F, D), F32), down(F // steps)),
        (vector, flat),
        (vector, flat),
        (vector, flat),
    )
    results = pl.pallas_call(
        partial(widen_kernel, steps - 1, T, D),
        grid=(steps,),
        out_shape=tuple(shape for shape, _ in outs),
        in_specs=[vmem] * 6,
        out_specs=tuple(spec for _, spec in outs),
        scratch_shapes=[pltpu.SemaphoreType.DMA((2,))],
        compiler_params=pltpu.CompilerParams(vmem_limit_bytes=VMEM_GRANT),
        name="widen",
    )(*parts)
    return (results[0][None], results[1][None]) + tuple(results[2:])


def solution(mesh):
    in_specs = (
        P("row", "seq", None),
        P("row", None),
        P(),
        P(),
        P(),
        P(),
        P(),
        P(),
        P(),
        P(),
        P(),
        P(),
        P(),
        P(),
        P(),
        P(),
        P(),
        P("row", "seq", None),
    )
    out_specs = (
        P("row", "seq", None),
        P("row", "seq", None),
        P(),
        P(),
        P(),
        P(),
        P(),
        P(),
        P(),
        P(),
        P(),
        P(),
        P(),
        P(),
        P(),
        P(),
        P(),
    )
    shape = dict(mesh.shape)
    fused = shape["row"] == 4 and shape["seq"] == 8
    return jax.shard_map(
        fused_layer if fused else per_device, mesh=mesh, in_specs=in_specs, out_specs=out_specs, check_vma=False
    )
```

```python
import contextlib
from functools import partial
import math

import jax
import jax.numpy as jnp
from jax import lax
from jax.experimental import pallas as pl
from jax.experimental.pallas import tpu as pltpu
from jax.sharding import PartitionSpec as P

H = 12
HD = 64


MASK_SCORE = -1e30
NORM_EPSILON = 1e-05


def from_behind(value, axis, by):
    count = lax.axis_size(axis)
    return lax.ppermute(value, axis, [(i, (i + by) % count) for i in range(count)])


def layer_norm(summed, norm_gain, norm_shift):
    centre = jnp.mean(summed, axis=-1, keepdims=True)
    centered = summed - centre
    inverse = lax.rsqrt(jnp.mean(centered * centered, axis=-1, keepdims=True) + NORM_EPSILON)
    normed = centered * inverse
    return (normed * norm_gain + norm_shift, normed, inverse)


def layer_norm_back(upstream, normed, inverse, norm_gain):
    scaled = upstream * norm_gain
    first_mean = jnp.mean(scaled, axis=-1, keepdims=True)
    second_mean = jnp.mean(scaled * normed, axis=-1, keepdims=True)
    summed_grad = inverse * (scaled - first_mean - normed * second_mean)
    return (summed_grad, jnp.sum(upstream * normed, axis=(0, 1)), jnp.sum(upstream, axis=(0, 1)))


def project(inputs, matrix):
    return jnp.einsum("rsk,kn->rsn", inputs, matrix, preferred_element_type=jnp.float32)


def project_back(upstream, matrix):
    return jnp.einsum("rsn,kn->rsk", upstream, matrix, preferred_element_type=jnp.float32)


def matrix_grad(inputs, upstream):
    return jnp.einsum("rsk,rsn->kn", inputs, upstream, preferred_element_type=jnp.float32)


def column_sum(upstream):
    return jnp.sum(upstream.astype(jnp.float32), axis=(0, 1))


def clip_numbers(clip_ends, position):
    return jnp.sum((clip_ends[:, None, :] <= position[None, :, None]).astype(jnp.int32), axis=-1)


def split_heads(tensor):
    return tensor.reshape(tensor.shape[0], tensor.shape[1], H, HD)


def join_heads(tensor):
    return tensor.reshape(tensor.shape[0], tensor.shape[1], H * HD)


def head_scores(queries, keys_block):
    return jnp.einsum(
        "rqhd,rkhd->rhqk", queries, keys_block, preferred_element_type=jnp.float32
    ) * HD ** (-0.5)


def allowed_pairs(query_numbers, key_numbers):
    return (query_numbers[:, :, None] == key_numbers[:, None, :])[:, None]


def online_update(running, queries, query_numbers, keys_block, values_block, key_numbers):
    run_peak, run_total, run_values = running
    allowed = allowed_pairs(query_numbers, key_numbers)
    masked = jnp.where(allowed, head_scores(queries, keys_block), MASK_SCORE)
    new_peak = jnp.maximum(run_peak, jnp.max(masked, axis=-1))
    weights = jnp.where(allowed, jnp.exp(masked - new_peak[..., None]), 0.0)
    rescale = jnp.exp(run_peak - new_peak)
    new_total = run_total * rescale + jnp.sum(weights, axis=-1)
    contrib = jnp.einsum(
        "rhqk,rkhd->rqhd",
        weights.astype(jnp.bfloat16),
        values_block,
        preferred_element_type=jnp.float32,
    )
    new_values = run_values * jnp.swapaxes(rescale, 1, 2)[..., None] + contrib
    return (new_peak, new_total, new_values)


def block_back(
    queries, grad_heads, log_total, delta_rows, query_numbers, keys_flat, values_flat, key_numbers
):
    keys_block = split_heads(keys_flat)
    values_block = split_heads(values_flat)
    allowed = allowed_pairs(query_numbers, key_numbers)
    shifted = jnp.where(
        allowed, head_scores(queries, keys_block) - log_total[..., None], MASK_SCORE
    )
    weights = jnp.exp(shifted)
    grad_weights = jnp.einsum(
        "rqhd,rkhd->rhqk", grad_heads, values_block, preferred_element_type=jnp.float32
    )
    grad_scores = (weights * (grad_weights - delta_rows[..., None])).astype(jnp.bfloat16)
    factor = HD ** (-0.5)
    query_part = (
        jnp.einsum("rhqk,rkhd->rqhd", grad_scores, keys_block, preferred_element_type=jnp.float32)
        * factor
    )
    key_part = (
        jnp.einsum("rhqk,rqhd->rkhd", grad_scores, queries, preferred_element_type=jnp.float32)
        * factor
    )
    value_part = jnp.einsum(
        "rhqk,rqhd->rkhd",
        weights.astype(jnp.bfloat16),
        grad_heads,
        preferred_element_type=jnp.float32,
    )
    return (join_heads(query_part), join_heads(key_part), join_heads(value_part))


def per_device(
    frames,
    clip_lengths,
    query_weight,
    query_bias,
    key_weight,
    value_weight,
    value_bias,
    out_weight,
    out_bias,
    norm1_gain,
    norm1_bias,
    up_weight,
    up_bias,
    down_weight,
    down_bias,
    norm2_gain,
    norm2_bias,
    cotangent,
):
    row_count = frames.shape[0]
    shard_len = frames.shape[1]
    cycle_size = lax.axis_size("seq")
    seq_place = lax.axis_index("seq")
    clip_ends = jnp.cumsum(clip_lengths, axis=1)
    offsets = jnp.arange(shard_len, dtype=jnp.int32)
    own_numbers = clip_numbers(clip_ends, seq_place * shard_len + offsets)
    frames_low = frames.astype(jnp.bfloat16)
    queries = split_heads((project(frames_low, query_weight) + query_bias).astype(jnp.bfloat16))
    keys_own = project(frames_low, key_weight).astype(jnp.bfloat16)
    values_own = (project(frames_low, value_weight) + value_bias).astype(jnp.bfloat16)
    initial = (
        jnp.full((row_count, H, shard_len), MASK_SCORE, jnp.float32),
        jnp.zeros((row_count, H, shard_len), jnp.float32),
        jnp.zeros((row_count, shard_len, H, HD), jnp.float32),
    )
    key_piece = lax.all_gather(keys_own, "seq", axis=1, tiled=True)
    value_piece = lax.all_gather(values_own, "seq", axis=1, tiled=True)
    piece_len = key_piece.shape[1]
    block_len = math.gcd(piece_len, 512)

    def attend_block(block_index, carried):
        offset = block_index * block_len
        key_block = lax.dynamic_slice_in_dim(key_piece, offset, block_len, 1)
        value_block = lax.dynamic_slice_in_dim(value_piece, offset, block_len, 1)
        position = offset + jnp.arange(block_len, dtype=jnp.int32)
        return online_update(
            carried,
            queries,
            own_numbers,
            split_heads(key_block),
            split_heads(value_block),
            clip_numbers(clip_ends, position),
        )

    run_peak, run_total, run_values = lax.fori_loop(
        0, piece_len // block_len, attend_block, initial
    )
    log_total = run_peak + jnp.log(run_total)
    attended_heads = run_values / jnp.swapaxes(run_total, 1, 2)[..., None]
    attended = join_heads(attended_heads)
    attended_low = attended.astype(jnp.bfloat16)
    branch = project(attended_low, out_weight) + out_bias
    hidden, unit_first, inverse_first = layer_norm(frames + branch, norm1_gain, norm1_bias)
    hidden_low = hidden.astype(jnp.bfloat16)
    before = project(hidden_low, up_weight) + up_bias
    active, gelu_back = jax.vjp(partial(jax.nn.gelu, approximate=False), before)
    active_low = active.astype(jnp.bfloat16)
    encoded, unit_second, inverse_second = layer_norm(
        hidden + project(active_low, down_weight) + down_bias, norm2_gain, norm2_bias
    )
    grad_mid, norm2_gain_grad, norm2_bias_grad = layer_norm_back(
        cotangent, unit_second, inverse_second, norm2_gain
    )
    grad_ffn = grad_mid.astype(jnp.bfloat16)
    down_weight_grad = matrix_grad(active_low, grad_ffn)
    down_bias_grad = column_sum(grad_ffn)
    grad_before = gelu_back(project_back(grad_ffn, down_weight))[0].astype(jnp.bfloat16)
    up_weight_grad = matrix_grad(hidden_low, grad_before)
    up_bias_grad = column_sum(grad_before)
    grad_hidden = grad_mid + project_back(grad_before, up_weight)
    grad_first, norm1_gain_grad, norm1_bias_grad = layer_norm_back(
        grad_hidden, unit_first, inverse_first, norm1_gain
    )
    grad_branch = grad_first.astype(jnp.bfloat16)
    out_weight_grad = matrix_grad(attended_low, grad_branch)
    out_bias_grad = column_sum(grad_branch)
    grad_attended = project_back(grad_branch, out_weight).astype(jnp.bfloat16)
    grad_heads = split_heads(grad_attended)
    delta_rows = jnp.swapaxes(
        jnp.sum(grad_heads.astype(jnp.float32) * attended_heads, axis=-1), 1, 2
    )
    query_start, key_start, value_start = block_back(
        queries, grad_heads, log_total, delta_rows, own_numbers, keys_own, values_own, own_numbers
    )

    def key_step(distance, carried):
        key_now, value_now, query_sum, key_sum, value_sum = carried
        key_now, value_now = from_behind((key_now, value_now), "seq", 1)
        key_sum, value_sum = (
            from_behind(key_sum.astype(jnp.bfloat16), "seq", 1).astype(key_sum.dtype),
            from_behind(value_sum.astype(jnp.bfloat16), "seq", 1).astype(value_sum.dtype),
        )
        source = (seq_place - distance) % cycle_size
        source_numbers = clip_numbers(clip_ends, source * shard_len + offsets)
        query_part, key_part, value_part = block_back(
            queries,
            grad_heads,
            log_total,
            delta_rows,
            own_numbers,
            key_now,
            value_now,
            source_numbers,
        )
        return (
            key_now,
            value_now,
            query_sum + query_part,
            key_sum + key_part,
            value_sum + value_part,
        )

    carried = lax.fori_loop(
        1, cycle_size, key_step, (keys_own, values_own, query_start, key_start, value_start)
    )
    query_total = carried[2]
    key_total, value_total = (
        from_behind(carried[3].astype(jnp.bfloat16), "seq", 1).astype(jnp.float32),
        from_behind(carried[4].astype(jnp.bfloat16), "seq", 1).astype(jnp.float32),
    )
    query_low = query_total.astype(jnp.bfloat16)
    key_low = key_total.astype(jnp.bfloat16)
    value_low = value_total.astype(jnp.bfloat16)
    query_weight_grad = matrix_grad(frames_low, query_low)
    query_bias_grad = column_sum(query_low)
    key_weight_grad = matrix_grad(frames_low, key_low)
    value_weight_grad = matrix_grad(frames_low, value_low)
    value_bias_grad = column_sum(value_low)
    frames_grad = (
        grad_first
        + project_back(query_low, query_weight)
        + project_back(key_low, key_weight)
        + project_back(value_low, value_weight)
    )
    shares = (
        lax.psum_scatter(query_weight_grad, "seq", scatter_dimension=0, tiled=True),
        lax.psum_scatter(query_bias_grad, "seq", scatter_dimension=0, tiled=True),
        lax.psum_scatter(key_weight_grad, "seq", scatter_dimension=0, tiled=True),
        lax.psum_scatter(value_weight_grad, "seq", scatter_dimension=0, tiled=True),
        lax.psum_scatter(value_bias_grad, "seq", scatter_dimension=0, tiled=True),
        lax.psum_scatter(out_weight_grad, "seq", scatter_dimension=0, tiled=True),
        lax.psum_scatter(out_bias_grad, "seq", scatter_dimension=0, tiled=True),
        lax.psum_scatter(norm1_gain_grad, "seq", scatter_dimension=0, tiled=True),
        lax.psum_scatter(norm1_bias_grad, "seq", scatter_dimension=0, tiled=True),
        lax.psum_scatter(up_weight_grad, "seq", scatter_dimension=0, tiled=True),
        lax.psum_scatter(up_bias_grad, "seq", scatter_dimension=0, tiled=True),
        lax.psum_scatter(down_weight_grad, "seq", scatter_dimension=0, tiled=True),
        lax.psum_scatter(down_bias_grad, "seq", scatter_dimension=0, tiled=True),
        lax.psum_scatter(norm2_gain_grad, "seq", scatter_dimension=0, tiled=True),
        lax.psum_scatter(norm2_bias_grad, "seq", scatter_dimension=0, tiled=True),
    )
    shares = (
        lax.psum(shares[0].astype(jnp.bfloat16), "row").astype(jnp.float32),
        lax.psum(shares[1].astype(jnp.bfloat16), "row").astype(jnp.float32),
        lax.psum(shares[2].astype(jnp.bfloat16), "row").astype(jnp.float32),
        lax.psum(shares[3].astype(jnp.bfloat16), "row").astype(jnp.float32),
        lax.psum(shares[4].astype(jnp.bfloat16), "row").astype(jnp.float32),
        lax.psum(shares[5].astype(jnp.bfloat16), "row").astype(jnp.float32),
        lax.psum(shares[6].astype(jnp.bfloat16), "row").astype(jnp.float32),
        lax.psum(shares[7].astype(jnp.bfloat16), "row").astype(jnp.float32),
        lax.psum(shares[8].astype(jnp.bfloat16), "row").astype(jnp.float32),
        lax.psum(shares[9].astype(jnp.bfloat16), "row").astype(jnp.float32),
        lax.psum(shares[10].astype(jnp.bfloat16), "row").astype(jnp.float32),
        lax.psum(shares[11].astype(jnp.bfloat16), "row").astype(jnp.float32),
        lax.psum(shares[12].astype(jnp.bfloat16), "row").astype(jnp.float32),
        lax.psum(shares[13].astype(jnp.bfloat16), "row").astype(jnp.float32),
        lax.psum(shares[14].astype(jnp.bfloat16), "row").astype(jnp.float32),
    )
    totals = (
        lax.all_gather(shares[0].astype(jnp.bfloat16), "seq", axis=0, tiled=True).astype(
            jnp.float32
        ),
        lax.all_gather(shares[1].astype(jnp.bfloat16), "seq", axis=0, tiled=True).astype(
            jnp.float32
        ),
        lax.all_gather(shares[2].astype(jnp.bfloat16), "seq", axis=0, tiled=True).astype(
            jnp.float32
        ),
        lax.all_gather(shares[3].astype(jnp.bfloat16), "seq", axis=0, tiled=True).astype(
            jnp.float32
        ),
        lax.all_gather(shares[4].astype(jnp.bfloat16), "seq", axis=0, tiled=True).astype(
            jnp.float32
        ),
        lax.all_gather(shares[5].astype(jnp.bfloat16), "seq", axis=0, tiled=True).astype(
            jnp.float32
        ),
        lax.all_gather(shares[6].astype(jnp.bfloat16), "seq", axis=0, tiled=True).astype(
            jnp.float32
        ),
        lax.all_gather(shares[7].astype(jnp.bfloat16), "seq", axis=0, tiled=True).astype(
            jnp.float32
        ),
        lax.all_gather(shares[8].astype(jnp.bfloat16), "seq", axis=0, tiled=True).astype(
            jnp.float32
        ),
        lax.all_gather(shares[9].astype(jnp.bfloat16), "seq", axis=0, tiled=True).astype(
            jnp.float32
        ),
        lax.all_gather(shares[10].astype(jnp.bfloat16), "seq", axis=0, tiled=True).astype(
            jnp.float32
        ),
        lax.all_gather(shares[11].astype(jnp.bfloat16), "seq", axis=0, tiled=True).astype(
            jnp.float32
        ),
        lax.all_gather(shares[12].astype(jnp.bfloat16), "seq", axis=0, tiled=True).astype(
            jnp.float32
        ),
        lax.all_gather(shares[13].astype(jnp.bfloat16), "seq", axis=0, tiled=True).astype(
            jnp.float32
        ),
        lax.all_gather(shares[14].astype(jnp.bfloat16), "seq", axis=0, tiled=True).astype(
            jnp.float32
        ),
    )
    return (
        encoded,
        frames_grad,
        totals[0],
        totals[1],
        totals[2],
        totals[3],
        totals[4],
        totals[5],
        totals[6],
        totals[7],
        totals[8],
        totals[9],
        totals[10],
        totals[11],
        totals[12],
        totals[13],
        totals[14],
    )


MESH = pl.DeviceIdType.MESH
LANES = 128
F32, BF16 = jnp.float32, jnp.bfloat16
VMEM_GRANT = 49 << 20
DOWN, UP, QUERY_OUT, KEY_VALUE = range(4)

PIECES = (
    (DOWN, "zyx", 0, 2),
    (DOWN, "zxy", 2, 3),
    (DOWN, "xyz", 5, 1),
    (UP, "zyx", 0, 3),
    (UP, "zxy", 3, 2),
    (UP, "xyz", 5, 1),
    (QUERY_OUT, "zxy", 0, 1),
    (QUERY_OUT, "yxz", 1, 2),
    (KEY_VALUE, "zyx", 0, 2),
    (KEY_VALUE, "zxy", 2, 1),
)


def dot(a, b):
    return jnp.dot(a, b, preferred_element_type=F32)


def dot_nt(a, b):
    return lax.dot_general(a, b, (((1,), (1,)), ((), ())), preferred_element_type=F32)


def dot_tn(a, b):
    return lax.dot_general(a, b, (((0,), (0,)), ((), ())), preferred_element_type=F32)


def rows_norm(value):
    centre = jnp.mean(value, axis=-1, keepdims=True)
    centered = value - centre
    inverse = lax.rsqrt(jnp.mean(centered * centered, axis=-1, keepdims=True) + NORM_EPSILON)
    return centered * inverse, inverse


def rows_norm_back(scaled, unit, inverse):
    first = jnp.mean(scaled, axis=-1, keepdims=True)
    second = jnp.mean(scaled * unit, axis=-1, keepdims=True)
    return inverse * (scaled - first - unit * second)


def layer_kernel(
    T,
    D,
    S,
    entries,
    frames,
    cotangent,
    lengths,
    query_w,
    key_w,
    value_w,
    out_w,
    up_w,
    down_w,
    query_b,
    value_b,
    out_b,
    gain1,
    bias1,
    up_b,
    down_b,
    gain2,
    bias2,
    encoded,
    frames_grad,
    vectors,
    sum_down,
    sum_up,
    sum_attn,
    bias_rows,
    up_rows,
    fall,
    wqkv,
    wo,
    wup,
    wdn,
    qall,
    kv,
    mask,
    probs,
    stat,
    lsed,
    att32,
    att16,
    attf,
    hq,
    fq,
    ar,
    br,
    actives,
    slopes,
    dgelu,
    hid32,
    unit1,
    rstd1,
    gmid,
    gfirst,
    gbr,
    doall,
    dkv32,
    dall,
    give_down,
    give_up,
    take_down,
    take_up,
    keep_down,
    keep_up,
    part_down,
    part_up,
    part_qo,
    part_kv,
    got_down,
    got_up,
    got_qo,
    got_kv,
    gm,
    dr,
    xs,
    xr,
    dxs,
    dxr,
    dxo,
    vsend,
    vrecv,
    vz,
    wsem,
    hes,
    her,
    frs,
    fss,
    msr,
    mss,
    dor,
    dos,
    zsr,
    zss,
    agr,
    ags,
    agdr,
    vzr,
    vzs,
):
    HW, T2, FO = D // 2, 2 * T, wup.shape[1] // 8
    blocks = HW // LANES
    EIGHTH, SIXTEENTH = D // 8, D // 16
    out_b, gain1, bias1, down_b, gain2, bias2 = (
        ref[...].reshape(1, D) for ref in (out_b, gain1, bias1, down_b, gain2, bias2)
    )
    row, seq = lax.axis_index("row"), lax.axis_index("seq")
    x, c = lax.div(row, 2), lax.rem(row, 2)
    z, y = lax.div(seq, 2), lax.rem(seq, 2)
    not_first, not_last = z > 0, z < 3

    def device(x_, c_, y_, z_=z):
        return (2 * x_ + c_, 2 * z_ + y_)

    def octant(x_, c_, y_):
        return 4 * y_ + 2 * x_ + c_

    sib, xn, yn = device(x, 1 - c, y), device(1 - x, c, y), device(x, c, 1 - y)
    zp, zm = device(x, c, y, jnp.minimum(z + 1, 3)), device(x, c, y, jnp.maximum(z - 1, 0))

    def many(value, of):
        return pl.multiple_of(value, of)

    def at(start, size, of=None):
        return pl.ds(many(start, size if of is None else of), size)

    waits = {}
    scope = contextlib.ExitStack()

    def phase(name):
        scope.close()
        if name:
            scope.enter_context(jax.named_scope(name))

    def send(src, dst, ssem, rsem, to):
        return pltpu.make_async_remote_copy(
            src_ref=src, dst_ref=dst, send_sem=ssem, recv_sem=rsem, device_id=to, device_id_type=MESH
        )

    def start(src, dst, ssem, rsem, to):
        send(src, dst, ssem, rsem, to).start()

    def arrived(ref, rsem):
        send(ref, ref, mss.at[0], rsem, sib).wait_recv()

    def sent(key, ref, ssem):
        waits.setdefault(key, lambda: send(ref, ref, ssem, msr.at[0], sib).wait_send())

    def sent_along_z(key, ref_of, ssem, rest=0, lines=1):
        for blocks_sent, when in ((1, (z == 0) | (z == 3)), (5, (z > 0) & (z < 3))):
            ref = ref_of(rest + lines * blocks_sent)
            wait = partial(lambda ref: send(ref, ref, ssem, msr.at[0], sib).wait_send(), ref)
            waits[key, blocks_sent] = partial(lambda when, wait: pl.when(when)(wait), when, wait)

    send_names, names = {}, {}

    def group(name):
        return mss.at[send_names.setdefault(name, len(send_names))]

    def one(name, family=None):
        return group(family or name), got_of(name)

    def got_of(name):
        return msr.at[names.setdefault(name, len(names))]

    phase("enter")
    heads_here = at(HW * y, HW)
    loads = [
        pltpu.make_async_copy(query_w.at[:, heads_here], wqkv.at[:, pl.ds(0, HW)], wsem.at[0]),
        pltpu.make_async_copy(key_w.at[:, heads_here], wqkv.at[:, pl.ds(HW, HW)], wsem.at[1]),
        pltpu.make_async_copy(value_w.at[:, heads_here], wqkv.at[:, pl.ds(2 * HW, HW)], wsem.at[2]),
        pltpu.make_async_copy(out_w, wo, wsem.at[3]),
        pltpu.make_async_copy(up_w, wup, wsem.at[4]),
        pltpu.make_async_copy(down_w, wdn, wsem.at[5]),
    ]
    barrier = pltpu.get_barrier_semaphore()
    peers = [sib, xn, yn, device(1 - x, c, 1 - y)]
    peers += [device(x, c, y, lax.rem(z + k, 4)) for k in (1, 2, 3)]
    for peer in peers:
        pl.semaphore_signal(barrier, inc=1, device_id=peer, device_id_type=MESH)
    for load in loads:
        load.start()
    fall[at(T * seq, T), :] = frames[...].astype(BF16)
    vectors[...] = jnp.zeros_like(vectors)
    bias_rows[0:1, :] = query_b[...].reshape(1, D)
    bias_rows[1:2, :] = value_b[...].reshape(1, D)
    for quarter in range(4):
        up_rows[quarter] = jnp.broadcast_to(up_b[pl.ds(D * quarter, D)].reshape(1, D), (8, D))
    pl.semaphore_wait(barrier, len(peers))

    phase("frames_gather")

    def slab(z_, y_):
        return fall.at[at(T * (2 * z_ + y_), T), :]

    def push(z_, direction):
        to = (zp, zm, yn)[direction]
        return send(slab(z_, y), slab(z_, y), fss.at[direction // 2], frs.at[2 * z_ + y], to)

    pl.when(not_last)(lambda: push(z, 0).start())
    pl.when(not_first)(lambda: push(z, 1).start())
    push(z, 2).start()
    query_bias, value_bias = bias_rows[0:1, heads_here], bias_rows[1:2, heads_here]
    for load in loads[:3]:
        load.wait()

    def project_slab(z_, y_):
        rows = at(T * (2 * z_ + y_), T)
        flat = dot(fall[rows, :], wqkv[...])
        query = (flat[:, :HW] + query_bias).astype(BF16).astype(F32) * HD ** (-0.5)
        qall[rows, :] = query.astype(BF16)
        kv[rows, pl.ds(0, HW)] = flat[:, HW : 2 * HW].astype(BF16)
        kv[rows, pl.ds(HW, HW)] = (flat[:, 2 * HW :] + value_bias).astype(BF16)

    project_slab(z, y)
    key_at = lax.broadcasted_iota(jnp.int32, (1, S), 1)
    query_at = lax.broadcasted_iota(jnp.int32, (T2, 1), 0) + T2 * z
    key_number, query_number = jnp.zeros((1, S), jnp.int32), jnp.zeros((T2, 1), jnp.int32)
    clip_end = jnp.int32(0)
    for entry in range(entries):
        clip_end = clip_end + lengths[0, entry]
        key_number = key_number + jnp.where(clip_end <= key_at, 1, 0)
        query_number = query_number + jnp.where(clip_end <= query_at, 1, 0)
    mask[...] = jnp.where(query_number == key_number, 0.0, MASK_SCORE)

    @pl.loop(0, 4)
    def _(k):
        left, right = z - k - 1, z + k + 1

        @pl.when(left >= 0)
        def _():
            arrived(slab(left, y), frs.at[2 * left + y])
            pl.when(not_last)(lambda: push(left, 0).start())
            push(left, 2).start()

        @pl.when(right <= 3)
        def _():
            arrived(slab(right, y), frs.at[2 * right + y])
            pl.when(not_first)(lambda: push(right, 1).start())
            push(right, 2).start()

        pl.when(left >= 0)(lambda: project_slab(left, y))
        pl.when(right <= 3)(lambda: project_slab(right, y))

        @pl.when(z - k >= 0)
        def _():
            arrived(slab(z - k, 1 - y), frs.at[2 * (z - k) + 1 - y])
            project_slab(z - k, 1 - y)

        @pl.when((k > 0) & (z + k <= 3))
        def _():
            arrived(slab(z + k, 1 - y), frs.at[2 * (z + k) + 1 - y])
            project_slab(z + k, 1 - y)

    sent("frames_y", fall.at[pl.ds(0, 4 * T), :], fss.at[1])
    sent_along_z("frames_z", lambda count: fall.at[pl.ds(0, T * count), :], fss.at[0])

    phase("attention")
    pair_rows = at(T2 * z, T2)
    lane = lax.broadcasted_iota(jnp.int32, (T2, LANES), 1)
    low_half = lane < HD

    def half(value, which):
        return jnp.where(low_half == (which == 0), value, 0.0)

    stat[...] = jnp.zeros_like(stat)
    mine, other = at(T * y, T), at(T * (1 - y), T)

    def heads_push(b):
        part, there = at(LANES * b, LANES), at(HW * y + LANES * b, LANES, LANES)
        return send(att16.at[other, part], attf.at[:, there], hes.at[0], her.at[b], yn)

    @pl.loop(0, blocks)
    def _(b):
        lanes, value_lanes = at(LANES * b, LANES), at(HW + LANES * b, LANES, LANES)
        queries = qall[pair_rows, lanes].astype(F32)
        outs = []
        for which in range(2):
            scores = dot_nt(half(queries, which).astype(BF16), kv[:, lanes]) + mask[...]
            peak = jnp.max(scores, axis=-1, keepdims=True)
            powers = jnp.exp(scores - peak)
            total = jnp.sum(powers, axis=-1, keepdims=True)
            low = (powers * (1.0 / total)).astype(BF16)
            probs[2 * b + which] = low
            outs.append(dot(low, kv[:, value_lanes]))
            stat[0] = jnp.where(lane == 2 * b + which, peak + jnp.log(total), stat[0])
        out = jnp.where(low_half, outs[0], outs[1])
        att32[:, lanes] = out
        att16[:, lanes] = out.astype(BF16)
        heads_push(b).start()

    phase("heads_exchange")
    attf[:, heads_here] = att16[mine, :]
    lsed[z, 0:8, :] = stat[0].T[0:8, :]
    loads[3].wait()
    for b in range(blocks):
        arrived(attf.at[:, at(HW * (1 - y) + LANES * b, LANES, LANES)], her.at[b])
    sent("heads", att16.at[pl.ds(0, T), :], hes.at[0])
    phase("out_norm1")
    branch = dot(attf[...], wo[...]) + out_b
    unit, inverse = rows_norm(frames[...] + branch)
    hidden = unit * gain1 + bias1
    unit1[...] = unit
    rstd1[...] = jnp.broadcast_to(inverse, (T, LANES))
    hid32[...] = hidden
    here = at(T * (2 * y + x), T)

    def rows_of(buffer, x_, y_):
        return buffer.at[at(T * (2 * y_ + x_), T), :]

    def halves_of(buffer, x_, y_):
        first = T * (2 * y_ + x_)
        return buffer.at[at(first, T // 2), :], buffer.at[at(first + T // 2, T // 2), :]

    def share_x(buffer, name):
        own = rows_of(buffer, x, y)
        start(own, own, *one(name + "_x", name), xn)

    def share_y(buffer, name):
        own = rows_of(buffer, x, y)
        start(own, own, *one(name + "_y", name), yn)

    def from_x(buffer, name):
        arrived(rows_of(buffer, 1 - x, y), got_of(name + "_x"))
        top = halves_of(buffer, 1 - x, y)[0]
        start(top, top, *one(name + "_top", name), yn)

    def from_y(buffer, name):
        arrived(rows_of(buffer, x, 1 - y), got_of(name + "_y"))
        bottom = halves_of(buffer, x, 1 - y)[1]
        start(bottom, bottom, *one(name + "_bottom", name), xn)

    def from_diagonal(buffer, name):
        top, bottom = halves_of(buffer, 1 - x, 1 - y)
        arrived(top, got_of(name + "_top"))
        arrived(bottom, got_of(name + "_bottom"))

    chips = ((1 - x, y), (x, 1 - y), (1 - x, 1 - y), (x, y))

    for buffer, name in ((hq, "hid"), (fq, "ffn")):
        sent(name, buffer.at[pl.ds(0, 3 * T), :], group(name))
    hq[here, :] = hidden.astype(BF16)
    share_x(hq, "hid")
    share_y(hq, "hid")

    phase("up_gelu")
    loads[4].wait()
    scale = 2.0 ** -0.5

    def active(hidden_rows, chip):
        before = dot(hidden_rows, wup[:, at(D * chip, D)]) + up_rows[chip][0:1, :]
        rise = 0.5 * (1.0 + lax.erf(before * scale))
        slope = rise + before * jnp.exp(-0.5 * before * before) * (2.0 * math.pi) ** -0.5
        return (before * rise).astype(BF16), slope

    def grad_before(ffn_rows, chip, slope):
        return (dot_nt(ffn_rows, wdn[at(D * chip, D), :]) * slope).astype(BF16)

    for x_, y_ in chips:
        chip = 2 * y_ + x_
        actives[chip], dgelu[chip] = active(hq[here, :], chip)
    ar[here, :] = actives[2 * y + x]
    phase("down_norm2")
    loads[5].wait()
    fed = hid32[...] + down_b
    for quarter in range(4):
        fed = fed + dot(actives[quarter], wdn[pl.ds(D * quarter, D), :])
    unit2, inverse2 = rows_norm(fed)
    encoded[...] = unit2 * gain2 + bias2
    cot = cotangent[...]
    grad_mid = rows_norm_back(cot * gain2, unit2, inverse2)
    vectors[10:11, :] = jnp.sum(cot * unit2, axis=0, keepdims=True)
    vectors[11:12, :] = jnp.sum(cot, axis=0, keepdims=True)
    gmid[...] = grad_mid
    fq[here, :] = grad_mid.astype(BF16)
    share_x(fq, "ffn")
    share_y(fq, "ffn")
    vectors[9:10, :] = jnp.sum(fq[here, :].astype(F32), axis=0, keepdims=True)
    phase("ffn_back")
    for x_, y_ in chips:
        chip = 2 * y_ + x_
        low = grad_before(fq[here, :], chip, dgelu[chip])
        vectors[pl.ds(5 + chip, 1), :] = jnp.sum(low.astype(F32), axis=0, keepdims=True)
        gmid[...] += dot_nt(low, wup[:, at(D * chip, D)])
    br[here, :] = low

    def plane_active(x_, y_):
        rows = at(T * (2 * y_ + x_), T)
        ar[rows, :], slopes[rows, :] = active(hq[rows, :], 2 * y + x)

    def plane_back(x_, y_):
        rows = at(T * (2 * y_ + x_), T)
        br[rows, :] = grad_before(fq[rows, :], 2 * y + x, slopes[rows, :])

    phase("norm1_back")
    grad_hidden = gmid[...]
    unit = unit1[...]
    grad_first = rows_norm_back(grad_hidden * gain1, unit, rstd1[:, 0:1])
    vectors[3:4, :] = jnp.sum(grad_hidden * unit, axis=0, keepdims=True)
    vectors[4:5, :] = jnp.sum(grad_hidden, axis=0, keepdims=True)
    gfirst[...] = grad_first
    gbr[mine, :] = grad_first.astype(BF16)
    start(gbr.at[mine, :], gbr.at[mine, :], *one("gbr"), yn)
    sent("gbr", gbr.at[mine, :], group("gbr"))
    vectors[2:3, :] = jnp.sum(gbr[mine, :].astype(F32), axis=0, keepdims=True)

    parts, gots = (part_down, part_up, part_qo, part_kv), (got_down, got_up, got_qo, got_kv)
    given, taken, kept = (give_down, give_up), (take_down, take_up), (keep_down, keep_up)
    HALF = HW // 2
    slab_rows = (FO // 4, D // 4, HALF // 4, HALF // 4)

    def part_slab(t, j):
        return parts[t].at[at(slab_rows[t] * j, slab_rows[t]), :]

    outer = (z == 0) | (z == 3)
    near = jnp.where(z < 2, 1 - z, 5 - z)
    inner_there, outer_there = jnp.where(z < 2, 2, 1), jnp.where(z < 2, 3, 0)

    def part_send(t, src, j, to, slot):
        start(src, gots[t].at[slot], zss.at[t], zsr.at[t, slot], device(x, c, y, to))

    def sum_send(t):

        @pl.when(outer)
        def _():
            for j in (outer_there, inner_there, near):
                part_send(t, part_slab(t, j), j, near, j)

        @pl.when(jnp.logical_not(outer))
        def _():
            part_send(t, part_slab(t, near), near, near, z)

    def sum_pass(t):
        @pl.when(jnp.logical_not(outer))
        def _():
            for j, slot in ((outer_there, z), (inner_there, outer_there)):
                got = gots[t].at[j]
                arrived(got, zsr.at[t, j])
                got[...] = (got[...].astype(F32) + part_slab(t, j)[...].astype(F32)).astype(BF16)
                part_send(t, got, j, j, slot)

    def attn_row(t, x_, y_, z_):
        matrix = 3 * x_ if t == QUERY_OUT else 1 + x_
        return D * matrix + HW * y_ + HALF * c + HALF // 4 * z_

    def own_tile(t):
        if t == DOWN:
            return sum_down.at[at(FO * octant(x, c, y) + EIGHTH // 2 * 2 * z, EIGHTH, EIGHTH), :]
        if t == UP:
            return sum_up.at[at(D // 4 * z, D // 4), at(FO * octant(x, c, y), FO)]
        return sum_attn.at[at(attn_row(t, x, y, z), HALF // 4), :]

    def sum_end(t):
        total = part_slab(t, z)[...].astype(F32)
        for slot in (jnp.where(outer, near, z), jnp.where(outer, inner_there, near)):
            arrived(gots[t].at[slot], zsr.at[t, slot])
            total = total + gots[t][slot].astype(F32)
        own_tile(t)[...] = total.astype(BF16)

    unit = SIXTEENTH // 3
    unit_rows = (unit, 2 * unit, unit, unit)

    def tile(u, x_, y_, z_):
        t, _, first, count = PIECES[u]
        rows = unit_rows[t]
        if t == DOWN:
            start_row = FO * octant(x_, c, y_) + EIGHTH * z_ + rows * first
            return sum_down.at[at(start_row, rows * count, rows), :]
        if t == UP:
            start_row = D // 4 * z_ + rows * first
            return sum_up.at[at(start_row, rows * count, rows), at(FO * octant(x_, c, y_), FO)]
        start_row = attn_row(t, x_, y_, z_) + rows * first
        return sum_attn.at[at(start_row, rows * count, rows), :]

    def gather_send(u, place, z_, ssem, rsem, to):
        part = tile(u, *place, z_)
        return send(part, part, ssem, rsem, to)

    def to_sibling(u, place, z_):
        gather_send(u, place, z_, ags.at[u], agdr.at[u], sib).start()

    places = ((x, y), (1 - x, y), (x, 1 - y), (1 - x, 1 - y))

    def order_of(u):
        over_y, over_x = (2, yn), (1, xn)
        return (over_y, over_x) if PIECES[u][1] in ("zyx", "yxz") else (over_x, over_y)

    def z_last(u):
        return PIECES[u][1][2] == "z"

    def along_z(u, p, z_, direction):
        to = (zp, zm)[direction]
        return gather_send(u, places[p], z_, ags.at[u], agr.at[u, 4 * p + z_], to)

    def z_out(u, p):
        pl.when(not_last)(lambda: along_z(u, p, z, 0).start())
        pl.when(not_first)(lambda: along_z(u, p, z, 1).start())

    def second_sem(u, z_):
        return agr.at[u, 16] if z_last(u) else agr.at[u, 4 + z_]

    def third_sem(u, slot):
        return agr.at[u, (17 if z_last(u) else 8) + slot]

    def to_second(u, place, z_):
        gather_send(u, place, z_, ags.at[u], second_sem(u, z_), order_of(u)[0][1]).start()

    def to_third(u, place, slot):
        z_ = z if z_last(u) else lax.rem(slot, 4)
        gather_send(u, place, z_, ags.at[u], third_sem(u, slot), order_of(u)[1][1]).start()

    def gather_own(t):
        for u in pieces_of(t, False):
            z_out(u, 0)
        for u in pieces_of(t):
            to_second(u, places[0], z)
            to_third(u, places[0], 0 if z_last(u) else z)
            to_sibling(u, places[0], z)

    def pieces_of(t, last=None):
        return [u for u in range(len(PIECES)) if PIECES[u][0] == t and last in (None, z_last(u))]

    def sides(k, take):
        pl.when(z - k >= 0)(lambda: take(z - k, not_last, 0))
        if k > 0:
            pl.when(z + k <= 3)(lambda: take(z + k, not_first, 1))

    def gather_z(t, k):
        for u in pieces_of(t, False):

            def take(z_, more, direction):
                arrived(tile(u, *places[0], z_), agr.at[u, z_])
                pl.when(more)(lambda: along_z(u, 0, z_, direction).start())
                to_second(u, places[0], z_)
                to_third(u, places[0], z_)
                to_sibling(u, places[0], z_)

            sides(k, take)

    def gather_second(t, k):
        for u in pieces_of(t, False):

            def take(z_, more, direction):
                place = places[order_of(u)[0][0]]
                arrived(tile(u, *place, z_), second_sem(u, z_))
                to_third(u, place, 4 + z_)
                to_sibling(u, place, z_)

            sides(k, take)

    def gather_third(t, k):
        for u in pieces_of(t, False):

            def take(z_, more, direction):
                for offset, p in ((0, order_of(u)[1][0]), (4, 3)):
                    arrived(tile(u, *places[p], z_), third_sem(u, offset + z_))
                    to_sibling(u, places[p], z_)

            sides(k, take)

    def plane_first(t):
        for u in pieces_of(t, True):
            p = order_of(u)[0][0]
            arrived(tile(u, *places[p], z), second_sem(u, z))
            to_third(u, places[p], 1)
            to_sibling(u, places[p], z)

    def plane_second(t):
        for u in pieces_of(t, True):
            for slot, p in ((0, order_of(u)[1][0]), (1, 3)):
                arrived(tile(u, *places[p], z), third_sem(u, slot))
                to_sibling(u, places[p], z)

    def plane_out(t):
        for u in pieces_of(t, True):
            for p in (0, order_of(u)[0][0], order_of(u)[1][0], 3):
                z_out(u, p)

    def plane_z(t, k):
        for u in pieces_of(t, True):
            for p in (0, order_of(u)[0][0], order_of(u)[1][0], 3):

                def take(z_, more, direction):
                    arrived(tile(u, *places[p], z_), agr.at[u, 4 * p + z_])
                    pl.when(more)(lambda: along_z(u, p, z_, direction).start())
                    to_sibling(u, places[p], z_)

                sides(k, take)

    def gather_end():
        for u, (_, _, _, count) in enumerate(PIECES):

            def as_many(blocks_sent):
                return sum_down.at[pl.ds(0, unit_rows[DOWN] * count * blocks_sent), :]

            arrived(as_many(16), agdr.at[u])
            if z_last(u):
                sent_along_z(("gather", u), as_many, ags.at[u], 19, 4)
            else:
                sent_along_z(("gather", u), as_many, ags.at[u], 28)

    def matrix_put(family, x_, value):
        for half_ in range(2):
            gm[family, half_, x_] = value[HALF * half_ : HALF * (half_ + 1), :].astype(BF16)

    def matrices_send(family):
        start(gm.at[family, 1 - c], dr.at[family], *one(("d", family)), sib)

    def out_back():
        arrived(gbr.at[other, :], got_of("gbr"))
        da = dot_nt(gbr[...], wo[heads_here, :]).astype(BF16)
        doall[pair_rows, :] = da
        product = da.astype(F32) * att32[...]
        stat[1] = jnp.zeros((T2, LANES), F32)
        for head in range(2 * blocks):
            lanes = slice(LANES * (head // 2), LANES * (head // 2 + 1))
            delta = jnp.sum(half(product[:, lanes], head % 2), axis=-1, keepdims=True)
            stat[1] = jnp.where(lane == head, delta, stat[1])
        lsed[z, 8:16, :] = stat[1].T[0:8, :]
        pl.when(not_last)(lambda: grads_push(z, zp))
        pl.when(not_first)(lambda: grads_push(z, zm))
        matrix_put(0, 1, dot_tn(att16[...], gbr[...]))

    def grads_rows(z_):
        return doall.at[at(T2 * z_, T2), :], lsed.at[z_]

    def grads_push(z_, to):
        for index, ref in enumerate(grads_rows(z_)):
            start(ref, ref, dos.at[index], dor.at[index, z_], to)

    sent_along_z("grads", lambda count: fall.at[pl.ds(0, T * count), :], dos.at[0])
    sent_along_z("logs", lambda count: lsed.at[pl.ds(0, count)], dos.at[1])

    def grads_arrive(k):
        def take(z_, more, direction):
            for index, ref in enumerate(grads_rows(z_)):
                arrived(ref, dor.at[index, z_])
            pl.when(more)(lambda: grads_push(z_, (zp, zm)[direction]))

        sides(k, take)

    def queries_back():
        @pl.loop(0, blocks)
        def _(b):
            lanes, value_lanes = at(LANES * b, LANES), at(HW + LANES * b, LANES, LANES)
            heads = doall[pair_rows, lanes].astype(F32)
            product = heads * att32[:, lanes]
            pieces = []
            for which in range(2):
                delta = jnp.sum(half(product, which), axis=-1, keepdims=True)
                grad_probs = dot_nt(half(heads, which).astype(BF16), kv[:, value_lanes])
                grad_scores = probs[2 * b + which].astype(F32) * (grad_probs - delta)
                pieces.append(dot(grad_scores.astype(BF16), kv[:, lanes]))
            total = jnp.where(low_half, pieces[0], pieces[1]) * HD ** (-0.5)
            dall[:, lanes] = total.astype(BF16)

    def keys_back(z_):
        rows = at(T2 * z_, T2)

        @pl.loop(0, blocks)
        def _(b):
            lanes, value_lanes = at(LANES * b, LANES), at(HW + LANES * b, LANES, LANES)
            keys, values = kv[pair_rows, lanes].astype(F32), kv[pair_rows, value_lanes].astype(F32)
            queries, grads = qall[rows, lanes], doall[rows, lanes]
            key_pieces, value_pieces = [], []
            for which in range(2):
                head = 2 * b + which
                scores = dot_nt(half(keys, which).astype(BF16), queries) + mask[:, rows]
                powers = jnp.exp(scores - lsed[z_, pl.ds(head, 1), :])
                grad_probs = dot_nt(half(values, which).astype(BF16), grads)
                grad_scores = powers * (grad_probs - lsed[z_, pl.ds(8 + head, 1), :])
                key_pieces.append(dot(grad_scores.astype(BF16), queries))
                value_pieces.append(dot(powers.astype(BF16), grads))
            dkv32[:, lanes] += jnp.where(low_half, key_pieces[0], key_pieces[1])
            dkv32[:, value_lanes] += jnp.where(low_half, value_pieces[0], value_pieces[1])

    def keys_back_at(k):
        pl.when(z - k >= 0)(lambda: keys_back(z - k))
        if k > 0:
            pl.when(z + k <= 3)(lambda: keys_back(z + k))

    def query_weights():
        matrix_put(0, 0, dot_tn(dall[:, pl.ds(0, HW)], fall[pair_rows, :]))
        matrices_send(0)

    def key_value_weights():
        dall[:, pl.ds(HW, D)] = dkv32[...].astype(BF16)
        grads = dot_tn(dall[:, pl.ds(HW, D)], fall[pair_rows, :])
        matrix_put(1, 0, grads[:HW, :])
        matrix_put(1, 1, grads[HW:, :])
        matrices_send(1)

    def input_grad():
        into = dot_nt(dall[...], wqkv[...])
        dxo[...] = into
        dxs[...] = dxo[other, :].astype(BF16)
        start(dxs, dxr, *one("dx"), yn)
        sums = jnp.sum(dall[...].astype(F32), axis=0, keepdims=True)
        vectors[0:1, heads_here] = sums[:, :HW]
        vectors[1:2, heads_here] = sums[:, 2 * HW :]

    def input_grad_end():
        arrived(dxr, got_of("dx"))
        frames_grad[...] = gfirst[...] + dxo[mine, :] + dxr[...].astype(F32)

    def attention_x(family):
        arrived(dr.at[family], got_of(("d", family)))
        xs[family] = (gm[family, c, 1 - x].astype(F32) + dr[family, 1 - x].astype(F32)).astype(BF16)
        start(xs.at[family], xr.at[family], *one(("xs", family)), xn)

    def attention_z(family):
        arrived(xr.at[family], got_of(("xs", family)))
        total = gm[family, c, x].astype(F32) + dr[family, x].astype(F32) + xr[family].astype(F32)
        parts[2 + family][...] = total.astype(BF16)
        sum_send(2 + family)

    def pair_half(t, half_):
        columns = at(FO * half_, FO)
        if t == DOWN:
            return dot_tn(ar[:, columns], fq[...])
        return dot_tn(hq[...], br[:, columns])

    def pair_send(t):
        given[t][...] = pair_half(t, 1 - c).astype(BF16)
        start(given[t], taken[t], *one(("pair", t)), sib)
        kept[t][...] = pair_half(t, c)

    def pair_add(t):
        arrived(taken[t], got_of(("pair", t)))
        parts[t][...] = (kept[t][...] + taken[t][...].astype(F32)).astype(BF16)
        sum_send(t)

    def vector_step(i, to):
        vsend[i] = vectors[...]
        start(vsend.at[i], vrecv.at[i], *one(("v", i)), to)

    def vector_add(i):
        arrived(vrecv.at[i], got_of(("v", i)))
        vectors[...] += vrecv[i]

    def vector_z():
        vsend[3] = vectors[...]
        vz[z] = vectors[...]
        for k in (1, 2, 3):
            j = lax.rem(z + k, 4)
            start(vsend.at[3], vz.at[z], vzs.at[0], vzr.at[z], device(x, c, y, j))

    def vector_end():
        for k in (1, 2, 3):
            j = lax.rem(z + k, 4)
            arrived(vz.at[j], vzr.at[j])
        vectors[...] = (vz[0] + vz[1]) + (vz[2] + vz[3])

    dkv32[...] = jnp.zeros_like(dkv32)
    for t in range(4):
        sent(("sum", t), parts[t].at[pl.ds(0, 3 * slab_rows[t]), :], zss.at[t])
    for t in (DOWN, UP):
        sent(("pair", t), given[t], group(("pair", t)))
    sent("dx", dxs, group("dx"))
    for family in range(2):
        sent(("d", family), dr.at[family], group(("d", family)))
        sent(("xs", family), xs.at[family], group(("xs", family)))
    for i in range(3):
        sent(("v", i), vsend.at[i], group(("v", i)))
    sent("vz", vz.at[pl.ds(0, 3)], vzs.at[0])
    from_y(hq, "hid")
    plane_active(x, 1 - y)
    out_back()
    from_x(hq, "hid")
    from_y(fq, "ffn")
    plane_active(1 - x, y)
    from_x(fq, "ffn")
    queries_back()
    from_diagonal(hq, "hid")
    query_weights()
    plane_active(1 - x, 1 - y)
    grads_arrive(1)
    from_diagonal(fq, "ffn")
    pair_send(DOWN)
    pair_add(DOWN)
    keys_back_at(0)
    plane_back(1 - x, y)
    plane_back(x, 1 - y)
    plane_back(1 - x, 1 - y)
    pair_send(UP)
    attention_x(0)
    grads_arrive(2)
    sum_pass(DOWN)
    keys_back_at(1)
    pair_add(UP)
    keys_back_at(2)
    grads_arrive(3)
    sum_end(DOWN)
    keys_back_at(3)
    key_value_weights()
    gather_own(DOWN)
    input_grad()
    sum_pass(UP)
    attention_x(1)
    attention_z(0)
    gather_z(DOWN, 1)
    sum_end(UP)
    gather_own(UP)
    vector_step(0, sib)
    sum_pass(QUERY_OUT)
    gather_z(DOWN, 2)
    vector_add(0)
    plane_first(DOWN)
    attention_z(1)
    gather_z(UP, 1)
    sum_end(QUERY_OUT)
    plane_second(DOWN)
    plane_first(UP)
    gather_z(UP, 2)
    sum_pass(KEY_VALUE)
    plane_out(DOWN)
    gather_own(QUERY_OUT)
    sum_end(KEY_VALUE)
    gather_own(KEY_VALUE)
    gather_second(DOWN, 0)
    gather_z(QUERY_OUT, 1)
    gather_z(KEY_VALUE, 1)
    gather_z(UP, 3)
    plane_second(UP)
    plane_out(UP)
    gather_z(DOWN, 3)
    plane_z(DOWN, 1)
    gather_z(QUERY_OUT, 2)
    gather_z(QUERY_OUT, 3)
    vector_step(1, xn)
    plane_first(QUERY_OUT)
    gather_second(QUERY_OUT, 0)
    gather_z(KEY_VALUE, 2)
    gather_second(UP, 3)
    plane_z(UP, 1)
    plane_z(DOWN, 2)
    plane_z(UP, 2)
    gather_second(KEY_VALUE, 1)
    plane_second(QUERY_OUT)
    gather_second(UP, 2)
    vector_add(1)
    gather_second(QUERY_OUT, 2)
    gather_z(KEY_VALUE, 3)
    gather_second(QUERY_OUT, 3)
    vector_step(2, yn)
    plane_out(QUERY_OUT)
    gather_third(KEY_VALUE, 1)
    gather_second(DOWN, 1)
    gather_second(KEY_VALUE, 2)
    gather_second(DOWN, 3)
    gather_third(DOWN, 0)
    plane_z(UP, 3)
    gather_third(UP, 3)
    gather_second(QUERY_OUT, 1)
    plane_z(QUERY_OUT, 1)
    gather_third(UP, 2)
    gather_second(DOWN, 2)
    gather_second(UP, 1)
    gather_second(KEY_VALUE, 0)
    vector_add(2)
    gather_third(DOWN, 1)
    gather_third(KEY_VALUE, 2)
    gather_third(QUERY_OUT, 2)
    gather_third(QUERY_OUT, 0)
    gather_third(QUERY_OUT, 3)
    plane_z(QUERY_OUT, 2)
    vector_z()
    gather_second(UP, 0)
    gather_third(DOWN, 3)
    gather_third(UP, 1)
    gather_second(KEY_VALUE, 3)
    gather_third(QUERY_OUT, 1)
    gather_third(DOWN, 2)
    plane_z(DOWN, 3)
    gather_third(KEY_VALUE, 0)
    input_grad_end()
    gather_third(UP, 0)
    gather_third(KEY_VALUE, 3)
    plane_z(QUERY_OUT, 3)
    vector_end()
    phase("gather_end")
    gather_end()
    phase("sends_end")
    assert (len(send_names), len(names)) == (mss.shape[0], msr.shape[0])
    for wait in waits.values():
        wait()
    phase(None)


def fused_layer(
    frames,
    clip_lengths,
    query_weight,
    query_bias,
    key_weight,
    value_weight,
    value_bias,
    out_weight,
    out_bias,
    norm1_gain,
    norm1_bias,
    up_weight,
    up_bias,
    down_weight,
    down_bias,
    norm2_gain,
    norm2_bias,
    cotangent,
):
    T, D = frames.shape[1], frames.shape[2]
    F = up_weight.shape[1]
    S = T * lax.axis_size("seq")
    HW, T2, EIGHTH, FO = D // 2, 2 * T, D // 8, F // 8
    blocks = HW // LANES
    entries = clip_lengths.shape[1]
    vmem, smem, hbm = (
        pl.BlockSpec(memory_space=pltpu.VMEM),
        pl.BlockSpec(memory_space=pltpu.SMEM),
        pl.BlockSpec(memory_space=pl.ANY),
    )
    dma, n = pltpu.SemaphoreType.DMA, len(PIECES)
    low, wide = (lambda *shape: pltpu.VMEM(shape, BF16)), (lambda *shape: pltpu.VMEM(shape, F32))
    scratch = dict(
        bias_rows=wide(8, D),
        up_rows=wide(4, 8, D),
        fall=low(S, D),
        wqkv=low(D, 3 * HW),
        wo=low(D, D),
        wup=low(D, F),
        wdn=low(F, D),
        qall=low(S, HW),
        kv=low(S, D),
        mask=wide(T2, S),
        probs=low(2 * blocks, T2, S),
        stat=wide(2, T2, LANES),
        lsed=wide(5, 16, T2),
        att32=wide(T2, HW),
        att16=low(T2, HW),
        attf=low(T, D),
        hq=low(4 * T, D),
        fq=low(4 * T, D),
        ar=low(4 * T, D),
        br=low(4 * T, D),
        actives=low(4, T, D),
        slopes=wide(4 * T, D),
        dgelu=wide(4, T, D),
        hid32=wide(T, D),
        unit1=wide(T, D),
        rstd1=wide(T, LANES),
        gmid=wide(T, D),
        gfirst=wide(T, D),
        gbr=low(T2, D),
        doall=low(S, HW),
        dkv32=wide(T2, D),
        dall=low(T2, 3 * HW),
        give_down=low(FO, D),
        give_up=low(D, FO),
        take_down=low(FO, D),
        take_up=low(D, FO),
        keep_down=wide(FO, D),
        keep_up=wide(D, FO),
        part_down=low(FO, D),
        part_up=low(D, FO),
        part_qo=low(HW // 2, D),
        part_kv=low(HW // 2, D),
        got_down=low(4, FO // 4, D),
        got_up=low(4, D // 4, FO),
        got_qo=low(4, HW // 8, D),
        got_kv=low(4, HW // 8, D),
        gm=low(2, 2, 2, HW // 2, D),
        dr=low(2, 2, HW // 2, D),
        xs=low(2, HW // 2, D),
        xr=low(2, HW // 2, D),
        dxs=low(T, D),
        dxr=low(T, D),
        dxo=wide(T2, D),
        vsend=wide(4, 16, D),
        vrecv=wide(3, 16, D),
        vz=wide(4, 16, D),
        wsem=dma((6,)),
        hes=dma((1,)),
        her=dma((blocks,)),
        frs=dma((8,)),
        fss=dma((2,)),
        msr=dma((19,)),
        mss=dma((13,)),
        dor=dma((2, 4)),
        dos=dma((2,)),
        zsr=dma((4, 4)),
        zss=dma((4,)),
        agr=dma((n, 19)),
        ags=dma((n,)),
        agdr=dma((n,)),
        vzr=dma((4,)),
        vzs=dma((1,)),
    )
    results = pl.pallas_call(
        partial(layer_kernel, T, D, S, entries),
        out_shape=(
            pltpu.VMEM((T, D), F32),
            pltpu.VMEM((T, D), F32),
            pltpu.VMEM((16, D), F32),
            pltpu.VMEM((F, D), BF16),
            pltpu.VMEM((D, F), BF16),
            pltpu.VMEM((4 * D, D), BF16),
        ),
        in_specs=[vmem, vmem, smem] + [hbm] * 6 + [vmem] * 9,
        out_specs=(vmem,) * 6,
        scratch_shapes=list(scratch.values()),
        compiler_params=pltpu.CompilerParams(
            collective_id=0, has_side_effects=True, vmem_limit_bytes=VMEM_GRANT
        ),
        name="layer",
    )(
        frames[0],
        cotangent[0],
        clip_lengths,
        query_weight,
        key_weight,
        value_weight,
        out_weight,
        up_weight,
        down_weight,
        query_bias,
        value_bias,
        out_bias,
        norm1_gain,
        norm1_bias,
        up_bias,
        down_bias,
        norm2_gain,
        norm2_bias,
    )
    return widen(*results)


def widen_kernel(
    last,
    T,
    D,
    encoded,
    frames_grad,
    vectors,
    down,
    up,
    attn,
    encoded_out,
    frames_grad_out,
    query_out,
    query_b,
    key_out,
    value_out,
    value_b,
    out_out,
    out_b,
    gain1,
    bias1,
    up_out,
    up_b,
    down_out,
    down_b,
    gain2,
    bias2,
    sems,
):
    step = pl.program_id(0)
    copies = [
        pltpu.make_async_copy(encoded, encoded_out, sems.at[0]),
        pltpu.make_async_copy(frames_grad, frames_grad_out, sems.at[1]),
    ]

    @pl.when(step == 0)
    def _():
        for copy in copies:
            copy.start()
        for ref, index in (
            (query_b, 0),
            (value_b, 1),
            (out_b, 2),
            (gain1, 3),
            (bias1, 4),
            (down_b, 9),
            (gain2, 10),
            (bias2, 11),
        ):
            ref[...] = vectors[index : index + 1, :].reshape(D)
        for quarter in range(4):
            up_b[pl.ds(D * quarter, D)] = vectors[5 + quarter : 6 + quarter, :].reshape(D)

    def rows(size, first=0):
        return pl.ds(pl.multiple_of(first + size * step, size), size)

    down_out[...] = down[rows(down_out.shape[0]), :].astype(F32)
    up_out[...] = up[rows(up_out.shape[0]), :].astype(F32)
    out_out[...] = attn[rows(LANES, 3 * D), :].astype(F32)
    for m, target in enumerate((query_out, key_out, value_out)):
        target[...] = attn[rows(LANES, m * D), :].astype(F32).T

    @pl.when(step == last)
    def _():
        for copy in copies:
            copy.wait()


def widen(encoded, frames_grad, vectors, sum_down, sum_up, sum_attn):
    T, D = encoded.shape
    F = sum_up.shape[1]
    steps = D // LANES
    hbm, vmem = pl.BlockSpec(memory_space=pl.ANY), pl.BlockSpec(memory_space=pltpu.VMEM)
    parts = (encoded, frames_grad, vectors, sum_down, sum_up, sum_attn)
    parts = [pltpu.with_memory_space_constraint(part, pltpu.VMEM) for part in parts]

    def down(width):
        return pl.BlockSpec((width, D), lambda i: (i, 0))

    up = pl.BlockSpec((D // steps, F), lambda i: (i, 0))
    turned = pl.BlockSpec((D, LANES), lambda i: (0, i))
    flat = pl.BlockSpec((D,), lambda i: (0,))
    wide_flat = pl.BlockSpec((F,), lambda i: (0,))
    square, vector = jax.ShapeDtypeStruct((D, D), F32), jax.ShapeDtypeStruct((D,), F32)
    tokens = jax.ShapeDtypeStruct((T, D), F32)
    outs = (
        (tokens, hbm),
        (tokens, hbm),
        (square, turned),
        (vector, flat),
        (square, turned),
        (square, turned),
        (vector, flat),
        (square, down(LANES)),
        (vector, flat),
        (vector, flat),
        (vector, flat),
        (jax.ShapeDtypeStruct((D, F), F32), up),
        (jax.ShapeDtypeStruct((F,), F32), wide_flat),
        (jax.ShapeDtypeStruct((F, D), F32), down(F // steps)),
        (vector, flat),
        (vector, flat),
        (vector, flat),
    )
    results = pl.pallas_call(
        partial(widen_kernel, steps - 1, T, D),
        grid=(steps,),
        out_shape=tuple(shape for shape, _ in outs),
        in_specs=[vmem] * 6,
        out_specs=tuple(spec for _, spec in outs),
        scratch_shapes=[pltpu.SemaphoreType.DMA((2,))],
        compiler_params=pltpu.CompilerParams(vmem_limit_bytes=VMEM_GRANT),
        name="widen",
    )(*parts)
    return (results[0][None], results[1][None]) + tuple(results[2:])


def solution(mesh):
    in_specs = (
        P("row", "seq", None),
        P("row", None),
        P(),
        P(),
        P(),
        P(),
        P(),
        P(),
        P(),
        P(),
        P(),
        P(),
        P(),
        P(),
        P(),
        P(),
        P(),
        P("row", "seq", None),
    )
    out_specs = (
        P("row", "seq", None),
        P("row", "seq", None),
        P(),
        P(),
        P(),
        P(),
        P(),
        P(),
        P(),
        P(),
        P(),
        P(),
        P(),
        P(),
        P(),
        P(),
        P(),
    )
    shape = dict(mesh.shape)
    fused = shape["row"] == 4 and shape["seq"] == 8
    return jax.shard_map(
        fused_layer if fused else per_device, mesh=mesh, in_specs=in_specs, out_specs=out_specs, check_vma=False
    )
```

```python
import contextlib
from functools import partial
import math

import jax
import jax.numpy as jnp
from jax import lax
from jax.experimental import pallas as pl
from jax.experimental.pallas import tpu as pltpu
from jax.sharding import PartitionSpec as P

H = 12
HD = 64


MASK_SCORE = -1e30
NORM_EPSILON = 1e-05


def from_behind(value, axis, by):
    count = lax.axis_size(axis)
    return lax.ppermute(value, axis, [(i, (i + by) % count) for i in range(count)])


def layer_norm(summed, norm_gain, norm_shift):
    centre = jnp.mean(summed, axis=-1, keepdims=True)
    centered = summed - centre
    inverse = lax.rsqrt(jnp.mean(centered * centered, axis=-1, keepdims=True) + NORM_EPSILON)
    normed = centered * inverse
    return (normed * norm_gain + norm_shift, normed, inverse)


def layer_norm_back(upstream, normed, inverse, norm_gain):
    scaled = upstream * norm_gain
    first_mean = jnp.mean(scaled, axis=-1, keepdims=True)
    second_mean = jnp.mean(scaled * normed, axis=-1, keepdims=True)
    summed_grad = inverse * (scaled - first_mean - normed * second_mean)
    return (summed_grad, jnp.sum(upstream * normed, axis=(0, 1)), jnp.sum(upstream, axis=(0, 1)))


def project(inputs, matrix):
    return jnp.einsum("rsk,kn->rsn", inputs, matrix, preferred_element_type=jnp.float32)


def project_back(upstream, matrix):
    return jnp.einsum("rsn,kn->rsk", upstream, matrix, preferred_element_type=jnp.float32)


def matrix_grad(inputs, upstream):
    return jnp.einsum("rsk,rsn->kn", inputs, upstream, preferred_element_type=jnp.float32)


def column_sum(upstream):
    return jnp.sum(upstream.astype(jnp.float32), axis=(0, 1))


def clip_numbers(clip_ends, position):
    return jnp.sum((clip_ends[:, None, :] <= position[None, :, None]).astype(jnp.int32), axis=-1)


def split_heads(tensor):
    return tensor.reshape(tensor.shape[0], tensor.shape[1], H, HD)


def join_heads(tensor):
    return tensor.reshape(tensor.shape[0], tensor.shape[1], H * HD)


def head_scores(queries, keys_block):
    return jnp.einsum(
        "rqhd,rkhd->rhqk", queries, keys_block, preferred_element_type=jnp.float32
    ) * HD ** (-0.5)


def allowed_pairs(query_numbers, key_numbers):
    return (query_numbers[:, :, None] == key_numbers[:, None, :])[:, None]


def online_update(running, queries, query_numbers, keys_block, values_block, key_numbers):
    run_peak, run_total, run_values = running
    allowed = allowed_pairs(query_numbers, key_numbers)
    masked = jnp.where(allowed, head_scores(queries, keys_block), MASK_SCORE)
    new_peak = jnp.maximum(run_peak, jnp.max(masked, axis=-1))
    weights = jnp.where(allowed, jnp.exp(masked - new_peak[..., None]), 0.0)
    rescale = jnp.exp(run_peak - new_peak)
    new_total = run_total * rescale + jnp.sum(weights, axis=-1)
    contrib = jnp.einsum(
        "rhqk,rkhd->rqhd",
        weights.astype(jnp.bfloat16),
        values_block,
        preferred_element_type=jnp.float32,
    )
    new_values = run_values * jnp.swapaxes(rescale, 1, 2)[..., None] + contrib
    return (new_peak, new_total, new_values)


def block_back(
    queries, grad_heads, log_total, delta_rows, query_numbers, keys_flat, values_flat, key_numbers
):
    keys_block = split_heads(keys_flat)
    values_block = split_heads(values_flat)
    allowed = allowed_pairs(query_numbers, key_numbers)
    shifted = jnp.where(
        allowed, head_scores(queries, keys_block) - log_total[..., None], MASK_SCORE
    )
    weights = jnp.exp(shifted)
    grad_weights = jnp.einsum(
        "rqhd,rkhd->rhqk", grad_heads, values_block, preferred_element_type=jnp.float32
    )
    grad_scores = (weights * (grad_weights - delta_rows[..., None])).astype(jnp.bfloat16)
    factor = HD ** (-0.5)
    query_part = (
        jnp.einsum("rhqk,rkhd->rqhd", grad_scores, keys_block, preferred_element_type=jnp.float32)
        * factor
    )
    key_part = (
        jnp.einsum("rhqk,rqhd->rkhd", grad_scores, queries, preferred_element_type=jnp.float32)
        * factor
    )
    value_part = jnp.einsum(
        "rhqk,rqhd->rkhd",
        weights.astype(jnp.bfloat16),
        grad_heads,
        preferred_element_type=jnp.float32,
    )
    return (join_heads(query_part), join_heads(key_part), join_heads(value_part))


def per_device(
    frames,
    clip_lengths,
    query_weight,
    query_bias,
    key_weight,
    value_weight,
    value_bias,
    out_weight,
    out_bias,
    norm1_gain,
    norm1_bias,
    up_weight,
    up_bias,
    down_weight,
    down_bias,
    norm2_gain,
    norm2_bias,
    cotangent,
):
    row_count = frames.shape[0]
    shard_len = frames.shape[1]
    cycle_size = lax.axis_size("seq")
    seq_place = lax.axis_index("seq")
    clip_ends = jnp.cumsum(clip_lengths, axis=1)
    offsets = jnp.arange(shard_len, dtype=jnp.int32)
    own_numbers = clip_numbers(clip_ends, seq_place * shard_len + offsets)
    frames_low = frames.astype(jnp.bfloat16)
    queries = split_heads((project(frames_low, query_weight) + query_bias).astype(jnp.bfloat16))
    keys_own = project(frames_low, key_weight).astype(jnp.bfloat16)
    values_own = (project(frames_low, value_weight) + value_bias).astype(jnp.bfloat16)
    initial = (
        jnp.full((row_count, H, shard_len), MASK_SCORE, jnp.float32),
        jnp.zeros((row_count, H, shard_len), jnp.float32),
        jnp.zeros((row_count, shard_len, H, HD), jnp.float32),
    )
    key_piece = lax.all_gather(keys_own, "seq", axis=1, tiled=True)
    value_piece = lax.all_gather(values_own, "seq", axis=1, tiled=True)
    piece_len = key_piece.shape[1]
    block_len = math.gcd(piece_len, 512)

    def attend_block(block_index, carried):
        offset = block_index * block_len
        key_block = lax.dynamic_slice_in_dim(key_piece, offset, block_len, 1)
        value_block = lax.dynamic_slice_in_dim(value_piece, offset, block_len, 1)
        position = offset + jnp.arange(block_len, dtype=jnp.int32)
        return online_update(
            carried,
            queries,
            own_numbers,
            split_heads(key_block),
            split_heads(value_block),
            clip_numbers(clip_ends, position),
        )

    run_peak, run_total, run_values = lax.fori_loop(
        0, piece_len // block_len, attend_block, initial
    )
    log_total = run_peak + jnp.log(run_total)
    attended_heads = run_values / jnp.swapaxes(run_total, 1, 2)[..., None]
    attended = join_heads(attended_heads)
    attended_low = attended.astype(jnp.bfloat16)
    branch = project(attended_low, out_weight) + out_bias
    hidden, unit_first, inverse_first = layer_norm(frames + branch, norm1_gain, norm1_bias)
    hidden_low = hidden.astype(jnp.bfloat16)
    before = project(hidden_low, up_weight) + up_bias
    active, gelu_back = jax.vjp(partial(jax.nn.gelu, approximate=False), before)
    active_low = active.astype(jnp.bfloat16)
    encoded, unit_second, inverse_second = layer_norm(
        hidden + project(active_low, down_weight) + down_bias, norm2_gain, norm2_bias
    )
    grad_mid, norm2_gain_grad, norm2_bias_grad = layer_norm_back(
        cotangent, unit_second, inverse_second, norm2_gain
    )
    grad_ffn = grad_mid.astype(jnp.bfloat16)
    down_weight_grad = matrix_grad(active_low, grad_ffn)
    down_bias_grad = column_sum(grad_ffn)
    grad_before = gelu_back(project_back(grad_ffn, down_weight))[0].astype(jnp.bfloat16)
    up_weight_grad = matrix_grad(hidden_low, grad_before)
    up_bias_grad = column_sum(grad_before)
    grad_hidden = grad_mid + project_back(grad_before, up_weight)
    grad_first, norm1_gain_grad, norm1_bias_grad = layer_norm_back(
        grad_hidden, unit_first, inverse_first, norm1_gain
    )
    grad_branch = grad_first.astype(jnp.bfloat16)
    out_weight_grad = matrix_grad(attended_low, grad_branch)
    out_bias_grad = column_sum(grad_branch)
    grad_attended = project_back(grad_branch, out_weight).astype(jnp.bfloat16)
    grad_heads = split_heads(grad_attended)
    delta_rows = jnp.swapaxes(
        jnp.sum(grad_heads.astype(jnp.float32) * attended_heads, axis=-1), 1, 2
    )
    query_start, key_start, value_start = block_back(
        queries, grad_heads, log_total, delta_rows, own_numbers, keys_own, values_own, own_numbers
    )

    def key_step(distance, carried):
        key_now, value_now, query_sum, key_sum, value_sum = carried
        key_now, value_now = from_behind((key_now, value_now), "seq", 1)
        key_sum, value_sum = (
            from_behind(key_sum.astype(jnp.bfloat16), "seq", 1).astype(key_sum.dtype),
            from_behind(value_sum.astype(jnp.bfloat16), "seq", 1).astype(value_sum.dtype),
        )
        source = (seq_place - distance) % cycle_size
        source_numbers = clip_numbers(clip_ends, source * shard_len + offsets)
        query_part, key_part, value_part = block_back(
            queries,
            grad_heads,
            log_total,
            delta_rows,
            own_numbers,
            key_now,
            value_now,
            source_numbers,
        )
        return (
            key_now,
            value_now,
            query_sum + query_part,
            key_sum + key_part,
            value_sum + value_part,
        )

    carried = lax.fori_loop(
        1, cycle_size, key_step, (keys_own, values_own, query_start, key_start, value_start)
    )
    query_total = carried[2]
    key_total, value_total = (
        from_behind(carried[3].astype(jnp.bfloat16), "seq", 1).astype(jnp.float32),
        from_behind(carried[4].astype(jnp.bfloat16), "seq", 1).astype(jnp.float32),
    )
    query_low = query_total.astype(jnp.bfloat16)
    key_low = key_total.astype(jnp.bfloat16)
    value_low = value_total.astype(jnp.bfloat16)
    query_weight_grad = matrix_grad(frames_low, query_low)
    query_bias_grad = column_sum(query_low)
    key_weight_grad = matrix_grad(frames_low, key_low)
    value_weight_grad = matrix_grad(frames_low, value_low)
    value_bias_grad = column_sum(value_low)
    frames_grad = (
        grad_first
        + project_back(query_low, query_weight)
        + project_back(key_low, key_weight)
        + project_back(value_low, value_weight)
    )
    shares = (
        lax.psum_scatter(query_weight_grad, "seq", scatter_dimension=0, tiled=True),
        lax.psum_scatter(query_bias_grad, "seq", scatter_dimension=0, tiled=True),
        lax.psum_scatter(key_weight_grad, "seq", scatter_dimension=0, tiled=True),
        lax.psum_scatter(value_weight_grad, "seq", scatter_dimension=0, tiled=True),
        lax.psum_scatter(value_bias_grad, "seq", scatter_dimension=0, tiled=True),
        lax.psum_scatter(out_weight_grad, "seq", scatter_dimension=0, tiled=True),
        lax.psum_scatter(out_bias_grad, "seq", scatter_dimension=0, tiled=True),
        lax.psum_scatter(norm1_gain_grad, "seq", scatter_dimension=0, tiled=True),
        lax.psum_scatter(norm1_bias_grad, "seq", scatter_dimension=0, tiled=True),
        lax.psum_scatter(up_weight_grad, "seq", scatter_dimension=0, tiled=True),
        lax.psum_scatter(up_bias_grad, "seq", scatter_dimension=0, tiled=True),
        lax.psum_scatter(down_weight_grad, "seq", scatter_dimension=0, tiled=True),
        lax.psum_scatter(down_bias_grad, "seq", scatter_dimension=0, tiled=True),
        lax.psum_scatter(norm2_gain_grad, "seq", scatter_dimension=0, tiled=True),
        lax.psum_scatter(norm2_bias_grad, "seq", scatter_dimension=0, tiled=True),
    )
    shares = (
        lax.psum(shares[0].astype(jnp.bfloat16), "row").astype(jnp.float32),
        lax.psum(shares[1].astype(jnp.bfloat16), "row").astype(jnp.float32),
        lax.psum(shares[2].astype(jnp.bfloat16), "row").astype(jnp.float32),
        lax.psum(shares[3].astype(jnp.bfloat16), "row").astype(jnp.float32),
        lax.psum(shares[4].astype(jnp.bfloat16), "row").astype(jnp.float32),
        lax.psum(shares[5].astype(jnp.bfloat16), "row").astype(jnp.float32),
        lax.psum(shares[6].astype(jnp.bfloat16), "row").astype(jnp.float32),
        lax.psum(shares[7].astype(jnp.bfloat16), "row").astype(jnp.float32),
        lax.psum(shares[8].astype(jnp.bfloat16), "row").astype(jnp.float32),
        lax.psum(shares[9].astype(jnp.bfloat16), "row").astype(jnp.float32),
        lax.psum(shares[10].astype(jnp.bfloat16), "row").astype(jnp.float32),
        lax.psum(shares[11].astype(jnp.bfloat16), "row").astype(jnp.float32),
        lax.psum(shares[12].astype(jnp.bfloat16), "row").astype(jnp.float32),
        lax.psum(shares[13].astype(jnp.bfloat16), "row").astype(jnp.float32),
        lax.psum(shares[14].astype(jnp.bfloat16), "row").astype(jnp.float32),
    )
    totals = (
        lax.all_gather(shares[0].astype(jnp.bfloat16), "seq", axis=0, tiled=True).astype(
            jnp.float32
        ),
        lax.all_gather(shares[1].astype(jnp.bfloat16), "seq", axis=0, tiled=True).astype(
            jnp.float32
        ),
        lax.all_gather(shares[2].astype(jnp.bfloat16), "seq", axis=0, tiled=True).astype(
            jnp.float32
        ),
        lax.all_gather(shares[3].astype(jnp.bfloat16), "seq", axis=0, tiled=True).astype(
            jnp.float32
        ),
        lax.all_gather(shares[4].astype(jnp.bfloat16), "seq", axis=0, tiled=True).astype(
            jnp.float32
        ),
        lax.all_gather(shares[5].astype(jnp.bfloat16), "seq", axis=0, tiled=True).astype(
            jnp.float32
        ),
        lax.all_gather(shares[6].astype(jnp.bfloat16), "seq", axis=0, tiled=True).astype(
            jnp.float32
        ),
        lax.all_gather(shares[7].astype(jnp.bfloat16), "seq", axis=0, tiled=True).astype(
            jnp.float32
        ),
        lax.all_gather(shares[8].astype(jnp.bfloat16), "seq", axis=0, tiled=True).astype(
            jnp.float32
        ),
        lax.all_gather(shares[9].astype(jnp.bfloat16), "seq", axis=0, tiled=True).astype(
            jnp.float32
        ),
        lax.all_gather(shares[10].astype(jnp.bfloat16), "seq", axis=0, tiled=True).astype(
            jnp.float32
        ),
        lax.all_gather(shares[11].astype(jnp.bfloat16), "seq", axis=0, tiled=True).astype(
            jnp.float32
        ),
        lax.all_gather(shares[12].astype(jnp.bfloat16), "seq", axis=0, tiled=True).astype(
            jnp.float32
        ),
        lax.all_gather(shares[13].astype(jnp.bfloat16), "seq", axis=0, tiled=True).astype(
            jnp.float32
        ),
        lax.all_gather(shares[14].astype(jnp.bfloat16), "seq", axis=0, tiled=True).astype(
            jnp.float32
        ),
    )
    return (
        encoded,
        frames_grad,
        totals[0],
        totals[1],
        totals[2],
        totals[3],
        totals[4],
        totals[5],
        totals[6],
        totals[7],
        totals[8],
        totals[9],
        totals[10],
        totals[11],
        totals[12],
        totals[13],
        totals[14],
    )


MESH = pl.DeviceIdType.MESH
LANES = 128
F32, BF16 = jnp.float32, jnp.bfloat16
VMEM_GRANT = 49 << 20
DOWN, UP = 0, 1
DOWN_0, DOWN_1, UP_0, UP_1, QUERY_OUT, KEY_VALUE = range(6)
CHUNKS = 2

PIECES = (
    (DOWN_0, "zxy", 0, 3),
    (DOWN_1, "zyx", 0, 2),
    (DOWN_1, "xyz", 2, 1),
    (UP_0, "zxy", 0, 3),
    (UP_1, "zyx", 0, 2),
    (UP_1, "xyz", 2, 1),
    (QUERY_OUT, "zxy", 0, 1),
    (QUERY_OUT, "yxz", 1, 2),
    (KEY_VALUE, "zyx", 0, 3),
)


def dot(a, b):
    return jnp.dot(a, b, preferred_element_type=F32)


def dot_nt(a, b):
    return lax.dot_general(a, b, (((1,), (1,)), ((), ())), preferred_element_type=F32)


def dot_tn(a, b):
    return lax.dot_general(a, b, (((0,), (0,)), ((), ())), preferred_element_type=F32)


def rows_norm(value):
    centre = jnp.mean(value, axis=-1, keepdims=True)
    centered = value - centre
    inverse = lax.rsqrt(jnp.mean(centered * centered, axis=-1, keepdims=True) + NORM_EPSILON)
    return centered * inverse, inverse


def rows_norm_back(scaled, unit, inverse):
    first = jnp.mean(scaled, axis=-1, keepdims=True)
    second = jnp.mean(scaled * unit, axis=-1, keepdims=True)
    return inverse * (scaled - first - unit * second)


def layer_kernel(
    T,
    D,
    S,
    entries,
    frames,
    cotangent,
    lengths,
    query_w,
    key_w,
    value_w,
    out_w,
    up_w,
    down_w,
    query_b,
    value_b,
    out_b,
    gain1,
    bias1,
    up_b,
    down_b,
    gain2,
    bias2,
    encoded,
    frames_grad,
    vectors,
    sum_down,
    sum_up,
    sum_attn,
    frames_v,
    cotangent_v,
    lengths_v,
    v0,
    v1,
    v2,
    v3,
    v4,
    v5,
    v6,
    v7,
    up_v,
    bias_rows,
    up_rows,
    fall,
    wqkv,
    wo,
    wup,
    wdn,
    qall,
    kv,
    mask,
    probs,
    stat,
    lsed,
    att32,
    att16,
    attf,
    hq,
    fq,
    ar,
    br,
    actives,
    slopes,
    dgelu,
    hid32,
    unit1,
    rstd1,
    gmid,
    gfirst,
    gbr,
    doall,
    dkv32,
    dall,
    give_down,
    give_up,
    take_down,
    take_up,
    keep_down,
    keep_up,
    part_down,
    part_up,
    part_qo,
    part_kv,
    got_down,
    got_up,
    got_qo,
    got_kv,
    gm,
    dr,
    xs,
    xr,
    dxs,
    dxr,
    dxo,
    vsend,
    vrecv,
    vz,
    wsem,
    asem,
    hes,
    her,
    frs,
    fss,
    msr,
    mss,
    dor,
    dos,
    zsr,
    zss,
    agr,
    ags,
    agdr,
    vzr,
    vzs,
):
    HW, T2, FO = D // 2, 2 * T, wup.shape[1] // 8
    blocks = HW // LANES
    EIGHTH, SIXTEENTH = D // 8, D // 16
    row, seq = lax.axis_index("row"), lax.axis_index("seq")
    x, c = lax.div(row, 2), lax.rem(row, 2)
    z, y = lax.div(seq, 2), lax.rem(seq, 2)
    not_first, not_last = z > 0, z < 3

    def device(x_, c_, y_, z_=z):
        return (2 * x_ + c_, 2 * z_ + y_)

    def octant(x_, c_, y_):
        return 4 * y_ + 2 * x_ + c_

    sib, xn, yn = device(x, 1 - c, y), device(1 - x, c, y), device(x, c, 1 - y)
    zp, zm = device(x, c, y, jnp.minimum(z + 1, 3)), device(x, c, y, jnp.maximum(z - 1, 0))

    def many(value, of):
        return pl.multiple_of(value, of)

    def at(start, size, of=None):
        return pl.ds(many(start, size if of is None else of), size)

    waits = {}
    scope = contextlib.ExitStack()

    def phase(name):
        scope.close()
        if name:
            scope.enter_context(jax.named_scope(name))

    def send(src, dst, ssem, rsem, to):
        return pltpu.make_async_remote_copy(
            src_ref=src, dst_ref=dst, send_sem=ssem, recv_sem=rsem, device_id=to, device_id_type=MESH
        )

    def start(src, dst, ssem, rsem, to):
        send(src, dst, ssem, rsem, to).start()

    def arrived(ref, rsem):
        send(ref, ref, mss.at[0], rsem, sib).wait_recv()

    def sent(key, ref, ssem):
        waits.setdefault(key, lambda: send(ref, ref, ssem, msr.at[0], sib).wait_send())

    def sent_along_z(key, ref_of, ssem, rest=0, lines=1):
        for blocks_sent, when in ((1, (z == 0) | (z == 3)), (5, (z > 0) & (z < 3))):
            ref = ref_of(rest + lines * blocks_sent)
            wait = partial(lambda ref: send(ref, ref, ssem, msr.at[0], sib).wait_send(), ref)
            waits[key, blocks_sent] = partial(lambda when, wait: pl.when(when)(wait), when, wait)

    send_names, names = {}, {}

    def group(name):
        return mss.at[send_names.setdefault(name, len(send_names))]

    def one(name, family=None):
        return group(family or name), got_of(name)

    def got_of(name):
        return msr.at[names.setdefault(name, len(names))]

    phase("enter")
    heads_here = at(HW * y, HW)
    loads = [
        pltpu.make_async_copy(query_w.at[:, heads_here], wqkv.at[:, pl.ds(0, HW)], wsem.at[0]),
        pltpu.make_async_copy(key_w.at[:, heads_here], wqkv.at[:, pl.ds(HW, HW)], wsem.at[1]),
        pltpu.make_async_copy(value_w.at[:, heads_here], wqkv.at[:, pl.ds(2 * HW, HW)], wsem.at[2]),
        pltpu.make_async_copy(out_w, wo, wsem.at[3]),
        pltpu.make_async_copy(up_w, wup, wsem.at[4]),
        pltpu.make_async_copy(down_w, wdn, wsem.at[5]),
    ]
    barrier = pltpu.get_barrier_semaphore()
    peers = [sib, xn, yn, device(1 - x, c, 1 - y)]
    peers += [device(x, c, y, lax.rem(z + k, 4)) for k in (1, 2, 3)]
    for peer in peers:
        pl.semaphore_signal(barrier, inc=1, device_id=peer, device_id_type=MESH)
    vectors_v = (v0, v1, v2, v3, v4, v5, v6, v7)
    arrays = (frames, cotangent, lengths, query_b, value_b, out_b, gain1, bias1, up_b, down_b, gain2, bias2)
    here_ = (frames_v, cotangent_v, lengths_v, *vectors_v[:5], up_v, *vectors_v[5:])
    small = [pltpu.make_async_copy(array, ref, asem.at[i]) for i, (array, ref) in enumerate(zip(arrays, here_))]
    small[0].start()
    for load in loads[:3] + small[1:] + loads[3:]:
        load.start()
    frames, cotangent, lengths = here_[:3]
    query_b, value_b, out_b, gain1, bias1, up_b, down_b, gain2, bias2 = here_[3:]
    vectors[...] = jnp.zeros_like(vectors)
    small[0].wait()
    fall[at(T * seq, T), :] = frames[...].astype(BF16)
    pl.semaphore_wait(barrier, len(peers))

    phase("frames_gather")

    CHUNK = T // CHUNKS

    def chunk(z_, y_, h):
        return fall.at[at(T * (2 * z_ + y_) + CHUNK * h, CHUNK), :]

    def push(z_, h, direction):
        to = (zp, zm, yn)[direction]
        start(chunk(z_, y, h), chunk(z_, y, h), fss.at[direction // 2], frs.at[h, 2 * z_ + y], to)

    for h in range(CHUNKS):
        pl.when(not_last)(lambda: push(z, h, 0))
        pl.when(not_first)(lambda: push(z, h, 1))
        push(z, h, 2)
    for load in small[1:]:
        load.wait()
    bias_rows[0:1, :] = query_b[...].reshape(1, D)
    bias_rows[1:2, :] = value_b[...].reshape(1, D)
    for quarter in range(4):
        up_rows[quarter] = jnp.broadcast_to(up_b[pl.ds(D * quarter, D)].reshape(1, D), (8, D))
    out_b, gain1, bias1, down_b, gain2, bias2 = (
        ref[...].reshape(1, D) for ref in (out_b, gain1, bias1, down_b, gain2, bias2)
    )
    query_bias, value_bias = bias_rows[0:1, heads_here], bias_rows[1:2, heads_here]
    for load in loads[:3]:
        load.wait()

    def project_slab(z_, y_):
        rows = at(T * (2 * z_ + y_), T)
        flat = dot(fall[rows, :], wqkv[...])
        query = (flat[:, :HW] + query_bias).astype(BF16).astype(F32) * HD ** (-0.5)
        qall[rows, :] = query.astype(BF16)
        kv[rows, pl.ds(0, HW)] = flat[:, HW : 2 * HW].astype(BF16)
        kv[rows, pl.ds(HW, HW)] = (flat[:, 2 * HW :] + value_bias).astype(BF16)

    project_slab(z, y)
    key_at = lax.broadcasted_iota(jnp.int32, (1, S), 1)
    query_at = lax.broadcasted_iota(jnp.int32, (T2, 1), 0) + T2 * z
    key_number, query_number = jnp.zeros((1, S), jnp.int32), jnp.zeros((T2, 1), jnp.int32)
    clip_end = jnp.zeros((1, 1), jnp.int32)
    for entry in range(entries):
        clip_end = clip_end + lengths[0:1, entry : entry + 1]
        key_number = key_number + jnp.where(clip_end <= key_at, 1, 0)
        query_number = query_number + jnp.where(clip_end <= query_at, 1, 0)
    mask[...] = jnp.where(query_number == key_number, 0.0, MASK_SCORE)

    @pl.loop(0, 4)
    def _(k):
        left, right = z - k - 1, z + k + 1

        for h in range(CHUNKS):

            @pl.when(left >= 0)
            def _():
                arrived(chunk(left, y, h), frs.at[h, 2 * left + y])
                pl.when(not_last)(lambda: push(left, h, 0))
                push(left, h, 2)

            @pl.when(right <= 3)
            def _():
                arrived(chunk(right, y, h), frs.at[h, 2 * right + y])
                pl.when(not_first)(lambda: push(right, h, 1))
                push(right, h, 2)

        def across_y(z_):
            for h in range(CHUNKS):
                arrived(chunk(z_, 1 - y, h), frs.at[h, 2 * z_ + 1 - y])
            project_slab(z_, 1 - y)

        pl.when(left >= 0)(lambda: project_slab(left, y))
        pl.when(right <= 3)(lambda: project_slab(right, y))
        pl.when(z - k >= 0)(lambda: across_y(z - k))
        pl.when((k > 0) & (z + k <= 3))(lambda: across_y(z + k))

    sent("frames_y", fall.at[pl.ds(0, 4 * T), :], fss.at[1])
    sent_along_z("frames_z", lambda count: fall.at[pl.ds(0, T * count), :], fss.at[0])

    phase("attention")
    pair_rows = at(T2 * z, T2)
    lane = lax.broadcasted_iota(jnp.int32, (T2, LANES), 1)
    low_half = lane < HD

    def half(value, which):
        return jnp.where(low_half == (which == 0), value, 0.0)

    stat[...] = jnp.zeros_like(stat)
    mine, other = at(T * y, T), at(T * (1 - y), T)

    def heads_push(b):
        part, there = at(LANES * b, LANES), at(HW * y + LANES * b, LANES, LANES)
        return send(att16.at[other, part], attf.at[:, there], hes.at[0], her.at[b], yn)

    def both(value):
        return jnp.concatenate([half(value, 0), half(value, 1)], axis=0).astype(BF16)

    def pick(stacked):
        return jnp.where(low_half, stacked[:T2], stacked[T2:])

    def block_lanes(b):
        return at(LANES * b, LANES), at(HW + LANES * b, LANES, LANES)

    @pl.loop(0, blocks)
    def _(b):
        lanes, value_lanes = block_lanes(b)
        queries = qall[pair_rows, lanes].astype(F32)
        outs = []
        for which in range(2):
            head = 2 * b + which
            scores = dot_nt(half(queries, which).astype(BF16), kv[:, lanes]) + mask[...]
            peak = jnp.max(scores, axis=-1, keepdims=True)
            powers = jnp.exp(scores - peak)
            total = jnp.sum(powers, axis=-1, keepdims=True)
            low = (powers * (1.0 / total)).astype(BF16)
            probs[head] = low
            outs.append(dot(low, kv[:, value_lanes]))
            stat[0] = jnp.where(lane == head, peak + jnp.log(total), stat[0])
        out = jnp.where(low_half, outs[0], outs[1])
        att32[:, lanes] = out
        att16[:, lanes] = out.astype(BF16)
        heads_push(b).start()

    phase("heads_exchange")
    attf[:, heads_here] = att16[mine, :]
    lsed[z, 0:8, :] = stat[0].T[0:8, :]
    loads[3].wait()
    for b in range(blocks):
        arrived(attf.at[:, at(HW * (1 - y) + LANES * b, LANES, LANES)], her.at[b])
    sent("heads", att16.at[pl.ds(0, T), :], hes.at[0])
    phase("out_norm1")
    branch = dot(attf[...], wo[...]) + out_b
    unit, inverse = rows_norm(frames[...] + branch)
    hidden = unit * gain1 + bias1
    unit1[...] = unit
    rstd1[...] = jnp.broadcast_to(inverse, (T, LANES))
    hid32[...] = hidden
    here = at(T * (2 * y + x), T)

    def rows_of(buffer, x_, y_):
        return buffer.at[at(T * (2 * y_ + x_), T), :]

    def halves_of(buffer, x_, y_):
        first = T * (2 * y_ + x_)
        return buffer.at[at(first, T // 2), :], buffer.at[at(first + T // 2, T // 2), :]

    def share_x(buffer, name):
        top, bottom = halves_of(buffer, x, y)
        start(top, top, *one(name + "_x", name), xn)
        start(bottom, bottom, *one(name + "_x_rest", name), xn)

    def share_y(buffer, name):
        top, bottom = halves_of(buffer, x, y)
        start(bottom, bottom, *one(name + "_y", name), yn)
        start(top, top, *one(name + "_y_rest", name), yn)

    def from_x(buffer, name):
        top = halves_of(buffer, 1 - x, y)[0]
        arrived(top, got_of(name + "_x"))
        start(top, top, *one(name + "_top", name), yn)

    def from_y(buffer, name):
        bottom = halves_of(buffer, x, 1 - y)[1]
        arrived(bottom, got_of(name + "_y"))
        start(bottom, bottom, *one(name + "_bottom", name), xn)

    def rest_x(buffer, name):
        arrived(halves_of(buffer, 1 - x, y)[1], got_of(name + "_x_rest"))

    def rest_y(buffer, name):
        arrived(halves_of(buffer, x, 1 - y)[0], got_of(name + "_y_rest"))

    def from_diagonal(buffer, name):
        top, bottom = halves_of(buffer, 1 - x, 1 - y)
        arrived(top, got_of(name + "_top"))
        arrived(bottom, got_of(name + "_bottom"))

    chips = ((1 - x, y), (x, 1 - y), (1 - x, 1 - y), (x, y))

    for buffer, name in ((hq, "hid"), (fq, "ffn")):
        sent(name, buffer.at[pl.ds(0, 3 * T), :], group(name))
    hq[here, :] = hidden.astype(BF16)
    share_x(hq, "hid")
    share_y(hq, "hid")

    phase("up_gelu")
    loads[4].wait()
    scale = 2.0 ** -0.5

    def active(hidden_rows, chip):
        before = dot(hidden_rows, wup[:, at(D * chip, D)]) + up_rows[chip][0:1, :]
        rise = 0.5 * (1.0 + lax.erf(before * scale))
        slope = rise + before * jnp.exp(-0.5 * before * before) * (2.0 * math.pi) ** -0.5
        return (before * rise).astype(BF16), slope

    def grad_before(ffn_rows, chip, slope):
        return (dot_nt(ffn_rows, wdn[at(D * chip, D), :]) * slope).astype(BF16)

    for x_, y_ in chips:
        chip = 2 * y_ + x_
        actives[chip], dgelu[chip] = active(hq[here, :], chip)
    ar[here, :] = actives[2 * y + x]
    phase("down_norm2")
    loads[5].wait()
    fed = hid32[...] + down_b
    for quarter in range(4):
        fed = fed + dot(actives[quarter], wdn[pl.ds(D * quarter, D), :])
    unit2, inverse2 = rows_norm(fed)
    encoded[...] = unit2 * gain2 + bias2
    cot = cotangent[...]
    grad_mid = rows_norm_back(cot * gain2, unit2, inverse2)
    vectors[10:11, :] = jnp.sum(cot * unit2, axis=0, keepdims=True)
    vectors[11:12, :] = jnp.sum(cot, axis=0, keepdims=True)
    gmid[...] = grad_mid
    fq[here, :] = grad_mid.astype(BF16)
    share_x(fq, "ffn")
    share_y(fq, "ffn")
    vectors[9:10, :] = jnp.sum(fq[here, :].astype(F32), axis=0, keepdims=True)
    phase("ffn_back")
    for x_, y_ in chips:
        chip = 2 * y_ + x_
        low = grad_before(fq[here, :], chip, dgelu[chip])
        vectors[pl.ds(5 + chip, 1), :] = jnp.sum(low.astype(F32), axis=0, keepdims=True)
        gmid[...] += dot_nt(low, wup[:, at(D * chip, D)])
    br[here, :] = low

    def plane_active(x_, y_):
        rows = at(T * (2 * y_ + x_), T)
        ar[rows, :], slopes[rows, :] = active(hq[rows, :], 2 * y + x)

    def plane_back(x_, y_):
        rows = at(T * (2 * y_ + x_), T)
        br[rows, :] = grad_before(fq[rows, :], 2 * y + x, slopes[rows, :])

    phase("norm1_back")
    grad_hidden = gmid[...]
    unit = unit1[...]
    grad_first = rows_norm_back(grad_hidden * gain1, unit, rstd1[:, 0:1])
    vectors[3:4, :] = jnp.sum(grad_hidden * unit, axis=0, keepdims=True)
    vectors[4:5, :] = jnp.sum(grad_hidden, axis=0, keepdims=True)
    gfirst[...] = grad_first
    gbr[mine, :] = grad_first.astype(BF16)
    start(gbr.at[mine, :], gbr.at[mine, :], *one("gbr"), yn)
    sent("gbr", gbr.at[mine, :], group("gbr"))
    vectors[2:3, :] = jnp.sum(gbr[mine, :].astype(F32), axis=0, keepdims=True)

    parts = (*(part_down.at[q] for q in range(2)), *(part_up.at[q] for q in range(2)), part_qo, part_kv)
    gots = (*(got_down.at[q] for q in range(2)), *(got_up.at[q] for q in range(2)), got_qo, got_kv)
    given, taken, kept = (give_down, give_up), (take_down, take_up), (keep_down, keep_up)
    HALF = HW // 2
    slab_rows = (FO // 8, FO // 8, D // 8, D // 8, HALF // 4, HALF // 4)

    def part_slab(t, j):
        return parts[t].at[at(slab_rows[t] * j, slab_rows[t]), :]

    outer = (z == 0) | (z == 3)
    near = jnp.where(z < 2, 1 - z, 5 - z)
    inner_there, outer_there = jnp.where(z < 2, 2, 1), jnp.where(z < 2, 3, 0)

    def part_send(t, src, j, to, slot):
        start(src, gots[t].at[slot], zss.at[t], zsr.at[t, slot], device(x, c, y, to))

    def sum_send(t):

        @pl.when(outer)
        def _():
            for j in (outer_there, inner_there, near):
                part_send(t, part_slab(t, j), j, near, j)

        @pl.when(jnp.logical_not(outer))
        def _():
            part_send(t, part_slab(t, near), near, near, z)

    def sum_pass(t):
        @pl.when(jnp.logical_not(outer))
        def _():
            for j, slot in ((outer_there, z), (inner_there, outer_there)):
                got = gots[t].at[j]
                arrived(got, zsr.at[t, j])
                got[...] = (got[...].astype(F32) + part_slab(t, j)[...].astype(F32)).astype(BF16)
                part_send(t, got, j, j, slot)

    def attn_row(t, x_, y_, z_):
        matrix = 3 * x_ if t == QUERY_OUT else 1 + x_
        return D * matrix + HW * y_ + HALF * c + HALF // 4 * z_

    def own_tile(t):
        if t <= DOWN_1:
            return sum_down.at[at(FO * octant(x, c, y) + FO // 2 * t + FO // 8 * z, FO // 8), :]
        if t <= UP_1:
            return sum_up.at[at(D // 2 * (t - UP_0) + D // 8 * z, D // 8), at(FO * octant(x, c, y), FO)]
        return sum_attn.at[at(attn_row(t, x, y, z), HALF // 4), :]

    def sum_end(t):
        total = part_slab(t, z)[...].astype(F32)
        for slot in (jnp.where(outer, near, z), jnp.where(outer, inner_there, near)):
            arrived(gots[t].at[slot], zsr.at[t, slot])
            total = total + gots[t][slot].astype(F32)
        own_tile(t)[...] = total.astype(BF16)

    unit = SIXTEENTH // 3
    unit_rows = (unit, unit, 2 * unit, 2 * unit, unit, unit)

    def tile(u, x_, y_, z_):
        t, _, first, count = PIECES[u]
        rows = unit_rows[t]
        if t <= DOWN_1:
            start_row = FO * octant(x_, c, y_) + FO // 2 * t + FO // 8 * z_ + rows * first
            return sum_down.at[at(start_row, rows * count, rows), :]
        if t <= UP_1:
            start_row = D // 2 * (t - UP_0) + D // 8 * z_ + rows * first
            return sum_up.at[at(start_row, rows * count, rows), at(FO * octant(x_, c, y_), FO)]
        start_row = attn_row(t, x_, y_, z_) + rows * first
        return sum_attn.at[at(start_row, rows * count, rows), :]

    def gather_send(u, place, z_, ssem, rsem, to):
        part = tile(u, *place, z_)
        return send(part, part, ssem, rsem, to)

    def to_sibling(u, place, z_):
        gather_send(u, place, z_, ags.at[u], agdr.at[u], sib).start()

    places = ((x, y), (1 - x, y), (x, 1 - y), (1 - x, 1 - y))

    def order_of(u):
        over_y, over_x = (2, yn), (1, xn)
        return (over_y, over_x) if PIECES[u][1] in ("zyx", "yxz") else (over_x, over_y)

    def z_last(u):
        return PIECES[u][1][2] == "z"

    def along_z(u, p, z_, direction):
        to = (zp, zm)[direction]
        return gather_send(u, places[p], z_, ags.at[u], agr.at[u, 4 * p + z_], to)

    def z_out(u, p):
        pl.when(not_last)(lambda: along_z(u, p, z, 0).start())
        pl.when(not_first)(lambda: along_z(u, p, z, 1).start())

    def second_sem(u, z_):
        return agr.at[u, 16] if z_last(u) else agr.at[u, 4 + z_]

    def third_sem(u, slot):
        return agr.at[u, (17 if z_last(u) else 8) + slot]

    def to_second(u, place, z_):
        gather_send(u, place, z_, ags.at[u], second_sem(u, z_), order_of(u)[0][1]).start()

    def to_third(u, place, slot):
        z_ = z if z_last(u) else lax.rem(slot, 4)
        gather_send(u, place, z_, ags.at[u], third_sem(u, slot), order_of(u)[1][1]).start()

    def gather_own(t):
        for u in pieces_of(t, False):
            z_out(u, 0)
        for u in pieces_of(t):
            to_second(u, places[0], z)
            to_third(u, places[0], 0 if z_last(u) else z)
            to_sibling(u, places[0], z)

    def pieces_of(t, last=None):
        return [u for u in range(len(PIECES)) if PIECES[u][0] == t and last in (None, z_last(u))]

    def sides(k, take):
        pl.when(z - k >= 0)(lambda: take(z - k, not_last, 0))
        if k > 0:
            pl.when(z + k <= 3)(lambda: take(z + k, not_first, 1))

    def gather_z(t, k):
        for u in pieces_of(t, False):

            def take(z_, more, direction):
                arrived(tile(u, *places[0], z_), agr.at[u, z_])
                pl.when(more)(lambda: along_z(u, 0, z_, direction).start())
                to_second(u, places[0], z_)
                to_third(u, places[0], z_)
                to_sibling(u, places[0], z_)

            sides(k, take)

    def gather_second(t, k):
        for u in pieces_of(t, False):

            def take(z_, more, direction):
                place = places[order_of(u)[0][0]]
                arrived(tile(u, *place, z_), second_sem(u, z_))
                to_third(u, place, 4 + z_)
                to_sibling(u, place, z_)

            sides(k, take)

    def gather_third(t, k):
        for u in pieces_of(t, False):

            def take(z_, more, direction):
                for offset, p in ((0, order_of(u)[1][0]), (4, 3)):
                    arrived(tile(u, *places[p], z_), third_sem(u, offset + z_))
                    to_sibling(u, places[p], z_)

            sides(k, take)

    def plane_first(t):
        for u in pieces_of(t, True):
            p = order_of(u)[0][0]
            arrived(tile(u, *places[p], z), second_sem(u, z))
            to_third(u, places[p], 1)
            to_sibling(u, places[p], z)

    def plane_second(t):
        for u in pieces_of(t, True):
            for slot, p in ((0, order_of(u)[1][0]), (1, 3)):
                arrived(tile(u, *places[p], z), third_sem(u, slot))
                to_sibling(u, places[p], z)

    def plane_out(t):
        for u in pieces_of(t, True):
            for p in (0, order_of(u)[0][0], order_of(u)[1][0], 3):
                z_out(u, p)

    def plane_z(t, k):
        for u in pieces_of(t, True):
            for p in (0, order_of(u)[0][0], order_of(u)[1][0], 3):

                def take(z_, more, direction):
                    arrived(tile(u, *places[p], z_), agr.at[u, 4 * p + z_])
                    pl.when(more)(lambda: along_z(u, p, z_, direction).start())
                    to_sibling(u, places[p], z_)

                sides(k, take)

    def gather_end():
        for u, (_, _, _, count) in enumerate(PIECES):

            def as_many(blocks_sent):
                return sum_down.at[pl.ds(0, unit * count * blocks_sent), :]

            arrived(as_many(16), agdr.at[u])
            if z_last(u):
                sent_along_z(("gather", u), as_many, ags.at[u], 19, 4)
            else:
                sent_along_z(("gather", u), as_many, ags.at[u], 28)

    def matrix_put(family, x_, value):
        for half_ in range(2):
            gm[family, half_, x_] = value[HALF * half_ : HALF * (half_ + 1), :].astype(BF16)

    def matrices_send(family):
        start(gm.at[family, 1 - c], dr.at[family], *one(("d", family)), sib)

    def out_back():
        arrived(gbr.at[other, :], got_of("gbr"))
        da = dot_nt(gbr[...], wo[heads_here, :]).astype(BF16)
        doall[pair_rows, :] = da
        product = da.astype(F32) * att32[...]
        stat[1] = jnp.zeros((T2, LANES), F32)
        for head in range(2 * blocks):
            lanes = slice(LANES * (head // 2), LANES * (head // 2 + 1))
            delta = jnp.sum(half(product[:, lanes], head % 2), axis=-1, keepdims=True)
            stat[1] = jnp.where(lane == head, delta, stat[1])
        lsed[z, 8:16, :] = stat[1].T[0:8, :]
        pl.when(not_last)(lambda: grads_push(z, zp))
        pl.when(not_first)(lambda: grads_push(z, zm))
        matrix_put(0, 1, dot_tn(att16[...], gbr[...]))

    def grads_rows(z_):
        return doall.at[at(T2 * z_, T2), :], lsed.at[z_]

    def grads_push(z_, to):
        for index, ref in enumerate(grads_rows(z_)):
            start(ref, ref, dos.at[index], dor.at[index, z_], to)

    sent_along_z("grads", lambda count: fall.at[pl.ds(0, T * count), :], dos.at[0])
    sent_along_z("logs", lambda count: lsed.at[pl.ds(0, count)], dos.at[1])

    def grads_arrive(k):
        def take(z_, more, direction):
            for index, ref in enumerate(grads_rows(z_)):
                arrived(ref, dor.at[index, z_])
            pl.when(more)(lambda: grads_push(z_, (zp, zm)[direction]))

        sides(k, take)

    def queries_back():
        @pl.loop(0, blocks)
        def _(b):
            lanes, value_lanes = block_lanes(b)
            heads = doall[pair_rows, lanes].astype(F32)
            product = heads * att32[:, lanes]
            pieces = []
            for which in range(2):
                delta = jnp.sum(half(product, which), axis=-1, keepdims=True)
                grad_probs = dot_nt(half(heads, which).astype(BF16), kv[:, value_lanes])
                grad_scores = probs[2 * b + which].astype(F32) * (grad_probs - delta)
                pieces.append(dot(grad_scores.astype(BF16), kv[:, lanes]))
            total = jnp.where(low_half, pieces[0], pieces[1]) * HD ** (-0.5)
            dall[:, lanes] = total.astype(BF16)

    def keys_back(z_):
        rows = at(T2 * z_, T2)

        @pl.loop(0, blocks)
        def _(b):
            lanes, value_lanes = block_lanes(b)
            queries, grads = qall[rows, lanes], doall[rows, lanes]
            scores = dot_nt(both(kv[pair_rows, lanes].astype(F32)), queries)
            grad_probs = dot_nt(both(kv[pair_rows, value_lanes].astype(F32)), grads)
            lows, grad_scores = [], []
            for which in range(2):
                part, head = slice(T2 * which, T2 * (which + 1)), 2 * b + which
                powers = jnp.exp(scores[part] + mask[:, rows] - lsed[z_, pl.ds(head, 1), :])
                shifted = grad_probs[part] - lsed[z_, pl.ds(8 + head, 1), :]
                lows.append(powers.astype(BF16))
                grad_scores.append((powers * shifted).astype(BF16))
            dkv32[:, lanes] += pick(dot(jnp.concatenate(grad_scores, axis=0), queries))
            dkv32[:, value_lanes] += pick(dot(jnp.concatenate(lows, axis=0), grads))

    def keys_back_at(k):
        pl.when(z - k >= 0)(lambda: keys_back(z - k))
        if k > 0:
            pl.when(z + k <= 3)(lambda: keys_back(z + k))

    def query_weights():
        matrix_put(0, 0, dot_tn(dall[:, pl.ds(0, HW)], fall[pair_rows, :]))
        matrices_send(0)

    def key_value_weights():
        dall[:, pl.ds(HW, D)] = dkv32[...].astype(BF16)
        grads = dot_tn(dall[:, pl.ds(HW, D)], fall[pair_rows, :])
        matrix_put(1, 0, grads[:HW, :])
        matrix_put(1, 1, grads[HW:, :])
        matrices_send(1)

    def input_grad():
        into = dot_nt(dall[...], wqkv[...])
        dxo[...] = into
        dxs[...] = dxo[other, :].astype(BF16)
        start(dxs, dxr, *one("dx"), yn)
        sums = jnp.sum(dall[...].astype(F32), axis=0, keepdims=True)
        vectors[0:1, heads_here] = sums[:, :HW]
        vectors[1:2, heads_here] = sums[:, 2 * HW :]

    def input_grad_end():
        arrived(dxr, got_of("dx"))
        frames_grad[...] = gfirst[...] + dxo[mine, :] + dxr[...].astype(F32)

    def attention_x(family):
        arrived(dr.at[family], got_of(("d", family)))
        xs[family] = (gm[family, c, 1 - x].astype(F32) + dr[family, 1 - x].astype(F32)).astype(BF16)
        start(xs.at[family], xr.at[family], *one(("xs", family)), xn)

    def attention_z(family):
        arrived(xr.at[family], got_of(("xs", family)))
        total = gm[family, c, x].astype(F32) + dr[family, x].astype(F32) + xr[family].astype(F32)
        parts[4 + family][...] = total.astype(BF16)
        sum_send(4 + family)

    def pair_half(t, half_):
        columns = at(FO * half_, FO)
        if t == DOWN:
            return dot_tn(ar[:, columns], fq[...])
        return dot_tn(hq[...], br[:, columns])

    def pair_send(t):
        half_ = pair_half(t, 1 - c).astype(BF16)
        rows = half_.shape[0] // 2
        for q in range(2):
            given[t][q] = half_[rows * q : rows * (q + 1)]
            start(given[t].at[q], taken[t].at[q], *one(("pair", t, q), ("pair", t)), sib)
        half_ = pair_half(t, c)
        for q in range(2):
            kept[t][q] = half_[rows * q : rows * (q + 1)]

    def pair_add(family):
        t, q = family // 2, family % 2
        arrived(taken[t].at[q], got_of(("pair", t, q)))
        parts[family][...] = (kept[t][q] + taken[t][q].astype(F32)).astype(BF16)
        sum_send(family)

    def vector_step(i, to):
        vsend[i] = vectors[...]
        start(vsend.at[i], vrecv.at[i], *one(("v", i)), to)

    def vector_add(i):
        arrived(vrecv.at[i], got_of(("v", i)))
        vectors[...] += vrecv[i]

    def vector_z():
        vsend[3] = vectors[...]
        vz[z] = vectors[...]
        for k in (1, 2, 3):
            j = lax.rem(z + k, 4)
            start(vsend.at[3], vz.at[z], vzs.at[0], vzr.at[z], device(x, c, y, j))

    def vector_end():
        for k in (1, 2, 3):
            j = lax.rem(z + k, 4)
            arrived(vz.at[j], vzr.at[j])
        vectors[...] = (vz[0] + vz[1]) + (vz[2] + vz[3])

    dkv32[...] = jnp.zeros_like(dkv32)
    for t in range(6):
        sent(("sum", t), parts[t].at[pl.ds(0, 3 * slab_rows[t]), :], zss.at[t])
    for t in (DOWN, UP):
        sent(("pair", t), given[t], group(("pair", t)))
    sent("dx", dxs, group("dx"))
    for family in range(2):
        sent(("d", family), dr.at[family], group(("d", family)))
        sent(("xs", family), xs.at[family], group(("xs", family)))
    for i in range(3):
        sent(("v", i), vsend.at[i], group(("v", i)))
    sent("vz", vz.at[pl.ds(0, 3)], vzs.at[0])
    from_x(hq, "hid")
    from_y(hq, "hid")
    rest_x(hq, "hid")
    rest_y(hq, "hid")
    from_y(fq, "ffn")
    plane_active(x, 1 - y)
    plane_active(1 - x, y)
    out_back()
    from_x(fq, "ffn")
    rest_y(fq, "ffn")
    queries_back()
    rest_x(fq, "ffn")
    from_diagonal(hq, "hid")
    plane_active(1 - x, 1 - y)
    from_diagonal(fq, "ffn")
    pair_send(DOWN)
    grads_arrive(1)
    pair_add(DOWN_0)
    plane_back(1 - x, 1 - y)
    query_weights()
    plane_back(x, 1 - y)
    keys_back_at(1)
    attention_x(0)
    sum_pass(DOWN_0)
    pair_add(DOWN_1)
    plane_back(1 - x, y)
    grads_arrive(2)
    pair_send(UP)
    sum_pass(DOWN_1)
    keys_back_at(2)
    sum_end(DOWN_0)
    gather_own(DOWN_0)
    keys_back_at(0)
    pair_add(UP_0)
    sum_end(DOWN_1)
    gather_own(DOWN_1)
    grads_arrive(3)
    keys_back_at(3)
    gather_z(DOWN_0, 1)
    key_value_weights()
    pair_add(UP_1)
    sum_pass(UP_0)
    attention_x(1)
    input_grad()
    gather_z(DOWN_0, 2)
    attention_z(0)
    sum_pass(UP_1)
    gather_z(DOWN_1, 1)
    vector_step(0, sib)
    plane_first(DOWN_1)
    gather_z(DOWN_0, 3)
    gather_second(DOWN_0, 0)
    sum_end(UP_0)
    gather_own(UP_0)
    sum_end(UP_1)
    gather_own(UP_1)
    attention_z(1)
    gather_z(DOWN_1, 2)
    sum_pass(QUERY_OUT)
    plane_second(DOWN_1)
    gather_z(UP_1, 1)
    vector_add(0)
    plane_out(DOWN_1)
    gather_second(DOWN_1, 0)
    gather_z(UP_1, 2)
    sum_pass(KEY_VALUE)
    sum_end(QUERY_OUT)
    gather_z(UP_0, 1)
    plane_first(UP_1)
    plane_z(DOWN_1, 1)
    gather_own(QUERY_OUT)
    sum_end(KEY_VALUE)
    gather_second(DOWN_0, 2)
    gather_own(KEY_VALUE)
    gather_second(DOWN_1, 2)
    gather_z(UP_1, 3)
    gather_z(UP_0, 2)
    plane_second(UP_1)
    gather_z(DOWN_1, 3)
    plane_out(UP_1)
    plane_first(QUERY_OUT)
    input_grad_end()
    gather_third(DOWN_0, 2)
    gather_second(UP_1, 1)
    gather_z(QUERY_OUT, 1)
    gather_z(KEY_VALUE, 1)
    gather_second(UP_1, 2)
    gather_second(DOWN_1, 3)
    vector_step(1, xn)
    gather_second(DOWN_0, 3)
    plane_z(DOWN_1, 2)
    gather_z(QUERY_OUT, 2)
    plane_second(QUERY_OUT)
    gather_z(UP_0, 3)
    gather_second(UP_0, 2)
    gather_second(DOWN_0, 1)
    plane_z(UP_1, 1)
    gather_z(KEY_VALUE, 2)
    plane_out(QUERY_OUT)
    gather_third(DOWN_1, 0)
    vector_add(1)
    gather_z(KEY_VALUE, 3)
    gather_second(DOWN_1, 1)
    vector_step(2, yn)
    gather_third(DOWN_1, 2)
    plane_z(QUERY_OUT, 1)
    gather_second(KEY_VALUE, 0)
    gather_second(QUERY_OUT, 1)
    gather_second(UP_1, 3)
    gather_second(QUERY_OUT, 2)
    gather_second(QUERY_OUT, 0)
    gather_third(UP_0, 2)
    gather_second(UP_1, 0)
    gather_second(KEY_VALUE, 3)
    gather_second(UP_0, 1)
    gather_third(DOWN_1, 3)
    gather_third(UP_1, 2)
    vector_add(2)
    gather_third(DOWN_0, 1)
    plane_z(UP_1, 2)
    gather_third(QUERY_OUT, 0)
    gather_second(UP_0, 0)
    plane_z(QUERY_OUT, 2)
    gather_second(UP_0, 3)
    gather_z(QUERY_OUT, 3)
    vector_z()
    gather_second(KEY_VALUE, 2)
    gather_third(UP_0, 1)
    plane_z(DOWN_1, 3)
    gather_third(DOWN_0, 0)
    gather_third(KEY_VALUE, 3)
    gather_third(DOWN_0, 3)
    gather_second(KEY_VALUE, 1)
    gather_second(QUERY_OUT, 3)
    gather_third(UP_1, 3)
    gather_third(UP_0, 0)
    gather_third(UP_1, 0)
    gather_third(DOWN_1, 1)
    gather_third(KEY_VALUE, 2)
    gather_third(UP_1, 1)
    plane_z(UP_1, 3)
    gather_third(KEY_VALUE, 0)
    gather_third(QUERY_OUT, 1)
    gather_third(UP_0, 3)
    gather_third(QUERY_OUT, 3)
    gather_third(KEY_VALUE, 1)
    gather_third(QUERY_OUT, 2)
    plane_z(QUERY_OUT, 3)
    vector_end()
    phase("gather_end")
    gather_end()
    phase("sends_end")
    assert (len(send_names), len(names)) == (mss.shape[0], msr.shape[0])
    for wait in waits.values():
        wait()
    phase(None)


def fused_layer(
    frames,
    clip_lengths,
    query_weight,
    query_bias,
    key_weight,
    value_weight,
    value_bias,
    out_weight,
    out_bias,
    norm1_gain,
    norm1_bias,
    up_weight,
    up_bias,
    down_weight,
    down_bias,
    norm2_gain,
    norm2_bias,
    cotangent,
):
    T, D = frames.shape[1], frames.shape[2]
    F = up_weight.shape[1]
    S = T * lax.axis_size("seq")
    HW, T2, EIGHTH, FO = D // 2, 2 * T, D // 8, F // 8
    blocks = HW // LANES
    entries = clip_lengths.shape[1]
    vmem, hbm = pl.BlockSpec(memory_space=pltpu.VMEM), pl.BlockSpec(memory_space=pl.ANY)
    dma, n = pltpu.SemaphoreType.DMA, len(PIECES)
    low, wide = (lambda *shape: pltpu.VMEM(shape, BF16)), (lambda *shape: pltpu.VMEM(shape, F32))
    scratch = dict(
        frames_v=wide(T, D),
        cotangent_v=wide(T, D),
        lengths_v=pltpu.VMEM((1, entries), jnp.int32),
        **{f"v{i}": wide(D) for i in range(8)},
        up_v=wide(F),
        bias_rows=wide(8, D),
        up_rows=wide(4, 8, D),
        fall=low(S, D),
        wqkv=low(D, 3 * HW),
        wo=low(D, D),
        wup=low(D, F),
        wdn=low(F, D),
        qall=low(S, HW),
        kv=low(S, D),
        mask=wide(T2, S),
        probs=low(2 * blocks, T2, S),
        stat=wide(2, T2, LANES),
        lsed=wide(5, 16, T2),
        att32=wide(T2, HW),
        att16=low(T2, HW),
        attf=low(T, D),
        hq=low(4 * T, D),
        fq=low(4 * T, D),
        ar=low(4 * T, D),
        br=low(4 * T, D),
        actives=low(4, T, D),
        slopes=wide(4 * T, D),
        dgelu=wide(4, T, D),
        hid32=wide(T, D),
        unit1=wide(T, D),
        rstd1=wide(T, LANES),
        gmid=wide(T, D),
        gfirst=wide(T, D),
        gbr=low(T2, D),
        doall=low(S, HW),
        dkv32=wide(T2, D),
        dall=low(T2, 3 * HW),
        give_down=low(2, FO // 2, D),
        give_up=low(2, D // 2, FO),
        take_down=low(2, FO // 2, D),
        take_up=low(2, D // 2, FO),
        keep_down=wide(2, FO // 2, D),
        keep_up=wide(2, D // 2, FO),
        part_down=low(2, FO // 2, D),
        part_up=low(2, D // 2, FO),
        part_qo=low(HW // 2, D),
        part_kv=low(HW // 2, D),
        got_down=low(2, 4, FO // 8, D),
        got_up=low(2, 4, D // 8, FO),
        got_qo=low(4, HW // 8, D),
        got_kv=low(4, HW // 8, D),
        gm=low(2, 2, 2, HW // 2, D),
        dr=low(2, 2, HW // 2, D),
        xs=low(2, HW // 2, D),
        xr=low(2, HW // 2, D),
        dxs=low(T, D),
        dxr=low(T, D),
        dxo=wide(T2, D),
        vsend=wide(4, 16, D),
        vrecv=wide(3, 16, D),
        vz=wide(4, 16, D),
        wsem=dma((6,)),
        asem=dma((12,)),
        hes=dma((1,)),
        her=dma((blocks,)),
        frs=dma((CHUNKS, 8)),
        fss=dma((2,)),
        msr=dma((25,)),
        mss=dma((13,)),
        dor=dma((2, 4)),
        dos=dma((2,)),
        zsr=dma((6, 4)),
        zss=dma((6,)),
        agr=dma((n, 19)),
        ags=dma((n,)),
        agdr=dma((n,)),
        vzr=dma((4,)),
        vzs=dma((1,)),
    )
    results = pl.pallas_call(
        partial(layer_kernel, T, D, S, entries),
        out_shape=(
            pltpu.VMEM((T, D), F32),
            pltpu.VMEM((T, D), F32),
            pltpu.VMEM((16, D), F32),
            pltpu.VMEM((F, D), BF16),
            pltpu.VMEM((D, F), BF16),
            pltpu.VMEM((4 * D, D), BF16),
        ),
        in_specs=[hbm] * 18,
        out_specs=(vmem,) * 6,
        scratch_shapes=list(scratch.values()),
        compiler_params=pltpu.CompilerParams(
            collective_id=0, has_side_effects=True, vmem_limit_bytes=VMEM_GRANT
        ),
        name="layer",
    )(
        frames[0],
        cotangent[0],
        clip_lengths,
        query_weight,
        key_weight,
        value_weight,
        out_weight,
        up_weight,
        down_weight,
        query_bias,
        value_bias,
        out_bias,
        norm1_gain,
        norm1_bias,
        up_bias,
        down_bias,
        norm2_gain,
        norm2_bias,
    )
    return widen(*results)


def widen_kernel(
    last,
    T,
    D,
    encoded,
    frames_grad,
    vectors,
    down,
    up,
    attn,
    encoded_out,
    frames_grad_out,
    query_out,
    query_b,
    key_out,
    value_out,
    value_b,
    out_out,
    out_b,
    gain1,
    bias1,
    up_out,
    up_b,
    down_out,
    down_b,
    gain2,
    bias2,
    sems,
):
    step = pl.program_id(0)
    copies = [
        pltpu.make_async_copy(encoded, encoded_out, sems.at[0]),
        pltpu.make_async_copy(frames_grad, frames_grad_out, sems.at[1]),
    ]

    @pl.when(step == 0)
    def _():
        for copy in copies:
            copy.start()
        for ref, index in (
            (query_b, 0),
            (value_b, 1),
            (out_b, 2),
            (gain1, 3),
            (bias1, 4),
            (down_b, 9),
            (gain2, 10),
            (bias2, 11),
        ):
            ref[...] = vectors[index : index + 1, :].reshape(D)
        for quarter in range(4):
            up_b[pl.ds(D * quarter, D)] = vectors[5 + quarter : 6 + quarter, :].reshape(D)

    def rows(size, first=0):
        return pl.ds(pl.multiple_of(first + size * step, size), size)

    down_out[...] = down[rows(down_out.shape[0]), :].astype(F32)
    up_out[...] = up[rows(up_out.shape[0]), :].astype(F32)
    out_out[...] = attn[rows(LANES, 3 * D), :].astype(F32)
    for m, target in enumerate((query_out, key_out, value_out)):
        target[...] = attn[rows(LANES, m * D), :].astype(F32).T

    @pl.when(step == last)
    def _():
        for copy in copies:
            copy.wait()


def widen(encoded, frames_grad, vectors, sum_down, sum_up, sum_attn):
    T, D = encoded.shape
    F = sum_up.shape[1]
    steps = D // LANES
    hbm, vmem = pl.BlockSpec(memory_space=pl.ANY), pl.BlockSpec(memory_space=pltpu.VMEM)
    parts = (encoded, frames_grad, vectors, sum_down, sum_up, sum_attn)
    parts = [pltpu.with_memory_space_constraint(part, pltpu.VMEM) for part in parts]

    def down(width):
        return pl.BlockSpec((width, D), lambda i: (i, 0))

    up = pl.BlockSpec((D // steps, F), lambda i: (i, 0))
    turned = pl.BlockSpec((D, LANES), lambda i: (0, i))
    flat = pl.BlockSpec((D,), lambda i: (0,))
    wide_flat = pl.BlockSpec((F,), lambda i: (0,))
    square, vector = jax.ShapeDtypeStruct((D, D), F32), jax.ShapeDtypeStruct((D,), F32)
    tokens = jax.ShapeDtypeStruct((T, D), F32)
    outs = (
        (tokens, hbm),
        (tokens, hbm),
        (square, turned),
        (vector, flat),
        (square, turned),
        (square, turned),
        (vector, flat),
        (square, down(LANES)),
        (vector, flat),
        (vector, flat),
        (vector, flat),
        (jax.ShapeDtypeStruct((D, F), F32), up),
        (jax.ShapeDtypeStruct((F,), F32), wide_flat),
        (jax.ShapeDtypeStruct((F, D), F32), down(F // steps)),
        (vector, flat),
        (vector, flat),
        (vector, flat),
    )
    results = pl.pallas_call(
        partial(widen_kernel, steps - 1, T, D),
        grid=(steps,),
        out_shape=tuple(shape for shape, _ in outs),
        in_specs=[vmem] * 6,
        out_specs=tuple(spec for _, spec in outs),
        scratch_shapes=[pltpu.SemaphoreType.DMA((2,))],
        compiler_params=pltpu.CompilerParams(vmem_limit_bytes=VMEM_GRANT),
        name="widen",
    )(*parts)
    return (results[0][None], results[1][None]) + tuple(results[2:])


def solution(mesh):
    in_specs = (
        P("row", "seq", None),
        P("row", None),
        P(),
        P(),
        P(),
        P(),
        P(),
        P(),
        P(),
        P(),
        P(),
        P(),
        P(),
        P(),
        P(),
        P(),
        P(),
        P("row", "seq", None),
    )
    out_specs = (
        P("row", "seq", None),
        P("row", "seq", None),
        P(),
        P(),
        P(),
        P(),
        P(),
        P(),
        P(),
        P(),
        P(),
        P(),
        P(),
        P(),
        P(),
        P(),
        P(),
    )
    shape = dict(mesh.shape)
    fused = shape["row"] == 4 and shape["seq"] == 8
    return jax.shard_map(
        fused_layer if fused else per_device, mesh=mesh, in_specs=in_specs, out_specs=out_specs, check_vma=False
    )
```

```python
import contextlib
from functools import partial
import math

import jax
import jax.numpy as jnp
from jax import lax
from jax.experimental import pallas as pl
from jax.experimental.pallas import tpu as pltpu
from jax.sharding import PartitionSpec as P

H = 12
HD = 64


MASK_SCORE = -1e30
NORM_EPSILON = 1e-05


def from_behind(value, axis, by):
    count = lax.axis_size(axis)
    return lax.ppermute(value, axis, [(i, (i + by) % count) for i in range(count)])


def layer_norm(summed, norm_gain, norm_shift):
    centre = jnp.mean(summed, axis=-1, keepdims=True)
    centered = summed - centre
    inverse = lax.rsqrt(jnp.mean(centered * centered, axis=-1, keepdims=True) + NORM_EPSILON)
    normed = centered * inverse
    return (normed * norm_gain + norm_shift, normed, inverse)


def layer_norm_back(upstream, normed, inverse, norm_gain):
    scaled = upstream * norm_gain
    first_mean = jnp.mean(scaled, axis=-1, keepdims=True)
    second_mean = jnp.mean(scaled * normed, axis=-1, keepdims=True)
    summed_grad = inverse * (scaled - first_mean - normed * second_mean)
    return (summed_grad, jnp.sum(upstream * normed, axis=(0, 1)), jnp.sum(upstream, axis=(0, 1)))


def project(inputs, matrix):
    return jnp.einsum("rsk,kn->rsn", inputs, matrix, preferred_element_type=jnp.float32)


def project_back(upstream, matrix):
    return jnp.einsum("rsn,kn->rsk", upstream, matrix, preferred_element_type=jnp.float32)


def matrix_grad(inputs, upstream):
    return jnp.einsum("rsk,rsn->kn", inputs, upstream, preferred_element_type=jnp.float32)


def column_sum(upstream):
    return jnp.sum(upstream.astype(jnp.float32), axis=(0, 1))


def clip_numbers(clip_ends, position):
    return jnp.sum((clip_ends[:, None, :] <= position[None, :, None]).astype(jnp.int32), axis=-1)


def split_heads(tensor):
    return tensor.reshape(tensor.shape[0], tensor.shape[1], H, HD)


def join_heads(tensor):
    return tensor.reshape(tensor.shape[0], tensor.shape[1], H * HD)


def head_scores(queries, keys_block):
    return jnp.einsum(
        "rqhd,rkhd->rhqk", queries, keys_block, preferred_element_type=jnp.float32
    ) * HD ** (-0.5)


def allowed_pairs(query_numbers, key_numbers):
    return (query_numbers[:, :, None] == key_numbers[:, None, :])[:, None]


def online_update(running, queries, query_numbers, keys_block, values_block, key_numbers):
    run_peak, run_total, run_values = running
    allowed = allowed_pairs(query_numbers, key_numbers)
    masked = jnp.where(allowed, head_scores(queries, keys_block), MASK_SCORE)
    new_peak = jnp.maximum(run_peak, jnp.max(masked, axis=-1))
    weights = jnp.where(allowed, jnp.exp(masked - new_peak[..., None]), 0.0)
    rescale = jnp.exp(run_peak - new_peak)
    new_total = run_total * rescale + jnp.sum(weights, axis=-1)
    contrib = jnp.einsum(
        "rhqk,rkhd->rqhd",
        weights.astype(jnp.bfloat16),
        values_block,
        preferred_element_type=jnp.float32,
    )
    new_values = run_values * jnp.swapaxes(rescale, 1, 2)[..., None] + contrib
    return (new_peak, new_total, new_values)


def block_back(
    queries, grad_heads, log_total, delta_rows, query_numbers, keys_flat, values_flat, key_numbers
):
    keys_block = split_heads(keys_flat)
    values_block = split_heads(values_flat)
    allowed = allowed_pairs(query_numbers, key_numbers)
    shifted = jnp.where(
        allowed, head_scores(queries, keys_block) - log_total[..., None], MASK_SCORE
    )
    weights = jnp.exp(shifted)
    grad_weights = jnp.einsum(
        "rqhd,rkhd->rhqk", grad_heads, values_block, preferred_element_type=jnp.float32
    )
    grad_scores = (weights * (grad_weights - delta_rows[..., None])).astype(jnp.bfloat16)
    factor = HD ** (-0.5)
    query_part = (
        jnp.einsum("rhqk,rkhd->rqhd", grad_scores, keys_block, preferred_element_type=jnp.float32)
        * factor
    )
    key_part = (
        jnp.einsum("rhqk,rqhd->rkhd", grad_scores, queries, preferred_element_type=jnp.float32)
        * factor
    )
    value_part = jnp.einsum(
        "rhqk,rqhd->rkhd",
        weights.astype(jnp.bfloat16),
        grad_heads,
        preferred_element_type=jnp.float32,
    )
    return (join_heads(query_part), join_heads(key_part), join_heads(value_part))


def per_device(
    frames,
    clip_lengths,
    query_weight,
    query_bias,
    key_weight,
    value_weight,
    value_bias,
    out_weight,
    out_bias,
    norm1_gain,
    norm1_bias,
    up_weight,
    up_bias,
    down_weight,
    down_bias,
    norm2_gain,
    norm2_bias,
    cotangent,
):
    row_count = frames.shape[0]
    shard_len = frames.shape[1]
    cycle_size = lax.axis_size("seq")
    seq_place = lax.axis_index("seq")
    clip_ends = jnp.cumsum(clip_lengths, axis=1)
    offsets = jnp.arange(shard_len, dtype=jnp.int32)
    own_numbers = clip_numbers(clip_ends, seq_place * shard_len + offsets)
    frames_low = frames.astype(jnp.bfloat16)
    queries = split_heads((project(frames_low, query_weight) + query_bias).astype(jnp.bfloat16))
    keys_own = project(frames_low, key_weight).astype(jnp.bfloat16)
    values_own = (project(frames_low, value_weight) + value_bias).astype(jnp.bfloat16)
    initial = (
        jnp.full((row_count, H, shard_len), MASK_SCORE, jnp.float32),
        jnp.zeros((row_count, H, shard_len), jnp.float32),
        jnp.zeros((row_count, shard_len, H, HD), jnp.float32),
    )
    key_piece = lax.all_gather(keys_own, "seq", axis=1, tiled=True)
    value_piece = lax.all_gather(values_own, "seq", axis=1, tiled=True)
    piece_len = key_piece.shape[1]
    block_len = math.gcd(piece_len, 512)

    def attend_block(block_index, carried):
        offset = block_index * block_len
        key_block = lax.dynamic_slice_in_dim(key_piece, offset, block_len, 1)
        value_block = lax.dynamic_slice_in_dim(value_piece, offset, block_len, 1)
        position = offset + jnp.arange(block_len, dtype=jnp.int32)
        return online_update(
            carried,
            queries,
            own_numbers,
            split_heads(key_block),
            split_heads(value_block),
            clip_numbers(clip_ends, position),
        )

    run_peak, run_total, run_values = lax.fori_loop(
        0, piece_len // block_len, attend_block, initial
    )
    log_total = run_peak + jnp.log(run_total)
    attended_heads = run_values / jnp.swapaxes(run_total, 1, 2)[..., None]
    attended = join_heads(attended_heads)
    attended_low = attended.astype(jnp.bfloat16)
    branch = project(attended_low, out_weight) + out_bias
    hidden, unit_first, inverse_first = layer_norm(frames + branch, norm1_gain, norm1_bias)
    hidden_low = hidden.astype(jnp.bfloat16)
    before = project(hidden_low, up_weight) + up_bias
    active, gelu_back = jax.vjp(partial(jax.nn.gelu, approximate=False), before)
    active_low = active.astype(jnp.bfloat16)
    encoded, unit_second, inverse_second = layer_norm(
        hidden + project(active_low, down_weight) + down_bias, norm2_gain, norm2_bias
    )
    grad_mid, norm2_gain_grad, norm2_bias_grad = layer_norm_back(
        cotangent, unit_second, inverse_second, norm2_gain
    )
    grad_ffn = grad_mid.astype(jnp.bfloat16)
    down_weight_grad = matrix_grad(active_low, grad_ffn)
    down_bias_grad = column_sum(grad_ffn)
    grad_before = gelu_back(project_back(grad_ffn, down_weight))[0].astype(jnp.bfloat16)
    up_weight_grad = matrix_grad(hidden_low, grad_before)
    up_bias_grad = column_sum(grad_before)
    grad_hidden = grad_mid + project_back(grad_before, up_weight)
    grad_first, norm1_gain_grad, norm1_bias_grad = layer_norm_back(
        grad_hidden, unit_first, inverse_first, norm1_gain
    )
    grad_branch = grad_first.astype(jnp.bfloat16)
    out_weight_grad = matrix_grad(attended_low, grad_branch)
    out_bias_grad = column_sum(grad_branch)
    grad_attended = project_back(grad_branch, out_weight).astype(jnp.bfloat16)
    grad_heads = split_heads(grad_attended)
    delta_rows = jnp.swapaxes(
        jnp.sum(grad_heads.astype(jnp.float32) * attended_heads, axis=-1), 1, 2
    )
    query_start, key_start, value_start = block_back(
        queries, grad_heads, log_total, delta_rows, own_numbers, keys_own, values_own, own_numbers
    )

    def key_step(distance, carried):
        key_now, value_now, query_sum, key_sum, value_sum = carried
        key_now, value_now = from_behind((key_now, value_now), "seq", 1)
        key_sum, value_sum = (
            from_behind(key_sum.astype(jnp.bfloat16), "seq", 1).astype(key_sum.dtype),
            from_behind(value_sum.astype(jnp.bfloat16), "seq", 1).astype(value_sum.dtype),
        )
        source = (seq_place - distance) % cycle_size
        source_numbers = clip_numbers(clip_ends, source * shard_len + offsets)
        query_part, key_part, value_part = block_back(
            queries,
            grad_heads,
            log_total,
            delta_rows,
            own_numbers,
            key_now,
            value_now,
            source_numbers,
        )
        return (
            key_now,
            value_now,
            query_sum + query_part,
            key_sum + key_part,
            value_sum + value_part,
        )

    carried = lax.fori_loop(
        1, cycle_size, key_step, (keys_own, values_own, query_start, key_start, value_start)
    )
    query_total = carried[2]
    key_total, value_total = (
        from_behind(carried[3].astype(jnp.bfloat16), "seq", 1).astype(jnp.float32),
        from_behind(carried[4].astype(jnp.bfloat16), "seq", 1).astype(jnp.float32),
    )
    query_low = query_total.astype(jnp.bfloat16)
    key_low = key_total.astype(jnp.bfloat16)
    value_low = value_total.astype(jnp.bfloat16)
    query_weight_grad = matrix_grad(frames_low, query_low)
    query_bias_grad = column_sum(query_low)
    key_weight_grad = matrix_grad(frames_low, key_low)
    value_weight_grad = matrix_grad(frames_low, value_low)
    value_bias_grad = column_sum(value_low)
    frames_grad = (
        grad_first
        + project_back(query_low, query_weight)
        + project_back(key_low, key_weight)
        + project_back(value_low, value_weight)
    )
    shares = (
        lax.psum_scatter(query_weight_grad, "seq", scatter_dimension=0, tiled=True),
        lax.psum_scatter(query_bias_grad, "seq", scatter_dimension=0, tiled=True),
        lax.psum_scatter(key_weight_grad, "seq", scatter_dimension=0, tiled=True),
        lax.psum_scatter(value_weight_grad, "seq", scatter_dimension=0, tiled=True),
        lax.psum_scatter(value_bias_grad, "seq", scatter_dimension=0, tiled=True),
        lax.psum_scatter(out_weight_grad, "seq", scatter_dimension=0, tiled=True),
        lax.psum_scatter(out_bias_grad, "seq", scatter_dimension=0, tiled=True),
        lax.psum_scatter(norm1_gain_grad, "seq", scatter_dimension=0, tiled=True),
        lax.psum_scatter(norm1_bias_grad, "seq", scatter_dimension=0, tiled=True),
        lax.psum_scatter(up_weight_grad, "seq", scatter_dimension=0, tiled=True),
        lax.psum_scatter(up_bias_grad, "seq", scatter_dimension=0, tiled=True),
        lax.psum_scatter(down_weight_grad, "seq", scatter_dimension=0, tiled=True),
        lax.psum_scatter(down_bias_grad, "seq", scatter_dimension=0, tiled=True),
        lax.psum_scatter(norm2_gain_grad, "seq", scatter_dimension=0, tiled=True),
        lax.psum_scatter(norm2_bias_grad, "seq", scatter_dimension=0, tiled=True),
    )
    shares = (
        lax.psum(shares[0].astype(jnp.bfloat16), "row").astype(jnp.float32),
        lax.psum(shares[1].astype(jnp.bfloat16), "row").astype(jnp.float32),
        lax.psum(shares[2].astype(jnp.bfloat16), "row").astype(jnp.float32),
        lax.psum(shares[3].astype(jnp.bfloat16), "row").astype(jnp.float32),
        lax.psum(shares[4].astype(jnp.bfloat16), "row").astype(jnp.float32),
        lax.psum(shares[5].astype(jnp.bfloat16), "row").astype(jnp.float32),
        lax.psum(shares[6].astype(jnp.bfloat16), "row").astype(jnp.float32),
        lax.psum(shares[7].astype(jnp.bfloat16), "row").astype(jnp.float32),
        lax.psum(shares[8].astype(jnp.bfloat16), "row").astype(jnp.float32),
        lax.psum(shares[9].astype(jnp.bfloat16), "row").astype(jnp.float32),
        lax.psum(shares[10].astype(jnp.bfloat16), "row").astype(jnp.float32),
        lax.psum(shares[11].astype(jnp.bfloat16), "row").astype(jnp.float32),
        lax.psum(shares[12].astype(jnp.bfloat16), "row").astype(jnp.float32),
        lax.psum(shares[13].astype(jnp.bfloat16), "row").astype(jnp.float32),
        lax.psum(shares[14].astype(jnp.bfloat16), "row").astype(jnp.float32),
    )
    totals = (
        lax.all_gather(shares[0].astype(jnp.bfloat16), "seq", axis=0, tiled=True).astype(
            jnp.float32
        ),
        lax.all_gather(shares[1].astype(jnp.bfloat16), "seq", axis=0, tiled=True).astype(
            jnp.float32
        ),
        lax.all_gather(shares[2].astype(jnp.bfloat16), "seq", axis=0, tiled=True).astype(
            jnp.float32
        ),
        lax.all_gather(shares[3].astype(jnp.bfloat16), "seq", axis=0, tiled=True).astype(
            jnp.float32
        ),
        lax.all_gather(shares[4].astype(jnp.bfloat16), "seq", axis=0, tiled=True).astype(
            jnp.float32
        ),
        lax.all_gather(shares[5].astype(jnp.bfloat16), "seq", axis=0, tiled=True).astype(
            jnp.float32
        ),
        lax.all_gather(shares[6].astype(jnp.bfloat16), "seq", axis=0, tiled=True).astype(
            jnp.float32
        ),
        lax.all_gather(shares[7].astype(jnp.bfloat16), "seq", axis=0, tiled=True).astype(
            jnp.float32
        ),
        lax.all_gather(shares[8].astype(jnp.bfloat16), "seq", axis=0, tiled=True).astype(
            jnp.float32
        ),
        lax.all_gather(shares[9].astype(jnp.bfloat16), "seq", axis=0, tiled=True).astype(
            jnp.float32
        ),
        lax.all_gather(shares[10].astype(jnp.bfloat16), "seq", axis=0, tiled=True).astype(
            jnp.float32
        ),
        lax.all_gather(shares[11].astype(jnp.bfloat16), "seq", axis=0, tiled=True).astype(
            jnp.float32
        ),
        lax.all_gather(shares[12].astype(jnp.bfloat16), "seq", axis=0, tiled=True).astype(
            jnp.float32
        ),
        lax.all_gather(shares[13].astype(jnp.bfloat16), "seq", axis=0, tiled=True).astype(
            jnp.float32
        ),
        lax.all_gather(shares[14].astype(jnp.bfloat16), "seq", axis=0, tiled=True).astype(
            jnp.float32
        ),
    )
    return (
        encoded,
        frames_grad,
        totals[0],
        totals[1],
        totals[2],
        totals[3],
        totals[4],
        totals[5],
        totals[6],
        totals[7],
        totals[8],
        totals[9],
        totals[10],
        totals[11],
        totals[12],
        totals[13],
        totals[14],
    )


MESH = pl.DeviceIdType.MESH
LANES = 128
F32, BF16 = jnp.float32, jnp.bfloat16
VMEM_GRANT = 49 << 20
DOWN, UP = 0, 1
DOWN_0, DOWN_1, UP_0, UP_1, QUERY_OUT, KEY_VALUE = range(6)
CHUNKS = 2

PIECES = (
    (DOWN_0, "zyx", 0, 1),
    (DOWN_0, "zxy", 1, 2),
    (DOWN_1, "zyx", 0, 2),
    (DOWN_1, "xyz", 2, 1),
    (UP_0, "zyx", 0, 3),
    (UP_1, "zxy", 0, 3),
    (QUERY_OUT, "zxy", 0, 1),
    (QUERY_OUT, "yxz", 1, 2),
    (KEY_VALUE, "zyx", 0, 1),
    (KEY_VALUE, "zxy", 1, 2),
)


def gather_sems(piece):
    return 12 + 1 + 1 if piece[1][2] == "z" else 3 + 4 + 4


def dot(a, b):
    return jnp.dot(a, b, preferred_element_type=F32)


def dot_nt(a, b):
    return lax.dot_general(a, b, (((1,), (1,)), ((), ())), preferred_element_type=F32)


def dot_tn(a, b):
    return lax.dot_general(a, b, (((0,), (0,)), ((), ())), preferred_element_type=F32)


def rows_norm(value):
    centre = jnp.mean(value, axis=-1, keepdims=True)
    centered = value - centre
    inverse = lax.rsqrt(jnp.mean(centered * centered, axis=-1, keepdims=True) + NORM_EPSILON)
    return centered * inverse, inverse


def rows_norm_back(scaled, unit, inverse):
    first = jnp.mean(scaled, axis=-1, keepdims=True)
    second = jnp.mean(scaled * unit, axis=-1, keepdims=True)
    return inverse * (scaled - first - unit * second)


def layer_kernel(
    T,
    D,
    S,
    entries,
    frames,
    cotangent,
    lengths,
    query_w,
    key_w,
    value_w,
    out_w,
    up_w,
    down_w,
    query_b,
    value_b,
    out_b,
    gain1,
    bias1,
    up_b,
    down_b,
    gain2,
    bias2,
    encoded,
    frames_grad,
    vectors,
    sum_down,
    sum_up,
    sum_attn,
    frames_v,
    cotangent_v,
    lengths_v,
    v0,
    v1,
    v2,
    v3,
    v4,
    v5,
    v6,
    v7,
    up_v,
    bias_rows,
    up_rows,
    fall,
    wqkv,
    wo,
    wup,
    wdn,
    qall,
    kv,
    mask,
    probs,
    stat,
    lsed,
    att32,
    att16,
    attf,
    hq,
    fq,
    ar,
    br,
    actives,
    slopes,
    dgelu,
    hid32,
    unit1,
    rstd1,
    gmid,
    gfirst,
    gbr,
    doall,
    dkv32,
    dall,
    give_down,
    give_up,
    take_down,
    take_up,
    keep_down,
    keep_up,
    part_down,
    part_up,
    part_qo,
    part_kv,
    got_down,
    got_up,
    got_qo,
    got_kv,
    gm,
    dr,
    xs,
    xr,
    dxs,
    dxr,
    dxo,
    vsend,
    vrecv,
    vz,
    wsem,
    asem,
    hes,
    her,
    frs,
    fss,
    msr,
    mss,
    dor,
    dos,
    zsr,
    zss,
    agr,
    ags,
    agdr,
    vzr,
    vzs,
):
    HW, T2, FO = D // 2, 2 * T, wup.shape[1] // 8
    blocks = HW // LANES
    EIGHTH, SIXTEENTH = D // 8, D // 16
    row, seq = lax.axis_index("row"), lax.axis_index("seq")
    x, c = lax.div(row, 2), lax.rem(row, 2)
    z, y = lax.div(seq, 2), lax.rem(seq, 2)
    not_first, not_last = z > 0, z < 3

    def device(x_, c_, y_, z_=z):
        return (2 * x_ + c_, 2 * z_ + y_)

    def octant(x_, c_, y_):
        return 4 * y_ + 2 * x_ + c_

    sib, xn, yn = device(x, 1 - c, y), device(1 - x, c, y), device(x, c, 1 - y)
    zp, zm = device(x, c, y, jnp.minimum(z + 1, 3)), device(x, c, y, jnp.maximum(z - 1, 0))

    def many(value, of):
        return pl.multiple_of(value, of)

    def at(start, size, of=None):
        return pl.ds(many(start, size if of is None else of), size)

    waits = {}
    scope = contextlib.ExitStack()

    def phase(name):
        scope.close()
        if name:
            scope.enter_context(jax.named_scope(name))

    def send(src, dst, ssem, rsem, to):
        return pltpu.make_async_remote_copy(
            src_ref=src, dst_ref=dst, send_sem=ssem, recv_sem=rsem, device_id=to, device_id_type=MESH
        )

    def start(src, dst, ssem, rsem, to):
        send(src, dst, ssem, rsem, to).start()

    def arrived(ref, rsem):
        send(ref, ref, mss.at[0], rsem, sib).wait_recv()

    def sent(key, ref, ssem):
        waits.setdefault(key, lambda: send(ref, ref, ssem, msr.at[0], sib).wait_send())

    def sent_along_z(key, ref_of, ssem, rest=0, lines=1):
        for blocks_sent, when in ((1, (z == 0) | (z == 3)), (5, (z > 0) & (z < 3))):
            ref = ref_of(rest + lines * blocks_sent)
            wait = partial(lambda ref: send(ref, ref, ssem, msr.at[0], sib).wait_send(), ref)
            waits[key, blocks_sent] = partial(lambda when, wait: pl.when(when)(wait), when, wait)

    send_names, names = {}, {}

    def group(name):
        return mss.at[send_names.setdefault(name, len(send_names))]

    def one(name, family=None):
        return group(family or name), got_of(name)

    def got_of(name):
        return msr.at[names.setdefault(name, len(names))]

    phase("enter")
    heads_here = at(HW * y, HW)
    loads = [
        pltpu.make_async_copy(query_w.at[:, heads_here], wqkv.at[:, pl.ds(0, HW)], wsem.at[0]),
        pltpu.make_async_copy(key_w.at[:, heads_here], wqkv.at[:, pl.ds(HW, HW)], wsem.at[1]),
        pltpu.make_async_copy(value_w.at[:, heads_here], wqkv.at[:, pl.ds(2 * HW, HW)], wsem.at[2]),
        pltpu.make_async_copy(out_w, wo, wsem.at[3]),
        pltpu.make_async_copy(up_w, wup, wsem.at[4]),
        pltpu.make_async_copy(down_w, wdn, wsem.at[5]),
    ]
    barrier = pltpu.get_barrier_semaphore()
    peers = [sib, xn, yn, device(1 - x, c, 1 - y)]
    peers += [device(x, c, y, lax.rem(z + k, 4)) for k in (1, 2, 3)]
    for peer in peers:
        pl.semaphore_signal(barrier, inc=1, device_id=peer, device_id_type=MESH)
    vectors_v = (v0, v1, v2, v3, v4, v5, v6, v7)
    arrays = (frames, cotangent, lengths, query_b, value_b, out_b, gain1, bias1, up_b, down_b, gain2, bias2)
    here_ = (frames_v, cotangent_v, lengths_v, *vectors_v[:5], up_v, *vectors_v[5:])
    small = [
        pltpu.make_async_copy(array, ref, asem.at[min(i, 3)]) for i, (array, ref) in enumerate(zip(arrays, here_))
    ]
    small[0].start()
    for load in loads[:3] + small[1:] + loads[3:]:
        load.start()
    frames, cotangent, lengths = here_[:3]
    query_b, value_b, out_b, gain1, bias1, up_b, down_b, gain2, bias2 = here_[3:]
    vectors[...] = jnp.zeros_like(vectors)
    small[0].wait()
    fall[at(T * seq, T), :] = frames[...].astype(BF16)
    pl.semaphore_wait(barrier, len(peers))

    phase("frames_gather")

    CHUNK = T // CHUNKS

    def chunk(z_, y_, h):
        return fall.at[at(T * (2 * z_ + y_) + CHUNK * h, CHUNK), :]

    def push(z_, h, direction):
        to = (zp, zm, yn)[direction]
        start(chunk(z_, y, h), chunk(z_, y, h), fss.at[direction // 2], frs.at[h, 2 * z_ + y], to)

    for h in range(CHUNKS):
        pl.when(not_last)(lambda: push(z, h, 0))
        pl.when(not_first)(lambda: push(z, h, 1))
        push(z, h, 2)
    for load in small[1:3]:
        load.wait()
    nine = att32.at[pl.ds(0, (8 * D + wup.shape[1]) // HW), :]
    pltpu.make_async_copy(nine, nine, asem.at[3]).wait()
    bias_rows[0:1, :] = query_b[...].reshape(1, D)
    bias_rows[1:2, :] = value_b[...].reshape(1, D)
    for quarter in range(4):
        up_rows[quarter] = jnp.broadcast_to(up_b[pl.ds(D * quarter, D)].reshape(1, D), (8, D))
    out_b, gain1, bias1, down_b, gain2, bias2 = (
        ref[...].reshape(1, D) for ref in (out_b, gain1, bias1, down_b, gain2, bias2)
    )
    query_bias, value_bias = bias_rows[0:1, heads_here], bias_rows[1:2, heads_here]
    for load in loads[:3]:
        load.wait()

    def project_slab(z_, y_):
        rows = at(T * (2 * z_ + y_), T)
        flat = dot(fall[rows, :], wqkv[...])
        query = (flat[:, :HW] + query_bias).astype(BF16).astype(F32) * HD ** (-0.5)
        qall[rows, :] = query.astype(BF16)
        kv[rows, pl.ds(0, HW)] = flat[:, HW : 2 * HW].astype(BF16)
        kv[rows, pl.ds(HW, HW)] = (flat[:, 2 * HW :] + value_bias).astype(BF16)

    project_slab(z, y)
    key_at = lax.broadcasted_iota(jnp.int32, (1, S), 1)
    query_at = lax.broadcasted_iota(jnp.int32, (T2, 1), 0) + T2 * z
    key_number, query_number = jnp.zeros((1, S), jnp.int32), jnp.zeros((T2, 1), jnp.int32)
    clip_end = jnp.zeros((1, 1), jnp.int32)
    for entry in range(entries):
        clip_end = clip_end + lengths[0:1, entry : entry + 1]
        key_number = key_number + jnp.where(clip_end <= key_at, 1, 0)
        query_number = query_number + jnp.where(clip_end <= query_at, 1, 0)
    mask[...] = jnp.where(query_number == key_number, 0.0, MASK_SCORE)

    @pl.loop(0, 4)
    def _(k):
        left, right = z - k - 1, z + k + 1

        for h in range(CHUNKS):

            @pl.when(left >= 0)
            def _():
                arrived(chunk(left, y, h), frs.at[h, 2 * left + y])
                pl.when(not_last)(lambda: push(left, h, 0))
                push(left, h, 2)

            @pl.when(right <= 3)
            def _():
                arrived(chunk(right, y, h), frs.at[h, 2 * right + y])
                pl.when(not_first)(lambda: push(right, h, 1))
                push(right, h, 2)

        def across_y(z_):
            for h in range(CHUNKS):
                arrived(chunk(z_, 1 - y, h), frs.at[h, 2 * z_ + 1 - y])
            project_slab(z_, 1 - y)

        pl.when(left >= 0)(lambda: project_slab(left, y))
        pl.when(right <= 3)(lambda: project_slab(right, y))
        pl.when(z - k >= 0)(lambda: across_y(z - k))
        pl.when((k > 0) & (z + k <= 3))(lambda: across_y(z + k))

    sent("frames_y", fall.at[pl.ds(0, 4 * T), :], fss.at[1])
    sent_along_z("frames_z", lambda count: fall.at[pl.ds(0, T * count), :], fss.at[0])

    phase("attention")
    pair_rows = at(T2 * z, T2)
    lane = lax.broadcasted_iota(jnp.int32, (T2, LANES), 1)
    low_half = lane < HD

    def half(value, which):
        return jnp.where(low_half == (which == 0), value, 0.0)

    stat[...] = jnp.zeros_like(stat)
    mine, other = at(T * y, T), at(T * (1 - y), T)

    def heads_push(b):
        part, there = at(LANES * b, LANES), at(HW * y + LANES * b, LANES, LANES)
        return send(att16.at[other, part], attf.at[:, there], hes.at[0], her.at[b], yn)

    def both(value):
        return jnp.concatenate([half(value, 0), half(value, 1)], axis=0).astype(BF16)

    def pick(stacked):
        return jnp.where(low_half, stacked[:T2], stacked[T2:])

    def block_lanes(b):
        return at(LANES * b, LANES), at(HW + LANES * b, LANES, LANES)

    @pl.loop(0, blocks)
    def _(b):
        lanes, value_lanes = block_lanes(b)
        queries = qall[pair_rows, lanes].astype(F32)
        outs = []
        for which in range(2):
            head = 2 * b + which
            scores = dot_nt(half(queries, which).astype(BF16), kv[:, lanes]) + mask[...]
            peak = jnp.max(scores, axis=-1, keepdims=True)
            powers = jnp.exp(scores - peak)
            total = jnp.sum(powers, axis=-1, keepdims=True)
            low = (powers * (1.0 / total)).astype(BF16)
            probs[head] = low
            outs.append(dot(low, kv[:, value_lanes]))
            stat[0] = jnp.where(lane == head, peak + jnp.log(total), stat[0])
        out = jnp.where(low_half, outs[0], outs[1])
        att32[:, lanes] = out
        att16[:, lanes] = out.astype(BF16)
        heads_push(b).start()

    phase("heads_exchange")
    attf[:, heads_here] = att16[mine, :]
    lsed[z, 0:8, :] = stat[0].T[0:8, :]
    loads[3].wait()
    for b in range(blocks):
        arrived(attf.at[:, at(HW * (1 - y) + LANES * b, LANES, LANES)], her.at[b])
    sent("heads", att16.at[pl.ds(0, T), :], hes.at[0])
    phase("out_norm1")
    branch = dot(attf[...], wo[...]) + out_b
    unit, inverse = rows_norm(frames[...] + branch)
    hidden = unit * gain1 + bias1
    unit1[...] = unit
    rstd1[...] = jnp.broadcast_to(inverse, (T, LANES))
    hid32[...] = hidden
    here = at(T * (2 * y + x), T)

    def rows_of(buffer, x_, y_):
        return buffer.at[at(T * (2 * y_ + x_), T), :]

    def halves_of(buffer, x_, y_):
        first = T * (2 * y_ + x_)
        return buffer.at[at(first, T // 2), :], buffer.at[at(first + T // 2, T // 2), :]

    def share_x(buffer, name):
        top, bottom = halves_of(buffer, x, y)
        start(top, top, *one(name + "_x", name), xn)
        start(bottom, bottom, *one(name + "_x_rest", name), xn)

    def share_y(buffer, name):
        top, bottom = halves_of(buffer, x, y)
        start(bottom, bottom, *one(name + "_y", name), yn)
        start(top, top, *one(name + "_y_rest", name), yn)

    def from_x(buffer, name):
        top = halves_of(buffer, 1 - x, y)[0]
        arrived(top, got_of(name + "_x"))
        start(top, top, *one(name + "_top", name), yn)

    def from_y(buffer, name):
        bottom = halves_of(buffer, x, 1 - y)[1]
        arrived(bottom, got_of(name + "_y"))
        start(bottom, bottom, *one(name + "_bottom", name), xn)

    def rest_x(buffer, name):
        arrived(halves_of(buffer, 1 - x, y)[1], got_of(name + "_x_rest"))

    def rest_y(buffer, name):
        arrived(halves_of(buffer, x, 1 - y)[0], got_of(name + "_y_rest"))

    def from_diagonal(buffer, name):
        top, bottom = halves_of(buffer, 1 - x, 1 - y)
        arrived(top, got_of(name + "_top"))
        arrived(bottom, got_of(name + "_bottom"))

    chips = ((1 - x, y), (x, 1 - y), (1 - x, 1 - y), (x, y))

    for buffer, name in ((hq, "hid"), (fq, "ffn")):
        sent(name, buffer.at[pl.ds(0, 3 * T), :], group(name))
    hq[here, :] = hidden.astype(BF16)
    share_x(hq, "hid")
    share_y(hq, "hid")

    phase("up_gelu")
    loads[4].wait()
    scale = 2.0 ** -0.5

    def active(hidden_rows, chip):
        before = dot(hidden_rows, wup[:, at(D * chip, D)]) + up_rows[chip][0:1, :]
        rise = 0.5 * (1.0 + lax.erf(before * scale))
        slope = rise + before * jnp.exp(-0.5 * before * before) * (2.0 * math.pi) ** -0.5
        return (before * rise).astype(BF16), slope

    def grad_before(ffn_rows, chip, slope):
        return (dot_nt(ffn_rows, wdn[at(D * chip, D), :]) * slope).astype(BF16)

    for x_, y_ in chips:
        chip = 2 * y_ + x_
        actives[chip], dgelu[chip] = active(hq[here, :], chip)
    ar[here, :] = actives[2 * y + x]
    phase("down_norm2")
    loads[5].wait()
    fed = hid32[...] + down_b
    for quarter in range(4):
        fed = fed + dot(actives[quarter], wdn[pl.ds(D * quarter, D), :])
    unit2, inverse2 = rows_norm(fed)
    encoded[...] = unit2 * gain2 + bias2
    cot = cotangent[...]
    grad_mid = rows_norm_back(cot * gain2, unit2, inverse2)
    vectors[10:11, :] = jnp.sum(cot * unit2, axis=0, keepdims=True)
    vectors[11:12, :] = jnp.sum(cot, axis=0, keepdims=True)
    gmid[...] = grad_mid
    fq[here, :] = grad_mid.astype(BF16)
    share_x(fq, "ffn")
    share_y(fq, "ffn")
    vectors[9:10, :] = jnp.sum(fq[here, :].astype(F32), axis=0, keepdims=True)
    phase("ffn_back")

    def ffn_back(order):
        x_, y_ = chips[order]
        chip = 2 * y_ + x_
        low = grad_before(fq[here, :], chip, dgelu[chip])
        vectors[pl.ds(5 + chip, 1), :] = jnp.sum(low.astype(F32), axis=0, keepdims=True)
        gmid[...] += dot_nt(low, wup[:, at(D * chip, D)])
        if order == 3:
            br[here, :] = low

    def norm1_back():
        grad_hidden = gmid[...]
        unit = unit1[...]
        grad_first = rows_norm_back(grad_hidden * gain1, unit, rstd1[:, 0:1])
        vectors[3:4, :] = jnp.sum(grad_hidden * unit, axis=0, keepdims=True)
        vectors[4:5, :] = jnp.sum(grad_hidden, axis=0, keepdims=True)
        gfirst[...] = grad_first
        low = grad_first.astype(BF16)
        gbr[mine, :] = low
        vectors[2:3, :] = jnp.sum(low.astype(F32), axis=0, keepdims=True)

    def branch_send():
        start(gbr.at[mine, :], gbr.at[mine, :], *one("gbr"), yn)

    sent("gbr", gbr.at[mine, :], group("gbr"))

    def plane_active(x_, y_):
        rows = at(T * (2 * y_ + x_), T)
        ar[rows, :], slopes[rows, :] = active(hq[rows, :], 2 * y + x)

    def plane_back(x_, y_):
        rows = at(T * (2 * y_ + x_), T)
        br[rows, :] = grad_before(fq[rows, :], 2 * y + x, slopes[rows, :])

    parts = (*(part_down.at[q] for q in range(2)), *(part_up.at[q] for q in range(2)), part_qo, part_kv)
    gots = (*(got_down.at[q] for q in range(2)), *(got_up.at[q] for q in range(2)), got_qo, got_kv)
    given, taken, kept = (give_down, give_up), (take_down, take_up), (keep_down, keep_up)
    HALF = HW // 2
    slab_rows = (FO // 8, FO // 8, D // 8, D // 8, HALF // 4, HALF // 4)

    def part_slab(t, j):
        return parts[t].at[at(slab_rows[t] * j, slab_rows[t]), :]

    outer = (z == 0) | (z == 3)
    near = jnp.where(z < 2, 1 - z, 5 - z)
    inner_there, outer_there = jnp.where(z < 2, 2, 1), jnp.where(z < 2, 3, 0)

    def part_send(t, src, j, to, slot):
        start(src, gots[t].at[slot], zss.at[t], zsr.at[t, slot], device(x, c, y, to))

    def sum_send(t):

        @pl.when(outer)
        def _():
            for j in (outer_there, inner_there, near):
                part_send(t, part_slab(t, j), j, near, j)

        @pl.when(jnp.logical_not(outer))
        def _():
            part_send(t, part_slab(t, near), near, near, z)

    def sum_pass(t):
        @pl.when(jnp.logical_not(outer))
        def _():
            for j, slot in ((outer_there, z), (inner_there, outer_there)):
                got = gots[t].at[j]
                arrived(got, zsr.at[t, j])
                got[...] = (got[...].astype(F32) + part_slab(t, j)[...].astype(F32)).astype(BF16)
                part_send(t, got, j, j, slot)

    def attn_row(t, x_, y_, z_):
        matrix = 3 * x_ if t == QUERY_OUT else 1 + x_
        return D * matrix + HW * y_ + HALF * c + HALF // 4 * z_

    def own_tile(t):
        if t <= DOWN_1:
            return sum_down.at[at(FO * octant(x, c, y) + FO // 2 * t + FO // 8 * z, FO // 8), :]
        if t <= UP_1:
            return sum_up.at[at(D // 2 * (t - UP_0) + D // 8 * z, D // 8), at(FO * octant(x, c, y), FO)]
        return sum_attn.at[at(attn_row(t, x, y, z), HALF // 4), :]

    def sum_end(t):
        total = part_slab(t, z)[...].astype(F32)
        for slot in (jnp.where(outer, near, z), jnp.where(outer, inner_there, near)):
            arrived(gots[t].at[slot], zsr.at[t, slot])
            total = total + gots[t][slot].astype(F32)
        own_tile(t)[...] = total.astype(BF16)

    unit = SIXTEENTH // 3
    unit_rows = (unit, unit, 2 * unit, 2 * unit, unit, unit)

    def tile(u, x_, y_, z_):
        t, _, first, count = PIECES[u]
        rows = unit_rows[t]
        if t <= DOWN_1:
            start_row = FO * octant(x_, c, y_) + FO // 2 * t + FO // 8 * z_ + rows * first
            return sum_down.at[at(start_row, rows * count, rows), :]
        if t <= UP_1:
            start_row = D // 2 * (t - UP_0) + D // 8 * z_ + rows * first
            return sum_up.at[at(start_row, rows * count, rows), at(FO * octant(x_, c, y_), FO)]
        start_row = attn_row(t, x_, y_, z_) + rows * first
        return sum_attn.at[at(start_row, rows * count, rows), :]

    def gather_send(u, place, z_, ssem, rsem, to):
        part = tile(u, *place, z_)
        return send(part, part, ssem, rsem, to)

    def to_sibling(u, place, z_):
        gather_send(u, place, z_, ags.at[u], agdr.at[u], sib).start()

    places = ((x, y), (1 - x, y), (x, 1 - y), (1 - x, 1 - y))

    def order_of(u):
        over_y, over_x = (2, yn), (1, xn)
        return (over_y, over_x) if PIECES[u][1] in ("zyx", "yxz") else (over_x, over_y)

    def z_last(u):
        return PIECES[u][1][2] == "z"

    first_sem = [sum(gather_sems(piece) for piece in PIECES[:u]) for u in range(len(PIECES))]

    def z_sem(u, p, z_, at_z):
        return agr.at[first_sem[u] + 3 * p + lax.rem(z_ - at_z + 4, 4) - 1]

    def along_z(u, p, z_, direction):
        to = (zp, zm)[direction]
        return gather_send(u, places[p], z_, ags.at[u], z_sem(u, p, z_, (z + 1, z - 1)[direction]), to)

    def z_out(u, p):
        pl.when(not_last)(lambda: along_z(u, p, z, 0).start())
        pl.when(not_first)(lambda: along_z(u, p, z, 1).start())

    def as_many(u, count):
        return sum_down.at[pl.ds(0, unit * PIECES[u][3] * count), :]

    def second_sem(u, z_):
        return agr.at[first_sem[u] + (12 if z_last(u) else 3 + z_)]

    def third_sem(u, slot):
        return agr.at[first_sem[u] + (13 if z_last(u) else 7 + lax.rem(slot, 4))]

    def to_second(u, place, z_):
        gather_send(u, place, z_, ags.at[u], second_sem(u, z_), order_of(u)[0][1]).start()

    def to_third(u, place, slot):
        z_ = z if z_last(u) else lax.rem(slot, 4)
        gather_send(u, place, z_, ags.at[u], third_sem(u, slot), order_of(u)[1][1]).start()

    def gather_own(t):
        for u in pieces_of(t, False):
            z_out(u, 0)
        for u in pieces_of(t):
            to_second(u, places[0], z)
            to_third(u, places[0], 0 if z_last(u) else z)
            to_sibling(u, places[0], z)

    def pieces_of(t, last=None):
        return [u for u in range(len(PIECES)) if PIECES[u][0] == t and last in (None, z_last(u))]

    def sides(k, take):
        pl.when(z - k >= 0)(lambda: take(z - k, not_last, 0))
        if k > 0:
            pl.when(z + k <= 3)(lambda: take(z + k, not_first, 1))

    def gather_z(t, k):
        for u in pieces_of(t, False):

            def take(z_, more, direction):
                arrived(tile(u, *places[0], z_), z_sem(u, 0, z_, z))
                pl.when(more)(lambda: along_z(u, 0, z_, direction).start())
                to_second(u, places[0], z_)
                to_third(u, places[0], z_)
                to_sibling(u, places[0], z_)

            sides(k, take)

    def gather_second(t, k):
        for u in pieces_of(t, False):

            def take(z_, more, direction):
                place = places[order_of(u)[0][0]]
                arrived(tile(u, *place, z_), second_sem(u, z_))
                to_third(u, place, 4 + z_)
                to_sibling(u, place, z_)

            sides(k, take)

    def gather_third(t, k):
        for u in pieces_of(t, False):

            def take(z_, more, direction):
                arrived(as_many(u, 2), third_sem(u, z_))
                for p in (order_of(u)[1][0], 3):
                    to_sibling(u, places[p], z_)

            sides(k, take)

    def plane_first(t):
        for u in pieces_of(t, True):
            p = order_of(u)[0][0]
            arrived(tile(u, *places[p], z), second_sem(u, z))
            to_third(u, places[p], 1)
            to_sibling(u, places[p], z)

    def plane_second(t):
        for u in pieces_of(t, True):
            arrived(as_many(u, 2), third_sem(u, 0))
            for p in (order_of(u)[1][0], 3):
                to_sibling(u, places[p], z)

    def plane_out(t):
        for u in pieces_of(t, True):
            for p in (0, order_of(u)[0][0], order_of(u)[1][0], 3):
                z_out(u, p)

    def plane_z(t, k):
        for u in pieces_of(t, True):
            for p in (0, order_of(u)[0][0], order_of(u)[1][0], 3):

                def take(z_, more, direction):
                    arrived(tile(u, *places[p], z_), z_sem(u, p, z_, z))
                    pl.when(more)(lambda: along_z(u, p, z_, direction).start())
                    to_sibling(u, places[p], z_)

                sides(k, take)

    def gather_end():
        for u in range(len(PIECES)):
            arrived(as_many(u, 16), agdr.at[u])
            if z_last(u):
                sent_along_z(("gather", u), partial(as_many, u), ags.at[u], 19, 4)
            else:
                sent_along_z(("gather", u), partial(as_many, u), ags.at[u], 28)

    def matrix_put(family, x_, value):
        for half_ in range(2):
            gm[family, half_, x_] = value[HALF * half_ : HALF * (half_ + 1), :].astype(BF16)

    def matrices_send(family):
        start(gm.at[family, 1 - c], dr.at[family], *one(("d", family)), sib)

    def out_back():
        arrived(gbr.at[other, :], got_of("gbr"))
        da = dot_nt(gbr[...], wo[heads_here, :]).astype(BF16)
        doall[pair_rows, :] = da
        product = da.astype(F32) * att32[...]
        stat[1] = jnp.zeros((T2, LANES), F32)
        for head in range(2 * blocks):
            lanes = slice(LANES * (head // 2), LANES * (head // 2 + 1))
            delta = jnp.sum(half(product[:, lanes], head % 2), axis=-1, keepdims=True)
            stat[1] = jnp.where(lane == head, delta, stat[1])
        lsed[z, 8:16, :] = stat[1].T[0:8, :]
        pl.when(not_last)(lambda: grads_push(z, zp))
        pl.when(not_first)(lambda: grads_push(z, zm))
        matrix_put(0, 1, dot_tn(att16[...], gbr[...]))

    def grads_rows(z_):
        return doall.at[at(T2 * z_, T2), :], lsed.at[z_]

    def grads_push(z_, to):
        for index, ref in enumerate(grads_rows(z_)):
            start(ref, ref, dos.at[index], dor.at[index, z_], to)

    sent_along_z("grads", lambda count: fall.at[pl.ds(0, T * count), :], dos.at[0])
    sent_along_z("logs", lambda count: lsed.at[pl.ds(0, count)], dos.at[1])

    def grads_arrive(k):
        def take(z_, more, direction):
            for index, ref in enumerate(grads_rows(z_)):
                arrived(ref, dor.at[index, z_])
            pl.when(more)(lambda: grads_push(z_, (zp, zm)[direction]))

        sides(k, take)

    def queries_back():
        @pl.loop(0, blocks)
        def _(b):
            lanes, value_lanes = block_lanes(b)
            heads = doall[pair_rows, lanes].astype(F32)
            product = heads * att32[:, lanes]
            pieces = []
            for which in range(2):
                delta = jnp.sum(half(product, which), axis=-1, keepdims=True)
                grad_probs = dot_nt(half(heads, which).astype(BF16), kv[:, value_lanes])
                grad_scores = probs[2 * b + which].astype(F32) * (grad_probs - delta)
                pieces.append(dot(grad_scores.astype(BF16), kv[:, lanes]))
            total = jnp.where(low_half, pieces[0], pieces[1]) * HD ** (-0.5)
            dall[:, lanes] = total.astype(BF16)

    def keys_back(z_):
        rows = at(T2 * z_, T2)

        @pl.loop(0, blocks)
        def _(b):
            lanes, value_lanes = block_lanes(b)
            queries, grads = qall[rows, lanes], doall[rows, lanes]
            scores = dot_nt(both(kv[pair_rows, lanes].astype(F32)), queries)
            grad_probs = dot_nt(both(kv[pair_rows, value_lanes].astype(F32)), grads)
            lows, grad_scores = [], []
            for which in range(2):
                part, head = slice(T2 * which, T2 * (which + 1)), 2 * b + which
                powers = jnp.exp(scores[part] + mask[:, rows] - lsed[z_, pl.ds(head, 1), :])
                shifted = grad_probs[part] - lsed[z_, pl.ds(8 + head, 1), :]
                lows.append(powers.astype(BF16))
                grad_scores.append((powers * shifted).astype(BF16))
            dkv32[:, lanes] += pick(dot(jnp.concatenate(grad_scores, axis=0), queries))
            dkv32[:, value_lanes] += pick(dot(jnp.concatenate(lows, axis=0), grads))

    def keys_back_at(k):
        pl.when(z - k >= 0)(lambda: keys_back(z - k))
        if k > 0:
            pl.when(z + k <= 3)(lambda: keys_back(z + k))

    def query_weights():
        matrix_put(0, 0, dot_tn(dall[:, pl.ds(0, HW)], fall[pair_rows, :]))
        matrices_send(0)

    def key_value_weights():
        dall[:, pl.ds(HW, D)] = dkv32[...].astype(BF16)
        grads = dot_tn(dall[:, pl.ds(HW, D)], fall[pair_rows, :])
        matrix_put(1, 0, grads[:HW, :])
        matrix_put(1, 1, grads[HW:, :])
        matrices_send(1)

    def input_grad():
        into = dot_nt(dall[...], wqkv[...])
        dxo[...] = into
        dxs[...] = dxo[other, :].astype(BF16)
        start(dxs, dxr, *one("dx"), yn)
        sums = jnp.sum(dall[...].astype(F32), axis=0, keepdims=True)
        vectors[0:1, heads_here] = sums[:, :HW]
        vectors[1:2, heads_here] = sums[:, 2 * HW :]

    def input_grad_end():
        arrived(dxr, got_of("dx"))
        frames_grad[...] = gfirst[...] + dxo[mine, :] + dxr[...].astype(F32)

    def attention_x(family):
        arrived(dr.at[family], got_of(("d", family)))
        xs[family] = (gm[family, c, 1 - x].astype(F32) + dr[family, 1 - x].astype(F32)).astype(BF16)
        start(xs.at[family], xr.at[family], *one(("xs", family)), xn)

    def attention_z(family):
        arrived(xr.at[family], got_of(("xs", family)))
        total = gm[family, c, x].astype(F32) + dr[family, x].astype(F32) + xr[family].astype(F32)
        parts[4 + family][...] = total.astype(BF16)
        sum_send(4 + family)

    def pair_half(t, half_):
        columns = at(FO * half_, FO)
        if t == DOWN:
            return dot_tn(ar[:, columns], fq[...])
        return dot_tn(hq[...], br[:, columns])

    def pair_send(t):
        half_ = pair_half(t, 1 - c).astype(BF16)
        rows = half_.shape[0] // 2
        for q in range(2):
            given[t][q] = half_[rows * q : rows * (q + 1)]
            start(given[t].at[q], taken[t].at[q], *one(("pair", t, q), ("pair", t)), sib)
        half_ = pair_half(t, c)
        for q in range(2):
            kept[t][q] = half_[rows * q : rows * (q + 1)]

    def pair_add(family):
        t, q = family // 2, family % 2
        arrived(taken[t].at[q], got_of(("pair", t, q)))
        parts[family][...] = (kept[t][q] + taken[t][q].astype(F32)).astype(BF16)
        sum_send(family)

    def vector_step(i, to):
        vsend[i] = vectors[...]
        start(vsend.at[i], vrecv.at[i], *one(("v", i)), to)

    def vector_add(i):
        arrived(vrecv.at[i], got_of(("v", i)))
        vectors[...] += vrecv[i]

    def vector_z():
        vsend[3] = vectors[...]
        vz[z] = vectors[...]
        for k in (1, 2, 3):
            j = lax.rem(z + k, 4)
            start(vsend.at[3], vz.at[z], vzs.at[0], vzr.at[z], device(x, c, y, j))

    def vector_end():
        for k in (1, 2, 3):
            j = lax.rem(z + k, 4)
            arrived(vz.at[j], vzr.at[j])
        vectors[...] = (vz[0] + vz[1]) + (vz[2] + vz[3])

    dkv32[...] = jnp.zeros_like(dkv32)
    for t in range(6):
        sent(("sum", t), parts[t].at[pl.ds(0, 3 * slab_rows[t]), :], zss.at[t])
    for t in (DOWN, UP):
        sent(("pair", t), given[t], group(("pair", t)))
    sent("dx", dxs, group("dx"))
    for family in range(2):
        sent(("d", family), dr.at[family], group(("d", family)))
        sent(("xs", family), xs.at[family], group(("xs", family)))
    for i in range(3):
        sent(("v", i), vsend.at[i], group(("v", i)))
    sent("vz", vz.at[pl.ds(0, 3)], vzs.at[0])
    ffn_back(0)
    from_y(hq, "hid")
    ffn_back(1)
    ffn_back(2)
    from_y(fq, "ffn")
    ffn_back(3)
    norm1_back()
    branch_send()
    from_x(hq, "hid")
    out_back()
    rest_y(fq, "ffn")
    rest_y(hq, "hid")
    plane_active(x, 1 - y)
    rest_x(hq, "hid")
    from_x(fq, "ffn")
    queries_back()
    plane_active(1 - x, y)
    from_diagonal(hq, "hid")
    query_weights()
    plane_active(1 - x, 1 - y)
    from_diagonal(fq, "ffn")
    rest_x(fq, "ffn")
    pair_send(DOWN)
    grads_arrive(1)
    attention_x(0)
    pair_add(DOWN_1)
    plane_back(1 - x, 1 - y)
    keys_back_at(1)
    pair_add(DOWN_0)
    plane_back(1 - x, y)
    sum_pass(DOWN_1)
    grads_arrive(2)
    plane_back(x, 1 - y)
    keys_back_at(2)
    pair_send(UP)
    sum_pass(DOWN_0)
    sum_end(DOWN_1)
    gather_own(DOWN_1)
    keys_back_at(0)
    pair_add(UP_0)
    sum_end(DOWN_0)
    gather_own(DOWN_0)
    gather_second(DOWN_1, 0)
    plane_first(DOWN_1)
    grads_arrive(3)
    keys_back_at(3)
    key_value_weights()
    gather_z(DOWN_1, 1)
    pair_add(UP_1)
    gather_second(DOWN_0, 0)
    sum_pass(UP_0)
    attention_z(0)
    gather_z(DOWN_0, 1)
    attention_x(1)
    input_grad()
    vector_step(0, sib)
    sum_pass(UP_1)
    gather_z(DOWN_1, 2)
    sum_pass(QUERY_OUT)
    sum_end(UP_0)
    gather_own(UP_0)
    gather_third(DOWN_1, 0)
    sum_end(UP_1)
    gather_own(UP_1)
    gather_z(DOWN_0, 2)
    sum_end(QUERY_OUT)
    vector_add(0)
    gather_z(DOWN_1, 3)
    gather_own(QUERY_OUT)
    plane_second(DOWN_1)
    gather_z(UP_1, 1)
    vector_step(1, xn)
    attention_z(1)
    gather_z(QUERY_OUT, 1)
    plane_first(QUERY_OUT)
    input_grad_end()
    gather_second(DOWN_0, 1)
    gather_z(DOWN_0, 3)
    gather_z(QUERY_OUT, 2)
    gather_z(UP_0, 1)
    gather_z(UP_1, 2)
    sum_pass(KEY_VALUE)
    gather_z(UP_1, 3)
    gather_z(UP_0, 2)
    sum_end(KEY_VALUE)
    gather_own(KEY_VALUE)
    plane_out(DOWN_1)
    gather_second(UP_0, 1)
    gather_second(QUERY_OUT, 1)
    gather_second(DOWN_0, 3)
    gather_second(UP_1, 1)
    gather_second(QUERY_OUT, 2)
    gather_z(QUERY_OUT, 3)
    plane_z(DOWN_1, 1)
    gather_second(UP_1, 2)
    gather_second(QUERY_OUT, 0)
    gather_z(UP_0, 3)
    plane_second(QUERY_OUT)
    vector_add(1)
    gather_second(DOWN_1, 3)
    gather_second(UP_0, 0)
    gather_second(QUERY_OUT, 3)
    vector_step(2, yn)
    gather_z(KEY_VALUE, 1)
    plane_out(QUERY_OUT)
    gather_second(UP_0, 2)
    gather_second(UP_1, 3)
    gather_third(DOWN_0, 3)
    gather_third(QUERY_OUT, 2)
    gather_z(KEY_VALUE, 2)
    gather_z(KEY_VALUE, 3)
    gather_second(DOWN_1, 1)
    gather_second(UP_1, 0)
    plane_z(DOWN_1, 2)
    gather_third(UP_0, 1)
    plane_z(QUERY_OUT, 1)
    gather_third(UP_1, 1)
    gather_third(DOWN_0, 0)
    gather_third(DOWN_1, 3)
    gather_second(DOWN_0, 2)
    gather_second(UP_0, 3)
    gather_third(UP_0, 2)
    gather_third(UP_0, 0)
    gather_second(KEY_VALUE, 1)
    plane_z(DOWN_1, 3)
    vector_add(2)
    gather_third(QUERY_OUT, 1)
    gather_third(QUERY_OUT, 3)
    gather_third(UP_1, 3)
    gather_third(UP_1, 2)
    gather_third(QUERY_OUT, 0)
    gather_second(KEY_VALUE, 0)
    plane_z(QUERY_OUT, 2)
    gather_second(DOWN_1, 2)
    gather_third(DOWN_1, 1)
    vector_z()
    gather_second(KEY_VALUE, 2)
    gather_third(UP_1, 0)
    gather_third(UP_0, 3)
    gather_third(DOWN_0, 2)
    gather_second(KEY_VALUE, 3)
    gather_third(DOWN_0, 1)
    gather_third(KEY_VALUE, 1)
    gather_third(KEY_VALUE, 0)
    plane_z(QUERY_OUT, 3)
    gather_third(DOWN_1, 2)
    gather_third(KEY_VALUE, 2)
    gather_third(KEY_VALUE, 3)
    vector_end()
    phase("gather_end")
    gather_end()
    phase("sends_end")
    assert (len(send_names), len(names)) == (mss.shape[0], msr.shape[0])
    for wait in waits.values():
        wait()
    phase(None)


def fused_layer(
    frames,
    clip_lengths,
    query_weight,
    query_bias,
    key_weight,
    value_weight,
    value_bias,
    out_weight,
    out_bias,
    norm1_gain,
    norm1_bias,
    up_weight,
    up_bias,
    down_weight,
    down_bias,
    norm2_gain,
    norm2_bias,
    cotangent,
):
    T, D = frames.shape[1], frames.shape[2]
    F = up_weight.shape[1]
    S = T * lax.axis_size("seq")
    HW, T2, EIGHTH, FO = D // 2, 2 * T, D // 8, F // 8
    blocks = HW // LANES
    entries = clip_lengths.shape[1]
    vmem, hbm = pl.BlockSpec(memory_space=pltpu.VMEM), pl.BlockSpec(memory_space=pl.ANY)
    dma, n = pltpu.SemaphoreType.DMA, len(PIECES)
    low, wide = (lambda *shape: pltpu.VMEM(shape, BF16)), (lambda *shape: pltpu.VMEM(shape, F32))
    scratch = dict(
        frames_v=wide(T, D),
        cotangent_v=wide(T, D),
        lengths_v=pltpu.VMEM((1, entries), jnp.int32),
        **{f"v{i}": wide(D) for i in range(8)},
        up_v=wide(F),
        bias_rows=wide(8, D),
        up_rows=wide(4, 8, D),
        fall=low(S, D),
        wqkv=low(D, 3 * HW),
        wo=low(D, D),
        wup=low(D, F),
        wdn=low(F, D),
        qall=low(S, HW),
        kv=low(S, D),
        mask=wide(T2, S),
        probs=low(2 * blocks, T2, S),
        stat=wide(2, T2, LANES),
        lsed=wide(5, 16, T2),
        att32=wide(T2, HW),
        att16=low(T2, HW),
        attf=low(T, D),
        hq=low(4 * T, D),
        fq=low(4 * T, D),
        ar=low(4 * T, D),
        br=low(4 * T, D),
        actives=low(4, T, D),
        slopes=wide(4 * T, D),
        dgelu=wide(4, T, D),
        hid32=wide(T, D),
        unit1=wide(T, D),
        rstd1=wide(T, LANES),
        gmid=wide(T, D),
        gfirst=wide(T, D),
        gbr=low(T2, D),
        doall=low(S, HW),
        dkv32=wide(T2, D),
        dall=low(T2, 3 * HW),
        give_down=low(2, FO // 2, D),
        give_up=low(2, D // 2, FO),
        take_down=low(2, FO // 2, D),
        take_up=low(2, D // 2, FO),
        keep_down=wide(2, FO // 2, D),
        keep_up=wide(2, D // 2, FO),
        part_down=low(2, FO // 2, D),
        part_up=low(2, D // 2, FO),
        part_qo=low(HW // 2, D),
        part_kv=low(HW // 2, D),
        got_down=low(2, 4, FO // 8, D),
        got_up=low(2, 4, D // 8, FO),
        got_qo=low(4, HW // 8, D),
        got_kv=low(4, HW // 8, D),
        gm=low(2, 2, 2, HW // 2, D),
        dr=low(2, 2, HW // 2, D),
        xs=low(2, HW // 2, D),
        xr=low(2, HW // 2, D),
        dxs=low(T, D),
        dxr=low(T, D),
        dxo=wide(T2, D),
        vsend=wide(4, 16, D),
        vrecv=wide(3, 16, D),
        vz=wide(4, 16, D),
        wsem=dma((6,)),
        asem=dma((4,)),
        hes=dma((1,)),
        her=dma((blocks,)),
        frs=dma((CHUNKS, 8)),
        fss=dma((2,)),
        msr=dma((25,)),
        mss=dma((13,)),
        dor=dma((2, 4)),
        dos=dma((2,)),
        zsr=dma((6, 4)),
        zss=dma((6,)),
        agr=dma((sum(map(gather_sems, PIECES)),)),
        ags=dma((n,)),
        agdr=dma((n,)),
        vzr=dma((4,)),
        vzs=dma((1,)),
    )
    results = pl.pallas_call(
        partial(layer_kernel, T, D, S, entries),
        out_shape=(
            pltpu.VMEM((T, D), F32),
            pltpu.VMEM((T, D), F32),
            pltpu.VMEM((16, D), F32),
            pltpu.VMEM((F, D), BF16),
            pltpu.VMEM((D, F), BF16),
            pltpu.VMEM((4 * D, D), BF16),
        ),
        in_specs=[hbm] * 18,
        out_specs=(vmem,) * 6,
        scratch_shapes=list(scratch.values()),
        compiler_params=pltpu.CompilerParams(
            collective_id=0, has_side_effects=True, vmem_limit_bytes=VMEM_GRANT
        ),
        name="layer",
    )(
        frames[0],
        cotangent[0],
        clip_lengths,
        query_weight,
        key_weight,
        value_weight,
        out_weight,
        up_weight,
        down_weight,
        query_bias,
        value_bias,
        out_bias,
        norm1_gain,
        norm1_bias,
        up_bias,
        down_bias,
        norm2_gain,
        norm2_bias,
    )
    return widen(*results)


def widen_kernel(
    last,
    T,
    D,
    encoded,
    frames_grad,
    vectors,
    down,
    up,
    attn,
    encoded_out,
    frames_grad_out,
    query_out,
    query_b,
    key_out,
    value_out,
    value_b,
    out_out,
    out_b,
    gain1,
    bias1,
    up_out,
    up_b,
    down_out,
    down_b,
    gain2,
    bias2,
    sems,
):
    step = pl.program_id(0)
    copies = [
        pltpu.make_async_copy(encoded, encoded_out, sems.at[0]),
        pltpu.make_async_copy(frames_grad, frames_grad_out, sems.at[1]),
    ]

    @pl.when(step == 0)
    def _():
        for copy in copies:
            copy.start()
        for ref, index in (
            (query_b, 0),
            (value_b, 1),
            (out_b, 2),
            (gain1, 3),
            (bias1, 4),
            (down_b, 9),
            (gain2, 10),
            (bias2, 11),
        ):
            ref[...] = vectors[index : index + 1, :].reshape(D)
        for quarter in range(4):
            up_b[pl.ds(D * quarter, D)] = vectors[5 + quarter : 6 + quarter, :].reshape(D)

    def rows(size, first=0):
        return pl.ds(pl.multiple_of(first + size * step, size), size)

    down_out[...] = down[rows(down_out.shape[0]), :].astype(F32)
    up_out[...] = up[rows(up_out.shape[0]), :].astype(F32)
    out_out[...] = attn[rows(LANES, 3 * D), :].astype(F32)
    for m, target in enumerate((query_out, key_out, value_out)):
        target[...] = attn[rows(LANES, m * D), :].astype(F32).T

    @pl.when(step == last)
    def _():
        for copy in copies:
            copy.wait()


def widen(encoded, frames_grad, vectors, sum_down, sum_up, sum_attn):
    T, D = encoded.shape
    F = sum_up.shape[1]
    steps = D // LANES
    hbm, vmem = pl.BlockSpec(memory_space=pl.ANY), pl.BlockSpec(memory_space=pltpu.VMEM)
    parts = (encoded, frames_grad, vectors, sum_down, sum_up, sum_attn)
    parts = [pltpu.with_memory_space_constraint(part, pltpu.VMEM) for part in parts]

    def down(width):
        return pl.BlockSpec((width, D), lambda i: (i, 0))

    up = pl.BlockSpec((D // steps, F), lambda i: (i, 0))
    turned = pl.BlockSpec((D, LANES), lambda i: (0, i))
    flat = pl.BlockSpec((D,), lambda i: (0,))
    wide_flat = pl.BlockSpec((F,), lambda i: (0,))
    square, vector = jax.ShapeDtypeStruct((D, D), F32), jax.ShapeDtypeStruct((D,), F32)
    tokens = jax.ShapeDtypeStruct((T, D), F32)
    outs = (
        (tokens, hbm),
        (tokens, hbm),
        (square, turned),
        (vector, flat),
        (square, turned),
        (square, turned),
        (vector, flat),
        (square, down(LANES)),
        (vector, flat),
        (vector, flat),
        (vector, flat),
        (jax.ShapeDtypeStruct((D, F), F32), up),
        (jax.ShapeDtypeStruct((F,), F32), wide_flat),
        (jax.ShapeDtypeStruct((F, D), F32), down(F // steps)),
        (vector, flat),
        (vector, flat),
        (vector, flat),
    )
    results = pl.pallas_call(
        partial(widen_kernel, steps - 1, T, D),
        grid=(steps,),
        out_shape=tuple(shape for shape, _ in outs),
        in_specs=[vmem] * 6,
        out_specs=tuple(spec for _, spec in outs),
        scratch_shapes=[pltpu.SemaphoreType.DMA((2,))],
        compiler_params=pltpu.CompilerParams(vmem_limit_bytes=VMEM_GRANT),
        name="widen",
    )(*parts)
    return (results[0][None], results[1][None]) + tuple(results[2:])


def solution(mesh):
    in_specs = (
        P("row", "seq", None),
        P("row", None),
        P(),
        P(),
        P(),
        P(),
        P(),
        P(),
        P(),
        P(),
        P(),
        P(),
        P(),
        P(),
        P(),
        P(),
        P(),
        P("row", "seq", None),
    )
    out_specs = (
        P("row", "seq", None),
        P("row", "seq", None),
        P(),
        P(),
        P(),
        P(),
        P(),
        P(),
        P(),
        P(),
        P(),
        P(),
        P(),
        P(),
        P(),
        P(),
        P(),
    )
    shape = dict(mesh.shape)
    fused = shape["row"] == 4 and shape["seq"] == 8
    return jax.shard_map(
        fused_layer if fused else per_device, mesh=mesh, in_specs=in_specs, out_specs=out_specs, check_vma=False
    )
```

```python
import contextlib
from functools import partial
import math

import jax
import jax.numpy as jnp
from jax import lax
from jax.experimental import pallas as pl
from jax.experimental.pallas import tpu as pltpu
from jax.sharding import PartitionSpec as P

H = 12
HD = 64


MASK_SCORE = -1e30
NORM_EPSILON = 1e-05


def from_behind(value, axis, by):
    count = lax.axis_size(axis)
    return lax.ppermute(value, axis, [(i, (i + by) % count) for i in range(count)])


def layer_norm(summed, norm_gain, norm_shift):
    centre = jnp.mean(summed, axis=-1, keepdims=True)
    centered = summed - centre
    inverse = lax.rsqrt(jnp.mean(centered * centered, axis=-1, keepdims=True) + NORM_EPSILON)
    normed = centered * inverse
    return (normed * norm_gain + norm_shift, normed, inverse)


def layer_norm_back(upstream, normed, inverse, norm_gain):
    scaled = upstream * norm_gain
    first_mean = jnp.mean(scaled, axis=-1, keepdims=True)
    second_mean = jnp.mean(scaled * normed, axis=-1, keepdims=True)
    summed_grad = inverse * (scaled - first_mean - normed * second_mean)
    return (summed_grad, jnp.sum(upstream * normed, axis=(0, 1)), jnp.sum(upstream, axis=(0, 1)))


def project(inputs, matrix):
    return jnp.einsum("rsk,kn->rsn", inputs, matrix, preferred_element_type=jnp.float32)


def project_back(upstream, matrix):
    return jnp.einsum("rsn,kn->rsk", upstream, matrix, preferred_element_type=jnp.float32)


def matrix_grad(inputs, upstream):
    return jnp.einsum("rsk,rsn->kn", inputs, upstream, preferred_element_type=jnp.float32)


def column_sum(upstream):
    return jnp.sum(upstream.astype(jnp.float32), axis=(0, 1))


def clip_numbers(clip_ends, position):
    return jnp.sum((clip_ends[:, None, :] <= position[None, :, None]).astype(jnp.int32), axis=-1)


def split_heads(tensor):
    return tensor.reshape(tensor.shape[0], tensor.shape[1], H, HD)


def join_heads(tensor):
    return tensor.reshape(tensor.shape[0], tensor.shape[1], H * HD)


def head_scores(queries, keys_block):
    return jnp.einsum(
        "rqhd,rkhd->rhqk", queries, keys_block, preferred_element_type=jnp.float32
    ) * HD ** (-0.5)


def allowed_pairs(query_numbers, key_numbers):
    return (query_numbers[:, :, None] == key_numbers[:, None, :])[:, None]


def online_update(running, queries, query_numbers, keys_block, values_block, key_numbers):
    run_peak, run_total, run_values = running
    allowed = allowed_pairs(query_numbers, key_numbers)
    masked = jnp.where(allowed, head_scores(queries, keys_block), MASK_SCORE)
    new_peak = jnp.maximum(run_peak, jnp.max(masked, axis=-1))
    weights = jnp.where(allowed, jnp.exp(masked - new_peak[..., None]), 0.0)
    rescale = jnp.exp(run_peak - new_peak)
    new_total = run_total * rescale + jnp.sum(weights, axis=-1)
    contrib = jnp.einsum(
        "rhqk,rkhd->rqhd",
        weights.astype(jnp.bfloat16),
        values_block,
        preferred_element_type=jnp.float32,
    )
    new_values = run_values * jnp.swapaxes(rescale, 1, 2)[..., None] + contrib
    return (new_peak, new_total, new_values)


def block_back(
    queries, grad_heads, log_total, delta_rows, query_numbers, keys_flat, values_flat, key_numbers
):
    keys_block = split_heads(keys_flat)
    values_block = split_heads(values_flat)
    allowed = allowed_pairs(query_numbers, key_numbers)
    shifted = jnp.where(
        allowed, head_scores(queries, keys_block) - log_total[..., None], MASK_SCORE
    )
    weights = jnp.exp(shifted)
    grad_weights = jnp.einsum(
        "rqhd,rkhd->rhqk", grad_heads, values_block, preferred_element_type=jnp.float32
    )
    grad_scores = (weights * (grad_weights - delta_rows[..., None])).astype(jnp.bfloat16)
    factor = HD ** (-0.5)
    query_part = (
        jnp.einsum("rhqk,rkhd->rqhd", grad_scores, keys_block, preferred_element_type=jnp.float32)
        * factor
    )
    key_part = (
        jnp.einsum("rhqk,rqhd->rkhd", grad_scores, queries, preferred_element_type=jnp.float32)
        * factor
    )
    value_part = jnp.einsum(
        "rhqk,rqhd->rkhd",
        weights.astype(jnp.bfloat16),
        grad_heads,
        preferred_element_type=jnp.float32,
    )
    return (join_heads(query_part), join_heads(key_part), join_heads(value_part))


def per_device(
    frames,
    clip_lengths,
    query_weight,
    query_bias,
    key_weight,
    value_weight,
    value_bias,
    out_weight,
    out_bias,
    norm1_gain,
    norm1_bias,
    up_weight,
    up_bias,
    down_weight,
    down_bias,
    norm2_gain,
    norm2_bias,
    cotangent,
):
    row_count = frames.shape[0]
    shard_len = frames.shape[1]
    cycle_size = lax.axis_size("seq")
    seq_place = lax.axis_index("seq")
    clip_ends = jnp.cumsum(clip_lengths, axis=1)
    offsets = jnp.arange(shard_len, dtype=jnp.int32)
    own_numbers = clip_numbers(clip_ends, seq_place * shard_len + offsets)
    frames_low = frames.astype(jnp.bfloat16)
    queries = split_heads((project(frames_low, query_weight) + query_bias).astype(jnp.bfloat16))
    keys_own = project(frames_low, key_weight).astype(jnp.bfloat16)
    values_own = (project(frames_low, value_weight) + value_bias).astype(jnp.bfloat16)
    initial = (
        jnp.full((row_count, H, shard_len), MASK_SCORE, jnp.float32),
        jnp.zeros((row_count, H, shard_len), jnp.float32),
        jnp.zeros((row_count, shard_len, H, HD), jnp.float32),
    )
    key_piece = lax.all_gather(keys_own, "seq", axis=1, tiled=True)
    value_piece = lax.all_gather(values_own, "seq", axis=1, tiled=True)
    piece_len = key_piece.shape[1]
    block_len = math.gcd(piece_len, 512)

    def attend_block(block_index, carried):
        offset = block_index * block_len
        key_block = lax.dynamic_slice_in_dim(key_piece, offset, block_len, 1)
        value_block = lax.dynamic_slice_in_dim(value_piece, offset, block_len, 1)
        position = offset + jnp.arange(block_len, dtype=jnp.int32)
        return online_update(
            carried,
            queries,
            own_numbers,
            split_heads(key_block),
            split_heads(value_block),
            clip_numbers(clip_ends, position),
        )

    run_peak, run_total, run_values = lax.fori_loop(
        0, piece_len // block_len, attend_block, initial
    )
    log_total = run_peak + jnp.log(run_total)
    attended_heads = run_values / jnp.swapaxes(run_total, 1, 2)[..., None]
    attended = join_heads(attended_heads)
    attended_low = attended.astype(jnp.bfloat16)
    branch = project(attended_low, out_weight) + out_bias
    hidden, unit_first, inverse_first = layer_norm(frames + branch, norm1_gain, norm1_bias)
    hidden_low = hidden.astype(jnp.bfloat16)
    before = project(hidden_low, up_weight) + up_bias
    active, gelu_back = jax.vjp(partial(jax.nn.gelu, approximate=False), before)
    active_low = active.astype(jnp.bfloat16)
    encoded, unit_second, inverse_second = layer_norm(
        hidden + project(active_low, down_weight) + down_bias, norm2_gain, norm2_bias
    )
    grad_mid, norm2_gain_grad, norm2_bias_grad = layer_norm_back(
        cotangent, unit_second, inverse_second, norm2_gain
    )
    grad_ffn = grad_mid.astype(jnp.bfloat16)
    down_weight_grad = matrix_grad(active_low, grad_ffn)
    down_bias_grad = column_sum(grad_ffn)
    grad_before = gelu_back(project_back(grad_ffn, down_weight))[0].astype(jnp.bfloat16)
    up_weight_grad = matrix_grad(hidden_low, grad_before)
    up_bias_grad = column_sum(grad_before)
    grad_hidden = grad_mid + project_back(grad_before, up_weight)
    grad_first, norm1_gain_grad, norm1_bias_grad = layer_norm_back(
        grad_hidden, unit_first, inverse_first, norm1_gain
    )
    grad_branch = grad_first.astype(jnp.bfloat16)
    out_weight_grad = matrix_grad(attended_low, grad_branch)
    out_bias_grad = column_sum(grad_branch)
    grad_attended = project_back(grad_branch, out_weight).astype(jnp.bfloat16)
    grad_heads = split_heads(grad_attended)
    delta_rows = jnp.swapaxes(
        jnp.sum(grad_heads.astype(jnp.float32) * attended_heads, axis=-1), 1, 2
    )
    query_start, key_start, value_start = block_back(
        queries, grad_heads, log_total, delta_rows, own_numbers, keys_own, values_own, own_numbers
    )

    def key_step(distance, carried):
        key_now, value_now, query_sum, key_sum, value_sum = carried
        key_now, value_now = from_behind((key_now, value_now), "seq", 1)
        key_sum, value_sum = (
            from_behind(key_sum.astype(jnp.bfloat16), "seq", 1).astype(key_sum.dtype),
            from_behind(value_sum.astype(jnp.bfloat16), "seq", 1).astype(value_sum.dtype),
        )
        source = (seq_place - distance) % cycle_size
        source_numbers = clip_numbers(clip_ends, source * shard_len + offsets)
        query_part, key_part, value_part = block_back(
            queries,
            grad_heads,
            log_total,
            delta_rows,
            own_numbers,
            key_now,
            value_now,
            source_numbers,
        )
        return (
            key_now,
            value_now,
            query_sum + query_part,
            key_sum + key_part,
            value_sum + value_part,
        )

    carried = lax.fori_loop(
        1, cycle_size, key_step, (keys_own, values_own, query_start, key_start, value_start)
    )
    query_total = carried[2]
    key_total, value_total = (
        from_behind(carried[3].astype(jnp.bfloat16), "seq", 1).astype(jnp.float32),
        from_behind(carried[4].astype(jnp.bfloat16), "seq", 1).astype(jnp.float32),
    )
    query_low = query_total.astype(jnp.bfloat16)
    key_low = key_total.astype(jnp.bfloat16)
    value_low = value_total.astype(jnp.bfloat16)
    query_weight_grad = matrix_grad(frames_low, query_low)
    query_bias_grad = column_sum(query_low)
    key_weight_grad = matrix_grad(frames_low, key_low)
    value_weight_grad = matrix_grad(frames_low, value_low)
    value_bias_grad = column_sum(value_low)
    frames_grad = (
        grad_first
        + project_back(query_low, query_weight)
        + project_back(key_low, key_weight)
        + project_back(value_low, value_weight)
    )
    shares = (
        lax.psum_scatter(query_weight_grad, "seq", scatter_dimension=0, tiled=True),
        lax.psum_scatter(query_bias_grad, "seq", scatter_dimension=0, tiled=True),
        lax.psum_scatter(key_weight_grad, "seq", scatter_dimension=0, tiled=True),
        lax.psum_scatter(value_weight_grad, "seq", scatter_dimension=0, tiled=True),
        lax.psum_scatter(value_bias_grad, "seq", scatter_dimension=0, tiled=True),
        lax.psum_scatter(out_weight_grad, "seq", scatter_dimension=0, tiled=True),
        lax.psum_scatter(out_bias_grad, "seq", scatter_dimension=0, tiled=True),
        lax.psum_scatter(norm1_gain_grad, "seq", scatter_dimension=0, tiled=True),
        lax.psum_scatter(norm1_bias_grad, "seq", scatter_dimension=0, tiled=True),
        lax.psum_scatter(up_weight_grad, "seq", scatter_dimension=0, tiled=True),
        lax.psum_scatter(up_bias_grad, "seq", scatter_dimension=0, tiled=True),
        lax.psum_scatter(down_weight_grad, "seq", scatter_dimension=0, tiled=True),
        lax.psum_scatter(down_bias_grad, "seq", scatter_dimension=0, tiled=True),
        lax.psum_scatter(norm2_gain_grad, "seq", scatter_dimension=0, tiled=True),
        lax.psum_scatter(norm2_bias_grad, "seq", scatter_dimension=0, tiled=True),
    )
    shares = (
        lax.psum(shares[0].astype(jnp.bfloat16), "row").astype(jnp.float32),
        lax.psum(shares[1].astype(jnp.bfloat16), "row").astype(jnp.float32),
        lax.psum(shares[2].astype(jnp.bfloat16), "row").astype(jnp.float32),
        lax.psum(shares[3].astype(jnp.bfloat16), "row").astype(jnp.float32),
        lax.psum(shares[4].astype(jnp.bfloat16), "row").astype(jnp.float32),
        lax.psum(shares[5].astype(jnp.bfloat16), "row").astype(jnp.float32),
        lax.psum(shares[6].astype(jnp.bfloat16), "row").astype(jnp.float32),
        lax.psum(shares[7].astype(jnp.bfloat16), "row").astype(jnp.float32),
        lax.psum(shares[8].astype(jnp.bfloat16), "row").astype(jnp.float32),
        lax.psum(shares[9].astype(jnp.bfloat16), "row").astype(jnp.float32),
        lax.psum(shares[10].astype(jnp.bfloat16), "row").astype(jnp.float32),
        lax.psum(shares[11].astype(jnp.bfloat16), "row").astype(jnp.float32),
        lax.psum(shares[12].astype(jnp.bfloat16), "row").astype(jnp.float32),
        lax.psum(shares[13].astype(jnp.bfloat16), "row").astype(jnp.float32),
        lax.psum(shares[14].astype(jnp.bfloat16), "row").astype(jnp.float32),
    )
    totals = (
        lax.all_gather(shares[0].astype(jnp.bfloat16), "seq", axis=0, tiled=True).astype(
            jnp.float32
        ),
        lax.all_gather(shares[1].astype(jnp.bfloat16), "seq", axis=0, tiled=True).astype(
            jnp.float32
        ),
        lax.all_gather(shares[2].astype(jnp.bfloat16), "seq", axis=0, tiled=True).astype(
            jnp.float32
        ),
        lax.all_gather(shares[3].astype(jnp.bfloat16), "seq", axis=0, tiled=True).astype(
            jnp.float32
        ),
        lax.all_gather(shares[4].astype(jnp.bfloat16), "seq", axis=0, tiled=True).astype(
            jnp.float32
        ),
        lax.all_gather(shares[5].astype(jnp.bfloat16), "seq", axis=0, tiled=True).astype(
            jnp.float32
        ),
        lax.all_gather(shares[6].astype(jnp.bfloat16), "seq", axis=0, tiled=True).astype(
            jnp.float32
        ),
        lax.all_gather(shares[7].astype(jnp.bfloat16), "seq", axis=0, tiled=True).astype(
            jnp.float32
        ),
        lax.all_gather(shares[8].astype(jnp.bfloat16), "seq", axis=0, tiled=True).astype(
            jnp.float32
        ),
        lax.all_gather(shares[9].astype(jnp.bfloat16), "seq", axis=0, tiled=True).astype(
            jnp.float32
        ),
        lax.all_gather(shares[10].astype(jnp.bfloat16), "seq", axis=0, tiled=True).astype(
            jnp.float32
        ),
        lax.all_gather(shares[11].astype(jnp.bfloat16), "seq", axis=0, tiled=True).astype(
            jnp.float32
        ),
        lax.all_gather(shares[12].astype(jnp.bfloat16), "seq", axis=0, tiled=True).astype(
            jnp.float32
        ),
        lax.all_gather(shares[13].astype(jnp.bfloat16), "seq", axis=0, tiled=True).astype(
            jnp.float32
        ),
        lax.all_gather(shares[14].astype(jnp.bfloat16), "seq", axis=0, tiled=True).astype(
            jnp.float32
        ),
    )
    return (
        encoded,
        frames_grad,
        totals[0],
        totals[1],
        totals[2],
        totals[3],
        totals[4],
        totals[5],
        totals[6],
        totals[7],
        totals[8],
        totals[9],
        totals[10],
        totals[11],
        totals[12],
        totals[13],
        totals[14],
    )


MESH = pl.DeviceIdType.MESH
LANES = 128
F32, BF16 = jnp.float32, jnp.bfloat16
VMEM_GRANT = 49 << 20
DOWN, UP = 0, 1
DOWN_0, DOWN_1, UP_0, UP_1, QUERY_OUT, KEY_VALUE = range(6)
CHUNKS = 4

PIECES = (
    (DOWN_0, "zyx", 0, 1),
    (DOWN_0, "zxy", 1, 2),
    (DOWN_1, "zyx", 0, 2),
    (DOWN_1, "xyz", 2, 1),
    (UP_0, "zyx", 0, 3),
    (UP_1, "zxy", 0, 3),
    (QUERY_OUT, "zxy", 0, 1),
    (QUERY_OUT, "yxz", 1, 2),
    (KEY_VALUE, "zyx", 0, 1),
    (KEY_VALUE, "zxy", 1, 2),
)


def gather_sems(piece):
    return 12 + 1 + 1 if piece[1][2] == "z" else 3 + 4 + 4


def dot(a, b):
    return jnp.dot(a, b, preferred_element_type=F32)


def dot_nt(a, b):
    return lax.dot_general(a, b, (((1,), (1,)), ((), ())), preferred_element_type=F32)


def dot_tn(a, b):
    return lax.dot_general(a, b, (((0,), (0,)), ((), ())), preferred_element_type=F32)


def rows_norm(value):
    centre = jnp.mean(value, axis=-1, keepdims=True)
    centered = value - centre
    inverse = lax.rsqrt(jnp.mean(centered * centered, axis=-1, keepdims=True) + NORM_EPSILON)
    return centered * inverse, inverse


def rows_norm_back(scaled, unit, inverse):
    first = jnp.mean(scaled, axis=-1, keepdims=True)
    second = jnp.mean(scaled * unit, axis=-1, keepdims=True)
    return inverse * (scaled - first - unit * second)


def layer_kernel(
    T,
    D,
    S,
    entries,
    frames,
    cotangent,
    lengths,
    query_w,
    key_w,
    value_w,
    out_w,
    up_w,
    down_w,
    query_b,
    value_b,
    out_b,
    gain1,
    bias1,
    up_b,
    down_b,
    gain2,
    bias2,
    encoded,
    frames_grad,
    vectors,
    sum_down,
    sum_up,
    sum_attn,
    frames_v,
    cotangent_v,
    lengths_v,
    v0,
    v1,
    v2,
    v3,
    v4,
    v5,
    v6,
    v7,
    up_v,
    bias_rows,
    up_rows,
    fall,
    wqkv,
    wo,
    wup,
    wdn,
    qall,
    kv,
    mask,
    probs,
    stat,
    lsed,
    att32,
    att16,
    attf,
    hq,
    fq,
    ar,
    br,
    actives,
    slopes,
    dgelu,
    hid32,
    unit1,
    rstd1,
    gmid,
    gfirst,
    gbr,
    doall,
    dkv32,
    dall,
    give_down,
    give_up,
    take_down,
    take_up,
    keep_down,
    keep_up,
    part_down,
    part_up,
    part_qo,
    part_kv,
    got_down,
    got_up,
    got_qo,
    got_kv,
    gm,
    dr,
    xs,
    xr,
    dxs,
    dxr,
    dxo,
    vsend,
    vrecv,
    vz,
    wsem,
    asem,
    hes,
    her,
    frs,
    fss,
    msr,
    mss,
    dor,
    dos,
    zsr,
    zss,
    agr,
    ags,
    agdr,
    vzr,
    vzs,
):
    HW, T2, FO = D // 2, 2 * T, wup.shape[1] // 8
    blocks = HW // LANES
    EIGHTH, SIXTEENTH = D // 8, D // 16
    row, seq = lax.axis_index("row"), lax.axis_index("seq")
    x, c = lax.div(row, 2), lax.rem(row, 2)
    z, y = lax.div(seq, 2), lax.rem(seq, 2)
    not_first, not_last = z > 0, z < 3

    def device(x_, c_, y_, z_=z):
        return (2 * x_ + c_, 2 * z_ + y_)

    def octant(x_, c_, y_):
        return 4 * y_ + 2 * x_ + c_

    sib, xn, yn = device(x, 1 - c, y), device(1 - x, c, y), device(x, c, 1 - y)
    zp, zm = device(x, c, y, jnp.minimum(z + 1, 3)), device(x, c, y, jnp.maximum(z - 1, 0))

    def many(value, of):
        return pl.multiple_of(value, of)

    def at(start, size, of=None):
        return pl.ds(many(start, size if of is None else of), size)

    waits = {}
    scope = contextlib.ExitStack()

    def phase(name):
        scope.close()
        if name:
            scope.enter_context(jax.named_scope(name))

    def send(src, dst, ssem, rsem, to):
        return pltpu.make_async_remote_copy(
            src_ref=src, dst_ref=dst, send_sem=ssem, recv_sem=rsem, device_id=to, device_id_type=MESH
        )

    def start(src, dst, ssem, rsem, to):
        send(src, dst, ssem, rsem, to).start()

    def arrived(ref, rsem):
        send(ref, ref, mss.at[0], rsem, sib).wait_recv()

    def sent(key, ref, ssem):
        waits.setdefault(key, lambda: send(ref, ref, ssem, msr.at[0], sib).wait_send())

    def sent_along_z(key, ref_of, ssem, rest=0, lines=1):
        for blocks_sent, when in ((1, (z == 0) | (z == 3)), (5, (z > 0) & (z < 3))):
            ref = ref_of(rest + lines * blocks_sent)
            wait = partial(lambda ref: send(ref, ref, ssem, msr.at[0], sib).wait_send(), ref)
            waits[key, blocks_sent] = partial(lambda when, wait: pl.when(when)(wait), when, wait)

    send_names, names = {}, {}

    def group(name):
        return mss.at[send_names.setdefault(name, len(send_names))]

    def one(name, family=None):
        return group(family or name), got_of(name)

    def got_of(name):
        return msr.at[names.setdefault(name, len(names))]

    phase("enter")
    heads_here = at(HW * y, HW)
    loads = [
        pltpu.make_async_copy(query_w.at[:, heads_here], wqkv.at[:, pl.ds(0, HW)], wsem.at[0]),
        pltpu.make_async_copy(key_w.at[:, heads_here], wqkv.at[:, pl.ds(HW, HW)], wsem.at[1]),
        pltpu.make_async_copy(value_w.at[:, heads_here], wqkv.at[:, pl.ds(2 * HW, HW)], wsem.at[2]),
        pltpu.make_async_copy(out_w, wo, wsem.at[3]),
        pltpu.make_async_copy(up_w, wup, wsem.at[4]),
        pltpu.make_async_copy(down_w, wdn, wsem.at[5]),
    ]
    barrier = pltpu.get_barrier_semaphore()
    peers = [sib, xn, yn, device(1 - x, c, 1 - y)]
    peers += [device(x, c, y, lax.rem(z + k, 4)) for k in (1, 2, 3)]
    for peer in peers:
        pl.semaphore_signal(barrier, inc=1, device_id=peer, device_id_type=MESH)
    vectors_v = (v0, v1, v2, v3, v4, v5, v6, v7)
    arrays = (frames, cotangent, lengths, query_b, value_b, out_b, gain1, bias1, up_b, down_b, gain2, bias2)
    here_ = (frames_v, cotangent_v, lengths_v, *vectors_v[:5], up_v, *vectors_v[5:])
    small = [
        pltpu.make_async_copy(array, ref, asem.at[min(i, 3)]) for i, (array, ref) in enumerate(zip(arrays, here_))
    ]
    small[0].start()
    for load in loads[:3] + small[1:] + loads[3:]:
        load.start()
    frames, cotangent, lengths = here_[:3]
    query_b, value_b, out_b, gain1, bias1, up_b, down_b, gain2, bias2 = here_[3:]
    vectors[...] = jnp.zeros_like(vectors)
    small[0].wait()
    fall[at(T * seq, T), :] = frames[...].astype(BF16)
    pl.semaphore_wait(barrier, len(peers))

    phase("frames_gather")

    CHUNK = T // CHUNKS

    def chunk(z_, y_, h):
        return fall.at[at(T * (2 * z_ + y_) + CHUNK * h, CHUNK), :]

    def push(z_, h, direction):
        to = (zp, zm, yn)[direction]
        start(chunk(z_, y, h), chunk(z_, y, h), fss.at[direction // 2], frs.at[h, 2 * z_ + y], to)

    for h in range(CHUNKS):
        pl.when(not_last)(lambda: push(z, h, 0))
        pl.when(not_first)(lambda: push(z, h, 1))
        push(z, h, 2)
    for load in small[1:3]:
        load.wait()
    nine = att32.at[pl.ds(0, (8 * D + wup.shape[1]) // HW), :]
    pltpu.make_async_copy(nine, nine, asem.at[3]).wait()
    bias_rows[0:1, :] = query_b[...].reshape(1, D)
    bias_rows[1:2, :] = value_b[...].reshape(1, D)
    for quarter in range(4):
        up_rows[quarter] = jnp.broadcast_to(up_b[pl.ds(D * quarter, D)].reshape(1, D), (8, D))
    out_b, gain1, bias1, down_b, gain2, bias2 = (
        ref[...].reshape(1, D) for ref in (out_b, gain1, bias1, down_b, gain2, bias2)
    )
    query_bias, value_bias = bias_rows[0:1, heads_here], bias_rows[1:2, heads_here]
    for load in loads[:3]:
        load.wait()

    def project_slab(z_, y_):
        rows = at(T * (2 * z_ + y_), T)
        flat = dot(fall[rows, :], wqkv[...])
        query = (flat[:, :HW] + query_bias).astype(BF16).astype(F32) * HD ** (-0.5)
        qall[rows, :] = query.astype(BF16)
        kv[rows, pl.ds(0, HW)] = flat[:, HW : 2 * HW].astype(BF16)
        kv[rows, pl.ds(HW, HW)] = (flat[:, 2 * HW :] + value_bias).astype(BF16)

    project_slab(z, y)
    key_at = lax.broadcasted_iota(jnp.int32, (1, S), 1)
    query_at = lax.broadcasted_iota(jnp.int32, (T2, 1), 0) + T2 * z
    key_number, query_number = jnp.zeros((1, S), jnp.int32), jnp.zeros((T2, 1), jnp.int32)
    clip_end = jnp.zeros((1, 1), jnp.int32)
    for entry in range(entries):
        clip_end = clip_end + lengths[0:1, entry : entry + 1]
        key_number = key_number + jnp.where(clip_end <= key_at, 1, 0)
        query_number = query_number + jnp.where(clip_end <= query_at, 1, 0)
    mask[...] = jnp.where(query_number == key_number, 0.0, MASK_SCORE)

    @pl.loop(0, 4)
    def _(k):
        left, right = z - k - 1, z + k + 1

        for h in range(CHUNKS):

            @pl.when(left >= 0)
            def _():
                arrived(chunk(left, y, h), frs.at[h, 2 * left + y])
                pl.when(not_last)(lambda: push(left, h, 0))
                push(left, h, 2)

            @pl.when(right <= 3)
            def _():
                arrived(chunk(right, y, h), frs.at[h, 2 * right + y])
                pl.when(not_first)(lambda: push(right, h, 1))
                push(right, h, 2)

        def across_y(z_):
            for h in range(CHUNKS):
                arrived(chunk(z_, 1 - y, h), frs.at[h, 2 * z_ + 1 - y])
            project_slab(z_, 1 - y)

        pl.when(left >= 0)(lambda: project_slab(left, y))
        pl.when(right <= 3)(lambda: project_slab(right, y))
        pl.when(z - k >= 0)(lambda: across_y(z - k))
        pl.when((k > 0) & (z + k <= 3))(lambda: across_y(z + k))

    sent("frames_y", fall.at[pl.ds(0, 4 * T), :], fss.at[1])
    sent_along_z("frames_z", lambda count: fall.at[pl.ds(0, T * count), :], fss.at[0])

    phase("attention")
    pair_rows = at(T2 * z, T2)
    lane = lax.broadcasted_iota(jnp.int32, (T2, LANES), 1)
    low_half = lane < HD

    def half(value, which):
        return jnp.where(low_half == (which == 0), value, 0.0)

    stat[...] = jnp.zeros_like(stat)
    mine, other = at(T * y, T), at(T * (1 - y), T)

    def heads_push(b):
        part, there = at(LANES * b, LANES), at(HW * y + LANES * b, LANES, LANES)
        return send(att16.at[other, part], attf.at[:, there], hes.at[0], her.at[b], yn)

    def both(value):
        return jnp.concatenate([half(value, 0), half(value, 1)], axis=0).astype(BF16)

    def pick(stacked):
        return jnp.where(low_half, stacked[:T2], stacked[T2:])

    def block_lanes(b):
        return at(LANES * b, LANES), at(HW + LANES * b, LANES, LANES)

    @pl.loop(0, blocks)
    def _(b):
        lanes, value_lanes = block_lanes(b)
        queries = qall[pair_rows, lanes].astype(F32)
        outs = []
        for which in range(2):
            head = 2 * b + which
            scores = dot_nt(half(queries, which).astype(BF16), kv[:, lanes]) + mask[...]
            peak = jnp.max(scores, axis=-1, keepdims=True)
            powers = jnp.exp(scores - peak)
            total = jnp.sum(powers, axis=-1, keepdims=True)
            low = (powers * (1.0 / total)).astype(BF16)
            probs[head] = low
            outs.append(dot(low, kv[:, value_lanes]))
            stat[0] = jnp.where(lane == head, peak + jnp.log(total), stat[0])
        out = jnp.where(low_half, outs[0], outs[1])
        att32[:, lanes] = out
        att16[:, lanes] = out.astype(BF16)
        heads_push(b).start()

    phase("heads_exchange")
    attf[:, heads_here] = att16[mine, :]
    lsed[z, 0:8, :] = stat[0].T[0:8, :]
    loads[3].wait()
    for b in range(blocks):
        arrived(attf.at[:, at(HW * (1 - y) + LANES * b, LANES, LANES)], her.at[b])
    sent("heads", att16.at[pl.ds(0, T), :], hes.at[0])
    phase("out_norm1")
    branch = dot(attf[...], wo[...]) + out_b
    unit, inverse = rows_norm(frames[...] + branch)
    hidden = unit * gain1 + bias1
    unit1[...] = unit
    rstd1[...] = jnp.broadcast_to(inverse, (T, LANES))
    hid32[...] = hidden
    here = at(T * (2 * y + x), T)

    def rows_of(buffer, x_, y_):
        return buffer.at[at(T * (2 * y_ + x_), T), :]

    def halves_of(buffer, x_, y_):
        first = T * (2 * y_ + x_)
        return buffer.at[at(first, T // 2), :], buffer.at[at(first + T // 2, T // 2), :]

    def share_x(buffer, name):
        top, bottom = halves_of(buffer, x, y)
        start(top, top, *one(name + "_x", name), xn)
        start(bottom, bottom, *one(name + "_x_rest", name), xn)

    def share_y(buffer, name):
        top, bottom = halves_of(buffer, x, y)
        start(bottom, bottom, *one(name + "_y", name), yn)
        start(top, top, *one(name + "_y_rest", name), yn)

    def from_x(buffer, name):
        top = halves_of(buffer, 1 - x, y)[0]
        arrived(top, got_of(name + "_x"))
        start(top, top, *one(name + "_top", name), yn)

    def from_y(buffer, name):
        bottom = halves_of(buffer, x, 1 - y)[1]
        arrived(bottom, got_of(name + "_y"))
        start(bottom, bottom, *one(name + "_bottom", name), xn)

    def rest_x(buffer, name):
        arrived(halves_of(buffer, 1 - x, y)[1], got_of(name + "_x_rest"))

    def rest_y(buffer, name):
        arrived(halves_of(buffer, x, 1 - y)[0], got_of(name + "_y_rest"))

    def from_diagonal(buffer, name):
        top, bottom = halves_of(buffer, 1 - x, 1 - y)
        arrived(top, got_of(name + "_top"))
        arrived(bottom, got_of(name + "_bottom"))

    chips = ((1 - x, y), (x, 1 - y), (1 - x, 1 - y), (x, y))

    for buffer, name in ((hq, "hid"), (fq, "ffn")):
        sent(name, buffer.at[pl.ds(0, 3 * T), :], group(name))
    hq[here, :] = hidden.astype(BF16)
    share_x(hq, "hid")
    share_y(hq, "hid")

    phase("up_gelu")
    loads[4].wait()
    scale = 2.0 ** -0.5

    def active(hidden_rows, chip):
        before = dot(hidden_rows, wup[:, at(D * chip, D)]) + up_rows[chip][0:1, :]
        rise = 0.5 * (1.0 + lax.erf(before * scale))
        slope = rise + before * jnp.exp(-0.5 * before * before) * (2.0 * math.pi) ** -0.5
        return (before * rise).astype(BF16), slope

    def grad_before(ffn_rows, chip, slope):
        return (dot_nt(ffn_rows, wdn[at(D * chip, D), :]) * slope).astype(BF16)

    for x_, y_ in chips:
        chip = 2 * y_ + x_
        actives[chip], dgelu[chip] = active(hq[here, :], chip)
    ar[here, :] = actives[2 * y + x]
    phase("down_norm2")
    loads[5].wait()
    fed = hid32[...] + down_b
    for quarter in range(4):
        fed = fed + dot(actives[quarter], wdn[pl.ds(D * quarter, D), :])
    unit2, inverse2 = rows_norm(fed)
    encoded[...] = unit2 * gain2 + bias2
    cot = cotangent[...]
    grad_mid = rows_norm_back(cot * gain2, unit2, inverse2)
    vectors[10:11, :] = jnp.sum(cot * unit2, axis=0, keepdims=True)
    vectors[11:12, :] = jnp.sum(cot, axis=0, keepdims=True)
    gmid[...] = grad_mid
    fq[here, :] = grad_mid.astype(BF16)
    share_x(fq, "ffn")
    share_y(fq, "ffn")
    vectors[9:10, :] = jnp.sum(fq[here, :].astype(F32), axis=0, keepdims=True)
    phase("ffn_back")

    def ffn_back(order):
        x_, y_ = chips[order]
        chip = 2 * y_ + x_
        low = grad_before(fq[here, :], chip, dgelu[chip])
        vectors[pl.ds(5 + chip, 1), :] = jnp.sum(low.astype(F32), axis=0, keepdims=True)
        gmid[...] += dot_nt(low, wup[:, at(D * chip, D)])
        if order == 3:
            br[here, :] = low

    def norm1_back():
        grad_hidden = gmid[...]
        unit = unit1[...]
        grad_first = rows_norm_back(grad_hidden * gain1, unit, rstd1[:, 0:1])
        vectors[3:4, :] = jnp.sum(grad_hidden * unit, axis=0, keepdims=True)
        vectors[4:5, :] = jnp.sum(grad_hidden, axis=0, keepdims=True)
        gfirst[...] = grad_first
        low = grad_first.astype(BF16)
        gbr[mine, :] = low
        vectors[2:3, :] = jnp.sum(low.astype(F32), axis=0, keepdims=True)

    def branch_send():
        start(gbr.at[mine, :], gbr.at[mine, :], *one("gbr"), yn)

    sent("gbr", gbr.at[mine, :], group("gbr"))

    def plane_active(x_, y_):
        rows = at(T * (2 * y_ + x_), T)
        ar[rows, :], slopes[rows, :] = active(hq[rows, :], 2 * y + x)

    def plane_back(x_, y_):
        rows = at(T * (2 * y_ + x_), T)
        br[rows, :] = grad_before(fq[rows, :], 2 * y + x, slopes[rows, :])

    parts = (*(part_down.at[q] for q in range(2)), *(part_up.at[q] for q in range(2)), part_qo, part_kv)
    gots = (*(got_down.at[q] for q in range(2)), *(got_up.at[q] for q in range(2)), got_qo, got_kv)
    given, taken, kept = (give_down, give_up), (take_down, take_up), (keep_down, keep_up)
    HALF = HW // 2
    slab_rows = (FO // 8, FO // 8, D // 8, D // 8, HALF // 4, HALF // 4)

    def part_slab(t, j):
        return parts[t].at[at(slab_rows[t] * j, slab_rows[t]), :]

    outer = (z == 0) | (z == 3)
    near = jnp.where(z < 2, 1 - z, 5 - z)
    inner_there, outer_there = jnp.where(z < 2, 2, 1), jnp.where(z < 2, 3, 0)

    def part_send(t, src, j, to, slot):
        start(src, gots[t].at[slot], zss.at[t], zsr.at[t, slot], device(x, c, y, to))

    def sum_send(t):

        @pl.when(outer)
        def _():
            for j in (outer_there, inner_there, near):
                part_send(t, part_slab(t, j), j, near, j)

        @pl.when(jnp.logical_not(outer))
        def _():
            part_send(t, part_slab(t, near), near, near, z)

    def sum_pass(t):
        @pl.when(jnp.logical_not(outer))
        def _():
            for j, slot in ((outer_there, z), (inner_there, outer_there)):
                got = gots[t].at[j]
                arrived(got, zsr.at[t, j])
                got[...] = (got[...].astype(F32) + part_slab(t, j)[...].astype(F32)).astype(BF16)
                part_send(t, got, j, j, slot)

    def attn_row(t, x_, y_, z_):
        matrix = 3 * x_ if t == QUERY_OUT else 1 + x_
        return D * matrix + HW * y_ + HALF * c + HALF // 4 * z_

    def own_tile(t):
        if t <= DOWN_1:
            return sum_down.at[at(FO * octant(x, c, y) + FO // 2 * t + FO // 8 * z, FO // 8), :]
        if t <= UP_1:
            return sum_up.at[at(D // 2 * (t - UP_0) + D // 8 * z, D // 8), at(FO * octant(x, c, y), FO)]
        return sum_attn.at[at(attn_row(t, x, y, z), HALF // 4), :]

    def sum_end(t):
        total = part_slab(t, z)[...].astype(F32)
        for slot in (jnp.where(outer, near, z), jnp.where(outer, inner_there, near)):
            arrived(gots[t].at[slot], zsr.at[t, slot])
            total = total + gots[t][slot].astype(F32)
        own_tile(t)[...] = total.astype(BF16)

    unit = SIXTEENTH // 3
    unit_rows = (unit, unit, 2 * unit, 2 * unit, unit, unit)

    def tile(u, x_, y_, z_):
        t, _, first, count = PIECES[u]
        rows = unit_rows[t]
        if t <= DOWN_1:
            start_row = FO * octant(x_, c, y_) + FO // 2 * t + FO // 8 * z_ + rows * first
            return sum_down.at[at(start_row, rows * count, rows), :]
        if t <= UP_1:
            start_row = D // 2 * (t - UP_0) + D // 8 * z_ + rows * first
            return sum_up.at[at(start_row, rows * count, rows), at(FO * octant(x_, c, y_), FO)]
        start_row = attn_row(t, x_, y_, z_) + rows * first
        return sum_attn.at[at(start_row, rows * count, rows), :]

    def gather_send(u, place, z_, ssem, rsem, to):
        part = tile(u, *place, z_)
        return send(part, part, ssem, rsem, to)

    def to_sibling(u, place, z_):
        gather_send(u, place, z_, ags.at[u], agdr.at[u], sib).start()

    places = ((x, y), (1 - x, y), (x, 1 - y), (1 - x, 1 - y))

    def order_of(u):
        over_y, over_x = (2, yn), (1, xn)
        return (over_y, over_x) if PIECES[u][1] in ("zyx", "yxz") else (over_x, over_y)

    def z_last(u):
        return PIECES[u][1][2] == "z"

    first_sem = [sum(gather_sems(piece) for piece in PIECES[:u]) for u in range(len(PIECES))]

    def z_sem(u, p, z_, at_z):
        return agr.at[first_sem[u] + 3 * p + lax.rem(z_ - at_z + 4, 4) - 1]

    def along_z(u, p, z_, direction):
        to = (zp, zm)[direction]
        return gather_send(u, places[p], z_, ags.at[u], z_sem(u, p, z_, (z + 1, z - 1)[direction]), to)

    def z_out(u, p):
        pl.when(not_last)(lambda: along_z(u, p, z, 0).start())
        pl.when(not_first)(lambda: along_z(u, p, z, 1).start())

    def as_many(u, count):
        return sum_down.at[pl.ds(0, unit * PIECES[u][3] * count), :]

    def second_sem(u, z_):
        return agr.at[first_sem[u] + (12 if z_last(u) else 3 + z_)]

    def third_sem(u, slot):
        return agr.at[first_sem[u] + (13 if z_last(u) else 7 + lax.rem(slot, 4))]

    def to_second(u, place, z_):
        gather_send(u, place, z_, ags.at[u], second_sem(u, z_), order_of(u)[0][1]).start()

    def to_third(u, place, slot):
        z_ = z if z_last(u) else lax.rem(slot, 4)
        gather_send(u, place, z_, ags.at[u], third_sem(u, slot), order_of(u)[1][1]).start()

    def gather_own(t):
        for u in pieces_of(t, False):
            z_out(u, 0)
        for u in pieces_of(t):
            to_second(u, places[0], z)
            to_third(u, places[0], 0 if z_last(u) else z)
            to_sibling(u, places[0], z)

    def pieces_of(t, last=None):
        return [u for u in range(len(PIECES)) if PIECES[u][0] == t and last in (None, z_last(u))]

    def sides(k, take):
        pl.when(z - k >= 0)(lambda: take(z - k, not_last, 0))
        if k > 0:
            pl.when(z + k <= 3)(lambda: take(z + k, not_first, 1))

    def gather_z(t, k):
        for u in pieces_of(t, False):

            def take(z_, more, direction):
                arrived(tile(u, *places[0], z_), z_sem(u, 0, z_, z))
                pl.when(more)(lambda: along_z(u, 0, z_, direction).start())
                to_second(u, places[0], z_)
                to_third(u, places[0], z_)
                to_sibling(u, places[0], z_)

            sides(k, take)

    def gather_second(t, k):
        for u in pieces_of(t, False):

            def take(z_, more, direction):
                place = places[order_of(u)[0][0]]
                arrived(tile(u, *place, z_), second_sem(u, z_))
                to_third(u, place, 4 + z_)
                to_sibling(u, place, z_)

            sides(k, take)

    def gather_third(t, k):
        for u in pieces_of(t, False):

            def take(z_, more, direction):
                arrived(as_many(u, 2), third_sem(u, z_))
                for p in (order_of(u)[1][0], 3):
                    to_sibling(u, places[p], z_)

            sides(k, take)

    def plane_first(t):
        for u in pieces_of(t, True):
            p = order_of(u)[0][0]
            arrived(tile(u, *places[p], z), second_sem(u, z))
            to_third(u, places[p], 1)
            to_sibling(u, places[p], z)

    def plane_second(t):
        for u in pieces_of(t, True):
            arrived(as_many(u, 2), third_sem(u, 0))
            for p in (order_of(u)[1][0], 3):
                to_sibling(u, places[p], z)

    def plane_out(t):
        for u in pieces_of(t, True):
            for p in (0, order_of(u)[0][0], order_of(u)[1][0], 3):
                z_out(u, p)

    def plane_z(t, k):
        for u in pieces_of(t, True):
            for p in (0, order_of(u)[0][0], order_of(u)[1][0], 3):

                def take(z_, more, direction):
                    arrived(tile(u, *places[p], z_), z_sem(u, p, z_, z))
                    pl.when(more)(lambda: along_z(u, p, z_, direction).start())
                    to_sibling(u, places[p], z_)

                sides(k, take)

    def gather_end():
        for u in range(len(PIECES)):
            arrived(as_many(u, 16), agdr.at[u])
            if z_last(u):
                sent_along_z(("gather", u), partial(as_many, u), ags.at[u], 19, 4)
            else:
                sent_along_z(("gather", u), partial(as_many, u), ags.at[u], 28)

    def matrix_put(family, x_, value):
        for half_ in range(2):
            gm[family, half_, x_] = value[HALF * half_ : HALF * (half_ + 1), :].astype(BF16)

    def matrices_send(family):
        start(gm.at[family, 1 - c], dr.at[family], *one(("d", family)), sib)

    def out_back():
        arrived(gbr.at[other, :], got_of("gbr"))
        da = dot_nt(gbr[...], wo[heads_here, :]).astype(BF16)
        doall[pair_rows, :] = da
        product = da.astype(F32) * att32[...]
        stat[1] = jnp.zeros((T2, LANES), F32)
        for head in range(2 * blocks):
            lanes = slice(LANES * (head // 2), LANES * (head // 2 + 1))
            delta = jnp.sum(half(product[:, lanes], head % 2), axis=-1, keepdims=True)
            stat[1] = jnp.where(lane == head, delta, stat[1])
        lsed[z, 8:16, :] = stat[1].T[0:8, :]
        pl.when(not_last)(lambda: grads_push(z, zp))
        pl.when(not_first)(lambda: grads_push(z, zm))
        matrix_put(0, 1, dot_tn(att16[...], gbr[...]))

    def grads_rows(z_):
        return doall.at[at(T2 * z_, T2), :], lsed.at[z_]

    def grads_push(z_, to):
        for index, ref in enumerate(grads_rows(z_)):
            start(ref, ref, dos.at[index], dor.at[index, z_], to)

    sent_along_z("grads", lambda count: fall.at[pl.ds(0, T * count), :], dos.at[0])
    sent_along_z("logs", lambda count: lsed.at[pl.ds(0, count)], dos.at[1])

    def grads_arrive(k):
        def take(z_, more, direction):
            for index, ref in enumerate(grads_rows(z_)):
                arrived(ref, dor.at[index, z_])
            pl.when(more)(lambda: grads_push(z_, (zp, zm)[direction]))

        sides(k, take)

    def queries_back():
        @pl.loop(0, blocks)
        def _(b):
            lanes, value_lanes = block_lanes(b)
            heads = doall[pair_rows, lanes].astype(F32)
            product = heads * att32[:, lanes]
            pieces = []
            for which in range(2):
                delta = jnp.sum(half(product, which), axis=-1, keepdims=True)
                grad_probs = dot_nt(half(heads, which).astype(BF16), kv[:, value_lanes])
                grad_scores = probs[2 * b + which].astype(F32) * (grad_probs - delta)
                pieces.append(dot(grad_scores.astype(BF16), kv[:, lanes]))
            total = jnp.where(low_half, pieces[0], pieces[1]) * HD ** (-0.5)
            dall[:, lanes] = total.astype(BF16)

    def keys_back(z_):
        rows = at(T2 * z_, T2)

        @pl.loop(0, blocks)
        def _(b):
            lanes, value_lanes = block_lanes(b)
            queries, grads = qall[rows, lanes], doall[rows, lanes]
            scores = dot_nt(both(kv[pair_rows, lanes].astype(F32)), queries)
            grad_probs = dot_nt(both(kv[pair_rows, value_lanes].astype(F32)), grads)
            lows, grad_scores = [], []
            for which in range(2):
                part, head = slice(T2 * which, T2 * (which + 1)), 2 * b + which
                powers = jnp.exp(scores[part] + mask[:, rows] - lsed[z_, pl.ds(head, 1), :])
                shifted = grad_probs[part] - lsed[z_, pl.ds(8 + head, 1), :]
                lows.append(powers.astype(BF16))
                grad_scores.append((powers * shifted).astype(BF16))
            dkv32[:, lanes] += pick(dot(jnp.concatenate(grad_scores, axis=0), queries))
            dkv32[:, value_lanes] += pick(dot(jnp.concatenate(lows, axis=0), grads))

    def keys_back_at(k):
        pl.when(z - k >= 0)(lambda: keys_back(z - k))
        if k > 0:
            pl.when(z + k <= 3)(lambda: keys_back(z + k))

    def query_weights():
        matrix_put(0, 0, dot_tn(dall[:, pl.ds(0, HW)], fall[pair_rows, :]))
        matrices_send(0)

    def key_value_weights():
        dall[:, pl.ds(HW, D)] = dkv32[...].astype(BF16)
        grads = dot_tn(dall[:, pl.ds(HW, D)], fall[pair_rows, :])
        matrix_put(1, 0, grads[:HW, :])
        matrix_put(1, 1, grads[HW:, :])
        matrices_send(1)

    def input_grad():
        into = dot_nt(dall[...], wqkv[...])
        dxo[...] = into
        dxs[...] = dxo[other, :].astype(BF16)
        start(dxs, dxr, *one("dx"), yn)
        sums = jnp.sum(dall[...].astype(F32), axis=0, keepdims=True)
        vectors[0:1, heads_here] = sums[:, :HW]
        vectors[1:2, heads_here] = sums[:, 2 * HW :]

    def input_grad_end():
        arrived(dxr, got_of("dx"))
        frames_grad[...] = gfirst[...] + dxo[mine, :] + dxr[...].astype(F32)

    def attention_x(family):
        arrived(dr.at[family], got_of(("d", family)))
        xs[family] = (gm[family, c, 1 - x].astype(F32) + dr[family, 1 - x].astype(F32)).astype(BF16)
        start(xs.at[family], xr.at[family], *one(("xs", family)), xn)

    def attention_z(family):
        arrived(xr.at[family], got_of(("xs", family)))
        total = gm[family, c, x].astype(F32) + dr[family, x].astype(F32) + xr[family].astype(F32)
        parts[4 + family][...] = total.astype(BF16)
        sum_send(4 + family)

    def pair_half(t, half_):
        columns = at(FO * half_, FO)
        if t == DOWN:
            return dot_tn(ar[:, columns], fq[...])
        return dot_tn(hq[...], br[:, columns])

    def pair_send(t):
        half_ = pair_half(t, 1 - c).astype(BF16)
        rows = half_.shape[0] // 2
        for q in range(2):
            given[t][q] = half_[rows * q : rows * (q + 1)]
            start(given[t].at[q], taken[t].at[q], *one(("pair", t, q), ("pair", t)), sib)
        half_ = pair_half(t, c)
        for q in range(2):
            kept[t][q] = half_[rows * q : rows * (q + 1)]

    def pair_add(family):
        t, q = family // 2, family % 2
        arrived(taken[t].at[q], got_of(("pair", t, q)))
        parts[family][...] = (kept[t][q] + taken[t][q].astype(F32)).astype(BF16)
        sum_send(family)

    def vector_step(i, to):
        vsend[i] = vectors[...]
        start(vsend.at[i], vrecv.at[i], *one(("v", i)), to)

    def vector_add(i):
        arrived(vrecv.at[i], got_of(("v", i)))
        vectors[...] += vrecv[i]

    def vector_z():
        vsend[3] = vectors[...]
        vz[z] = vectors[...]
        for k in (1, 2, 3):
            j = lax.rem(z + k, 4)
            start(vsend.at[3], vz.at[z], vzs.at[0], vzr.at[z], device(x, c, y, j))

    def vector_end():
        for k in (1, 2, 3):
            j = lax.rem(z + k, 4)
            arrived(vz.at[j], vzr.at[j])
        vectors[...] = (vz[0] + vz[1]) + (vz[2] + vz[3])

    dkv32[...] = jnp.zeros_like(dkv32)
    for t in range(6):
        sent(("sum", t), parts[t].at[pl.ds(0, 3 * slab_rows[t]), :], zss.at[t])
    for t in (DOWN, UP):
        sent(("pair", t), given[t], group(("pair", t)))
    sent("dx", dxs, group("dx"))
    for family in range(2):
        sent(("d", family), dr.at[family], group(("d", family)))
        sent(("xs", family), xs.at[family], group(("xs", family)))
    for i in range(3):
        sent(("v", i), vsend.at[i], group(("v", i)))
    sent("vz", vz.at[pl.ds(0, 3)], vzs.at[0])
    ffn_back(0)
    from_y(hq, "hid")
    ffn_back(1)
    ffn_back(2)
    from_y(fq, "ffn")
    ffn_back(3)
    norm1_back()
    branch_send()
    from_x(hq, "hid")
    out_back()
    rest_y(fq, "ffn")
    rest_y(hq, "hid")
    plane_active(x, 1 - y)
    rest_x(hq, "hid")
    from_x(fq, "ffn")
    queries_back()
    plane_active(1 - x, y)
    from_diagonal(hq, "hid")
    query_weights()
    plane_active(1 - x, 1 - y)
    from_diagonal(fq, "ffn")
    rest_x(fq, "ffn")
    pair_send(DOWN)
    grads_arrive(1)
    attention_x(0)
    pair_add(DOWN_1)
    plane_back(1 - x, 1 - y)
    keys_back_at(1)
    pair_add(DOWN_0)
    plane_back(1 - x, y)
    sum_pass(DOWN_1)
    grads_arrive(2)
    plane_back(x, 1 - y)
    keys_back_at(2)
    pair_send(UP)
    sum_pass(DOWN_0)
    sum_end(DOWN_1)
    gather_own(DOWN_1)
    keys_back_at(0)
    pair_add(UP_0)
    sum_end(DOWN_0)
    gather_own(DOWN_0)
    gather_second(DOWN_1, 0)
    plane_first(DOWN_1)
    grads_arrive(3)
    keys_back_at(3)
    key_value_weights()
    gather_z(DOWN_1, 1)
    pair_add(UP_1)
    gather_second(DOWN_0, 0)
    sum_pass(UP_0)
    attention_z(0)
    gather_z(DOWN_0, 1)
    attention_x(1)
    input_grad()
    vector_step(0, sib)
    sum_pass(UP_1)
    gather_z(DOWN_1, 2)
    sum_pass(QUERY_OUT)
    sum_end(UP_0)
    gather_own(UP_0)
    gather_third(DOWN_1, 0)
    sum_end(UP_1)
    gather_own(UP_1)
    gather_z(DOWN_0, 2)
    sum_end(QUERY_OUT)
    vector_add(0)
    gather_z(DOWN_1, 3)
    gather_own(QUERY_OUT)
    plane_second(DOWN_1)
    gather_z(UP_1, 1)
    vector_step(1, xn)
    attention_z(1)
    gather_z(QUERY_OUT, 1)
    plane_first(QUERY_OUT)
    input_grad_end()
    gather_second(DOWN_0, 1)
    gather_z(DOWN_0, 3)
    gather_z(QUERY_OUT, 2)
    gather_z(UP_0, 1)
    gather_z(UP_1, 2)
    sum_pass(KEY_VALUE)
    gather_z(UP_1, 3)
    gather_z(UP_0, 2)
    sum_end(KEY_VALUE)
    gather_own(KEY_VALUE)
    plane_out(DOWN_1)
    gather_second(UP_0, 1)
    gather_second(QUERY_OUT, 1)
    gather_second(DOWN_0, 3)
    gather_second(UP_1, 1)
    gather_second(QUERY_OUT, 2)
    gather_z(QUERY_OUT, 3)
    plane_z(DOWN_1, 1)
    gather_second(UP_1, 2)
    gather_second(QUERY_OUT, 0)
    gather_z(UP_0, 3)
    plane_second(QUERY_OUT)
    vector_add(1)
    gather_second(DOWN_1, 3)
    gather_second(UP_0, 0)
    gather_second(QUERY_OUT, 3)
    vector_step(2, yn)
    gather_z(KEY_VALUE, 1)
    plane_out(QUERY_OUT)
    gather_second(UP_0, 2)
    gather_second(UP_1, 3)
    gather_third(DOWN_0, 3)
    gather_third(QUERY_OUT, 2)
    gather_z(KEY_VALUE, 2)
    gather_z(KEY_VALUE, 3)
    gather_second(DOWN_1, 1)
    gather_second(UP_1, 0)
    plane_z(DOWN_1, 2)
    gather_third(UP_0, 1)
    plane_z(QUERY_OUT, 1)
    gather_third(UP_1, 1)
    gather_third(DOWN_0, 0)
    gather_third(DOWN_1, 3)
    gather_second(DOWN_0, 2)
    gather_second(UP_0, 3)
    gather_third(UP_0, 2)
    gather_third(UP_0, 0)
    gather_second(KEY_VALUE, 1)
    plane_z(DOWN_1, 3)
    vector_add(2)
    gather_third(QUERY_OUT, 1)
    gather_third(QUERY_OUT, 3)
    gather_third(UP_1, 3)
    gather_third(UP_1, 2)
    gather_third(QUERY_OUT, 0)
    gather_second(KEY_VALUE, 0)
    plane_z(QUERY_OUT, 2)
    gather_second(DOWN_1, 2)
    gather_third(DOWN_1, 1)
    vector_z()
    gather_second(KEY_VALUE, 2)
    gather_third(UP_1, 0)
    gather_third(UP_0, 3)
    gather_third(DOWN_0, 2)
    gather_second(KEY_VALUE, 3)
    gather_third(DOWN_0, 1)
    gather_third(KEY_VALUE, 1)
    gather_third(KEY_VALUE, 0)
    plane_z(QUERY_OUT, 3)
    gather_third(DOWN_1, 2)
    gather_third(KEY_VALUE, 2)
    gather_third(KEY_VALUE, 3)
    vector_end()
    phase("gather_end")
    gather_end()
    phase("sends_end")
    assert (len(send_names), len(names)) == (mss.shape[0], msr.shape[0])
    for wait in waits.values():
        wait()
    phase(None)


def fused_layer(
    frames,
    clip_lengths,
    query_weight,
    query_bias,
    key_weight,
    value_weight,
    value_bias,
    out_weight,
    out_bias,
    norm1_gain,
    norm1_bias,
    up_weight,
    up_bias,
    down_weight,
    down_bias,
    norm2_gain,
    norm2_bias,
    cotangent,
):
    T, D = frames.shape[1], frames.shape[2]
    F = up_weight.shape[1]
    S = T * lax.axis_size("seq")
    HW, T2, EIGHTH, FO = D // 2, 2 * T, D // 8, F // 8
    blocks = HW // LANES
    entries = clip_lengths.shape[1]
    vmem, hbm = pl.BlockSpec(memory_space=pltpu.VMEM), pl.BlockSpec(memory_space=pl.ANY)
    dma, n = pltpu.SemaphoreType.DMA, len(PIECES)
    low, wide = (lambda *shape: pltpu.VMEM(shape, BF16)), (lambda *shape: pltpu.VMEM(shape, F32))
    scratch = dict(
        frames_v=wide(T, D),
        cotangent_v=wide(T, D),
        lengths_v=pltpu.VMEM((1, entries), jnp.int32),
        **{f"v{i}": wide(D) for i in range(8)},
        up_v=wide(F),
        bias_rows=wide(8, D),
        up_rows=wide(4, 8, D),
        fall=low(S, D),
        wqkv=low(D, 3 * HW),
        wo=low(D, D),
        wup=low(D, F),
        wdn=low(F, D),
        qall=low(S, HW),
        kv=low(S, D),
        mask=wide(T2, S),
        probs=low(2 * blocks, T2, S),
        stat=wide(2, T2, LANES),
        lsed=wide(5, 16, T2),
        att32=wide(T2, HW),
        att16=low(T2, HW),
        attf=low(T, D),
        hq=low(4 * T, D),
        fq=low(4 * T, D),
        ar=low(4 * T, D),
        br=low(4 * T, D),
        actives=low(4, T, D),
        slopes=wide(4 * T, D),
        dgelu=wide(4, T, D),
        hid32=wide(T, D),
        unit1=wide(T, D),
        rstd1=wide(T, LANES),
        gmid=wide(T, D),
        gfirst=wide(T, D),
        gbr=low(T2, D),
        doall=low(S, HW),
        dkv32=wide(T2, D),
        dall=low(T2, 3 * HW),
        give_down=low(2, FO // 2, D),
        give_up=low(2, D // 2, FO),
        take_down=low(2, FO // 2, D),
        take_up=low(2, D // 2, FO),
        keep_down=wide(2, FO // 2, D),
        keep_up=wide(2, D // 2, FO),
        part_down=low(2, FO // 2, D),
        part_up=low(2, D // 2, FO),
        part_qo=low(HW // 2, D),
        part_kv=low(HW // 2, D),
        got_down=low(2, 4, FO // 8, D),
        got_up=low(2, 4, D // 8, FO),
        got_qo=low(4, HW // 8, D),
        got_kv=low(4, HW // 8, D),
        gm=low(2, 2, 2, HW // 2, D),
        dr=low(2, 2, HW // 2, D),
        xs=low(2, HW // 2, D),
        xr=low(2, HW // 2, D),
        dxs=low(T, D),
        dxr=low(T, D),
        dxo=wide(T2, D),
        vsend=wide(4, 16, D),
        vrecv=wide(3, 16, D),
        vz=wide(4, 16, D),
        wsem=dma((6,)),
        asem=dma((4,)),
        hes=dma((1,)),
        her=dma((blocks,)),
        frs=dma((CHUNKS, 8)),
        fss=dma((2,)),
        msr=dma((25,)),
        mss=dma((13,)),
        dor=dma((2, 4)),
        dos=dma((2,)),
        zsr=dma((6, 4)),
        zss=dma((6,)),
        agr=dma((sum(map(gather_sems, PIECES)),)),
        ags=dma((n,)),
        agdr=dma((n,)),
        vzr=dma((4,)),
        vzs=dma((1,)),
    )
    results = pl.pallas_call(
        partial(layer_kernel, T, D, S, entries),
        out_shape=(
            pltpu.VMEM((T, D), F32),
            pltpu.VMEM((T, D), F32),
            pltpu.VMEM((16, D), F32),
            pltpu.VMEM((F, D), BF16),
            pltpu.VMEM((D, F), BF16),
            pltpu.VMEM((4 * D, D), BF16),
        ),
        in_specs=[hbm] * 18,
        out_specs=(vmem,) * 6,
        scratch_shapes=list(scratch.values()),
        compiler_params=pltpu.CompilerParams(
            collective_id=0, has_side_effects=True, vmem_limit_bytes=VMEM_GRANT
        ),
        name="layer",
    )(
        frames[0],
        cotangent[0],
        clip_lengths,
        query_weight,
        key_weight,
        value_weight,
        out_weight,
        up_weight,
        down_weight,
        query_bias,
        value_bias,
        out_bias,
        norm1_gain,
        norm1_bias,
        up_bias,
        down_bias,
        norm2_gain,
        norm2_bias,
    )
    return widen(*results)


def widen_kernel(
    last,
    T,
    D,
    encoded,
    frames_grad,
    vectors,
    down,
    up,
    attn,
    encoded_out,
    frames_grad_out,
    query_out,
    query_b,
    key_out,
    value_out,
    value_b,
    out_out,
    out_b,
    gain1,
    bias1,
    up_out,
    up_b,
    down_out,
    down_b,
    gain2,
    bias2,
    sems,
):
    step = pl.program_id(0)
    copies = [
        pltpu.make_async_copy(encoded, encoded_out, sems.at[0]),
        pltpu.make_async_copy(frames_grad, frames_grad_out, sems.at[1]),
    ]

    @pl.when(step == 0)
    def _():
        for copy in copies:
            copy.start()
        for ref, index in (
            (query_b, 0),
            (value_b, 1),
            (out_b, 2),
            (gain1, 3),
            (bias1, 4),
            (down_b, 9),
            (gain2, 10),
            (bias2, 11),
        ):
            ref[...] = vectors[index : index + 1, :].reshape(D)
        for quarter in range(4):
            up_b[pl.ds(D * quarter, D)] = vectors[5 + quarter : 6 + quarter, :].reshape(D)

    def rows(size, first=0):
        return pl.ds(pl.multiple_of(first + size * step, size), size)

    down_out[...] = down[rows(down_out.shape[0]), :].astype(F32)
    up_out[...] = up[rows(up_out.shape[0]), :].astype(F32)
    out_out[...] = attn[rows(LANES, 3 * D), :].astype(F32)
    for m, target in enumerate((query_out, key_out, value_out)):
        target[...] = attn[rows(LANES, m * D), :].astype(F32).T

    @pl.when(step == last)
    def _():
        for copy in copies:
            copy.wait()


def widen(encoded, frames_grad, vectors, sum_down, sum_up, sum_attn):
    T, D = encoded.shape
    F = sum_up.shape[1]
    steps = D // LANES
    hbm, vmem = pl.BlockSpec(memory_space=pl.ANY), pl.BlockSpec(memory_space=pltpu.VMEM)
    parts = (encoded, frames_grad, vectors, sum_down, sum_up, sum_attn)
    parts = [pltpu.with_memory_space_constraint(part, pltpu.VMEM) for part in parts]

    def down(width):
        return pl.BlockSpec((width, D), lambda i: (i, 0))

    up = pl.BlockSpec((D // steps, F), lambda i: (i, 0))
    turned = pl.BlockSpec((D, LANES), lambda i: (0, i))
    flat = pl.BlockSpec((D,), lambda i: (0,))
    wide_flat = pl.BlockSpec((F,), lambda i: (0,))
    square, vector = jax.ShapeDtypeStruct((D, D), F32), jax.ShapeDtypeStruct((D,), F32)
    tokens = jax.ShapeDtypeStruct((T, D), F32)
    outs = (
        (tokens, hbm),
        (tokens, hbm),
        (square, turned),
        (vector, flat),
        (square, turned),
        (square, turned),
        (vector, flat),
        (square, down(LANES)),
        (vector, flat),
        (vector, flat),
        (vector, flat),
        (jax.ShapeDtypeStruct((D, F), F32), up),
        (jax.ShapeDtypeStruct((F,), F32), wide_flat),
        (jax.ShapeDtypeStruct((F, D), F32), down(F // steps)),
        (vector, flat),
        (vector, flat),
        (vector, flat),
    )
    results = pl.pallas_call(
        partial(widen_kernel, steps - 1, T, D),
        grid=(steps,),
        out_shape=tuple(shape for shape, _ in outs),
        in_specs=[vmem] * 6,
        out_specs=tuple(spec for _, spec in outs),
        scratch_shapes=[pltpu.SemaphoreType.DMA((2,))],
        compiler_params=pltpu.CompilerParams(vmem_limit_bytes=VMEM_GRANT),
        name="widen",
    )(*parts)
    return (results[0][None], results[1][None]) + tuple(results[2:])


def solution(mesh):
    in_specs = (
        P("row", "seq", None),
        P("row", None),
        P(),
        P(),
        P(),
        P(),
        P(),
        P(),
        P(),
        P(),
        P(),
        P(),
        P(),
        P(),
        P(),
        P(),
        P(),
        P("row", "seq", None),
    )
    out_specs = (
        P("row", "seq", None),
        P("row", "seq", None),
        P(),
        P(),
        P(),
        P(),
        P(),
        P(),
        P(),
        P(),
        P(),
        P(),
        P(),
        P(),
        P(),
        P(),
        P(),
    )
    shape = dict(mesh.shape)
    fused = shape["row"] == 4 and shape["seq"] == 8
    return jax.shard_map(
        fused_layer if fused else per_device, mesh=mesh, in_specs=in_specs, out_specs=out_specs, check_vma=False
    )
```

```python
import contextlib
from functools import partial
import math

import jax
import jax.numpy as jnp
from jax import lax
from jax.experimental import pallas as pl
from jax.experimental.pallas import tpu as pltpu
from jax.sharding import PartitionSpec as P

H = 12
HD = 64


MASK_SCORE = -1e30
NORM_EPSILON = 1e-05


def from_behind(value, axis, by):
    count = lax.axis_size(axis)
    return lax.ppermute(value, axis, [(i, (i + by) % count) for i in range(count)])


def layer_norm(summed, norm_gain, norm_shift):
    centre = jnp.mean(summed, axis=-1, keepdims=True)
    centered = summed - centre
    inverse = lax.rsqrt(jnp.mean(centered * centered, axis=-1, keepdims=True) + NORM_EPSILON)
    normed = centered * inverse
    return (normed * norm_gain + norm_shift, normed, inverse)


def layer_norm_back(upstream, normed, inverse, norm_gain):
    scaled = upstream * norm_gain
    first_mean = jnp.mean(scaled, axis=-1, keepdims=True)
    second_mean = jnp.mean(scaled * normed, axis=-1, keepdims=True)
    summed_grad = inverse * (scaled - first_mean - normed * second_mean)
    return (summed_grad, jnp.sum(upstream * normed, axis=(0, 1)), jnp.sum(upstream, axis=(0, 1)))


def project(inputs, matrix):
    return jnp.einsum("rsk,kn->rsn", inputs, matrix, preferred_element_type=jnp.float32)


def project_back(upstream, matrix):
    return jnp.einsum("rsn,kn->rsk", upstream, matrix, preferred_element_type=jnp.float32)


def matrix_grad(inputs, upstream):
    return jnp.einsum("rsk,rsn->kn", inputs, upstream, preferred_element_type=jnp.float32)


def column_sum(upstream):
    return jnp.sum(upstream.astype(jnp.float32), axis=(0, 1))


def clip_numbers(clip_ends, position):
    return jnp.sum((clip_ends[:, None, :] <= position[None, :, None]).astype(jnp.int32), axis=-1)


def split_heads(tensor):
    return tensor.reshape(tensor.shape[0], tensor.shape[1], H, HD)


def join_heads(tensor):
    return tensor.reshape(tensor.shape[0], tensor.shape[1], H * HD)


def head_scores(queries, keys_block):
    return jnp.einsum(
        "rqhd,rkhd->rhqk", queries, keys_block, preferred_element_type=jnp.float32
    ) * HD ** (-0.5)


def allowed_pairs(query_numbers, key_numbers):
    return (query_numbers[:, :, None] == key_numbers[:, None, :])[:, None]


def online_update(running, queries, query_numbers, keys_block, values_block, key_numbers):
    run_peak, run_total, run_values = running
    allowed = allowed_pairs(query_numbers, key_numbers)
    masked = jnp.where(allowed, head_scores(queries, keys_block), MASK_SCORE)
    new_peak = jnp.maximum(run_peak, jnp.max(masked, axis=-1))
    weights = jnp.where(allowed, jnp.exp(masked - new_peak[..., None]), 0.0)
    rescale = jnp.exp(run_peak - new_peak)
    new_total = run_total * rescale + jnp.sum(weights, axis=-1)
    contrib = jnp.einsum(
        "rhqk,rkhd->rqhd",
        weights.astype(jnp.bfloat16),
        values_block,
        preferred_element_type=jnp.float32,
    )
    new_values = run_values * jnp.swapaxes(rescale, 1, 2)[..., None] + contrib
    return (new_peak, new_total, new_values)


def block_back(
    queries, grad_heads, log_total, delta_rows, query_numbers, keys_flat, values_flat, key_numbers
):
    keys_block = split_heads(keys_flat)
    values_block = split_heads(values_flat)
    allowed = allowed_pairs(query_numbers, key_numbers)
    shifted = jnp.where(
        allowed, head_scores(queries, keys_block) - log_total[..., None], MASK_SCORE
    )
    weights = jnp.exp(shifted)
    grad_weights = jnp.einsum(
        "rqhd,rkhd->rhqk", grad_heads, values_block, preferred_element_type=jnp.float32
    )
    grad_scores = (weights * (grad_weights - delta_rows[..., None])).astype(jnp.bfloat16)
    factor = HD ** (-0.5)
    query_part = (
        jnp.einsum("rhqk,rkhd->rqhd", grad_scores, keys_block, preferred_element_type=jnp.float32)
        * factor
    )
    key_part = (
        jnp.einsum("rhqk,rqhd->rkhd", grad_scores, queries, preferred_element_type=jnp.float32)
        * factor
    )
    value_part = jnp.einsum(
        "rhqk,rqhd->rkhd",
        weights.astype(jnp.bfloat16),
        grad_heads,
        preferred_element_type=jnp.float32,
    )
    return (join_heads(query_part), join_heads(key_part), join_heads(value_part))


def per_device(
    frames,
    clip_lengths,
    query_weight,
    query_bias,
    key_weight,
    value_weight,
    value_bias,
    out_weight,
    out_bias,
    norm1_gain,
    norm1_bias,
    up_weight,
    up_bias,
    down_weight,
    down_bias,
    norm2_gain,
    norm2_bias,
    cotangent,
):
    row_count = frames.shape[0]
    shard_len = frames.shape[1]
    cycle_size = lax.axis_size("seq")
    seq_place = lax.axis_index("seq")
    clip_ends = jnp.cumsum(clip_lengths, axis=1)
    offsets = jnp.arange(shard_len, dtype=jnp.int32)
    own_numbers = clip_numbers(clip_ends, seq_place * shard_len + offsets)
    frames_low = frames.astype(jnp.bfloat16)
    queries = split_heads((project(frames_low, query_weight) + query_bias).astype(jnp.bfloat16))
    keys_own = project(frames_low, key_weight).astype(jnp.bfloat16)
    values_own = (project(frames_low, value_weight) + value_bias).astype(jnp.bfloat16)
    initial = (
        jnp.full((row_count, H, shard_len), MASK_SCORE, jnp.float32),
        jnp.zeros((row_count, H, shard_len), jnp.float32),
        jnp.zeros((row_count, shard_len, H, HD), jnp.float32),
    )
    key_piece = lax.all_gather(keys_own, "seq", axis=1, tiled=True)
    value_piece = lax.all_gather(values_own, "seq", axis=1, tiled=True)
    piece_len = key_piece.shape[1]
    block_len = math.gcd(piece_len, 512)

    def attend_block(block_index, carried):
        offset = block_index * block_len
        key_block = lax.dynamic_slice_in_dim(key_piece, offset, block_len, 1)
        value_block = lax.dynamic_slice_in_dim(value_piece, offset, block_len, 1)
        position = offset + jnp.arange(block_len, dtype=jnp.int32)
        return online_update(
            carried,
            queries,
            own_numbers,
            split_heads(key_block),
            split_heads(value_block),
            clip_numbers(clip_ends, position),
        )

    run_peak, run_total, run_values = lax.fori_loop(
        0, piece_len // block_len, attend_block, initial
    )
    log_total = run_peak + jnp.log(run_total)
    attended_heads = run_values / jnp.swapaxes(run_total, 1, 2)[..., None]
    attended = join_heads(attended_heads)
    attended_low = attended.astype(jnp.bfloat16)
    branch = project(attended_low, out_weight) + out_bias
    hidden, unit_first, inverse_first = layer_norm(frames + branch, norm1_gain, norm1_bias)
    hidden_low = hidden.astype(jnp.bfloat16)
    before = project(hidden_low, up_weight) + up_bias
    active, gelu_back = jax.vjp(partial(jax.nn.gelu, approximate=False), before)
    active_low = active.astype(jnp.bfloat16)
    encoded, unit_second, inverse_second = layer_norm(
        hidden + project(active_low, down_weight) + down_bias, norm2_gain, norm2_bias
    )
    grad_mid, norm2_gain_grad, norm2_bias_grad = layer_norm_back(
        cotangent, unit_second, inverse_second, norm2_gain
    )
    grad_ffn = grad_mid.astype(jnp.bfloat16)
    down_weight_grad = matrix_grad(active_low, grad_ffn)
    down_bias_grad = column_sum(grad_ffn)
    grad_before = gelu_back(project_back(grad_ffn, down_weight))[0].astype(jnp.bfloat16)
    up_weight_grad = matrix_grad(hidden_low, grad_before)
    up_bias_grad = column_sum(grad_before)
    grad_hidden = grad_mid + project_back(grad_before, up_weight)
    grad_first, norm1_gain_grad, norm1_bias_grad = layer_norm_back(
        grad_hidden, unit_first, inverse_first, norm1_gain
    )
    grad_branch = grad_first.astype(jnp.bfloat16)
    out_weight_grad = matrix_grad(attended_low, grad_branch)
    out_bias_grad = column_sum(grad_branch)
    grad_attended = project_back(grad_branch, out_weight).astype(jnp.bfloat16)
    grad_heads = split_heads(grad_attended)
    delta_rows = jnp.swapaxes(
        jnp.sum(grad_heads.astype(jnp.float32) * attended_heads, axis=-1), 1, 2
    )
    query_start, key_start, value_start = block_back(
        queries, grad_heads, log_total, delta_rows, own_numbers, keys_own, values_own, own_numbers
    )

    def key_step(distance, carried):
        key_now, value_now, query_sum, key_sum, value_sum = carried
        key_now, value_now = from_behind((key_now, value_now), "seq", 1)
        key_sum, value_sum = (
            from_behind(key_sum.astype(jnp.bfloat16), "seq", 1).astype(key_sum.dtype),
            from_behind(value_sum.astype(jnp.bfloat16), "seq", 1).astype(value_sum.dtype),
        )
        source = (seq_place - distance) % cycle_size
        source_numbers = clip_numbers(clip_ends, source * shard_len + offsets)
        query_part, key_part, value_part = block_back(
            queries,
            grad_heads,
            log_total,
            delta_rows,
            own_numbers,
            key_now,
            value_now,
            source_numbers,
        )
        return (
            key_now,
            value_now,
            query_sum + query_part,
            key_sum + key_part,
            value_sum + value_part,
        )

    carried = lax.fori_loop(
        1, cycle_size, key_step, (keys_own, values_own, query_start, key_start, value_start)
    )
    query_total = carried[2]
    key_total, value_total = (
        from_behind(carried[3].astype(jnp.bfloat16), "seq", 1).astype(jnp.float32),
        from_behind(carried[4].astype(jnp.bfloat16), "seq", 1).astype(jnp.float32),
    )
    query_low = query_total.astype(jnp.bfloat16)
    key_low = key_total.astype(jnp.bfloat16)
    value_low = value_total.astype(jnp.bfloat16)
    query_weight_grad = matrix_grad(frames_low, query_low)
    query_bias_grad = column_sum(query_low)
    key_weight_grad = matrix_grad(frames_low, key_low)
    value_weight_grad = matrix_grad(frames_low, value_low)
    value_bias_grad = column_sum(value_low)
    frames_grad = (
        grad_first
        + project_back(query_low, query_weight)
        + project_back(key_low, key_weight)
        + project_back(value_low, value_weight)
    )
    shares = (
        lax.psum_scatter(query_weight_grad, "seq", scatter_dimension=0, tiled=True),
        lax.psum_scatter(query_bias_grad, "seq", scatter_dimension=0, tiled=True),
        lax.psum_scatter(key_weight_grad, "seq", scatter_dimension=0, tiled=True),
        lax.psum_scatter(value_weight_grad, "seq", scatter_dimension=0, tiled=True),
        lax.psum_scatter(value_bias_grad, "seq", scatter_dimension=0, tiled=True),
        lax.psum_scatter(out_weight_grad, "seq", scatter_dimension=0, tiled=True),
        lax.psum_scatter(out_bias_grad, "seq", scatter_dimension=0, tiled=True),
        lax.psum_scatter(norm1_gain_grad, "seq", scatter_dimension=0, tiled=True),
        lax.psum_scatter(norm1_bias_grad, "seq", scatter_dimension=0, tiled=True),
        lax.psum_scatter(up_weight_grad, "seq", scatter_dimension=0, tiled=True),
        lax.psum_scatter(up_bias_grad, "seq", scatter_dimension=0, tiled=True),
        lax.psum_scatter(down_weight_grad, "seq", scatter_dimension=0, tiled=True),
        lax.psum_scatter(down_bias_grad, "seq", scatter_dimension=0, tiled=True),
        lax.psum_scatter(norm2_gain_grad, "seq", scatter_dimension=0, tiled=True),
        lax.psum_scatter(norm2_bias_grad, "seq", scatter_dimension=0, tiled=True),
    )
    shares = (
        lax.psum(shares[0].astype(jnp.bfloat16), "row").astype(jnp.float32),
        lax.psum(shares[1].astype(jnp.bfloat16), "row").astype(jnp.float32),
        lax.psum(shares[2].astype(jnp.bfloat16), "row").astype(jnp.float32),
        lax.psum(shares[3].astype(jnp.bfloat16), "row").astype(jnp.float32),
        lax.psum(shares[4].astype(jnp.bfloat16), "row").astype(jnp.float32),
        lax.psum(shares[5].astype(jnp.bfloat16), "row").astype(jnp.float32),
        lax.psum(shares[6].astype(jnp.bfloat16), "row").astype(jnp.float32),
        lax.psum(shares[7].astype(jnp.bfloat16), "row").astype(jnp.float32),
        lax.psum(shares[8].astype(jnp.bfloat16), "row").astype(jnp.float32),
        lax.psum(shares[9].astype(jnp.bfloat16), "row").astype(jnp.float32),
        lax.psum(shares[10].astype(jnp.bfloat16), "row").astype(jnp.float32),
        lax.psum(shares[11].astype(jnp.bfloat16), "row").astype(jnp.float32),
        lax.psum(shares[12].astype(jnp.bfloat16), "row").astype(jnp.float32),
        lax.psum(shares[13].astype(jnp.bfloat16), "row").astype(jnp.float32),
        lax.psum(shares[14].astype(jnp.bfloat16), "row").astype(jnp.float32),
    )
    totals = (
        lax.all_gather(shares[0].astype(jnp.bfloat16), "seq", axis=0, tiled=True).astype(
            jnp.float32
        ),
        lax.all_gather(shares[1].astype(jnp.bfloat16), "seq", axis=0, tiled=True).astype(
            jnp.float32
        ),
        lax.all_gather(shares[2].astype(jnp.bfloat16), "seq", axis=0, tiled=True).astype(
            jnp.float32
        ),
        lax.all_gather(shares[3].astype(jnp.bfloat16), "seq", axis=0, tiled=True).astype(
            jnp.float32
        ),
        lax.all_gather(shares[4].astype(jnp.bfloat16), "seq", axis=0, tiled=True).astype(
            jnp.float32
        ),
        lax.all_gather(shares[5].astype(jnp.bfloat16), "seq", axis=0, tiled=True).astype(
            jnp.float32
        ),
        lax.all_gather(shares[6].astype(jnp.bfloat16), "seq", axis=0, tiled=True).astype(
            jnp.float32
        ),
        lax.all_gather(shares[7].astype(jnp.bfloat16), "seq", axis=0, tiled=True).astype(
            jnp.float32
        ),
        lax.all_gather(shares[8].astype(jnp.bfloat16), "seq", axis=0, tiled=True).astype(
            jnp.float32
        ),
        lax.all_gather(shares[9].astype(jnp.bfloat16), "seq", axis=0, tiled=True).astype(
            jnp.float32
        ),
        lax.all_gather(shares[10].astype(jnp.bfloat16), "seq", axis=0, tiled=True).astype(
            jnp.float32
        ),
        lax.all_gather(shares[11].astype(jnp.bfloat16), "seq", axis=0, tiled=True).astype(
            jnp.float32
        ),
        lax.all_gather(shares[12].astype(jnp.bfloat16), "seq", axis=0, tiled=True).astype(
            jnp.float32
        ),
        lax.all_gather(shares[13].astype(jnp.bfloat16), "seq", axis=0, tiled=True).astype(
            jnp.float32
        ),
        lax.all_gather(shares[14].astype(jnp.bfloat16), "seq", axis=0, tiled=True).astype(
            jnp.float32
        ),
    )
    return (
        encoded,
        frames_grad,
        totals[0],
        totals[1],
        totals[2],
        totals[3],
        totals[4],
        totals[5],
        totals[6],
        totals[7],
        totals[8],
        totals[9],
        totals[10],
        totals[11],
        totals[12],
        totals[13],
        totals[14],
    )


MESH = pl.DeviceIdType.MESH
LANES = 128
F32, BF16 = jnp.float32, jnp.bfloat16
VMEM_GRANT = 49 << 20
DOWN, UP = 0, 1
DOWN_0, DOWN_1, UP_0, UP_1, QUERY_OUT, KEY_VALUE = range(6)
CHUNKS = 4

PIECES = (
    (DOWN_0, "zyx", 0, 1),
    (DOWN_0, "zxy", 1, 2),
    (DOWN_1, "zyx", 0, 2),
    (DOWN_1, "xyz", 2, 1),
    (UP_0, "zyx", 0, 3),
    (UP_1, "zxy", 0, 3),
    (QUERY_OUT, "zxy", 0, 1),
    (QUERY_OUT, "yxz", 1, 2),
    (KEY_VALUE, "zyx", 0, 1),
    (KEY_VALUE, "zxy", 1, 2),
)


def gather_sems(piece):
    return 12 + 1 + 1 if piece[1][2] == "z" else 3 + 4 + 4


def dot(a, b):
    return jnp.dot(a, b, preferred_element_type=F32)


def dot_nt(a, b):
    return lax.dot_general(a, b, (((1,), (1,)), ((), ())), preferred_element_type=F32)


def dot_tn(a, b):
    return lax.dot_general(a, b, (((0,), (0,)), ((), ())), preferred_element_type=F32)


def rows_norm(value):
    centre = jnp.mean(value, axis=-1, keepdims=True)
    centered = value - centre
    inverse = lax.rsqrt(jnp.mean(centered * centered, axis=-1, keepdims=True) + NORM_EPSILON)
    return centered * inverse, inverse


def rows_norm_back(scaled, unit, inverse):
    first = jnp.mean(scaled, axis=-1, keepdims=True)
    second = jnp.mean(scaled * unit, axis=-1, keepdims=True)
    return inverse * (scaled - first - unit * second)


def layer_kernel(
    T,
    D,
    S,
    entries,
    frames,
    cotangent,
    lengths,
    query_w,
    key_w,
    value_w,
    out_w,
    up_w,
    down_w,
    query_b,
    value_b,
    out_b,
    gain1,
    bias1,
    up_b,
    down_b,
    gain2,
    bias2,
    encoded,
    frames_grad,
    vectors,
    sum_down,
    sum_up,
    sum_attn,
    frames_v,
    cotangent_v,
    lengths_v,
    v0,
    v1,
    v2,
    v3,
    v4,
    v5,
    v6,
    v7,
    up_v,
    bias_rows,
    up_rows,
    fall,
    wqkv,
    wo,
    wup,
    wdn,
    qall,
    kv,
    mask,
    probs,
    stat,
    lsed,
    att32,
    att16,
    attf,
    hq,
    fq,
    ar,
    br,
    actives,
    slopes,
    dgelu,
    hid32,
    unit1,
    rstd1,
    gmid,
    gfirst,
    gbr,
    doall,
    dkv32,
    dall,
    give_down,
    give_up,
    take_down,
    take_up,
    keep_down,
    keep_up,
    part_down,
    part_up,
    part_qo,
    part_kv,
    got_down,
    got_up,
    got_qo,
    got_kv,
    gm,
    dr,
    xs,
    xr,
    dxs,
    dxr,
    dxo,
    vsend,
    vrecv,
    vz,
    wsem,
    asem,
    hes,
    her,
    frs,
    fry,
    fss,
    msr,
    mss,
    dor,
    dos,
    zsr,
    zss,
    agr,
    ags,
    agdr,
    vzr,
    vzs,
):
    HW, T2, FO = D // 2, 2 * T, wup.shape[1] // 8
    blocks = HW // LANES
    EIGHTH, SIXTEENTH = D // 8, D // 16
    row, seq = lax.axis_index("row"), lax.axis_index("seq")
    x, c = lax.div(row, 2), lax.rem(row, 2)
    z, y = lax.div(seq, 2), lax.rem(seq, 2)
    not_first, not_last = z > 0, z < 3

    def device(x_, c_, y_, z_=z):
        return (2 * x_ + c_, 2 * z_ + y_)

    def octant(x_, c_, y_):
        return 4 * y_ + 2 * x_ + c_

    sib, xn, yn = device(x, 1 - c, y), device(1 - x, c, y), device(x, c, 1 - y)
    zp, zm = device(x, c, y, jnp.minimum(z + 1, 3)), device(x, c, y, jnp.maximum(z - 1, 0))

    def many(value, of):
        return pl.multiple_of(value, of)

    def at(start, size, of=None):
        return pl.ds(many(start, size if of is None else of), size)

    waits = {}
    scope = contextlib.ExitStack()

    def phase(name):
        scope.close()
        if name:
            scope.enter_context(jax.named_scope(name))

    def send(src, dst, ssem, rsem, to):
        return pltpu.make_async_remote_copy(
            src_ref=src, dst_ref=dst, send_sem=ssem, recv_sem=rsem, device_id=to, device_id_type=MESH
        )

    def start(src, dst, ssem, rsem, to):
        send(src, dst, ssem, rsem, to).start()

    def arrived(ref, rsem):
        send(ref, ref, mss.at[0], rsem, sib).wait_recv()

    def sent(key, ref, ssem):
        waits.setdefault(key, lambda: send(ref, ref, ssem, msr.at[0], sib).wait_send())

    def sent_along_z(key, ref_of, ssem, rest=0, lines=1):
        for blocks_sent, when in ((1, (z == 0) | (z == 3)), (5, (z > 0) & (z < 3))):
            ref = ref_of(rest + lines * blocks_sent)
            wait = partial(lambda ref: send(ref, ref, ssem, msr.at[0], sib).wait_send(), ref)
            waits[key, blocks_sent] = partial(lambda when, wait: pl.when(when)(wait), when, wait)

    send_names, names = {}, {}

    def group(name):
        return mss.at[send_names.setdefault(name, len(send_names))]

    def one(name, family=None):
        return group(family or name), got_of(name)

    def got_of(name):
        return msr.at[names.setdefault(name, len(names))]

    phase("enter")
    heads_here = at(HW * y, HW)
    loads = [
        pltpu.make_async_copy(query_w.at[:, heads_here], wqkv.at[:, pl.ds(0, HW)], wsem.at[0]),
        pltpu.make_async_copy(key_w.at[:, heads_here], wqkv.at[:, pl.ds(HW, HW)], wsem.at[1]),
        pltpu.make_async_copy(value_w.at[:, heads_here], wqkv.at[:, pl.ds(2 * HW, HW)], wsem.at[2]),
        pltpu.make_async_copy(out_w, wo, wsem.at[3]),
        pltpu.make_async_copy(up_w, wup, wsem.at[4]),
        pltpu.make_async_copy(down_w, wdn, wsem.at[5]),
    ]
    barrier = pltpu.get_barrier_semaphore()
    peers = [sib, xn, yn, device(1 - x, c, 1 - y)]
    peers += [device(x, c, y, lax.rem(z + k, 4)) for k in (1, 2, 3)]
    for peer in peers:
        pl.semaphore_signal(barrier, inc=1, device_id=peer, device_id_type=MESH)
    vectors_v = (v0, v1, v2, v3, v4, v5, v6, v7)
    arrays = (frames, cotangent, lengths, query_b, value_b, out_b, gain1, bias1, up_b, down_b, gain2, bias2)
    here_ = (frames_v, cotangent_v, lengths_v, *vectors_v[:5], up_v, *vectors_v[5:])
    small = [
        pltpu.make_async_copy(array, ref, asem.at[min(i, 3)]) for i, (array, ref) in enumerate(zip(arrays, here_))
    ]
    small[0].start()
    for load in loads[:3] + small[1:] + loads[3:]:
        load.start()
    frames, cotangent, lengths = here_[:3]
    query_b, value_b, out_b, gain1, bias1, up_b, down_b, gain2, bias2 = here_[3:]
    vectors[...] = jnp.zeros_like(vectors)
    small[0].wait()
    fall[at(T * seq, T), :] = frames[...].astype(BF16)
    pl.semaphore_wait(barrier, len(peers))

    phase("frames_gather")

    CHUNK = T // CHUNKS

    def chunk(z_, y_, h):
        return fall.at[at(T * (2 * z_ + y_) + CHUNK * h, CHUNK), :]

    def push(z_, h, direction):
        to = (zp, zm, yn)[direction]
        rsem = fry.at[z_] if direction == 2 else frs.at[h, z_]
        start(chunk(z_, y, h), chunk(z_, y, h), fss.at[direction // 2], rsem, to)

    for h in range(CHUNKS):
        pl.when(not_last)(lambda: push(z, h, 0))
        pl.when(not_first)(lambda: push(z, h, 1))
        push(z, h, 2)
    for load in small[1:3]:
        load.wait()
    nine = att32.at[pl.ds(0, (8 * D + wup.shape[1]) // HW), :]
    pltpu.make_async_copy(nine, nine, asem.at[3]).wait()
    bias_rows[0:1, :] = query_b[...].reshape(1, D)
    bias_rows[1:2, :] = value_b[...].reshape(1, D)
    for quarter in range(4):
        up_rows[quarter] = jnp.broadcast_to(up_b[pl.ds(D * quarter, D)].reshape(1, D), (8, D))
    out_b, gain1, bias1, down_b, gain2, bias2 = (
        ref[...].reshape(1, D) for ref in (out_b, gain1, bias1, down_b, gain2, bias2)
    )
    query_bias, value_bias = bias_rows[0:1, heads_here], bias_rows[1:2, heads_here]
    for load in loads[:3]:
        load.wait()

    def project_slab(z_, y_):
        rows = at(T * (2 * z_ + y_), T)
        flat = dot(fall[rows, :], wqkv[...])
        query = (flat[:, :HW] + query_bias).astype(BF16).astype(F32) * HD ** (-0.5)
        qall[rows, :] = query.astype(BF16)
        kv[rows, pl.ds(0, HW)] = flat[:, HW : 2 * HW].astype(BF16)
        kv[rows, pl.ds(HW, HW)] = (flat[:, 2 * HW :] + value_bias).astype(BF16)

    project_slab(z, y)
    key_at = lax.broadcasted_iota(jnp.int32, (1, S), 1)
    query_at = lax.broadcasted_iota(jnp.int32, (T2, 1), 0) + T2 * z
    key_number, query_number = jnp.zeros((1, S), jnp.int32), jnp.zeros((T2, 1), jnp.int32)
    clip_end = jnp.zeros((1, 1), jnp.int32)
    for entry in range(entries):
        clip_end = clip_end + lengths[0:1, entry : entry + 1]
        key_number = key_number + jnp.where(clip_end <= key_at, 1, 0)
        query_number = query_number + jnp.where(clip_end <= query_at, 1, 0)
    mask[...] = jnp.where(query_number == key_number, 0.0, MASK_SCORE)

    @pl.loop(0, 4)
    def _(k):
        left, right = z - k - 1, z + k + 1

        for h in range(CHUNKS):

            @pl.when(left >= 0)
            def _():
                arrived(chunk(left, y, h), frs.at[h, left])
                pl.when(not_last)(lambda: push(left, h, 0))
                push(left, h, 2)

            @pl.when(right <= 3)
            def _():
                arrived(chunk(right, y, h), frs.at[h, right])
                pl.when(not_first)(lambda: push(right, h, 1))
                push(right, h, 2)

        def across_y(z_):
            arrived(fall.at[at(T * (2 * z_ + 1 - y), T), :], fry.at[z_])
            project_slab(z_, 1 - y)

        pl.when(left >= 0)(lambda: project_slab(left, y))
        pl.when(right <= 3)(lambda: project_slab(right, y))
        pl.when(z - k >= 0)(lambda: across_y(z - k))
        pl.when((k > 0) & (z + k <= 3))(lambda: across_y(z + k))

    sent("frames_y", fall.at[pl.ds(0, 4 * T), :], fss.at[1])
    sent_along_z("frames_z", lambda count: fall.at[pl.ds(0, T * count), :], fss.at[0])

    phase("attention")
    pair_rows = at(T2 * z, T2)
    lane = lax.broadcasted_iota(jnp.int32, (T2, LANES), 1)
    low_half = lane < HD

    def half(value, which):
        return jnp.where(low_half == (which == 0), value, 0.0)

    stat[...] = jnp.zeros_like(stat)
    mine, other = at(T * y, T), at(T * (1 - y), T)

    def heads_push(b):
        part, there = at(LANES * b, LANES), at(HW * y + LANES * b, LANES, LANES)
        return send(att16.at[other, part], attf.at[:, there], hes.at[0], her.at[b], yn)

    def both(value):
        return jnp.concatenate([half(value, 0), half(value, 1)], axis=0).astype(BF16)

    def pick(stacked):
        return jnp.where(low_half, stacked[:T2], stacked[T2:])

    def block_lanes(b):
        return at(LANES * b, LANES), at(HW + LANES * b, LANES, LANES)

    @pl.loop(0, blocks)
    def _(b):
        lanes, value_lanes = block_lanes(b)
        queries = qall[pair_rows, lanes].astype(F32)
        outs = []
        for which in range(2):
            head = 2 * b + which
            scores = dot_nt(half(queries, which).astype(BF16), kv[:, lanes]) + mask[...]
            peak = jnp.max(scores, axis=-1, keepdims=True)
            powers = jnp.exp(scores - peak)
            total = jnp.sum(powers, axis=-1, keepdims=True)
            low = (powers * (1.0 / total)).astype(BF16)
            probs[head] = low
            outs.append(dot(low, kv[:, value_lanes]))
            stat[0] = jnp.where(lane == head, peak + jnp.log(total), stat[0])
        out = jnp.where(low_half, outs[0], outs[1])
        att32[:, lanes] = out
        att16[:, lanes] = out.astype(BF16)
        heads_push(b).start()

    phase("heads_exchange")
    attf[:, heads_here] = att16[mine, :]
    lsed[z, 0:8, :] = stat[0].T[0:8, :]
    loads[3].wait()
    for b in range(blocks):
        arrived(attf.at[:, at(HW * (1 - y) + LANES * b, LANES, LANES)], her.at[b])
    sent("heads", att16.at[pl.ds(0, T), :], hes.at[0])
    phase("out_norm1")
    branch = dot(attf[...], wo[...]) + out_b
    unit, inverse = rows_norm(frames[...] + branch)
    hidden = unit * gain1 + bias1
    unit1[...] = unit
    rstd1[...] = jnp.broadcast_to(inverse, (T, LANES))
    hid32[...] = hidden
    here = at(T * (2 * y + x), T)

    def rows_of(buffer, x_, y_):
        return buffer.at[at(T * (2 * y_ + x_), T), :]

    def halves_of(buffer, x_, y_):
        first = T * (2 * y_ + x_)
        return buffer.at[at(first, T // 2), :], buffer.at[at(first + T // 2, T // 2), :]

    def share_x(buffer, name):
        top, bottom = halves_of(buffer, x, y)
        start(top, top, *one(name + "_x", name), xn)
        start(bottom, bottom, *one(name + "_x_rest", name), xn)

    def share_y(buffer, name):
        top, bottom = halves_of(buffer, x, y)
        start(bottom, bottom, *one(name + "_y", name), yn)
        start(top, top, *one(name + "_y_rest", name), yn)

    def from_x(buffer, name):
        top = halves_of(buffer, 1 - x, y)[0]
        arrived(top, got_of(name + "_x"))
        start(top, top, *one(name + "_top", name), yn)

    def from_y(buffer, name):
        bottom = halves_of(buffer, x, 1 - y)[1]
        arrived(bottom, got_of(name + "_y"))
        start(bottom, bottom, *one(name + "_bottom", name), xn)

    def rest_x(buffer, name):
        arrived(halves_of(buffer, 1 - x, y)[1], got_of(name + "_x_rest"))

    def rest_y(buffer, name):
        arrived(halves_of(buffer, x, 1 - y)[0], got_of(name + "_y_rest"))

    def from_diagonal(buffer, name):
        top, bottom = halves_of(buffer, 1 - x, 1 - y)
        arrived(top, got_of(name + "_top"))
        arrived(bottom, got_of(name + "_bottom"))

    chips = ((1 - x, y), (x, 1 - y), (1 - x, 1 - y), (x, y))

    for buffer, name in ((hq, "hid"), (fq, "ffn")):
        sent(name, buffer.at[pl.ds(0, 3 * T), :], group(name))
    hq[here, :] = hidden.astype(BF16)
    share_x(hq, "hid")
    share_y(hq, "hid")

    phase("up_gelu")
    loads[4].wait()
    scale = 2.0 ** -0.5

    def active(hidden_rows, chip):
        before = dot(hidden_rows, wup[:, at(D * chip, D)]) + up_rows[chip][0:1, :]
        rise = 0.5 * (1.0 + lax.erf(before * scale))
        slope = rise + before * jnp.exp(-0.5 * before * before) * (2.0 * math.pi) ** -0.5
        return (before * rise).astype(BF16), slope

    def grad_before(ffn_rows, chip, slope):
        return (dot_nt(ffn_rows, wdn[at(D * chip, D), :]) * slope).astype(BF16)

    for x_, y_ in chips:
        chip = 2 * y_ + x_
        actives[chip], dgelu[chip] = active(hq[here, :], chip)
    ar[here, :] = actives[2 * y + x]
    phase("down_norm2")
    loads[5].wait()
    fed = hid32[...] + down_b
    for quarter in range(4):
        fed = fed + dot(actives[quarter], wdn[pl.ds(D * quarter, D), :])
    unit2, inverse2 = rows_norm(fed)
    encoded[...] = unit2 * gain2 + bias2
    cot = cotangent[...]
    grad_mid = rows_norm_back(cot * gain2, unit2, inverse2)
    vectors[10:11, :] = jnp.sum(cot * unit2, axis=0, keepdims=True)
    vectors[11:12, :] = jnp.sum(cot, axis=0, keepdims=True)
    gmid[...] = grad_mid
    fq[here, :] = grad_mid.astype(BF16)
    share_x(fq, "ffn")
    share_y(fq, "ffn")
    vectors[9:10, :] = jnp.sum(fq[here, :].astype(F32), axis=0, keepdims=True)
    phase("ffn_back")

    def ffn_back(order):
        x_, y_ = chips[order]
        chip = 2 * y_ + x_
        low = grad_before(fq[here, :], chip, dgelu[chip])
        vectors[pl.ds(5 + chip, 1), :] = jnp.sum(low.astype(F32), axis=0, keepdims=True)
        gmid[...] += dot_nt(low, wup[:, at(D * chip, D)])
        if order == 3:
            br[here, :] = low

    def norm1_back():
        grad_hidden = gmid[...]
        unit = unit1[...]
        grad_first = rows_norm_back(grad_hidden * gain1, unit, rstd1[:, 0:1])
        vectors[3:4, :] = jnp.sum(grad_hidden * unit, axis=0, keepdims=True)
        vectors[4:5, :] = jnp.sum(grad_hidden, axis=0, keepdims=True)
        gfirst[...] = grad_first
        low = grad_first.astype(BF16)
        gbr[mine, :] = low
        vectors[2:3, :] = jnp.sum(low.astype(F32), axis=0, keepdims=True)

    def branch_send():
        start(gbr.at[mine, :], gbr.at[mine, :], *one("gbr"), yn)

    sent("gbr", gbr.at[mine, :], group("gbr"))

    def plane_active(x_, y_):
        rows = at(T * (2 * y_ + x_), T)
        ar[rows, :], slopes[rows, :] = active(hq[rows, :], 2 * y + x)

    def plane_back(x_, y_):
        rows = at(T * (2 * y_ + x_), T)
        br[rows, :] = grad_before(fq[rows, :], 2 * y + x, slopes[rows, :])

    parts = (*(part_down.at[q] for q in range(2)), *(part_up.at[q] for q in range(2)), part_qo, part_kv)
    gots = (*(got_down.at[q] for q in range(2)), *(got_up.at[q] for q in range(2)), got_qo, got_kv)
    given, taken, kept = (give_down, give_up), (take_down, take_up), (keep_down, keep_up)
    HALF = HW // 2
    slab_rows = (FO // 8, FO // 8, D // 8, D // 8, HALF // 4, HALF // 4)

    def part_slab(t, j):
        return parts[t].at[at(slab_rows[t] * j, slab_rows[t]), :]

    outer = (z == 0) | (z == 3)
    near = jnp.where(z < 2, 1 - z, 5 - z)
    inner_there, outer_there = jnp.where(z < 2, 2, 1), jnp.where(z < 2, 3, 0)

    def part_send(t, src, j, to, slot):
        start(src, gots[t].at[slot], zss.at[t], zsr.at[t, slot], device(x, c, y, to))

    def sum_send(t):

        @pl.when(outer)
        def _():
            for j in (outer_there, inner_there, near):
                part_send(t, part_slab(t, j), j, near, j)

        @pl.when(jnp.logical_not(outer))
        def _():
            part_send(t, part_slab(t, near), near, near, z)

    def sum_pass(t):
        @pl.when(jnp.logical_not(outer))
        def _():
            for j, slot in ((outer_there, z), (inner_there, outer_there)):
                got = gots[t].at[j]
                arrived(got, zsr.at[t, j])
                got[...] = (got[...].astype(F32) + part_slab(t, j)[...].astype(F32)).astype(BF16)
                part_send(t, got, j, j, slot)

    def attn_row(t, x_, y_, z_):
        matrix = 3 * x_ if t == QUERY_OUT else 1 + x_
        return D * matrix + HW * y_ + HALF * c + HALF // 4 * z_

    def own_tile(t):
        if t <= DOWN_1:
            return sum_down.at[at(FO * octant(x, c, y) + FO // 2 * t + FO // 8 * z, FO // 8), :]
        if t <= UP_1:
            return sum_up.at[at(D // 2 * (t - UP_0) + D // 8 * z, D // 8), at(FO * octant(x, c, y), FO)]
        return sum_attn.at[at(attn_row(t, x, y, z), HALF // 4), :]

    def sum_end(t):
        total = part_slab(t, z)[...].astype(F32)
        for slot in (jnp.where(outer, near, z), jnp.where(outer, inner_there, near)):
            arrived(gots[t].at[slot], zsr.at[t, slot])
            total = total + gots[t][slot].astype(F32)
        own_tile(t)[...] = total.astype(BF16)

    unit = SIXTEENTH // 3
    unit_rows = (unit, unit, 2 * unit, 2 * unit, unit, unit)

    def tile(u, x_, y_, z_):
        t, _, first, count = PIECES[u]
        rows = unit_rows[t]
        if t <= DOWN_1:
            start_row = FO * octant(x_, c, y_) + FO // 2 * t + FO // 8 * z_ + rows * first
            return sum_down.at[at(start_row, rows * count, rows), :]
        if t <= UP_1:
            start_row = D // 2 * (t - UP_0) + D // 8 * z_ + rows * first
            return sum_up.at[at(start_row, rows * count, rows), at(FO * octant(x_, c, y_), FO)]
        start_row = attn_row(t, x_, y_, z_) + rows * first
        return sum_attn.at[at(start_row, rows * count, rows), :]

    def gather_send(u, place, z_, ssem, rsem, to):
        part = tile(u, *place, z_)
        return send(part, part, ssem, rsem, to)

    def to_sibling(u, place, z_):
        gather_send(u, place, z_, ags.at[u], agdr.at[u], sib).start()

    places = ((x, y), (1 - x, y), (x, 1 - y), (1 - x, 1 - y))

    def order_of(u):
        over_y, over_x = (2, yn), (1, xn)
        return (over_y, over_x) if PIECES[u][1] in ("zyx", "yxz") else (over_x, over_y)

    def z_last(u):
        return PIECES[u][1][2] == "z"

    first_sem = [sum(gather_sems(piece) for piece in PIECES[:u]) for u in range(len(PIECES))]

    def z_sem(u, p, z_, at_z):
        return agr.at[first_sem[u] + 3 * p + lax.rem(z_ - at_z + 4, 4) - 1]

    def along_z(u, p, z_, direction):
        to = (zp, zm)[direction]
        return gather_send(u, places[p], z_, ags.at[u], z_sem(u, p, z_, (z + 1, z - 1)[direction]), to)

    def z_out(u, p):
        pl.when(not_last)(lambda: along_z(u, p, z, 0).start())
        pl.when(not_first)(lambda: along_z(u, p, z, 1).start())

    def as_many(u, count):
        return sum_down.at[pl.ds(0, unit * PIECES[u][3] * count), :]

    def second_sem(u, z_):
        return agr.at[first_sem[u] + (12 if z_last(u) else 3 + z_)]

    def third_sem(u, slot):
        return agr.at[first_sem[u] + (13 if z_last(u) else 7 + lax.rem(slot, 4))]

    def to_second(u, place, z_):
        gather_send(u, place, z_, ags.at[u], second_sem(u, z_), order_of(u)[0][1]).start()

    def to_third(u, place, slot):
        z_ = z if z_last(u) else lax.rem(slot, 4)
        gather_send(u, place, z_, ags.at[u], third_sem(u, slot), order_of(u)[1][1]).start()

    def gather_own(t):
        for u in pieces_of(t, False):
            z_out(u, 0)
        for u in pieces_of(t):
            to_second(u, places[0], z)
            to_third(u, places[0], 0 if z_last(u) else z)
            to_sibling(u, places[0], z)

    def pieces_of(t, last=None):
        return [u for u in range(len(PIECES)) if PIECES[u][0] == t and last in (None, z_last(u))]

    def sides(k, take):
        pl.when(z - k >= 0)(lambda: take(z - k, not_last, 0))
        if k > 0:
            pl.when(z + k <= 3)(lambda: take(z + k, not_first, 1))

    def gather_z(t, k):
        for u in pieces_of(t, False):

            def take(z_, more, direction):
                arrived(tile(u, *places[0], z_), z_sem(u, 0, z_, z))
                pl.when(more)(lambda: along_z(u, 0, z_, direction).start())
                to_second(u, places[0], z_)
                to_third(u, places[0], z_)
                to_sibling(u, places[0], z_)

            sides(k, take)

    def gather_second(t, k):
        for u in pieces_of(t, False):

            def take(z_, more, direction):
                place = places[order_of(u)[0][0]]
                arrived(tile(u, *place, z_), second_sem(u, z_))
                to_third(u, place, 4 + z_)
                to_sibling(u, place, z_)

            sides(k, take)

    def gather_third(t, k):
        for u in pieces_of(t, False):

            def take(z_, more, direction):
                arrived(as_many(u, 2), third_sem(u, z_))
                for p in (order_of(u)[1][0], 3):
                    to_sibling(u, places[p], z_)

            sides(k, take)

    def plane_first(t):
        for u in pieces_of(t, True):
            p = order_of(u)[0][0]
            arrived(tile(u, *places[p], z), second_sem(u, z))
            to_third(u, places[p], 1)
            to_sibling(u, places[p], z)

    def plane_second(t):
        for u in pieces_of(t, True):
            arrived(as_many(u, 2), third_sem(u, 0))
            for p in (order_of(u)[1][0], 3):
                to_sibling(u, places[p], z)

    def plane_out(t):
        for u in pieces_of(t, True):
            for p in (0, order_of(u)[0][0], order_of(u)[1][0], 3):
                z_out(u, p)

    def plane_z(t, k):
        for u in pieces_of(t, True):
            for p in (0, order_of(u)[0][0], order_of(u)[1][0], 3):

                def take(z_, more, direction):
                    arrived(tile(u, *places[p], z_), z_sem(u, p, z_, z))
                    pl.when(more)(lambda: along_z(u, p, z_, direction).start())
                    to_sibling(u, places[p], z_)

                sides(k, take)

    def gather_end():
        for u in range(len(PIECES)):
            arrived(as_many(u, 16), agdr.at[u])
            if z_last(u):
                sent_along_z(("gather", u), partial(as_many, u), ags.at[u], 19, 4)
            else:
                sent_along_z(("gather", u), partial(as_many, u), ags.at[u], 28)

    def matrix_put(family, x_, value):
        for half_ in range(2):
            gm[family, half_, x_] = value[HALF * half_ : HALF * (half_ + 1), :].astype(BF16)

    def matrices_send(family):
        start(gm.at[family, 1 - c], dr.at[family], *one(("d", family)), sib)

    def out_back():
        arrived(gbr.at[other, :], got_of("gbr"))
        da = dot_nt(gbr[...], wo[heads_here, :]).astype(BF16)
        doall[pair_rows, :] = da
        product = da.astype(F32) * att32[...]
        stat[1] = jnp.zeros((T2, LANES), F32)
        for head in range(2 * blocks):
            lanes = slice(LANES * (head // 2), LANES * (head // 2 + 1))
            delta = jnp.sum(half(product[:, lanes], head % 2), axis=-1, keepdims=True)
            stat[1] = jnp.where(lane == head, delta, stat[1])
        lsed[z, 8:16, :] = stat[1].T[0:8, :]
        pl.when(not_last)(lambda: grads_push(z, zp))
        pl.when(not_first)(lambda: grads_push(z, zm))
        matrix_put(0, 1, dot_tn(att16[...], gbr[...]))

    def grads_rows(z_):
        return doall.at[at(T2 * z_, T2), :], lsed.at[z_]

    def grads_push(z_, to):
        for index, ref in enumerate(grads_rows(z_)):
            start(ref, ref, dos.at[index], dor.at[index, z_], to)

    sent_along_z("grads", lambda count: fall.at[pl.ds(0, T * count), :], dos.at[0])
    sent_along_z("logs", lambda count: lsed.at[pl.ds(0, count)], dos.at[1])

    def grads_arrive(k):
        def take(z_, more, direction):
            for index, ref in enumerate(grads_rows(z_)):
                arrived(ref, dor.at[index, z_])
            pl.when(more)(lambda: grads_push(z_, (zp, zm)[direction]))

        sides(k, take)

    def queries_back():
        @pl.loop(0, blocks)
        def _(b):
            lanes, value_lanes = block_lanes(b)
            heads = doall[pair_rows, lanes].astype(F32)
            product = heads * att32[:, lanes]
            pieces = []
            for which in range(2):
                delta = jnp.sum(half(product, which), axis=-1, keepdims=True)
                grad_probs = dot_nt(half(heads, which).astype(BF16), kv[:, value_lanes])
                grad_scores = probs[2 * b + which].astype(F32) * (grad_probs - delta)
                pieces.append(dot(grad_scores.astype(BF16), kv[:, lanes]))
            total = jnp.where(low_half, pieces[0], pieces[1]) * HD ** (-0.5)
            dall[:, lanes] = total.astype(BF16)

    def keys_back(z_):
        rows = at(T2 * z_, T2)

        @pl.loop(0, blocks)
        def _(b):
            lanes, value_lanes = block_lanes(b)
            queries, grads = qall[rows, lanes], doall[rows, lanes]
            scores = dot_nt(both(kv[pair_rows, lanes].astype(F32)), queries)
            grad_probs = dot_nt(both(kv[pair_rows, value_lanes].astype(F32)), grads)
            lows, grad_scores = [], []
            for which in range(2):
                part, head = slice(T2 * which, T2 * (which + 1)), 2 * b + which
                powers = jnp.exp(scores[part] + mask[:, rows] - lsed[z_, pl.ds(head, 1), :])
                shifted = grad_probs[part] - lsed[z_, pl.ds(8 + head, 1), :]
                lows.append(powers.astype(BF16))
                grad_scores.append((powers * shifted).astype(BF16))
            dkv32[:, lanes] += pick(dot(jnp.concatenate(grad_scores, axis=0), queries))
            dkv32[:, value_lanes] += pick(dot(jnp.concatenate(lows, axis=0), grads))

    def keys_back_at(k):
        pl.when(z - k >= 0)(lambda: keys_back(z - k))
        if k > 0:
            pl.when(z + k <= 3)(lambda: keys_back(z + k))

    def query_weights():
        matrix_put(0, 0, dot_tn(dall[:, pl.ds(0, HW)], fall[pair_rows, :]))
        matrices_send(0)

    def key_value_weights():
        dall[:, pl.ds(HW, D)] = dkv32[...].astype(BF16)
        grads = dot_tn(dall[:, pl.ds(HW, D)], fall[pair_rows, :])
        matrix_put(1, 0, grads[:HW, :])
        matrix_put(1, 1, grads[HW:, :])
        matrices_send(1)

    def input_grad():
        into = dot_nt(dall[...], wqkv[...])
        dxo[...] = into
        dxs[...] = dxo[other, :].astype(BF16)
        start(dxs, dxr, *one("dx"), yn)
        sums = jnp.sum(dall[...].astype(F32), axis=0, keepdims=True)
        vectors[0:1, heads_here] = sums[:, :HW]
        vectors[1:2, heads_here] = sums[:, 2 * HW :]

    def input_grad_end():
        arrived(dxr, got_of("dx"))
        frames_grad[...] = gfirst[...] + dxo[mine, :] + dxr[...].astype(F32)

    def attention_x(family):
        arrived(dr.at[family], got_of(("d", family)))
        xs[family] = (gm[family, c, 1 - x].astype(F32) + dr[family, 1 - x].astype(F32)).astype(BF16)
        start(xs.at[family], xr.at[family], *one(("xs", family)), xn)

    def attention_z(family):
        arrived(xr.at[family], got_of(("xs", family)))
        total = gm[family, c, x].astype(F32) + dr[family, x].astype(F32) + xr[family].astype(F32)
        parts[4 + family][...] = total.astype(BF16)
        sum_send(4 + family)

    def pair_half(t, half_):
        columns = at(FO * half_, FO)
        if t == DOWN:
            return dot_tn(ar[:, columns], fq[...])
        return dot_tn(hq[...], br[:, columns])

    def pair_send(t):
        half_ = pair_half(t, 1 - c).astype(BF16)
        rows = half_.shape[0] // 2
        for q in range(2):
            given[t][q] = half_[rows * q : rows * (q + 1)]
            start(given[t].at[q], taken[t].at[q], *one(("pair", t, q), ("pair", t)), sib)
        half_ = pair_half(t, c)
        for q in range(2):
            kept[t][q] = half_[rows * q : rows * (q + 1)]

    def pair_add(family):
        t, q = family // 2, family % 2
        arrived(taken[t].at[q], got_of(("pair", t, q)))
        parts[family][...] = (kept[t][q] + taken[t][q].astype(F32)).astype(BF16)
        sum_send(family)

    def vector_step(i, to):
        vsend[i] = vectors[...]
        start(vsend.at[i], vrecv.at[i], *one(("v", i)), to)

    def vector_add(i):
        arrived(vrecv.at[i], got_of(("v", i)))
        vectors[...] += vrecv[i]

    def vector_z():
        vsend[3] = vectors[...]
        vz[z] = vectors[...]
        for k in (1, 2, 3):
            j = lax.rem(z + k, 4)
            start(vsend.at[3], vz.at[z], vzs.at[0], vzr.at[z], device(x, c, y, j))

    def vector_end():
        for k in (1, 2, 3):
            j = lax.rem(z + k, 4)
            arrived(vz.at[j], vzr.at[j])
        vectors[...] = (vz[0] + vz[1]) + (vz[2] + vz[3])

    dkv32[...] = jnp.zeros_like(dkv32)
    for t in range(6):
        sent(("sum", t), parts[t].at[pl.ds(0, 3 * slab_rows[t]), :], zss.at[t])
    for t in (DOWN, UP):
        sent(("pair", t), given[t], group(("pair", t)))
    sent("dx", dxs, group("dx"))
    for family in range(2):
        sent(("d", family), dr.at[family], group(("d", family)))
        sent(("xs", family), xs.at[family], group(("xs", family)))
    for i in range(3):
        sent(("v", i), vsend.at[i], group(("v", i)))
    sent("vz", vz.at[pl.ds(0, 3)], vzs.at[0])
    ffn_back(0)
    from_y(hq, "hid")
    ffn_back(1)
    ffn_back(2)
    from_y(fq, "ffn")
    ffn_back(3)
    norm1_back()
    branch_send()
    from_x(hq, "hid")
    out_back()
    rest_y(fq, "ffn")
    rest_y(hq, "hid")
    plane_active(x, 1 - y)
    rest_x(hq, "hid")
    from_x(fq, "ffn")
    queries_back()
    plane_active(1 - x, y)
    from_diagonal(hq, "hid")
    query_weights()
    plane_active(1 - x, 1 - y)
    from_diagonal(fq, "ffn")
    rest_x(fq, "ffn")
    pair_send(DOWN)
    grads_arrive(1)
    attention_x(0)
    pair_add(DOWN_1)
    plane_back(1 - x, 1 - y)
    keys_back_at(1)
    pair_add(DOWN_0)
    plane_back(1 - x, y)
    sum_pass(DOWN_1)
    grads_arrive(2)
    plane_back(x, 1 - y)
    keys_back_at(2)
    pair_send(UP)
    sum_pass(DOWN_0)
    sum_end(DOWN_1)
    gather_own(DOWN_1)
    keys_back_at(0)
    pair_add(UP_0)
    sum_end(DOWN_0)
    gather_own(DOWN_0)
    gather_second(DOWN_1, 0)
    plane_first(DOWN_1)
    grads_arrive(3)
    keys_back_at(3)
    key_value_weights()
    gather_z(DOWN_1, 1)
    pair_add(UP_1)
    gather_second(DOWN_0, 0)
    sum_pass(UP_0)
    attention_z(0)
    gather_z(DOWN_0, 1)
    attention_x(1)
    input_grad()
    vector_step(0, sib)
    sum_pass(UP_1)
    gather_z(DOWN_1, 2)
    sum_pass(QUERY_OUT)
    sum_end(UP_0)
    gather_own(UP_0)
    gather_third(DOWN_1, 0)
    sum_end(UP_1)
    gather_own(UP_1)
    gather_z(DOWN_0, 2)
    sum_end(QUERY_OUT)
    vector_add(0)
    gather_z(DOWN_1, 3)
    gather_own(QUERY_OUT)
    plane_second(DOWN_1)
    gather_z(UP_1, 1)
    vector_step(1, xn)
    attention_z(1)
    gather_z(QUERY_OUT, 1)
    plane_first(QUERY_OUT)
    input_grad_end()
    gather_second(DOWN_0, 1)
    gather_z(DOWN_0, 3)
    gather_z(QUERY_OUT, 2)
    gather_z(UP_0, 1)
    gather_z(UP_1, 2)
    sum_pass(KEY_VALUE)
    gather_z(UP_1, 3)
    gather_z(UP_0, 2)
    sum_end(KEY_VALUE)
    gather_own(KEY_VALUE)
    plane_out(DOWN_1)
    gather_second(UP_0, 1)
    gather_second(QUERY_OUT, 1)
    gather_second(DOWN_0, 3)
    gather_second(UP_1, 1)
    gather_second(QUERY_OUT, 2)
    gather_z(QUERY_OUT, 3)
    plane_z(DOWN_1, 1)
    gather_second(UP_1, 2)
    gather_second(QUERY_OUT, 0)
    gather_z(UP_0, 3)
    plane_second(QUERY_OUT)
    vector_add(1)
    gather_second(DOWN_1, 3)
    gather_second(UP_0, 0)
    gather_second(QUERY_OUT, 3)
    vector_step(2, yn)
    gather_z(KEY_VALUE, 1)
    plane_out(QUERY_OUT)
    gather_second(UP_0, 2)
    gather_second(UP_1, 3)
    gather_third(DOWN_0, 3)
    gather_third(QUERY_OUT, 2)
    gather_z(KEY_VALUE, 2)
    gather_z(KEY_VALUE, 3)
    gather_second(DOWN_1, 1)
    gather_second(UP_1, 0)
    plane_z(DOWN_1, 2)
    gather_third(UP_0, 1)
    plane_z(QUERY_OUT, 1)
    gather_third(UP_1, 1)
    gather_third(DOWN_0, 0)
    gather_third(DOWN_1, 3)
    gather_second(DOWN_0, 2)
    gather_second(UP_0, 3)
    gather_third(UP_0, 2)
    gather_third(UP_0, 0)
    gather_second(KEY_VALUE, 1)
    plane_z(DOWN_1, 3)
    vector_add(2)
    gather_third(QUERY_OUT, 1)
    gather_third(QUERY_OUT, 3)
    gather_third(UP_1, 3)
    gather_third(UP_1, 2)
    gather_third(QUERY_OUT, 0)
    gather_second(KEY_VALUE, 0)
    plane_z(QUERY_OUT, 2)
    gather_second(DOWN_1, 2)
    gather_third(DOWN_1, 1)
    vector_z()
    gather_second(KEY_VALUE, 2)
    gather_third(UP_1, 0)
    gather_third(UP_0, 3)
    gather_third(DOWN_0, 2)
    gather_second(KEY_VALUE, 3)
    gather_third(DOWN_0, 1)
    gather_third(KEY_VALUE, 1)
    gather_third(KEY_VALUE, 0)
    plane_z(QUERY_OUT, 3)
    gather_third(DOWN_1, 2)
    gather_third(KEY_VALUE, 2)
    gather_third(KEY_VALUE, 3)
    vector_end()
    phase("gather_end")
    gather_end()
    phase("sends_end")
    assert (len(send_names), len(names)) == (mss.shape[0], msr.shape[0])
    for wait in waits.values():
        wait()
    phase(None)


def fused_layer(
    frames,
    clip_lengths,
    query_weight,
    query_bias,
    key_weight,
    value_weight,
    value_bias,
    out_weight,
    out_bias,
    norm1_gain,
    norm1_bias,
    up_weight,
    up_bias,
    down_weight,
    down_bias,
    norm2_gain,
    norm2_bias,
    cotangent,
):
    T, D = frames.shape[1], frames.shape[2]
    F = up_weight.shape[1]
    S = T * lax.axis_size("seq")
    HW, T2, EIGHTH, FO = D // 2, 2 * T, D // 8, F // 8
    blocks = HW // LANES
    entries = clip_lengths.shape[1]
    vmem, hbm = pl.BlockSpec(memory_space=pltpu.VMEM), pl.BlockSpec(memory_space=pl.ANY)
    dma, n = pltpu.SemaphoreType.DMA, len(PIECES)
    low, wide = (lambda *shape: pltpu.VMEM(shape, BF16)), (lambda *shape: pltpu.VMEM(shape, F32))
    scratch = dict(
        frames_v=wide(T, D),
        cotangent_v=wide(T, D),
        lengths_v=pltpu.VMEM((1, entries), jnp.int32),
        **{f"v{i}": wide(D) for i in range(8)},
        up_v=wide(F),
        bias_rows=wide(8, D),
        up_rows=wide(4, 8, D),
        fall=low(S, D),
        wqkv=low(D, 3 * HW),
        wo=low(D, D),
        wup=low(D, F),
        wdn=low(F, D),
        qall=low(S, HW),
        kv=low(S, D),
        mask=wide(T2, S),
        probs=low(2 * blocks, T2, S),
        stat=wide(2, T2, LANES),
        lsed=wide(5, 16, T2),
        att32=wide(T2, HW),
        att16=low(T2, HW),
        attf=low(T, D),
        hq=low(4 * T, D),
        fq=low(4 * T, D),
        ar=low(4 * T, D),
        br=low(4 * T, D),
        actives=low(4, T, D),
        slopes=wide(4 * T, D),
        dgelu=wide(4, T, D),
        hid32=wide(T, D),
        unit1=wide(T, D),
        rstd1=wide(T, LANES),
        gmid=wide(T, D),
        gfirst=wide(T, D),
        gbr=low(T2, D),
        doall=low(S, HW),
        dkv32=wide(T2, D),
        dall=low(T2, 3 * HW),
        give_down=low(2, FO // 2, D),
        give_up=low(2, D // 2, FO),
        take_down=low(2, FO // 2, D),
        take_up=low(2, D // 2, FO),
        keep_down=wide(2, FO // 2, D),
        keep_up=wide(2, D // 2, FO),
        part_down=low(2, FO // 2, D),
        part_up=low(2, D // 2, FO),
        part_qo=low(HW // 2, D),
        part_kv=low(HW // 2, D),
        got_down=low(2, 4, FO // 8, D),
        got_up=low(2, 4, D // 8, FO),
        got_qo=low(4, HW // 8, D),
        got_kv=low(4, HW // 8, D),
        gm=low(2, 2, 2, HW // 2, D),
        dr=low(2, 2, HW // 2, D),
        xs=low(2, HW // 2, D),
        xr=low(2, HW // 2, D),
        dxs=low(T, D),
        dxr=low(T, D),
        dxo=wide(T2, D),
        vsend=wide(4, 16, D),
        vrecv=wide(3, 16, D),
        vz=wide(4, 16, D),
        wsem=dma((6,)),
        asem=dma((4,)),
        hes=dma((1,)),
        her=dma((blocks,)),
        frs=dma((CHUNKS, 4)),
        fry=dma((4,)),
        fss=dma((2,)),
        msr=dma((25,)),
        mss=dma((13,)),
        dor=dma((2, 4)),
        dos=dma((2,)),
        zsr=dma((6, 4)),
        zss=dma((6,)),
        agr=dma((sum(map(gather_sems, PIECES)),)),
        ags=dma((n,)),
        agdr=dma((n,)),
        vzr=dma((4,)),
        vzs=dma((1,)),
    )
    results = pl.pallas_call(
        partial(layer_kernel, T, D, S, entries),
        out_shape=(
            pltpu.VMEM((T, D), F32),
            pltpu.VMEM((T, D), F32),
            pltpu.VMEM((16, D), F32),
            pltpu.VMEM((F, D), BF16),
            pltpu.VMEM((D, F), BF16),
            pltpu.VMEM((4 * D, D), BF16),
        ),
        in_specs=[hbm] * 18,
        out_specs=(vmem,) * 6,
        scratch_shapes=list(scratch.values()),
        compiler_params=pltpu.CompilerParams(
            collective_id=0, has_side_effects=True, vmem_limit_bytes=VMEM_GRANT
        ),
        name="layer",
    )(
        frames[0],
        cotangent[0],
        clip_lengths,
        query_weight,
        key_weight,
        value_weight,
        out_weight,
        up_weight,
        down_weight,
        query_bias,
        value_bias,
        out_bias,
        norm1_gain,
        norm1_bias,
        up_bias,
        down_bias,
        norm2_gain,
        norm2_bias,
    )
    return widen(*results)


def widen_kernel(
    last,
    T,
    D,
    encoded,
    frames_grad,
    vectors,
    down,
    up,
    attn,
    encoded_out,
    frames_grad_out,
    query_out,
    query_b,
    key_out,
    value_out,
    value_b,
    out_out,
    out_b,
    gain1,
    bias1,
    up_out,
    up_b,
    down_out,
    down_b,
    gain2,
    bias2,
    sems,
):
    step = pl.program_id(0)
    copies = [
        pltpu.make_async_copy(encoded, encoded_out, sems.at[0]),
        pltpu.make_async_copy(frames_grad, frames_grad_out, sems.at[1]),
    ]

    @pl.when(step == 0)
    def _():
        for copy in copies:
            copy.start()
        for ref, index in (
            (query_b, 0),
            (value_b, 1),
            (out_b, 2),
            (gain1, 3),
            (bias1, 4),
            (down_b, 9),
            (gain2, 10),
            (bias2, 11),
        ):
            ref[...] = vectors[index : index + 1, :].reshape(D)
        for quarter in range(4):
            up_b[pl.ds(D * quarter, D)] = vectors[5 + quarter : 6 + quarter, :].reshape(D)

    def rows(size, first=0):
        return pl.ds(pl.multiple_of(first + size * step, size), size)

    down_out[...] = down[rows(down_out.shape[0]), :].astype(F32)
    up_out[...] = up[rows(up_out.shape[0]), :].astype(F32)
    out_out[...] = attn[rows(LANES, 3 * D), :].astype(F32)
    for m, target in enumerate((query_out, key_out, value_out)):
        target[...] = attn[rows(LANES, m * D), :].astype(F32).T

    @pl.when(step == last)
    def _():
        for copy in copies:
            copy.wait()


def widen(encoded, frames_grad, vectors, sum_down, sum_up, sum_attn):
    T, D = encoded.shape
    F = sum_up.shape[1]
    steps = D // LANES
    hbm, vmem = pl.BlockSpec(memory_space=pl.ANY), pl.BlockSpec(memory_space=pltpu.VMEM)
    parts = (encoded, frames_grad, vectors, sum_down, sum_up, sum_attn)
    parts = [pltpu.with_memory_space_constraint(part, pltpu.VMEM) for part in parts]

    def down(width):
        return pl.BlockSpec((width, D), lambda i: (i, 0))

    up = pl.BlockSpec((D // steps, F), lambda i: (i, 0))
    turned = pl.BlockSpec((D, LANES), lambda i: (0, i))
    flat = pl.BlockSpec((D,), lambda i: (0,))
    wide_flat = pl.BlockSpec((F,), lambda i: (0,))
    square, vector = jax.ShapeDtypeStruct((D, D), F32), jax.ShapeDtypeStruct((D,), F32)
    tokens = jax.ShapeDtypeStruct((T, D), F32)
    outs = (
        (tokens, hbm),
        (tokens, hbm),
        (square, turned),
        (vector, flat),
        (square, turned),
        (square, turned),
        (vector, flat),
        (square, down(LANES)),
        (vector, flat),
        (vector, flat),
        (vector, flat),
        (jax.ShapeDtypeStruct((D, F), F32), up),
        (jax.ShapeDtypeStruct((F,), F32), wide_flat),
        (jax.ShapeDtypeStruct((F, D), F32), down(F // steps)),
        (vector, flat),
        (vector, flat),
        (vector, flat),
    )
    results = pl.pallas_call(
        partial(widen_kernel, steps - 1, T, D),
        grid=(steps,),
        out_shape=tuple(shape for shape, _ in outs),
        in_specs=[vmem] * 6,
        out_specs=tuple(spec for _, spec in outs),
        scratch_shapes=[pltpu.SemaphoreType.DMA((2,))],
        compiler_params=pltpu.CompilerParams(vmem_limit_bytes=VMEM_GRANT),
        name="widen",
    )(*parts)
    return (results[0][None], results[1][None]) + tuple(results[2:])


def solution(mesh):
    in_specs = (
        P("row", "seq", None),
        P("row", None),
        P(),
        P(),
        P(),
        P(),
        P(),
        P(),
        P(),
        P(),
        P(),
        P(),
        P(),
        P(),
        P(),
        P(),
        P(),
        P("row", "seq", None),
    )
    out_specs = (
        P("row", "seq", None),
        P("row", "seq", None),
        P(),
        P(),
        P(),
        P(),
        P(),
        P(),
        P(),
        P(),
        P(),
        P(),
        P(),
        P(),
        P(),
        P(),
        P(),
    )
    shape = dict(mesh.shape)
    fused = shape["row"] == 4 and shape["seq"] == 8
    return jax.shard_map(
        fused_layer if fused else per_device, mesh=mesh, in_specs=in_specs, out_specs=out_specs, check_vma=False
    )
```
